32 devices in a mesh: expert: 2 (over x), tensor: 4 (over y, core), dp: 4 (over z).
Axes of the slice: x: 2, y: 2, z: 4, core: 2. Of those that a mesh axis runs over, the one named last changes fastest.
Arguments:
- tokens: bfloat16 [4096, 1024], P(('expert', 'dp')), may hold values from -6 to 6
- cotangent: bfloat16 [4096, 1024], P(('expert', 'dp')), may hold values from -6 to 6
- seq_lengths: int32 [2, 4], P('expert'), may hold values from 1 to 512, 1536 in all within a row
- deal_order: int32 [2, 4], P('expert'), may hold values from 0 to 3, each once within a row
- routes: int32 [4096, 8], P(('expert', 'dp')), may hold values from 0 to 31, all different within a row
- slot_order: int32 [8, 4096], P(('expert', 'dp')), may hold values from 0 to 4095, each once within a row
- first_gain: bfloat16 [1024], replicated, may hold values from 0.5 to 1.5
- w_query: bfloat16 [1024, 1024], P(None, 'tensor'), may hold values from -0.1875 to 0.1875
- w_key: bfloat16 [1024, 512], P(None, 'tensor'), may hold values from -0.1875 to 0.1875
- w_value: bfloat16 [1024, 512], P(None, 'tensor'), may hold values from -0.1875 to 0.1875
- w_out: bfloat16 [1024, 1024], P('tensor'), may hold values from -3 to 3
- second_gain: bfloat16 [1024], replicated, may hold values from 0.5 to 1.5
- w_router: bfloat16 [1024, 32], replicated, may hold values from -0.09375 to 0.09375
- w_gate: bfloat16 [32, 1024, 512], P('expert', None, 'tensor'), may hold values from -0.1875 to 0.1875
- w_up: bfloat16 [32, 1024, 512], P('expert', None, 'tensor'), may hold values from -0.1875 to 0.1875
- w_down: bfloat16 [32, 512, 1024], P('expert', 'tensor'), may hold values from -1 to 1
Outputs:
- block_out: bfloat16 [4096, 1024], P(('expert', 'dp'), 'tensor')
- input_grad: bfloat16 [4096, 1024], P(('expert', 'dp'), 'tensor')
- first_gain_grad: float32 [1024], replicated
- query_grad: float32 [1024, 1024], P(None, 'tensor')
- key_grad: float32 [1024, 512], P(None, 'tensor')
- value_grad: float32 [1024, 512], P(None, 'tensor')
- out_grad: float32 [1024, 1024], P('tensor')
- second_gain_grad: float32 [1024], replicated
- router_grad: float32 [1024, 32], replicated
- gate_grad: float32 [32, 1024, 512], P('expert', None, 'tensor')
- up_grad: float32 [32, 1024, 512], P('expert', None, 'tensor')
- down_grad: float32 [32, 512, 1024], P('expert', 'tensor')
The draws below stay inside these ranges and needn't reach their ends.
Inputs may be any that keep to these rules, and one draw needn't show every extreme that they name: `seq_lengths`: in each row the lengths sum to 1536. `deal_order`: each row is a permutation of the 4 sequences of one group. `routes`: a row's 8 experts are distinct. `slot_order`: each row is a permutation of the 4096 entries of one unit.
All inputs are finite; a program needn't handle non-finite values.
Results may differ from the reference program's by a relative error of at most 0.018.
Values may be sent and summed in bfloat16 or wider, within the bound.
A program may use at most 192 MiB of HBM per device.

```python
import math
import jax
import jax.numpy as jnp
import numpy as np
from jax import lax

D = 1024
HEADS = 16
KV_HEADS = 8
HEAD_DIM = 64
EXPERTS = 32
TOP = 8
FF = 512
SLOT = 512
SEQ_DEV = 1
TOK_DEV = 512
DEAL_GROUPS = 2
DEAL = 4
GROUPS = 8
TOKENS = 4096
HID_PARTS = 4


def level_of(own_key, dims, split, low, largest):
    factor_of = 1.0
    for position, shards_of in split:
        draws = jax.random.uniform(jax.random.fold_in(jax.random.fold_in(own_key, 6), position), (shards_of,), jnp.float32, low / len(split), largest / len(split))
        factor_of = factor_of * jnp.repeat(jnp.exp(draws), dims[position] // shards_of).reshape((-1,) + (1,) * (len(dims) - 1 - position))
    return factor_of


def different_ones(key, rows, number_of, top, lift):
    ranking = jax.random.permutation(jax.random.fold_in(key, 1), number_of)
    boost = ranking
    for power in range(3):
        boost = boost * boost // number_of
    boost = boost * lift // number_of
    lots = jax.random.randint(jax.random.fold_in(key, 2), (rows, number_of), 0, 4096) + boost
    sure = jax.random.permutation(jax.random.fold_in(key, 3), rows)[jnp.arange(number_of) % rows]
    lots = jnp.where(jnp.arange(rows)[:, None] == sure[None, :], 1 << 14, lots)
    priority = lots * number_of + jnp.arange(number_of)
    return lax.top_k(priority.astype(jnp.int32), top)[1].astype(jnp.int32)


def length_profile(amount, total, limit, lean):
    portions = [(1 << 20) // math.isqrt(standing ** lean) + 1 for standing in range(2, amount + 1)]
    surplus, holding = total - limit - (amount - 1), [1] * (amount - 1)
    while surplus > 0:
        free = [i for i in range(amount - 1) if holding[i] < limit]
        whole, left = sum([portions[i] for i in free]), surplus
        for i in free:
            more = min(limit - holding[i], max(1, left * portions[i] // whole), surplus)
            holding[i] = holding[i] + more
            surplus = surplus - more
    return np.array([limit] + holding)


def uneven(stream_key, amount, total, bound, lean):
    if amount == 2:
        one = jax.random.randint(stream_key, (), max(1, total - bound), min(bound, total - 1) + 1)
        return jnp.stack([one, total - one])
    sizes = jnp.asarray(length_profile(amount, total, bound, lean), jnp.int32)
    couples = (amount - 1) // 2
    source_of, sink = sizes[1:1 + 2 * couples:2], sizes[2:2 + 2 * couples:2]
    margin = jnp.minimum(source_of - 1, bound - sink)
    shifted = jax.random.randint(jax.random.fold_in(stream_key, 1), (couples,), 0, 1 << 20) % (margin + 1)
    sizes = sizes.at[1:1 + 2 * couples:2].set(source_of - shifted).at[2:2 + 2 * couples:2].set(sink + shifted)
    return sizes[jax.random.permutation(jax.random.fold_in(stream_key, 2), amount)]


def centred(stream_key, shape, scale, reach, cuts=(), held_as=jnp.bfloat16):
    array = scale * jax.random.normal(stream_key, shape, jnp.float32)
    if cuts:
        array = array * level_of(stream_key, shape, cuts, -0.22, 0.18)
    return jnp.clip(array, -reach, reach).astype(held_as)


def setup_inputs(seed: int = 0) -> dict:
    streams_of = jax.random.split(jax.random.key(seed), 17)
    tokens = centred(streams_of[0], (TOKENS, D), 1.0, 6.0, ((0, 8),))
    cotangent = centred(streams_of[1], (TOKENS, D), 1.0, 6.0, ((0, 8),))
    seq_lengths = jax.vmap(lambda own: uneven(own, DEAL, 3 * DEAL * SLOT // 4, SLOT, 0))(jax.random.split(streams_of[2], DEAL_GROUPS)).reshape((DEAL_GROUPS, DEAL)).astype(jnp.int32)
    deal_order = jax.vmap(lambda own: jax.random.permutation(own, DEAL))(jax.random.split(streams_of[3], DEAL_GROUPS)).reshape((DEAL_GROUPS, DEAL)).astype(jnp.int32)
    routes = different_ones(streams_of[4], TOKENS, EXPERTS, TOP, 2048)
    slot_order = jax.vmap(lambda own: jax.random.permutation(own, TOK_DEV * TOP))(jax.random.split(streams_of[5], GROUPS)).reshape((GROUPS, TOK_DEV * TOP)).astype(jnp.int32)
    first_gain = jnp.clip(1.0 + 0.1 * jax.random.normal(streams_of[6], (D,), jnp.float32), 0.5, 1.5).astype(jnp.bfloat16)
    w_query = centred(streams_of[7], (D, HEADS * HEAD_DIM), D ** -0.5, 0.1875, ((1, 4),))
    w_key = centred(streams_of[8], (D, KV_HEADS * HEAD_DIM), D ** -0.5, 0.1875, ((1, 4),))
    w_value = centred(streams_of[9], (D, KV_HEADS * HEAD_DIM), D ** -0.5, 0.1875, ((1, 4),))
    w_out = centred(streams_of[10], (HEADS * HEAD_DIM, D), (max(4, D // 256)) ** -0.5, 3.0, ((0, 4),))
    second_gain = jnp.clip(1.0 + 0.1 * jax.random.normal(streams_of[11], (D,), jnp.float32), 0.5, 1.5).astype(jnp.bfloat16)
    w_router = centred(streams_of[12], (D, EXPERTS), (4 * D) ** -0.5, 0.09375)
    w_gate = centred(streams_of[13], (EXPERTS, D, FF), D ** -0.5, 0.1875, ((0, 2), (2, 4)))
    w_up = centred(streams_of[14], (EXPERTS, D, FF), D ** -0.5, 0.1875, ((0, 2), (2, 4)))
    w_down = centred(streams_of[15], (EXPERTS, FF, D), (FF // 16) ** -0.5, 1.0, ((0, 2), (1, 4)))
    return dict(tokens=tokens, cotangent=cotangent, seq_lengths=seq_lengths, deal_order=deal_order, routes=routes, slot_order=slot_order, first_gain=first_gain, w_query=w_query, w_key=w_key, w_value=w_value, w_out=w_out, second_gain=second_gain, w_router=w_router, w_gate=w_gate, w_up=w_up, w_down=w_down)


EPS = 1e-06
THETA = 10000.0
NEG = -1e+30
HIGH = lax.Precision.HIGHEST

@jax.custom_vjp
def low(v):
    return lax.optimization_barrier(v.astype(jnp.bfloat16)).astype(jnp.float32)

@jax.custom_vjp
def low_back(v):
    return v

def low_keep(v):
    return (low(v), None)

def low_pass(kept, grad):
    return (grad,)

def back_keep(v):
    return (v, None)

def back_low(kept, grad):
    return (low(grad),)
low.defvjp(low_keep, low_pass)
low_back.defvjp(back_keep, back_low)

def product(left_side, right_side):
    return jnp.dot(left_side, right_side, precision=HIGH, preferred_element_type=jnp.float32)

def rms_scale(values):
    return lax.rsqrt(lax.optimization_barrier(jnp.mean(values * values, axis=-1, keepdims=True)) + EPS)

def rotate(values, direction):
    row_count, head_count, head_width = values.shape
    halfway = head_width // 2
    places = (jnp.arange(row_count, dtype=jnp.int32) % SLOT).astype(jnp.float32)
    spread = THETA ** (-2.0 * jnp.arange(halfway, dtype=jnp.float32) / head_width)
    angles = places[:, None] * spread[None, :]
    cosine = jnp.cos(angles)[:, None, :]
    sine_part = direction * jnp.sin(angles)[:, None, :]
    lower_half = values[..., :halfway]
    upper_half = values[..., halfway:]
    return jnp.concatenate([lower_half * cosine - upper_half * sine_part, upper_half * cosine + lower_half * sine_part], axis=-1)

def route_tables(routes, entry_order, live_rows, capacity):
    token_count, route_count = routes.shape
    entry_count = token_count * route_count
    slot_count = EXPERTS * capacity
    experts_flat = routes.reshape(entry_count)
    entry_live = jnp.repeat(live_rows, route_count, total_repeat_length=entry_count)
    ordered = experts_flat[entry_order]
    ordered_live = entry_live[entry_order]
    onehot = ((ordered[:, None] == jnp.arange(EXPERTS, dtype=jnp.int32)[None, :]) & ordered_live[:, None]).astype(jnp.int32)
    before = jnp.cumsum(onehot, axis=0) - onehot
    ranked = lax.optimization_barrier(jnp.sum(before * onehot, axis=1)).astype(jnp.int32)
    placing = jnp.zeros((entry_count,), jnp.int32).at[entry_order].set(ranked)
    kept_entry = entry_live & (placing < capacity)
    target = jnp.where(kept_entry, experts_flat * capacity + placing, slot_count).astype(jnp.int32)
    filler = jnp.full((slot_count,), -1, jnp.int32).at[target].set(jnp.arange(entry_count, dtype=jnp.int32), mode='drop')
    filled = filler >= 0
    source_entry = jnp.maximum(filler, 0)
    return (kept_entry.reshape(token_count, route_count), jnp.minimum(target, slot_count - 1).reshape(token_count, route_count), filled, source_entry // route_count, source_entry)

def attend_slot(packed):
    queries, key_rows, value_rows, length = packed
    score_scale = 1.0 / math.sqrt(HEAD_DIM)
    scaled = low_back(jnp.einsum('qkgd,jkd->kgqj', queries, key_rows, precision=HIGH) * score_scale)
    places = jnp.arange(SLOT, dtype=jnp.int32)
    allowed = (places[None, :] <= places[:, None]) & (places[None, :] < length)
    scores = jnp.where(allowed[None, None], scaled, NEG)
    highest = lax.optimization_barrier(jnp.max(scores, axis=-1, keepdims=True))
    weights = jnp.exp(scores - highest)
    probability = low(weights / lax.optimization_barrier(jnp.sum(weights, axis=-1, keepdims=True)))
    return jnp.einsum('kgqj,jkd->qkgd', probability, value_rows, precision=HIGH)

def layer_forward(inputs, params, live_float, slot_lengths, routes, tables):
    first_gain, w_query, w_key, w_value, w_out, second_gain, w_router, w_gate, w_up, w_down = params
    kept_entry, target, filled, slot_token, slot_entry = tables
    token_count = inputs.shape[0]
    slot_local = token_count // SLOT
    group_size = HEADS // KV_HEADS
    capacity = token_count * TOP // EXPERTS
    first_normed = low(inputs * rms_scale(inputs) * first_gain)
    query_pre = low_back(product(first_normed, w_query))
    key_pre = low_back(product(first_normed, w_key))
    value_rows = low_back(low(product(first_normed, w_value)))
    queries = low(rotate(query_pre.reshape(token_count, HEADS, HEAD_DIM), 1.0))
    key_rows = low(rotate(key_pre.reshape(token_count, KV_HEADS, HEAD_DIM), 1.0))
    mixed = lax.map(jax.checkpoint(attend_slot), (queries.reshape(slot_local, SLOT, KV_HEADS, group_size, HEAD_DIM), key_rows.reshape(slot_local, SLOT, KV_HEADS, HEAD_DIM), value_rows.reshape(slot_local, SLOT, KV_HEADS, HEAD_DIM), slot_lengths))
    heads_out = low_back(low(mixed.reshape(token_count, HEADS * HEAD_DIM)))
    hidden = inputs + low_back(product(heads_out, w_out)) * live_float
    second_normed = low(hidden * rms_scale(hidden) * second_gain)
    logits = low_back(product(second_normed, w_router))
    chosen = jnp.take_along_axis(logits, routes, axis=1)
    gate_exp = jnp.exp(chosen - lax.optimization_barrier(jnp.max(chosen, axis=-1, keepdims=True)))
    gate_values = gate_exp / lax.optimization_barrier(jnp.sum(gate_exp, axis=-1, keepdims=True))
    kept_gates = jnp.where(kept_entry, gate_values, 0.0)
    slot_rows = jnp.where(filled[:, None], second_normed[slot_token], 0.0).reshape(EXPERTS, capacity, D)
    part_width = FF // HID_PARTS
    returned = jnp.zeros((EXPERTS * capacity, D), inputs.dtype)
    for part_index in range(HID_PARTS):
        first_unit = part_index * part_width
        rows_part = low_back(slot_rows)
        gate_part = low_back(jnp.einsum('ecd,edf->ecf', rows_part, w_gate[:, :, first_unit:first_unit + part_width], precision=HIGH))
        up_part = low_back(jnp.einsum('ecd,edf->ecf', rows_part, w_up[:, :, first_unit:first_unit + part_width], precision=HIGH))
        activated = low(jax.nn.silu(gate_part) * up_part)
        produced = low_back(low(jnp.einsum('ecf,efd->ecd', activated, w_down[:, first_unit:first_unit + part_width, :], precision=HIGH)))
        returned = returned + produced.reshape(EXPERTS * capacity, D)
    combined = hidden
    for route_index in range(TOP):
        combined = combined + kept_gates[:, route_index:route_index + 1] * returned[target[:, route_index]]
    return combined

def reference(tokens, cotangent, seq_lengths, deal_order, routes, slot_order, first_gain, w_query, w_key, w_value, w_out, second_gain, w_router, w_gate, w_up, w_down):
    params = tuple((weight.astype(jnp.float32) for weight in (first_gain, w_query, w_key, w_value, w_out, second_gain, w_router, w_gate, w_up, w_down)))
    group_rows = jnp.arange(DEAL_GROUPS, dtype=jnp.int32)[:, None]

    def dealt(values):
        blocks = values.astype(jnp.float32).reshape(DEAL_GROUPS, DEAL, SLOT, D)
        return blocks[group_rows, deal_order].reshape(GROUPS, TOK_DEV, D)
    dealt_lengths = jnp.take_along_axis(seq_lengths, deal_order, axis=1).reshape(GROUPS, SEQ_DEV)

    def one_unit(totals, packed):
        inputs, grads_out, slot_lengths, unit_routes, entry_order = packed
        live_rows = jnp.arange(TOK_DEV, dtype=jnp.int32) % SLOT < jnp.repeat(slot_lengths, SLOT, total_repeat_length=TOK_DEV)
        tables = route_tables(unit_routes, entry_order, live_rows, TOK_DEV * TOP // EXPERTS)
        live_float = live_rows.astype(jnp.float32)[:, None]
        outputs, pullback = jax.vjp(lambda moved, weights: layer_forward(moved, weights, live_float, slot_lengths, unit_routes, tables), inputs, params)
        input_grad, weight_grads = pullback(grads_out)
        totals = jax.tree.map(lambda running, adding: running + adding, totals, weight_grads)
        return (totals, (outputs.astype(jnp.bfloat16), input_grad.astype(jnp.bfloat16)))
    initial = jax.tree.map(jnp.zeros_like, params)
    totals, (outputs, input_grads) = lax.scan(one_unit, initial, (dealt(tokens), dealt(cotangent), dealt_lengths, routes.reshape(GROUPS, TOK_DEV, TOP), slot_order))
    inverse = jax.vmap(lambda dealing: jnp.zeros((DEAL,), jnp.int32).at[dealing].set(jnp.arange(DEAL, dtype=jnp.int32)))(deal_order)

    def undealt(values):
        blocks = values.reshape(DEAL_GROUPS, DEAL, SLOT, D)
        return blocks[group_rows, inverse].reshape(TOKENS, D)
    return (undealt(outputs), undealt(input_grads), totals[0], totals[1], totals[2], totals[3], totals[4], totals[5], totals[6], totals[7], totals[8], totals[9])
```

```python
import functools

import jax
import jax.numpy as jnp
import numpy as np
from jax import lax
from jax.experimental import pallas as pl
from jax.experimental.pallas import tpu as pltpu
from jax.sharding import PartitionSpec as P

HEADS = 16
KV_HEADS = 8
HEAD_DIM = 64
EXPERTS = 32
TOP = 8
SLOT = 512

EPS = 1e-06
THETA = 10000.0
NEG = -1e30
BF = jnp.bfloat16
F32 = jnp.float32
MIB = 1 << 20


def dot(a, b, ca=1, cb=0):
    return lax.dot_general(a, b, (((ca,), (cb,)), ((), ())), preferred_element_type=F32)


def vmem(count=1):
    return [pl.BlockSpec(memory_space=pltpu.VMEM)] * count


def params(mib, **more):
    return pltpu.CompilerParams(vmem_limit_bytes=mib * MIB, **more)


def rotary_tables(rows):
    places = np.arange(rows, dtype=np.float32)[:, None]
    halfway = HEAD_DIM // 2
    spread = np.float32(THETA) ** (-2.0 * np.arange(halfway, dtype=np.float32) / HEAD_DIM)
    angles = (places * spread.astype(np.float32)[None, :]).astype(np.float32)
    copies = 128 // halfway
    return (
        np.tile(np.cos(angles), (1, copies)).astype(np.float32),
        np.tile(np.sin(angles), (1, copies)).astype(np.float32),
    )


def rotate128(values, cosine, sine, low_half):
    half = HEAD_DIM // 2
    up = pltpu.roll(values, 128 - half, 1)
    down = pltpu.roll(values, half, 1)
    return values * cosine + jnp.where(low_half, -up, down) * sine


def lanes(shape):
    return lax.broadcasted_iota(jnp.int32, shape, len(shape) - 1)


def sublanes(shape):
    return lax.broadcasted_iota(jnp.int32, shape, len(shape) - 2)


def table_kernel(length_ref, routes_ref, order_ref, table_ref):
    rows = routes_ref.shape[0]
    capacity = rows * TOP // EXPERTS
    entries = rows * TOP
    chunk = 512
    length = length_ref[0]
    routes_t = jnp.transpose(routes_ref[...].astype(F32)).astype(BF)
    upper = (sublanes((chunk, chunk)) < lanes((chunk, chunk))).astype(F32).astype(BF)
    expert_row = sublanes((EXPERTS, chunk))

    def body(step, carried):
        counts, table = carried
        entry = order_ref[:, pl.ds(pl.multiple_of(step * chunk, chunk), chunk)]
        row, choice = entry // TOP, entry % TOP
        onehot_row = (sublanes((rows, chunk)) == row).astype(F32).astype(BF)
        picked = dot(routes_t, onehot_row)
        expert = jnp.sum(jnp.where(sublanes((TOP, chunk)) == choice, picked, 0.0), axis=0, keepdims=True)
        member = (expert_row == expert.astype(jnp.int32)) & (row < length)
        member_f = member.astype(F32)
        before = dot(member_f.astype(BF), upper) + counts
        value = jnp.where(member, jnp.minimum(before, float(capacity)) + 1.0, 0.0)
        table = table + dot(value.astype(BF), onehot_row, 1, 1)
        return counts + jnp.sum(member_f, axis=1, keepdims=True), table

    _, table = lax.fori_loop(
        0, entries // chunk, body, (jnp.zeros((EXPERTS, 1), F32), jnp.zeros((EXPERTS, rows), F32))
    )
    table_ref[...] = table.astype(BF)


def make_table(length, routes, order):
    rows = routes.shape[0]
    return pl.pallas_call(
        table_kernel,
        out_shape=jax.ShapeDtypeStruct((EXPERTS, rows), BF),
        in_specs=[pl.BlockSpec(memory_space=pltpu.SMEM)] + vmem(2),
        out_specs=vmem()[0],
        compiler_params=params(32),
        name="tables",
    )(length, routes, order)


def head_parts(q, k_a, k_b, index, low_lane):
    block = q[:, (index // 2) * 128 : (index // 2) * 128 + 128]
    mine = low_lane if index % 2 == 0 else jnp.logical_not(low_lane)
    return jnp.where(mine, block, jnp.zeros((), block.dtype)), (k_a if index % 2 == (index // 2) % 2 else k_b)


def swap(block):
    return pltpu.roll(block.astype(F32), HEAD_DIM, 1).astype(BF)


def attend_kernel(
    length_ref, x_ref, gain_ref, wq_ref, wk_ref, wv_ref, wo_ref, cos_ref, sin_ref,
    part_ref, normed_ref, q_ref, k_ref, v_ref, heads_ref, logsum_ref,
):
    rows = x_ref.shape[0]
    length = length_ref[0]
    x = x_ref[...].astype(F32)
    scale = lax.rsqrt(jnp.mean(x * x, axis=-1, keepdims=True) + EPS)
    normed = (x * scale * gain_ref[...].astype(F32)).astype(BF)
    normed_ref[...] = normed
    cosine, sine = cos_ref[...], sin_ref[...]
    lane = lanes((rows, 128))
    low_half = lane % HEAD_DIM < HEAD_DIM // 2
    low_lane = lane < HEAD_DIM
    q_pre = dot(normed, wq_ref[...])
    for block in range(q_pre.shape[1] // 128):
        cut = slice(block * 128, block * 128 + 128)
        q_ref[:, cut] = rotate128(q_pre[:, cut], cosine, sine, low_half).astype(BF)
    k = rotate128(dot(normed, wk_ref[...]), cosine, sine, low_half).astype(BF)
    v = dot(normed, wv_ref[...]).astype(BF)
    k_ref[...] = k
    v_ref[...] = v
    q = q_ref[...]
    k_b, v_b = swap(k), swap(v)
    row, col = sublanes((rows, rows)), lanes((rows, rows))
    allowed = (col <= row) & (col < length)
    logsum = jnp.zeros((rows, 128), F32)
    pair = None
    for index in range(q.shape[1] // HEAD_DIM):
        q_one, k_one = head_parts(q, k, k_b, index, low_lane)
        v_one = v if index % 2 == (index // 2) % 2 else v_b
        scores = jnp.where(allowed, dot(q_one, k_one, 1, 1) * (HEAD_DIM**-0.5), NEG)
        highest = jnp.max(scores, axis=-1, keepdims=True)
        weights = jnp.exp(scores - highest)
        total = jnp.sum(weights, axis=-1, keepdims=True)
        mixed = dot((weights / total).astype(BF), v_one)
        logsum = jnp.where(lane == index, highest + jnp.log(total), logsum)
        if index % 2 == 0:
            pair = mixed
        else:
            cut = slice((index // 2) * 128, (index // 2) * 128 + 128)
            heads_ref[:, cut] = jnp.where(low_lane, pair, mixed).astype(BF)
    logsum_ref[...] = logsum
    live = (sublanes((rows, 1)) < length).astype(F32)
    part_ref[...] = (dot(heads_ref[...], wo_ref[...]) * live).astype(BF)


def attend(length, x, gain, wq, wk, wv, wo, cosine, sine):
    rows, width = x.shape
    shape = jax.ShapeDtypeStruct
    return pl.pallas_call(
        attend_kernel,
        out_shape=(
            shape((rows, width), BF), shape((rows, width), BF), shape((rows, wq.shape[1]), BF),
            shape((rows, wk.shape[1]), BF), shape((rows, wv.shape[1]), BF), shape((rows, wq.shape[1]), BF),
            shape((rows, 128), F32),
        ),
        in_specs=[pl.BlockSpec(memory_space=pltpu.SMEM)] + vmem(8),
        out_specs=tuple(vmem(7)),
        compiler_params=params(48),
        name="attend",
    )(length, x, gain, wq, wk, wv, wo, cosine, sine)


def attend_back_kernel(
    length_ref, hidden_grad_ref, x_ref, gain_ref, normed_ref, q_ref, k_ref, v_ref, heads_ref, logsum_ref,
    wq_ref, wk_ref, wv_ref, wo_ref, cos_ref, sin_ref,
    first_ref, stat_ref, gain_grad_ref, q_grad_ref, k_grad_ref, v_grad_ref, back_ref,
):
    rows, width = hidden_grad_ref.shape
    length = length_ref[0]
    inv = HEAD_DIM**-0.5
    live = (sublanes((rows, 1)) < length).astype(F32)
    branch = (hidden_grad_ref[...].astype(F32) * live).astype(BF)
    heads_grad = dot(branch, wo_ref[...], 1, 1).astype(BF)
    cosine, sine = cos_ref[...], -sin_ref[...]
    lane = lanes((rows, 128))
    low_half = lane % HEAD_DIM < HEAD_DIM // 2
    low_lane = lane < HEAD_DIM
    q, k, v = q_ref[...], k_ref[...], v_ref[...]
    k_b, v_b = swap(k), swap(v)
    key, query = sublanes((rows, rows)), lanes((rows, rows))
    allowed = (key <= query) & (key < length)
    logsum_rows = jnp.transpose(logsum_ref[...])
    dk = [jnp.zeros((rows, 128), F32), jnp.zeros((rows, 128), F32)]
    dv = [jnp.zeros((rows, 128), F32), jnp.zeros((rows, 128), F32)]
    q_width = q.shape[1]
    pair = None
    for index in range(q_width // HEAD_DIM):
        same = index % 2 == (index // 2) % 2
        q_one, k_one = head_parts(q, k, k_b, index, low_lane)
        g_one, v_one = head_parts(heads_grad, v, v_b, index, low_lane)
        scores = jnp.where(allowed, dot(k_one, q_one, 1, 1) * inv, NEG)
        prob = jnp.exp(scores - logsum_rows[index : index + 1, :])
        grad_prob = dot(v_one, g_one, 1, 1)
        center = jnp.sum(prob * grad_prob, axis=0, keepdims=True)
        score_grad = (prob * (grad_prob - center)).astype(BF)
        dq = dot(score_grad, k_one, 0, 0) * inv
        place = 0 if same else 1
        dk[place] = dk[place] + dot(score_grad, q_one) * inv
        dv[place] = dv[place] + dot(prob.astype(BF), g_one)
        if index % 2 == 0:
            pair = dq
        else:
            cut = slice((index // 2) * 128, (index // 2) * 128 + 128)
            both = jnp.where(low_lane, pair, dq)
            back_ref[:, cut] = rotate128(both, cosine, sine, low_half).astype(BF)
    k_width = k.shape[1]
    k_total = dk[0] + pltpu.roll(dk[1], HEAD_DIM, 1)
    v_total = dv[0] + pltpu.roll(dv[1], HEAD_DIM, 1)
    back_ref[:, q_width : q_width + k_width] = rotate128(k_total, cosine, sine, low_half).astype(BF)
    back_ref[:, q_width + k_width :] = v_total.astype(BF)
    back = back_ref[...]
    grads = dot(normed_ref[...], back, 0, 0)
    q_grad_ref[...] = grads[:, :q_width].astype(BF)
    k_grad_ref[...] = grads[:, q_width : q_width + k_width].astype(BF)
    v_grad_ref[...] = grads[:, q_width + k_width :].astype(BF)
    first = (
        dot(back[:, :q_width], wq_ref[...], 1, 1)
        + dot(back[:, q_width : q_width + k_width], wk_ref[...], 1, 1)
        + dot(back[:, q_width + k_width :], wv_ref[...], 1, 1)
    )
    x = x_ref[...].astype(F32)
    hat = x * lax.rsqrt(jnp.mean(x * x, axis=-1, keepdims=True) + EPS)
    along = first * hat
    gain_grad_ref[...] = jnp.sum(along, axis=0, keepdims=True)
    stat_ref[...] = jnp.broadcast_to(
        jnp.sum(along * gain_ref[...].astype(F32), axis=-1, keepdims=True), (rows, 128)
    )
    first_ref[...] = first.astype(BF)


def attend_back(length, hidden_grad, x, gain, normed, q, k, v, heads, logsum, wq, wk, wv, wo, cosine, sine):
    rows, width = x.shape
    shape = jax.ShapeDtypeStruct
    return pl.pallas_call(
        attend_back_kernel,
        out_shape=(
            shape((rows, width), BF), shape((rows, 128), F32), shape((1, width), F32),
            shape(wq.shape, BF), shape(wk.shape, BF), shape(wv.shape, BF),
        ),
        in_specs=[pl.BlockSpec(memory_space=pltpu.SMEM)] + vmem(15),
        out_specs=tuple(vmem(6)),
        scratch_shapes=[pltpu.VMEM((rows, wq.shape[1] + wk.shape[1] + wv.shape[1]), BF)],
        compiler_params=params(56),
        name="attend_back",
    )(length, hidden_grad, x, gain, normed, q, k, v, heads, logsum, wq, wk, wv, wo, cosine, sine)


def gate_rows(router_t, rows, table):
    logits = dot(router_t, rows, 1, 1)
    chosen = table > 0.5
    masked = jnp.where(chosen, logits, NEG)
    weights = jnp.where(chosen, jnp.exp(masked - jnp.max(masked, axis=0, keepdims=True)), 0.0)
    total = jnp.sum(weights, axis=0, keepdims=True)
    return weights / jnp.where(total > 0.0, total, 1.0)


def expert_kernel(
    own, groups, dp_count, capacity,
    place_ref, x_ref, dy_ref, table_ref, router_ref, wg_ref, wu_ref, wd_ref, *rest,
):
    if own:
        out_c_ref, out_g_ref, gi_ref, gg_ref, gu_ref, gd_ref, gates, xs, ys, gs, mats, gi_rows, acc_c_ref, acc_g_ref = rest
    else:
        gin_g_ref, gin_u_ref, gin_d_ref, gg_ref, gu_ref, gd_ref, gates, xs, ys, gs, mats = rest
    chunk, pair = pl.program_id(0), pl.program_id(1)
    first_expert = place_ref[1] + pair * 2
    dp_here = place_ref[0]
    rows = x_ref.shape[2]
    per_group = 1 if own else dp_count - 1
    units = groups * per_group
    slots = 2 * capacity

    def unit_place(i):
        if own:
            return i, 0
        d = dp_here + 1 + i % per_group
        return i // per_group, jnp.where(d >= dp_count, d - dp_count, d)

    @pl.when(pair == 0)
    def _():
        @pl.loop(0, units)
        def _(i):
            g, d = unit_place(i)
            gates[i] = gate_rows(router_ref[...], x_ref[g, d], table_ref[g, d].astype(F32))

    slot_id = sublanes((capacity, rows))

    @pl.loop(0, units)
    def _(i):
        g, d = unit_place(i)
        table = table_ref[g, d].astype(F32)
        pieces = []
        for j in range(2):
            pick = sublanes((EXPERTS, rows)) == first_expert + j
            ranks = jnp.sum(jnp.where(pick, table, 0.0), axis=0, keepdims=True).astype(jnp.int32) - 1
            gate = jnp.sum(jnp.where(pick, gates[i], 0.0), axis=0, keepdims=True)
            hit = slot_id == ranks
            hit_f = jnp.where(hit, 1.0, 0.0)
            gs[j, i] = jnp.broadcast_to(
                jnp.sum(jnp.where(hit, gate, 0.0), axis=-1, keepdims=True), (capacity, 128)
            )
            pieces.append(hit_f.astype(BF))
        onehot = jnp.concatenate(pieces, axis=0)
        if own:
            mats[i] = onehot
        moved_x = dot(onehot, x_ref[g, d]).astype(BF)
        moved_y = dot(onehot, dy_ref[g, d]).astype(BF)
        for j in range(2):
            cut = slice(j * capacity, (j + 1) * capacity)
            xs[j, i] = moved_x[cut]
            ys[j, i] = moved_y[cut]

    width = x_ref.shape[3]
    hidden = wg_ref.shape[2]
    terms_c, terms_g = [], []
    for j in range(2):
        x_here = xs[j].reshape(units * capacity, width)
        y_here = ys[j].reshape(units * capacity, width)
        scale = gs[j].reshape(units * capacity, 128)
        both = dot(x_here, jnp.concatenate([wg_ref[j], wu_ref[j]], axis=1))
        g_here, u_here = both[:, :hidden], both[:, hidden:]
        act_back = dot(y_here, wd_ref[j], 1, 1)
        sig = 1.0 / (1.0 + jnp.exp(-g_here))
        silu = g_here * sig
        act = silu * u_here
        act_gated = (act * scale).astype(BF)
        grad_act = act_back * scale
        grad_gate = (grad_act * u_here * sig * (1.0 + g_here * (1.0 - sig))).astype(BF)
        grad_up = (grad_act * silu).astype(BF)
        grads = jnp.concatenate([grad_gate, grad_up], axis=1)
        weight_grads = dot(x_here, grads, 0, 0)
        down = dot(act_gated, y_here, 0, 0)
        if own:
            gg_ref[j] = weight_grads[:, :hidden]
            gu_ref[j] = weight_grads[:, hidden:]
            gd_ref[j] = down
            inner = jnp.sum(act * act_back, axis=-1, keepdims=True)
            stacked = jnp.concatenate([act_gated, grads], axis=1)
            for i in range(units):
                cut = slice(i * capacity, (i + 1) * capacity)
                back = mats[i, j * capacity : (j + 1) * capacity, :]
                mats_t = dot(back, stacked[cut], 0, 0).astype(BF)
                terms_c.append(mats_t[:, :hidden])
                terms_g.append(mats_t[:, hidden:])
                gi_rows[i, j : j + 1, :] = jnp.sum(back.astype(F32) * inner[cut], axis=0, keepdims=True)
        else:
            gg_ref[j] = gin_g_ref[j] + weight_grads[:, :hidden]
            gu_ref[j] = gin_u_ref[j] + weight_grads[:, hidden:]
            gd_ref[j] = gin_d_ref[j] + down
    if own:
        down_pair = wd_ref[...].reshape(2 * hidden, width)
        in_pair = jnp.concatenate([wg_ref[0], wu_ref[0], wg_ref[1], wu_ref[1]], axis=1)
        for i in range(units):
            left_c = jnp.concatenate([terms_c[i], terms_c[units + i]], axis=1)
            left_g = jnp.concatenate([terms_g[i], terms_g[units + i]], axis=1)
            add_c = dot(left_c, down_pair)
            add_g = dot(left_g, in_pair, 1, 1)

            @pl.when(pair == 0)
            def _():
                acc_c_ref[i] = add_c
                acc_g_ref[i] = add_g
                gi_ref[i] = jnp.zeros_like(gi_ref[i])

            @pl.when(pair != 0)
            def _():
                acc_c_ref[i] += add_c
                acc_g_ref[i] += add_g

            @pl.when(pair == pl.num_programs(1) - 1)
            def _():
                out_c_ref[i] = acc_c_ref[i].astype(BF)
                out_g_ref[i] = acc_g_ref[i].astype(BF)

            pick = sublanes((EXPERTS, rows))
            gi_ref[i] = jnp.where(
                pick == first_expert, gi_rows[i, 0:1, :],
                jnp.where(pick == first_expert + 1, gi_rows[i, 1:2, :], gi_ref[i]),
            )


def expert_call(own, place, x, dy, table, router_t, wg, wu, wd, partial=None):
    groups_all, dp_count, rows, width = x.shape
    chunk_groups = 2
    chunks = groups_all // chunk_groups
    local, _, hidden = wg.shape
    pairs = local // 2
    assert chunks == 1 or pairs == 1
    capacity = rows * TOP // EXPERTS
    shape = jax.ShapeDtypeStruct
    units = chunk_groups * (1 if own else dp_count - 1)
    dp_block = 1 if own else dp_count
    dp_at = (lambda s: s[0]) if own else (lambda s: 0)
    row_block = pl.BlockSpec(
        (chunk_groups, dp_block, rows, width), lambda c, p, s: (c, dp_at(s), 0, 0), pipeline_mode=pl.Buffered(1)
    )
    in_block = pl.BlockSpec((2, width, hidden), lambda c, p, s: (p, 0, 0))
    down_block = pl.BlockSpec((2, hidden, width), lambda c, p, s: (p, 0, 0))
    in_specs = [
        row_block, row_block,
        pl.BlockSpec((chunk_groups, dp_block, EXPERTS, rows), lambda c, p, s: (c, dp_at(s), 0, 0)),
        pl.BlockSpec((EXPERTS, width), lambda c, p, s: (0, 0)),
        in_block, in_block, down_block,
    ]
    grads_out = (shape(wg.shape, F32), shape(wu.shape, F32), shape(wd.shape, F32))
    grad_specs = (in_block, in_block, down_block)
    scratch = [
        pltpu.VMEM((units, EXPERTS, rows), F32),
        pltpu.VMEM((2, units, capacity, width), BF),
        pltpu.VMEM((2, units, capacity, width), BF),
        pltpu.VMEM((2, units, capacity, 128), F32),
        pltpu.VMEM((units, 2 * capacity, rows), BF),
    ]
    operands = [x, dy, table, router_t, wg, wu, wd]
    if own:
        acc = pl.BlockSpec((chunk_groups, rows, width), lambda c, p, s: (c, 0, 0))
        out_shape = (
            shape((groups_all, rows, width), BF), shape((groups_all, rows, width), BF),
            shape((groups_all, EXPERTS, rows), F32), *grads_out,
        )
        out_specs = (acc, acc, pl.BlockSpec((chunk_groups, EXPERTS, rows), lambda c, p, s: (c, 0, 0)), *grad_specs)
        scratch += [pltpu.VMEM((units, 2, rows), F32)] + [pltpu.VMEM((units, rows, width), F32)] * 2
        aliases = {}
    else:
        out_shape, out_specs = grads_out, grad_specs
        in_specs += list(grad_specs)
        operands += list(partial)
        aliases = {8: 0, 9: 1, 10: 2}
    return pl.pallas_call(
        functools.partial(expert_kernel, own, chunk_groups, dp_count, capacity),
        out_shape=out_shape,
        grid_spec=pltpu.PrefetchScalarGridSpec(
            num_scalar_prefetch=1, grid=(chunks, pairs), in_specs=in_specs, out_specs=out_specs, scratch_shapes=scratch
        ),
        input_output_aliases=aliases,
        compiler_params=params(60, dimension_semantics=("arbitrary", "arbitrary")),
        name="experts_own" if own else "experts_other",
    )(place, *operands)


def on_device(
    tokens, cotangent, seq_lengths, deal_order, routes, slot_order, first_gain, w_query, w_key, w_value, w_out,
    second_gain, w_router, w_gate, w_up, w_down,
):
    dp_count = lax.axis_size("dp")
    dp_index = lax.axis_index("dp")
    tensor_count = lax.axis_size("tensor")
    tensor_index = lax.axis_index("tensor")
    expert_count = lax.axis_size("expert")
    expert_index = lax.axis_index("expert")
    rows, width = tokens.shape
    row_share, col_share = rows // tensor_count, width // tensor_count
    row_start = tensor_index * row_share
    everywhere = ("expert", "dp", "tensor")
    rows_all = ("expert", "dp")

    def own_rows(values):
        return lax.dynamic_slice_in_dim(values, row_start, row_share, 0)

    order = deal_order[0]
    dealt_length = seq_lengths[0][order[dp_index]]
    table = make_table(dealt_length.reshape(1), routes, slot_order)
    tables_dealt = lax.all_gather(table, "dp", axis=0)
    inverse = jnp.sum(
        jnp.where(
            order[None, :] == jnp.arange(dp_count, dtype=jnp.int32)[:, None],
            jnp.arange(dp_count, dtype=jnp.int32)[None, :], 0,
        ), axis=1,
    )
    my_table = tables_dealt[inverse[dp_index]]
    tables = lax.all_gather(my_table, rows_all, axis=0).reshape(expert_count, dp_count, EXPERTS, rows)
    length = seq_lengths[0][dp_index].reshape(1)

    dy_all = lax.all_gather(own_rows(cotangent), everywhere, axis=0, tiled=True)
    dy_all = dy_all.reshape(expert_count, dp_count, rows, width)

    cosine, sine = (jnp.asarray(values) for values in rotary_tables(rows))
    gain1 = first_gain.reshape(1, width)
    gain2 = second_gain.reshape(1, width).astype(F32)
    part, normed, q, k, v, heads, logsum = attend(
        length, tokens, gain1, w_query, w_key, w_value, w_out, cosine, sine
    )
    attention = lax.psum_scatter(part, "tensor", scatter_dimension=0, tiled=True)
    x_share = own_rows(tokens).astype(F32)
    hidden = x_share + attention.astype(F32)
    scale2 = lax.rsqrt(jnp.mean(hidden * hidden, axis=-1, keepdims=True) + EPS)
    hat2 = hidden * scale2
    second_normed = (hat2 * gain2).astype(BF)
    x_all = lax.all_gather(second_normed, everywhere, axis=0, tiled=True).reshape(expert_count, dp_count, rows, width)

    router_t = w_router.T
    place = jnp.stack([dp_index, expert_index * w_gate.shape[0]]).astype(jnp.int32)
    acc_c, acc_g, gi, pg, pu, pd = expert_call(
        True, place, x_all, dy_all, tables, router_t, w_gate, w_up, w_down
    )
    both = ("expert", "tensor")
    moe_rows = lax.psum_scatter(acc_c.reshape(-1, width), both, scatter_dimension=0, tiled=True)
    moe_grad = lax.psum_scatter(acc_g.reshape(-1, width), both, scatter_dimension=0, tiled=True)
    gate_in = lax.psum_scatter(
        gi.transpose(0, 2, 1).reshape(-1, EXPERTS), both, scatter_dimension=0, tiled=True
    )
    out_rows = (hidden + moe_rows.astype(F32)).astype(BF)
    block_out = lax.all_to_all(out_rows, "tensor", split_axis=1, concat_axis=0, tiled=True)

    share_table = own_rows(my_table.astype(F32).T)
    logits = jnp.dot(second_normed, w_router, preferred_element_type=F32)
    chosen = share_table > 0.5
    masked = jnp.where(chosen, logits, NEG)
    weights = jnp.where(chosen, jnp.exp(masked - jnp.max(masked, axis=-1, keepdims=True)), 0.0)
    total = jnp.sum(weights, axis=-1, keepdims=True)
    gates = weights / jnp.where(total > 0.0, total, 1.0)
    logit_grad = (gates * (gate_in - jnp.sum(gates * gate_in, axis=-1, keepdims=True))).astype(BF)
    router_term = jnp.einsum("td,te->de", second_normed, logit_grad, preferred_element_type=F32)
    normed_grad = moe_grad.astype(F32) + jnp.einsum("te,de->td", logit_grad, w_router, preferred_element_type=F32)
    second_term = jnp.sum(normed_grad * hat2, axis=0)
    scaled = normed_grad * gain2
    hidden_grad = own_rows(cotangent).astype(F32) + scale2 * (
        scaled - hat2 * jnp.mean(scaled * hat2, axis=-1, keepdims=True)
    )
    hidden_grad_all = lax.all_gather(hidden_grad.astype(BF), "tensor", axis=0, tiled=True)
    live = (jnp.arange(rows, dtype=jnp.int32) < length[0])[:, None]
    branch = jnp.where(live, hidden_grad_all, jnp.zeros((), BF))
    out_term = jnp.einsum("ta,td->ad", heads, branch, preferred_element_type=F32).astype(BF)
    first, stat, gain1_term, q_term, k_term, v_term = attend_back(
        length, hidden_grad_all, tokens, gain1, normed, q, k, v, heads, logsum,
        w_query, w_key, w_value, w_out, cosine, sine,
    )
    gate_grad, up_grad, down_grad = expert_call(
        False, place, x_all, dy_all, tables, router_t, w_gate, w_up, w_down, (pg, pu, pd)
    )
    first_cols = lax.psum_scatter(first, "tensor", scatter_dimension=1, tiled=True).astype(F32)
    stat_sum = lax.psum(stat[:, 0], "tensor")[:, None] / width
    out_sum, q_sum, k_sum, v_sum = lax.psum((out_term, q_term, k_term, v_term), rows_all)
    gain1_sum, gain2_sum, router_sum = lax.psum((gain1_term, second_term, router_term), everywhere)
    cols = functools.partial(lax.dynamic_slice_in_dim, start_index=tensor_index * col_share, slice_size=col_share, axis=1)
    x32 = tokens.astype(F32)
    scale1 = lax.rsqrt(jnp.mean(x32 * x32, axis=-1, keepdims=True) + EPS)
    input_grad = cols(hidden_grad_all).astype(F32) + scale1 * (
        first_cols * cols(gain1.astype(F32)) - cols(x32) * scale1 * stat_sum
    )
    return (
        block_out, input_grad.astype(BF), gain1_sum.reshape(width), q_sum.astype(F32), k_sum.astype(F32),
        v_sum.astype(F32), out_sum.astype(F32), gain2_sum, router_sum, gate_grad, up_grad, down_grad,
    )


def solution(mesh):
    rows2 = P(("expert", "dp"), None)
    placed = (
        rows2, rows2, P("expert", None), P("expert", None), rows2, rows2, P(),
        P(None, "tensor"), P(None, "tensor"), P(None, "tensor"), P("tensor", None), P(), P(),
        P("expert", None, "tensor"), P("expert", None, "tensor"), P("expert", "tensor", None),
    )
    return jax.shard_map(
        on_device,
        mesh=mesh,
        in_specs=placed,
        out_specs=(
            P(("expert", "dp"), "tensor"), P(("expert", "dp"), "tensor"), P(),
            P(None, "tensor"), P(None, "tensor"), P(None, "tensor"), P("tensor", None), P(), P(),
            P("expert", None, "tensor"), P("expert", None, "tensor"), P("expert", "tensor", None),
        ),
        check_vma=False,
    )
```

```python
import functools

import jax
import jax.numpy as jnp
import numpy as np
from jax import lax
from jax.experimental import pallas as pl
from jax.experimental.pallas import tpu as pltpu
from jax.sharding import PartitionSpec as P

HEADS = 16
KV_HEADS = 8
HEAD_DIM = 64
EXPERTS = 32
TOP = 8
SLOT = 512

EPS = 1e-06
THETA = 10000.0
NEG = -1e30
BF = jnp.bfloat16
F32 = jnp.float32
MIB = 1 << 20


def dot(a, b, ca=1, cb=0):
    return lax.dot_general(a, b, (((ca,), (cb,)), ((), ())), preferred_element_type=F32)


def vmem(count=1):
    return [pl.BlockSpec(memory_space=pltpu.VMEM)] * count


def params(mib, **more):
    return pltpu.CompilerParams(vmem_limit_bytes=mib * MIB, **more)


def rotary_tables(rows):
    places = np.arange(rows, dtype=np.float32)[:, None]
    halfway = HEAD_DIM // 2
    spread = np.float32(THETA) ** (-2.0 * np.arange(halfway, dtype=np.float32) / HEAD_DIM)
    angles = (places * spread.astype(np.float32)[None, :]).astype(np.float32)
    copies = 128 // halfway
    return (
        np.tile(np.cos(angles), (1, copies)).astype(np.float32),
        np.tile(np.sin(angles), (1, copies)).astype(np.float32),
    )


def rotate128(values, cosine, sine, low_half):
    half = HEAD_DIM // 2
    up = pltpu.roll(values, 128 - half, 1)
    down = pltpu.roll(values, half, 1)
    return values * cosine + jnp.where(low_half, -up, down) * sine


def lanes(shape):
    return lax.broadcasted_iota(jnp.int32, shape, len(shape) - 1)


def sublanes(shape):
    return lax.broadcasted_iota(jnp.int32, shape, len(shape) - 2)


def bits_of(count):
    return [1 << i for i in range(count.bit_length() - 1)]


def flip(value, mask):
    for bit in bits_of(1 << 16):
        if mask & bit:
            value = value + bit - 2 * bit * lax.rem(lax.div(value, bit), 2)
    return value


class Net:
    def __init__(self, send_sem, recv_sem):
        self.send_sem, self.recv_sem, self.used, self.copies = send_sem, recv_sem, 0, []
        self.me = {axis: lax.axis_index(axis) for axis in ("expert", "tensor", "dp")}

    def barrier(self, partners):
        sem = pltpu.get_barrier_semaphore()
        for axis, mask in partners:
            pl.semaphore_signal(
                sem, inc=1, device_id={axis: flip(self.me[axis], mask)}, device_id_type=pl.DeviceIdType.MESH
            )
        pl.semaphore_wait(sem, len(partners))

    def send(self, source, target, axis, mask):
        k = self.used
        self.used += 1
        copy = pltpu.make_async_remote_copy(
            src_ref=source, dst_ref=target, send_sem=self.send_sem.at[k], recv_sem=self.recv_sem.at[k],
            device_id={axis: flip(self.me[axis], mask)}, device_id_type=pl.DeviceIdType.MESH,
        )
        copy.start()
        self.copies.append(copy)
        return copy

    def close(self):
        for copy in self.copies:
            copy.wait_send()


class Gather:
    def __init__(self, net, at, steps, known=((0, 0),), first=None):
        self.net, self.at, self.steps, self.known, self.first, self.flight = net, at, list(steps), list(known), first, []

    def start(self):
        axis, mask = self.steps.pop(0)
        fresh = []
        for re, rt in self.known:
            place = self.at(re, rt)
            source = self.first if self.first is not None and (re, rt) == (0, 0) else place
            self.flight.append(self.net.send(source, place, axis, mask))
            fresh.append((re ^ mask, rt) if axis == "expert" else (re, rt ^ mask))
        self.known += fresh

    def finish(self):
        for copy in self.flight:
            copy.wait_recv()
        self.flight = []


class Reduce:
    def __init__(self, net, at, landing, steps, chunks):
        self.net, self.at, self.landing, self.steps, self.live = net, at, landing, list(steps), list(chunks)
        self.used, self.flight = 0, []

    def start(self):
        axis, mask = self.steps.pop(0)
        side = 0 if axis == "expert" else 1
        going = [r for r in self.live if r[side] & mask]
        self.live = [r for r in self.live if not r[side] & mask]
        for r in going:
            kept = (r[0] ^ mask, r[1]) if side == 0 else (r[0], r[1] ^ mask)
            copy = self.net.send(self.at(*r), self.landing(self.used), axis, mask)
            self.flight.append((kept, copy, self.used))
            self.used += 1
        if self.steps:
            axis, mask = self.steps[0]
            side = 0 if axis == "expert" else 1
            self.flight.sort(key=lambda item: 0 if item[0][side] & mask else 1)

    def finish(self):
        for kept, copy, slot in self.flight:
            copy.wait_recv()
            place = self.at(*kept)
            place[...] = (place[...].astype(F32) + self.landing(slot)[...].astype(F32)).astype(BF)
        self.flight = []


TABLE_ROWS = 48


def table_of(length, routes_ref, order_ref):
    rows = routes_ref.shape[1]
    capacity = rows * TOP // EXPERTS
    entries = rows * TOP
    chunk = 512
    routes_t = routes_ref[...].astype(F32).astype(BF)
    upper = (sublanes((chunk, chunk)) < lanes((chunk, chunk))).astype(F32).astype(BF)
    expert_row = sublanes((EXPERTS, chunk))

    def body(step, carried):
        counts, table = carried
        entry = order_ref[:, pl.ds(pl.multiple_of(step * chunk, chunk), chunk)]
        row, choice = entry // TOP, entry % TOP
        onehot_row = (sublanes((rows, chunk)) == row).astype(F32).astype(BF)
        picked = dot(routes_t, onehot_row)
        expert = jnp.sum(jnp.where(sublanes((TOP, chunk)) == choice, picked, 0.0), axis=0, keepdims=True)
        member = (expert_row.astype(F32) == expert) & (row < length)
        member_f = member.astype(F32)
        before = dot(member_f.astype(BF), upper) + counts
        value = jnp.where(member, jnp.minimum(before, float(capacity)) + 1.0, 0.0)
        table = table + dot(value.astype(BF), onehot_row, 1, 1)
        return counts + jnp.sum(member_f, axis=1, keepdims=True), table

    _, table = lax.fori_loop(
        0, entries // chunk, body, (jnp.zeros((EXPERTS, 1), F32), jnp.zeros((EXPERTS, rows), F32))
    )
    return table


def given_table(tables, index, dp_here):
    total = 0.0
    for j in range(tables.shape[1]):
        source = tables[index, j, EXPERTS : EXPERTS + 16, :].astype(F32)[0:1]
        total = total + jnp.where(source == dp_here, tables[index, j, 0:EXPERTS, :].astype(F32), 0.0)
    return total


def head_parts(q, k_a, k_b, index, low_lane):
    block = q[:, (index // 2) * 128 : (index // 2) * 128 + 128]
    mine = low_lane if index % 2 == 0 else jnp.logical_not(low_lane)
    return jnp.where(mine, block, jnp.zeros((), block.dtype)), (k_a if index % 2 == (index // 2) % 2 else k_b)


def swap(block):
    return pltpu.roll(block.astype(F32), HEAD_DIM, 1).astype(BF)


def front_kernel(
    sizes,
    lengths_ref, order_of_ref, x_ref, gain_ref, wq_ref, wk_ref, wv_ref, wo_ref, cos_ref, sin_ref, gain2_ref, routes_ref, order_ref, dy_ref,
    normed_ref, q_ref, k_ref, v_ref, heads_ref, logsum_ref, hidden_ref, share_ref, tables_ref, xown_ref, dyown_ref,
    part, landing, send_sem, recv_sem, local_sem,
):
    expert_count, tensor_count, dp_count = sizes
    rows, width = x_ref.shape
    share = rows // tensor_count
    half = rows // 2
    net = Net(send_sem, recv_sem)
    me_e, me_t, me_d = net.me["expert"], net.me["tensor"], net.me["dp"]
    expert_bits = [("expert", b) for b in bits_of(expert_count)]
    tensor_bits = [("tensor", b) for b in bits_of(tensor_count)]
    net.barrier(expert_bits + tensor_bits + [("dp", m) for m in range(1, dp_count)])

    keep_dy = pltpu.make_async_copy(dy_ref, dyown_ref.at[me_e], local_sem.at[0])
    keep_dy.start()
    half_start = pl.multiple_of(lax.rem(me_t, 2) * half, half)
    dy_half = Gather(
        net, lambda re, rt: dyown_ref.at[flip(me_e, re), pl.ds(half_start, half)], expert_bits,
        first=dy_ref.at[pl.ds(half_start, half)],
    )
    dy_half.start()

    length, source, dealt_length = lengths_ref[0, me_d], order_of_ref[0, me_d], 0
    for i in range(dp_count):
        dealt_length = jnp.where(source == i, lengths_ref[0, i], dealt_length)
    x = x_ref[...].astype(F32)
    scale = lax.rsqrt(jnp.mean(x * x, axis=-1, keepdims=True) + EPS)
    normed = (x * scale * gain_ref[...].astype(F32)[None, :]).astype(BF)
    normed_ref[...] = normed
    cosine, sine = cos_ref[...], sin_ref[...]
    lane = lanes((rows, 128))
    low_half = lane % HEAD_DIM < HEAD_DIM // 2
    low_lane = lane < HEAD_DIM
    q_pre = dot(normed, wq_ref[...])
    for block in range(q_pre.shape[1] // 128):
        cut = slice(block * 128, block * 128 + 128)
        q_ref[:, cut] = rotate128(q_pre[:, cut], cosine, sine, low_half).astype(BF)
    k = rotate128(dot(normed, wk_ref[...]), cosine, sine, low_half).astype(BF)
    v = dot(normed, wv_ref[...]).astype(BF)
    k_ref[...] = k
    v_ref[...] = v
    q = q_ref[...]
    k_b, v_b = swap(k), swap(v)
    row, col = sublanes((rows, rows)), lanes((rows, rows))
    allowed = (col <= row) & (col < length)
    logsum = jnp.zeros((rows, 128), F32)
    pair = None
    for index in range(q.shape[1] // HEAD_DIM):
        q_one, k_one = head_parts(q, k, k_b, index, low_lane)
        v_one = v if index % 2 == (index // 2) % 2 else v_b
        scores = jnp.where(allowed, dot(q_one, k_one, 1, 1) * (HEAD_DIM**-0.5), NEG)
        highest = jnp.max(scores, axis=-1, keepdims=True)
        weights = jnp.exp(scores - highest)
        total = jnp.sum(weights, axis=-1, keepdims=True)
        mixed = dot((weights / total).astype(BF), v_one)
        logsum = jnp.where(lane == index, highest + jnp.log(total), logsum)
        if index % 2 == 0:
            pair = mixed
        else:
            cut = slice((index // 2) * 128, (index // 2) * 128 + 128)
            heads_ref[:, cut] = jnp.where(low_lane, pair, mixed).astype(BF)
    logsum_ref[...] = logsum
    live = (sublanes((rows, 1)) < length).astype(F32)
    part[...] = (dot(heads_ref[...], wo_ref[...]) * live).astype(BF).reshape(part.shape)

    attn = Reduce(
        net, lambda re, rt: part.at[flip(me_t, rt)], lambda i: landing.at[i], tensor_bits,
        [(0, r) for r in range(tensor_count)],
    )
    attn.start()
    table = table_of(dealt_length, routes_ref, order_ref)
    source = jnp.broadcast_to(source.astype(F32), (TABLE_ROWS - EXPERTS, rows))
    tables_ref[me_e, me_d] = jnp.concatenate([table, source], axis=0).astype(BF)
    mine = tables_ref.at[me_e, me_d]
    table_copies = [net.send(mine, mine, "dp", m) for m in range(1, dp_count)]
    attn.finish()
    while attn.steps:
        attn.start()
        if not attn.steps:
            dy_half.finish()
            while dy_half.steps:
                dy_half.start()
                dy_half.finish()
            for re, _ in dy_half.known[1:]:
                place = dy_half.at(re, 0)
                dy_half.flight.append(net.send(place, place, "tensor", 1))
        attn.finish()

    start = pl.multiple_of(me_t * share, share)
    hidden = x_ref[pl.ds(start, share), :].astype(F32) + part[me_t].astype(F32)
    hidden_ref[...] = hidden
    scale2 = lax.rsqrt(jnp.mean(hidden * hidden, axis=-1, keepdims=True) + EPS)
    share_ref[...] = (hidden * scale2 * gain2_ref[...].astype(F32)[None, :]).astype(BF)
    keep_x = pltpu.make_async_copy(share_ref, xown_ref.at[me_e, pl.ds(start, share)], local_sem.at[1])
    keep_x.start()
    high_bits = tensor_bits[1:][::-1]
    gathers = []
    for part_index, steps in enumerate((high_bits + expert_bits, expert_bits + high_bits)):
        size = share // 2

        def at(re, rt, offset=part_index * size):
            begin = pl.multiple_of(flip(me_t, rt) * share + offset, size)
            return xown_ref.at[flip(me_e, re), pl.ds(begin, size)]

        gathers.append(
            Gather(net, at, steps + tensor_bits[:1], first=share_ref.at[pl.ds(part_index * size, size)])
        )
    table_all = Gather(net, lambda re, rt: tables_ref.at[flip(me_e, re)], expert_bits)
    first_step = True
    while gathers[0].steps:
        for gather in gathers:
            gather.start()
        if first_step:
            for copy in table_copies:
                copy.wait_recv()
            first_step = False
        else:
            table_all.finish()
        if table_all.steps:
            table_all.start()
        for gather in gathers:
            gather.finish()
    table_all.finish()
    dy_half.finish()
    net.close()
    keep_dy.wait()
    keep_x.wait()


def front(lengths, order_of, x, gain, wq, wk, wv, wo, cosine, sine, gain2, routes, order, dy):
    rows, width = x.shape
    sizes = tuple(lax.axis_size(axis) for axis in ("expert", "tensor", "dp"))
    expert_count, tensor_count, dp_count = sizes
    share = rows // tensor_count
    shape = jax.ShapeDtypeStruct
    copies = 96
    return pl.pallas_call(
        functools.partial(front_kernel, sizes),
        out_shape=(
            shape((rows, width), BF), shape((rows, wq.shape[1]), BF), shape((rows, wk.shape[1]), BF),
            shape((rows, wv.shape[1]), BF), shape((rows, wq.shape[1]), BF), shape((rows, 128), F32),
            shape((share, width), F32), shape((share, width), BF), shape((expert_count, dp_count, TABLE_ROWS, rows), BF),
            shape((expert_count, rows, width), BF), shape((expert_count, rows, width), BF),
        ),
        in_specs=[pl.BlockSpec(memory_space=pltpu.SMEM)] * 2 + vmem(11) + [pl.BlockSpec(memory_space=pl.ANY)],
        out_specs=tuple(vmem(9)) + (pl.BlockSpec(memory_space=pl.ANY),) * 2,
        scratch_shapes=[
            pltpu.VMEM((tensor_count, share, width), BF),
            pltpu.VMEM((tensor_count - 1, share, width), BF),
            pltpu.SemaphoreType.DMA((copies,)),
            pltpu.SemaphoreType.DMA((copies,)),
            pltpu.SemaphoreType.DMA((2,)),
        ],
        compiler_params=params(56, collective_id=1, has_side_effects=True),
        cost_estimate=pl.CostEstimate(flops=2 * rows * width * 4096, bytes_accessed=16 * MIB, transcendentals=0),
        name="front",
    )(lengths, order_of, x, gain, wq, wk, wv, wo, cosine, sine, gain2, routes, order, dy)


def back_kernel(
    sizes, wait_count,
    lengths_ref, dy_ref, x_ref, gain_ref, gain2_ref, router_ref, hidden_ref, tables_ref,
    normed_ref, q_ref, k_ref, v_ref, heads_ref, logsum_ref, wq_ref, wk_ref, wv_ref, wo_ref, cos_ref, sin_ref,
    grad_in_ref, out_in_ref, xown_ref, *rest,
):
    (
        block_ref, input_ref, q_grad_ref, k_grad_ref, v_grad_ref, out_grad_ref, small_ref,
        grad, grad_landing, out, out_landing, normed2, spread, first_part, first_landing, tiny, tiny_landing, back_ref, picked,
        send_sem, recv_sem, local_sem,
    ) = rest[wait_count:]
    group_count, tensor_count, dp_count = sizes
    rows, width = x_ref.shape
    share = rows // tensor_count
    net = Net(send_sem, recv_sem)
    me_e, me_t, me_d = net.me["expert"], net.me["tensor"], net.me["dp"]
    here = me_e if group_count > 1 else 0
    expert_bits = [("expert", b) for b in bits_of(group_count)]
    tensor_bits = [("tensor", b) for b in bits_of(tensor_count)]
    load_grad = pltpu.make_async_copy(grad_in_ref, grad, local_sem.at[0])
    load_out = pltpu.make_async_copy(out_in_ref, out, local_sem.at[1])
    load_x = pltpu.make_async_copy(xown_ref.at[here], normed2, local_sem.at[2])
    load_grad.start()
    load_out.start()
    load_x.start()
    net.barrier(expert_bits + tensor_bits + [("tensor", m) for m in range(3, tensor_count)])
    load_grad.wait()
    load_out.wait()
    high_bits = tensor_bits[1:]
    chunks = [(e, t) for e in range(group_count) for t in range(tensor_count)]
    sums = []
    size = share // 2
    for part_index, steps in enumerate((high_bits + expert_bits, expert_bits + high_bits)):

        def at(re, rt, offset=part_index * size):
            begin = pl.multiple_of(flip(me_t, rt) * share + offset, size)
            return grad.at[flip(here, re) if re else here, pl.ds(begin, size)]

        sums.append(Reduce(
            net, at, lambda i, p=part_index: grad_landing.at[p, i], tensor_bits[:1] + steps, chunks
        ))
    out_sum = Reduce(
        net, lambda re, rt: out.at[flip(here, re) if re else here, flip(me_t, rt)], lambda i: out_landing.at[i],
        tensor_bits[:1] + high_bits + expert_bits, chunks,
    )

    def advance(reduction):
        if reduction.flight:
            reduction.finish()
        if reduction.steps:
            reduction.start()

    step = 0
    while sums[0].steps:
        for one in sums:
            one.start()
        if step == 1:
            out_sum.start()
        step += 1
        for one in sums:
            one.finish()

    start = pl.multiple_of(me_t * share, share)
    gain2 = gain2_ref[...].astype(F32)[None, :]
    hidden = hidden_ref[...]
    scale2 = lax.rsqrt(jnp.mean(hidden * hidden, axis=-1, keepdims=True) + EPS)
    hat2 = hidden * scale2
    second_normed = (hat2 * gain2).astype(BF)
    picked[...] = given_table(tables_ref, me_e, me_d.astype(F32))
    table = picked[:, pl.ds(start, share)]
    table = jnp.concatenate([table, jnp.zeros((128 - EXPERTS, share), F32)], axis=0)
    table = jnp.transpose(table)[:, :EXPERTS]
    logits = dot(second_normed, router_ref[...], 1, 1)
    chosen = table > 0.5
    masked = jnp.where(chosen, logits, NEG)
    weights = jnp.where(chosen, jnp.exp(masked - jnp.max(masked, axis=-1, keepdims=True)), 0.0)
    total = jnp.sum(weights, axis=-1, keepdims=True)
    gates = weights / jnp.where(total > 0.0, total, 1.0)
    gate_in = grad[here, pl.ds(start, share), width:].astype(F32)[:, :EXPERTS]
    logit_grad = (gates * (gate_in - jnp.sum(gates * gate_in, axis=-1, keepdims=True))).astype(BF)
    normed_grad = grad[here, pl.ds(start, share), :width].astype(F32) + dot(logit_grad, router_ref[...])
    along2 = normed_grad * hat2
    gain2_part = jnp.sum(along2, axis=0, keepdims=True)
    scaled = normed_grad * gain2
    hidden_grad = dy_ref[pl.ds(start, share), :].astype(F32) + scale2 * (
        scaled - hat2 * jnp.mean(scaled * hat2, axis=-1, keepdims=True)
    )
    spread[me_t, 0:share, :width] = hidden_grad.astype(BF)
    spread[me_t, 0:share, width:] = jnp.concatenate(
        [logit_grad.astype(F32), jnp.zeros((share, 128 - EXPERTS), F32)], axis=1
    ).astype(BF)
    high = gain2_part.astype(BF).astype(F32)
    spread[me_t, share : share + 16, :width] = jnp.concatenate(
        [high, gain2_part - high, jnp.zeros((14, width), F32)], axis=0
    ).astype(BF)
    spread[me_t, share : share + 16, width:] = jnp.zeros((16, 128), BF)
    gather = Gather(net, lambda re, rt: spread.at[flip(me_t, rt)], high_bits[::-1] + tensor_bits[:1])
    while gather.steps:
        gather.start()
        advance(out_sum)
        gather.finish()

    length = lengths_ref[0, me_d]
    inv = HEAD_DIM**-0.5
    live = (sublanes((rows, 1)) < length).astype(F32)
    hidden_grad_all = spread[:, 0:share, :width].reshape(rows, width)
    branch = (hidden_grad_all.astype(F32) * live).astype(BF)
    heads_grad = dot(branch, wo_ref[...], 1, 1).astype(BF)
    cosine, sine = cos_ref[...], -sin_ref[...]
    lane = lanes((rows, 128))
    low_half = lane % HEAD_DIM < HEAD_DIM // 2
    low_lane = lane < HEAD_DIM
    q, k, v = q_ref[...], k_ref[...], v_ref[...]
    k_b, v_b = swap(k), swap(v)
    key, query = sublanes((rows, rows)), lanes((rows, rows))
    allowed = (key <= query) & (key < length)
    logsum_rows = jnp.transpose(logsum_ref[...])
    dk = [jnp.zeros((rows, 128), F32), jnp.zeros((rows, 128), F32)]
    dv = [jnp.zeros((rows, 128), F32), jnp.zeros((rows, 128), F32)]
    q_width = q.shape[1]
    pair = None
    for index in range(q_width // HEAD_DIM):
        same = index % 2 == (index // 2) % 2
        q_one, k_one = head_parts(q, k, k_b, index, low_lane)
        g_one, v_one = head_parts(heads_grad, v, v_b, index, low_lane)
        scores = jnp.where(allowed, dot(k_one, q_one, 1, 1) * inv, NEG)
        prob = jnp.exp(scores - logsum_rows[index : index + 1, :])
        grad_prob = dot(v_one, g_one, 1, 1)
        center = jnp.sum(prob * grad_prob, axis=0, keepdims=True)
        score_grad = (prob * (grad_prob - center)).astype(BF)
        dq = dot(score_grad, k_one, 0, 0) * inv
        place = 0 if same else 1
        dk[place] = dk[place] + dot(score_grad, q_one) * inv
        dv[place] = dv[place] + dot(prob.astype(BF), g_one)
        if index % 2 == 0:
            pair = dq
        else:
            cut = slice((index // 2) * 128, (index // 2) * 128 + 128)
            both = jnp.where(low_lane, pair, dq)
            back_ref[:, cut] = rotate128(both, cosine, sine, low_half).astype(BF)
            advance(out_sum)
    k_width = k.shape[1]
    k_total = dk[0] + pltpu.roll(dk[1], HEAD_DIM, 1)
    v_total = dv[0] + pltpu.roll(dv[1], HEAD_DIM, 1)
    back_ref[:, q_width : q_width + k_width] = rotate128(k_total, cosine, sine, low_half).astype(BF)
    back_ref[:, q_width + k_width :] = v_total.astype(BF)
    back = back_ref[...]
    first = (
        dot(back[:, :q_width], wq_ref[...], 1, 1)
        + dot(back[:, q_width : q_width + k_width], wk_ref[...], 1, 1)
        + dot(back[:, q_width + k_width :], wv_ref[...], 1, 1)
    )
    columns = width // tensor_count
    for t in range(tensor_count):
        first_part[t] = first[:, t * columns : (t + 1) * columns].astype(BF)
    first_sum = Reduce(
        net, lambda re, rt: first_part.at[flip(me_t, rt)], lambda i: first_landing.at[i], tensor_bits,
        [(0, r) for r in range(tensor_count)],
    )
    first_sum.start()
    x = x_ref[...].astype(F32)
    scale = lax.rsqrt(jnp.mean(x * x, axis=-1, keepdims=True) + EPS)
    along = first * (x * scale)
    stat = jnp.sum(along * gain_ref[...].astype(F32)[None, :], axis=-1, keepdims=True)
    stat_row = jnp.transpose(jnp.broadcast_to(stat, (rows, 128)))[0:8, :]
    tiny[:, :width] = jnp.broadcast_to(jnp.sum(along, axis=0, keepdims=True), (8, width))
    tiny[:, width:] = stat_row
    tiny_copies = [net.send(tiny, tiny_landing.at[m - 1], "tensor", m) for m in range(1, tensor_count)]
    first_sum.finish()
    while first_sum.steps:
        first_sum.start()
        grads = dot(normed_ref[...], back, 0, 0)
        q_grad_ref[...] = grads[:, :q_width].astype(BF)
        k_grad_ref[...] = grads[:, q_width : q_width + k_width].astype(BF)
        v_grad_ref[...] = grads[:, q_width + k_width :].astype(BF)
        out_grad_ref[...] = dot(heads_ref[...], branch, 0, 0).astype(BF)
        load_x.wait()
        router_rows = dot(spread[:, 0:share, width:].reshape(rows, 128), normed2[...], 0, 0)
        small_ref[0:EXPERTS, :] = router_rows[0:EXPERTS].astype(BF)
        first_sum.finish()
    for copy in tiny_copies:
        copy.wait_recv()
    tiny_all = tiny[...]
    for m in range(1, tensor_count):
        tiny_all = tiny_all + tiny_landing[m - 1]
    gain2_sum = jnp.zeros((1, width), F32)
    for t in range(tensor_count):
        block = spread[t, share : share + 16, :width].astype(F32)
        gain2_sum = gain2_sum + block[0:1] + block[1:2]
    small_ref[EXPERTS:, :] = jnp.concatenate(
        [tiny_all[0:1, :width], gain2_sum, jnp.zeros((14, width), F32)], axis=0
    ).astype(BF)
    stat_all = jnp.transpose(
        jnp.concatenate([tiny_all[:, width:], jnp.zeros((120, rows), F32)], axis=0)
    )[:, 0:1] / width
    begin = pl.multiple_of(me_t * columns, columns)
    cut = pl.ds(begin, columns)
    old = jnp.concatenate([spread[t, 0:share, cut] for t in range(tensor_count)], axis=0).astype(F32)
    input_ref[...] = (
        old + scale * (
            first_part[me_t].astype(F32) * gain_ref[cut].astype(F32)[None, :] - x_ref[:, cut].astype(F32) * scale * stat_all
        )
    ).astype(BF)
    while out_sum.flight or out_sum.steps:
        advance(out_sum)
    block_ref[...] = out[here, me_t]
    net.close()


def back_call(group_count, lengths, vmem_operands, grad, out, xown, waits):
    dy, x = vmem_operands[0], vmem_operands[1]
    rows, width = x.shape
    wq, wk, wv, wo = vmem_operands[13:17]
    tensor_count, dp_count = lax.axis_size("tensor"), lax.axis_size("dp")
    share, columns = rows // tensor_count, width // tensor_count
    chunks = group_count * tensor_count
    shape = jax.ShapeDtypeStruct
    copies = 96
    return pl.pallas_call(
        functools.partial(back_kernel, (group_count, tensor_count, dp_count), len(waits)),
        out_shape=(
            shape((rows, columns), BF), shape((rows, columns), BF),
            shape(wq.shape, BF), shape(wk.shape, BF), shape(wv.shape, BF), shape(wo.shape, BF),
            shape((TABLE_ROWS, width), BF),
        ),
        in_specs=[pl.BlockSpec(memory_space=pltpu.SMEM)] + vmem(len(vmem_operands)) + [pl.BlockSpec(memory_space=pl.ANY)] * (3 + len(waits)),
        out_specs=tuple(vmem(7)),
        scratch_shapes=[
            pltpu.VMEM(grad.shape, BF),
            pltpu.VMEM((2, chunks - 1, share // 2, width + 128), BF),
            pltpu.VMEM(out.shape, BF),
            pltpu.VMEM((chunks - 1, rows, columns), BF),
            pltpu.VMEM((rows, width), BF),
            pltpu.VMEM((tensor_count, share + 16, width + 128), BF),
            pltpu.VMEM((tensor_count, rows, columns), BF),
            pltpu.VMEM((tensor_count - 1, rows, columns), BF),
            pltpu.VMEM((8, width + rows), F32),
            pltpu.VMEM((tensor_count - 1, 8, width + rows), F32),
            pltpu.VMEM((rows, wq.shape[1] + wk.shape[1] + wv.shape[1]), BF),
            pltpu.VMEM((EXPERTS, rows), F32),
            pltpu.SemaphoreType.DMA((copies,)),
            pltpu.SemaphoreType.DMA((copies,)),
            pltpu.SemaphoreType.DMA((3,)),
        ],
        compiler_params=params(60, collective_id=2, has_side_effects=True),
        cost_estimate=pl.CostEstimate(flops=2 * rows * width * 8192, bytes_accessed=16 * MIB, transcendentals=0),
        name="back",
    )(lengths, *vmem_operands, grad, out, xown, *waits)


def gate_rows(router_t, rows, table):
    logits = dot(router_t, rows, 1, 1)
    chosen = table > 0.5
    masked = jnp.where(chosen, logits, NEG)
    weights = jnp.where(chosen, jnp.exp(masked - jnp.max(masked, axis=0, keepdims=True)), 0.0)
    total = jnp.sum(weights, axis=0, keepdims=True)
    return weights / jnp.where(total > 0.0, total, 1.0)


def expert_kernel(own, groups, dp_count, capacity, local, distance, x_ref, dy_ref, table_ref, router_ref, wg_ref, wu_ref, wd_ref, *rest):
    if own:
        hidden_ref, *rest = rest
        out_c_ref, out_g_ref, gg_ref, gu_ref, gd_ref, gates, ranks, xs, ys, gs, mats, gi_rows, acc_c, acc_g = rest[-14:]
    else:
        gin_g_ref, gin_u_ref, gin_d_ref, gg_ref, gu_ref, gd_ref, gates, ranks, xs, ys, gs = rest
    chunk, pair = pl.program_id(0), pl.program_id(1)
    dp_here, me_t, me_e = lax.axis_index("dp"), lax.axis_index("tensor"), lax.axis_index("expert")
    first_expert = me_e * local + pair * 2
    rows, width = x_ref.shape[-2:]
    single = own or distance > 0
    per_group = 1 if single else dp_count - 1
    units = groups * per_group

    def unit_place(i):
        if single:
            return (i,), i, lax.rem(dp_here + distance, dp_count)
        d = dp_here + 1 + i % per_group
        d = jnp.where(d >= dp_count, d - dp_count, d)
        return (i // per_group, d), i // per_group, d

    @pl.when(pair == 0)
    def _():
        @pl.loop(0, units)
        def _(i):
            at, group, d = unit_place(i)
            table = given_table(table_ref, group, d.astype(F32))
            ranks[i] = table
            gates[i] = gate_rows(router_ref[...], x_ref[at], table)

    slot_id = sublanes((capacity, rows))

    @pl.loop(0, units)
    def _(i):
        at, _, _ = unit_place(i)
        pieces = []
        for j in range(2):
            rank = ranks[i, pl.ds(first_expert + j, 1), :].astype(jnp.int32) - 1
            gate = gates[i, pl.ds(first_expert + j, 1), :]
            hit = slot_id == rank
            gs[j, i] = jnp.broadcast_to(
                jnp.sum(jnp.where(hit, gate, 0.0), axis=-1, keepdims=True), (capacity, 128)
            )
            pieces.append(jnp.where(hit, 1.0, 0.0).astype(BF))
        onehot = jnp.concatenate(pieces, axis=0)
        if own:
            mats[i] = onehot
        moved_x = dot(onehot, x_ref[at]).astype(BF)
        moved_y = dot(onehot, dy_ref[at]).astype(BF)
        for j in range(2):
            cut = slice(j * capacity, (j + 1) * capacity)
            xs[j, i] = moved_x[cut]
            ys[j, i] = moved_y[cut]

    hidden = wg_ref.shape[2]
    if own:

        @pl.when(pair == 0)
        def _():
            gi_rows[...] = jnp.zeros_like(gi_rows)

    terms_c, terms_g = [], []
    for j in range(2):
        x_here = xs[j].reshape(units * capacity, width)
        y_here = ys[j].reshape(units * capacity, width)
        scale = gs[j].reshape(units * capacity, 128)
        both = dot(x_here, jnp.concatenate([wg_ref[j], wu_ref[j]], axis=1))
        g_here, u_here = both[:, :hidden], both[:, hidden:]
        act_back = dot(y_here, wd_ref[j], 1, 1)
        sig = 1.0 / (1.0 + jnp.exp(-g_here))
        silu = g_here * sig
        act = silu * u_here
        act_gated = (act * scale).astype(BF)
        grad_act = act_back * scale
        grad_gate = (grad_act * u_here * sig * (1.0 + g_here * (1.0 - sig))).astype(BF)
        grad_up = (grad_act * silu).astype(BF)
        grads = jnp.concatenate([grad_gate, grad_up], axis=1)
        weight_grads = dot(x_here, grads, 0, 0)
        down = dot(act_gated, y_here, 0, 0)
        if own:
            gg_ref[j] = weight_grads[:, :hidden]
            gu_ref[j] = weight_grads[:, hidden:]
            gd_ref[j] = down
            inner = jnp.sum(act * act_back, axis=-1, keepdims=True)
            stacked = jnp.concatenate([act_gated, grads], axis=1)
            for i in range(units):
                cut = slice(i * capacity, (i + 1) * capacity)
                back = mats[i, j * capacity : (j + 1) * capacity, :]
                mats_t = dot(back, stacked[cut], 0, 0).astype(BF)
                terms_c.append(mats_t[:, :hidden])
                terms_g.append(mats_t[:, hidden:])
                gi_rows[i, pl.ds(first_expert + j, 1), :] = jnp.sum(back.astype(F32) * inner[cut], axis=0, keepdims=True)
        else:
            gg_ref[j] = gin_g_ref[j] + weight_grads[:, :hidden]
            gu_ref[j] = gin_u_ref[j] + weight_grads[:, hidden:]
            gd_ref[j] = gin_d_ref[j] + down
    if own:
        down_pair = wd_ref[...].reshape(2 * hidden, width)
        in_pair = jnp.concatenate([wg_ref[0], wu_ref[0], wg_ref[1], wu_ref[1]], axis=1)
        blocks, columns = out_c_ref.shape[1], out_c_ref.shape[3]
        share = hidden_ref.shape[0]
        for i in range(units):
            left_c = jnp.concatenate([terms_c[i], terms_c[units + i]], axis=1)
            left_g = jnp.concatenate([terms_g[i], terms_g[units + i]], axis=1)
            add_c = dot(left_c, down_pair)
            add_g = dot(left_g, in_pair, 1, 1)

            @pl.when(pair == 0)
            def _():
                acc_c[i] = add_c
                acc_g[i] = add_g

            @pl.when(pair != 0)
            def _():
                acc_c[i] += add_c
                acc_g[i] += add_g

        @pl.when(pair == pl.num_programs(1) - 1)
        def _():
            for i in range(units):

                @pl.when(chunk * groups + i == me_e)
                def _():
                    cut = pl.ds(pl.multiple_of(me_t * share, share), share)
                    acc_c[i, cut, :] += hidden_ref[...]

                for t in range(blocks):
                    out_c_ref[i, t] = acc_c[i, :, t * columns : (t + 1) * columns].astype(BF)
                out_g_ref[i, :, :width] = acc_g[i].astype(BF)
                out_g_ref[i, :, width:] = jnp.transpose(gi_rows[i]).astype(BF)


def expert_call(own, x, dy, table, router_t, wg, wu, wd, more, distance=0):
    groups_all, dp_count = table.shape[:2]
    rows, width = x.shape[-2:]
    chunk_groups = 2
    chunks = groups_all // chunk_groups
    local, _, hidden = wg.shape
    pairs = local // 2
    assert chunks == 1 or pairs == 1
    capacity = rows * TOP // EXPERTS
    shape = jax.ShapeDtypeStruct
    units = chunk_groups * (1 if own or distance else dp_count - 1)
    row_shape = (chunk_groups, *x.shape[1:])
    row_block = pl.BlockSpec(
        row_shape, lambda c, p: (c,) + (0,) * (len(row_shape) - 1), pipeline_mode=pl.Buffered(1)
    )
    in_block = pl.BlockSpec((2, width, hidden), lambda c, p: (p, 0, 0))
    down_block = pl.BlockSpec((2, hidden, width), lambda c, p: (p, 0, 0))
    in_specs = [
        row_block, row_block,
        pl.BlockSpec((chunk_groups, dp_count, TABLE_ROWS, rows), lambda c, p: (c, 0, 0, 0)),
        pl.BlockSpec((EXPERTS, width), lambda c, p: (0, 0)),
        in_block, in_block, down_block,
    ]
    grads_out = (shape(wg.shape, F32), shape(wu.shape, F32), shape(wd.shape, F32))
    grad_specs = (in_block, in_block, down_block)
    scratch = [
        pltpu.VMEM((units, EXPERTS, rows), F32),
        pltpu.VMEM((units, EXPERTS, rows), F32),
        pltpu.VMEM((2, units, capacity, width), BF),
        pltpu.VMEM((2, units, capacity, width), BF),
        pltpu.VMEM((2, units, capacity, 128), F32),
    ]
    operands = [x, dy, table, router_t, wg, wu, wd]
    if own:
        hidden_share, *waits = more
        blocks = lax.axis_size("tensor")
        columns = width // blocks
        in_specs.append(pl.BlockSpec(hidden_share.shape, lambda c, p: (0, 0)))
        operands.append(hidden_share)
        in_specs += [pl.BlockSpec(memory_space=pl.ANY)] * len(waits)
        operands += waits
        out_shape = (
            shape((groups_all, blocks, rows, columns), BF), shape((groups_all, rows, width + 128), BF), *grads_out,
        )
        out_specs = (
            pl.BlockSpec((chunk_groups, blocks, rows, columns), lambda c, p: (c, 0, 0, 0)),
            pl.BlockSpec((chunk_groups, rows, width + 128), lambda c, p: (c, 0, 0)),
            *grad_specs,
        )
        scratch += [pltpu.VMEM((units, 2 * capacity, rows), BF), pltpu.VMEM((units, 128, rows), F32)]
        scratch += [pltpu.VMEM((units, rows, width), F32)] * 2
        aliases = {}
    else:
        out_shape, out_specs = grads_out, grad_specs
        in_specs += list(grad_specs)
        operands += list(more)
        aliases = {7: 0, 8: 1, 9: 2}
    flops = 2 * chunks * pairs * 2 * units * capacity * width * hidden * (28 if own else 14)
    return pl.pallas_call(
        functools.partial(expert_kernel, own, chunk_groups, dp_count, capacity, local, distance),
        out_shape=out_shape,
        grid=(chunks, pairs),
        in_specs=in_specs,
        out_specs=out_specs,
        scratch_shapes=scratch,
        input_output_aliases=aliases,
        compiler_params=params(60, dimension_semantics=("arbitrary", "arbitrary")),
        cost_estimate=pl.CostEstimate(flops=2 * flops, bytes_accessed=60 * MIB, transcendentals=0),
        name="experts_own" if own else "experts_other",
    )(*operands)


def on_device(
    tokens, cotangent, seq_lengths, deal_order, routes, slot_order, first_gain, w_query, w_key, w_value, w_out,
    second_gain, w_router, w_gate, w_up, w_down,
):
    dp_count = lax.axis_size("dp")
    dp_index = lax.axis_index("dp")
    tensor_count = lax.axis_size("tensor")
    tensor_index = lax.axis_index("tensor")
    expert_count = lax.axis_size("expert")
    expert_index = lax.axis_index("expert")
    rows, width = tokens.shape
    share = rows // tensor_count
    everywhere = ("expert", "dp", "tensor")
    unit_shape = (expert_count, dp_count, rows, width)

    cosine, sine = (jnp.asarray(values) for values in rotary_tables(rows))
    gain1, gain2 = first_gain, second_gain
    router_t = w_router.T
    normed, q, k, v, heads, logsum, hidden, normed_share, tables, x_own, dy_own = front(
        seq_lengths, deal_order, tokens, gain1, w_query, w_key, w_value, w_out, cosine, sine, gain2, routes.T, slot_order, cotangent
    )
    dy_share = lax.dynamic_slice_in_dim(cotangent, tensor_index * share, share, 0)
    never = seq_lengths[0, 0] < 0

    def after(values, other):
        return jnp.where(never, other.astype(values.dtype), values)

    def gathered(values):
        return lax.all_gather(values, everywhere, axis=0, tiled=True).reshape(unit_shape)

    small_mesh = expert_count == 2
    extra = ()
    if small_mesh:
        dy_all = gathered(dy_share)
        x_all = gathered(normed_share)
    out_c, out_g, pg, pu, pd = expert_call(
        True, x_own, dy_own, tables, router_t, w_gate, w_up, w_down, (hidden,) + ((dy_all,) if small_mesh else ())
    )
    group_count = expert_count
    if small_mesh:
        extra = (x_all,)
    else:
        out_c = lax.psum_scatter(out_c, "expert", scatter_dimension=0, tiled=True)
        out_g = lax.psum_scatter(out_g, "expert", scatter_dimension=0, tiled=True)
        x_own = lax.dynamic_slice_in_dim(x_own, expert_index, 1, 0)
        group_count = 1
    block_out, input_grad, q_term, k_term, v_term, out_term, small = back_call(
        group_count, seq_lengths,
        (cotangent, tokens, gain1, gain2, router_t, hidden, tables, normed, q, k, v, heads, logsum,
         w_query, w_key, w_value, w_out, cosine, sine),
        out_g, out_c, x_own, extra,
    )
    out_sum, q_sum, k_sum, v_sum, small_sum = lax.psum((out_term, q_term, k_term, v_term, small), ("expert", "dp"))
    grads = (pg, pu, pd)
    if small_mesh:
        grads = expert_call(False, x_all, dy_all, tables, router_t, w_gate, w_up, w_down, grads)
    else:
        for distance in range(1, dp_count):
            pairs = [(i, (i - distance) % dp_count) for i in range(dp_count)]
            moved = (
                lax.all_gather(
                    lax.ppermute(after(values, small[0, 0] + grads[2][0, 0, 0].astype(BF)), "dp", pairs),
                    ("expert", "tensor"), axis=0, tiled=True,
                ).reshape(expert_count, rows, width)
                for values in (normed_share, dy_share)
            )
            grads = expert_call(False, *moved, tables, router_t, w_gate, w_up, w_down, grads, distance)
    gate_grad, up_grad, down_grad = grads
    last = down_grad[0, 0, 0]
    out_sum, q_sum, k_sum, v_sum, small_sum = (
        after(values.astype(F32), last) for values in (out_sum, q_sum, k_sum, v_sum, small_sum)
    )
    return (
        block_out, input_grad, small_sum[EXPERTS], q_sum.astype(F32), k_sum.astype(F32), v_sum.astype(F32),
        out_sum.astype(F32), small_sum[EXPERTS + 1], small_sum[:EXPERTS].T, gate_grad, up_grad, down_grad,
    )


def solution(mesh):
    rows2 = P(("expert", "dp"), None)
    placed = (
        rows2, rows2, P("expert", None), P("expert", None), rows2, rows2, P(),
        P(None, "tensor"), P(None, "tensor"), P(None, "tensor"), P("tensor", None), P(), P(),
        P("expert", None, "tensor"), P("expert", None, "tensor"), P("expert", "tensor", None),
    )
    return jax.shard_map(
        on_device,
        mesh=mesh,
        in_specs=placed,
        out_specs=(
            P(("expert", "dp"), "tensor"), P(("expert", "dp"), "tensor"), P(),
            P(None, "tensor"), P(None, "tensor"), P(None, "tensor"), P("tensor", None), P(), P(),
            P("expert", None, "tensor"), P("expert", None, "tensor"), P("expert", "tensor", None),
        ),
        check_vma=False,
    )
```

```python
import functools

import jax
import jax.numpy as jnp
import numpy as np
from jax import lax
from jax.experimental import pallas as pl
from jax.experimental.pallas import tpu as pltpu
from jax.sharding import PartitionSpec as P

HEADS = 16
KV_HEADS = 8
HEAD_DIM = 64
EXPERTS = 32
TOP = 8
SLOT = 512

EPS = 1e-06
THETA = 10000.0
NEG = -1e30
BF = jnp.bfloat16
F32 = jnp.float32
MIB = 1 << 20


def dot(a, b, ca=1, cb=0):
    return lax.dot_general(a, b, (((ca,), (cb,)), ((), ())), preferred_element_type=F32)


def vmem(count=1):
    return [pl.BlockSpec(memory_space=pltpu.VMEM)] * count


def params(mib, **more):
    return pltpu.CompilerParams(vmem_limit_bytes=mib * MIB, **more)


def rotary_tables(rows):
    places = np.arange(rows, dtype=np.float32)[:, None]
    halfway = HEAD_DIM // 2
    spread = np.float32(THETA) ** (-2.0 * np.arange(halfway, dtype=np.float32) / HEAD_DIM)
    angles = (places * spread.astype(np.float32)[None, :]).astype(np.float32)
    copies = 128 // halfway
    return (
        np.tile(np.cos(angles), (1, copies)).astype(np.float32),
        np.tile(np.sin(angles), (1, copies)).astype(np.float32),
    )


def rotate128(values, cosine, sine, low_half):
    half = HEAD_DIM // 2
    up = pltpu.roll(values, 128 - half, 1)
    down = pltpu.roll(values, half, 1)
    return values * cosine + jnp.where(low_half, -up, down) * sine


def lanes(shape):
    return lax.broadcasted_iota(jnp.int32, shape, len(shape) - 1)


def sublanes(shape):
    return lax.broadcasted_iota(jnp.int32, shape, len(shape) - 2)


def bits_of(count):
    return [1 << i for i in range(count.bit_length() - 1)]


def flip(value, mask):
    for bit in bits_of(1 << 16):
        if mask & bit:
            value = value + bit - 2 * bit * lax.rem(lax.div(value, bit), 2)
    return value


class Net:
    def __init__(self, send_sem, recv_sem):
        self.send_sem, self.recv_sem, self.used, self.copies = send_sem, recv_sem, 0, []
        self.me = {axis: lax.axis_index(axis) for axis in ("expert", "tensor", "dp")}

    def barrier(self, partners):
        sem = pltpu.get_barrier_semaphore()
        for axis, mask in partners:
            pl.semaphore_signal(
                sem, inc=1, device_id={axis: flip(self.me[axis], mask)}, device_id_type=pl.DeviceIdType.MESH
            )
        pl.semaphore_wait(sem, len(partners))

    def send(self, source, target, axis, mask):
        k = self.used
        self.used += 1
        copy = Copy(self, k, source, target, axis, mask)
        copy.build().start()
        self.copies.append(copy)
        return copy

    def close(self):
        for copy in self.copies:
            copy.build().wait_send()


class Copy:
    def __init__(self, net, index, source, target, axis, mask):
        self.net, self.index, self.source, self.target, self.axis, self.mask = net, index, source, target, axis, mask

    def build(self):
        source = self.source() if callable(self.source) else self.source
        target = self.target() if callable(self.target) else self.target
        return pltpu.make_async_remote_copy(
            src_ref=source, dst_ref=target,
            send_sem=self.net.send_sem.at[self.index], recv_sem=self.net.recv_sem.at[self.index],
            device_id={self.axis: flip(self.net.me[self.axis], self.mask)}, device_id_type=pl.DeviceIdType.MESH,
        )

    def wait_recv(self):
        self.build().wait_recv()


class Gather:
    def __init__(self, net, at, steps, known=((0, 0),), first=None):
        self.net, self.at, self.steps, self.known, self.first, self.flight = net, at, list(steps), list(known), first, []

    def start(self):
        axis, mask = self.steps.pop(0)
        fresh = []
        for re, rt in self.known:
            place = functools.partial(self.at, re, rt)
            source = self.first if self.first is not None and (re, rt) == (0, 0) else place
            self.flight.append(self.net.send(source, place, axis, mask))
            fresh.append((re ^ mask, rt) if axis == "expert" else (re, rt ^ mask))
        self.known += fresh

    def finish(self):
        for copy in self.flight:
            copy.wait_recv()
        self.flight = []


class Reduce:
    def __init__(self, net, at, landing, steps, chunks):
        self.net, self.at, self.landing, self.steps, self.live = net, at, landing, list(steps), list(chunks)
        self.used, self.flight = 0, []

    def start(self):
        axis, mask = self.steps.pop(0)
        side = 0 if axis == "expert" else 1
        going = [r for r in self.live if r[side] & mask]
        self.live = [r for r in self.live if not r[side] & mask]
        for r in going:
            kept = (r[0] ^ mask, r[1]) if side == 0 else (r[0], r[1] ^ mask)
            copy = self.net.send(functools.partial(self.at, *r), functools.partial(self.landing, self.used), axis, mask)
            self.flight.append((kept, copy, self.used))
            self.used += 1
        if self.steps:
            axis, mask = self.steps[0]
            side = 0 if axis == "expert" else 1
            self.flight.sort(key=lambda item: 0 if item[0][side] & mask else 1)

    def finish(self):
        for kept, copy, slot in self.flight:
            copy.wait_recv()
            place = self.at(*kept)
            place[...] = (place[...].astype(F32) + self.landing(slot)[...].astype(F32)).astype(BF)
        self.flight = []


class AllReduce:
    def __init__(self, net, stages, landing, steps):
        self.net, self.stages, self.landing, self.steps, self.flight = net, stages, landing, list(steps), []

    def finish(self):
        k = len(self.flight)
        self.flight[-1].wait_recv()
        self.stages[k] = self.stages[k - 1] + self.landing[k - 1]

    def start(self):
        k = len(self.flight)
        axis, mask = self.steps[k]
        self.flight.append(self.net.send(lambda: self.stages.at[k], lambda: self.landing.at[k], axis, mask))

    def advance(self, k):
        if 1 <= k <= len(self.steps):
            self.finish()
        if k < len(self.steps):
            self.start()


TABLE_ROWS = 48
SMALL_ROWS = 128


def table_of(length, routes_ref, order_ref):
    rows = routes_ref.shape[1]
    capacity = rows * TOP // EXPERTS
    entries = rows * TOP
    chunk = 512
    routes_t = routes_ref[...].astype(F32).astype(BF)
    upper = (sublanes((chunk, chunk)) < lanes((chunk, chunk))).astype(F32).astype(BF)
    expert_row = sublanes((EXPERTS, chunk))

    def body(step, carried):
        counts, table = carried
        entry = order_ref[:, pl.ds(pl.multiple_of(step * chunk, chunk), chunk)]
        row, choice = entry // TOP, entry % TOP
        onehot_row = (sublanes((rows, chunk)) == row).astype(F32).astype(BF)
        picked = dot(routes_t, onehot_row)
        expert = jnp.sum(jnp.where(sublanes((TOP, chunk)) == choice, picked, 0.0), axis=0, keepdims=True)
        member = (expert_row.astype(F32) == expert) & (row < length)
        member_f = member.astype(F32)
        before = dot(member_f.astype(BF), upper) + counts
        value = jnp.where(member, jnp.minimum(before, float(capacity)) + 1.0, 0.0)
        table = table + dot(value.astype(BF), onehot_row, 1, 1)
        return counts + jnp.sum(member_f, axis=1, keepdims=True), table

    _, table = lax.fori_loop(
        0, entries // chunk, body, (jnp.zeros((EXPERTS, 1), F32), jnp.zeros((EXPERTS, rows), F32))
    )
    return table


def given_table(tables, index, dp_here):
    total = 0.0
    for j in range(tables.shape[1]):
        source = tables[index, j, EXPERTS : EXPERTS + 16, :].astype(F32)[0:1]
        total = total + jnp.where(source == dp_here, tables[index, j, 0:EXPERTS, :].astype(F32), 0.0)
    return total


def head_parts(q, k_a, k_b, index, low_lane):
    block = q[:, (index // 2) * 128 : (index // 2) * 128 + 128]
    mine = low_lane if index % 2 == 0 else jnp.logical_not(low_lane)
    return jnp.where(mine, block, jnp.zeros((), block.dtype)), (k_a if index % 2 == (index // 2) % 2 else k_b)


def swap(block):
    return pltpu.roll(block.astype(F32), HEAD_DIM, 1).astype(BF)


def front_kernel(
    sizes,
    lengths_ref, order_of_ref, x_ref, gain_ref, wq_ref, wk_ref, wv_ref, wo_ref, cos_ref, sin_ref, gain2_ref, routes_ref, order_ref, dy_ref,
    normed_ref, q_ref, k_ref, v_ref, heads_ref, logsum_ref, hidden_ref, share_ref, tables_ref, far_dy_ref, xown_ref, dyown_ref,
    part, landing, send_sem, recv_sem, local_sem,
):
    expert_count, tensor_count, dp_count = sizes
    rows, width = x_ref.shape
    share = rows // tensor_count
    half = rows // 2
    net = Net(send_sem, recv_sem)
    me_e, me_t, me_d = net.me["expert"], net.me["tensor"], net.me["dp"]
    expert_bits = [("expert", b) for b in bits_of(expert_count)]
    tensor_bits = [("tensor", b) for b in bits_of(tensor_count)]
    net.barrier(expert_bits + tensor_bits + [("dp", m) for m in range(1, dp_count)])

    keep_dy = pltpu.make_async_copy(dy_ref, dyown_ref.at[me_e], local_sem.at[0])
    keep_dy.start()
    half_start = pl.multiple_of(lax.rem(me_t, 2) * half, half)
    dy_half = Gather(
        net, lambda re, rt: dyown_ref.at[flip(me_e, re), pl.ds(half_start, half)], expert_bits,
        first=dy_ref.at[pl.ds(half_start, half)],
    )
    dy_half.start()
    mine_rows = pl.multiple_of(me_t * share, share)
    far_copies = [
        net.send(dy_ref.at[pl.ds(mine_rows, share)], far_dy_ref.at[m - 1], "dp", m) for m in range(1, dp_count)
    ]

    length, source, dealt_length = lengths_ref[0, me_d], order_of_ref[0, me_d], 0
    for i in range(dp_count):
        dealt_length = jnp.where(source == i, lengths_ref[0, i], dealt_length)
    x = x_ref[...].astype(F32)
    scale = lax.rsqrt(jnp.mean(x * x, axis=-1, keepdims=True) + EPS)
    normed = (x * scale * gain_ref[...].astype(F32)[None, :]).astype(BF)
    normed_ref[...] = normed
    cosine, sine = cos_ref[...], sin_ref[...]
    lane = lanes((rows, 128))
    low_half = lane % HEAD_DIM < HEAD_DIM // 2
    low_lane = lane < HEAD_DIM
    q_pre = dot(normed, wq_ref[...])
    for block in range(q_pre.shape[1] // 128):
        cut = slice(block * 128, block * 128 + 128)
        q_ref[:, cut] = rotate128(q_pre[:, cut], cosine, sine, low_half).astype(BF)
    k = rotate128(dot(normed, wk_ref[...]), cosine, sine, low_half).astype(BF)
    v = dot(normed, wv_ref[...]).astype(BF)
    k_ref[...] = k
    v_ref[...] = v
    q = q_ref[...]
    k_b, v_b = swap(k), swap(v)
    row, col = sublanes((rows, rows)), lanes((rows, rows))
    allowed = (col <= row) & (col < length)
    logsum = jnp.zeros((rows, 128), F32)
    pair = None
    for index in range(q.shape[1] // HEAD_DIM):
        q_one, k_one = head_parts(q, k, k_b, index, low_lane)
        v_one = v if index % 2 == (index // 2) % 2 else v_b
        scores = jnp.where(allowed, dot(q_one, k_one, 1, 1) * (HEAD_DIM**-0.5), NEG)
        highest = jnp.max(scores, axis=-1, keepdims=True)
        weights = jnp.exp(scores - highest)
        total = jnp.sum(weights, axis=-1, keepdims=True)
        mixed = dot((weights / total).astype(BF), v_one)
        logsum = jnp.where(lane == index, highest + jnp.log(total), logsum)
        if index % 2 == 0:
            pair = mixed
        else:
            cut = slice((index // 2) * 128, (index // 2) * 128 + 128)
            heads_ref[:, cut] = jnp.where(low_lane, pair, mixed).astype(BF)
    logsum_ref[...] = logsum
    live = (sublanes((rows, 1)) < length).astype(F32)
    part[...] = (dot(heads_ref[...], wo_ref[...]) * live).astype(BF).reshape(part.shape)

    attn = Reduce(
        net, lambda re, rt: part.at[flip(me_t, rt)], lambda i: landing.at[i], tensor_bits,
        [(0, r) for r in range(tensor_count)],
    )
    attn.start()
    table = table_of(dealt_length, routes_ref, order_ref)
    source = jnp.broadcast_to(source.astype(F32), (TABLE_ROWS - EXPERTS, rows))
    tables_ref[me_e, me_d] = jnp.concatenate([table, source], axis=0).astype(BF)
    mine = tables_ref.at[me_e, me_d]
    table_copies = [net.send(mine, mine, "dp", m) for m in range(1, dp_count)]
    attn.finish()
    while attn.steps:
        attn.start()
        if not attn.steps:
            dy_half.finish()
            while dy_half.steps:
                dy_half.start()
                dy_half.finish()
            for re, _ in dy_half.known[1:]:
                place = dy_half.at(re, 0)
                dy_half.flight.append(net.send(place, place, "tensor", 1))
        attn.finish()

    start = pl.multiple_of(me_t * share, share)
    hidden = x_ref[pl.ds(start, share), :].astype(F32) + part[me_t].astype(F32)
    hidden_ref[...] = hidden
    scale2 = lax.rsqrt(jnp.mean(hidden * hidden, axis=-1, keepdims=True) + EPS)
    share_ref[...] = (hidden * scale2 * gain2_ref[...].astype(F32)[None, :]).astype(BF)
    keep_x = pltpu.make_async_copy(share_ref, xown_ref.at[me_e, pl.ds(start, share)], local_sem.at[1])
    keep_x.start()
    high_bits = tensor_bits[1:][::-1]
    gathers = []
    for part_index, steps in enumerate((high_bits + expert_bits, expert_bits + high_bits)):
        size = share // 2

        def at(re, rt, offset=part_index * size):
            begin = pl.multiple_of(flip(me_t, rt) * share + offset, size)
            return xown_ref.at[flip(me_e, re), pl.ds(begin, size)]

        gathers.append(
            Gather(net, at, steps + tensor_bits[:1], first=share_ref.at[pl.ds(part_index * size, size)])
        )
    table_all = Gather(net, lambda re, rt: tables_ref.at[flip(me_e, re)], expert_bits)
    first_step = True
    while gathers[0].steps:
        for gather in gathers:
            gather.start()
        if first_step:
            for copy in table_copies:
                copy.wait_recv()
            first_step = False
        else:
            table_all.finish()
        if table_all.steps:
            table_all.start()
        for gather in gathers:
            gather.finish()
    table_all.finish()
    dy_half.finish()
    for copy in far_copies:
        copy.wait_recv()
    net.close()
    keep_dy.wait()
    keep_x.wait()


def front(lengths, order_of, x, gain, wq, wk, wv, wo, cosine, sine, gain2, routes, order, dy):
    rows, width = x.shape
    sizes = tuple(lax.axis_size(axis) for axis in ("expert", "tensor", "dp"))
    expert_count, tensor_count, dp_count = sizes
    share = rows // tensor_count
    shape = jax.ShapeDtypeStruct
    copies = 96
    return pl.pallas_call(
        functools.partial(front_kernel, sizes),
        out_shape=(
            shape((rows, width), BF), shape((rows, wq.shape[1]), BF), shape((rows, wk.shape[1]), BF),
            shape((rows, wv.shape[1]), BF), shape((rows, wq.shape[1]), BF), shape((rows, 128), F32),
            shape((share, width), F32), shape((share, width), BF), shape((expert_count, dp_count, TABLE_ROWS, rows), BF),
            shape((dp_count - 1, share, width), BF), shape((expert_count, rows, width), BF), shape((expert_count, rows, width), BF),
        ),
        in_specs=[pl.BlockSpec(memory_space=pltpu.SMEM)] * 2 + vmem(11) + [pl.BlockSpec(memory_space=pl.ANY)],
        out_specs=tuple(vmem(10)) + (pl.BlockSpec(memory_space=pl.ANY),) * 2,
        scratch_shapes=[
            pltpu.VMEM((tensor_count, share, width), BF),
            pltpu.VMEM((tensor_count - 1, share, width), BF),
            pltpu.SemaphoreType.DMA((copies,)),
            pltpu.SemaphoreType.DMA((copies,)),
            pltpu.SemaphoreType.DMA((2,)),
        ],
        compiler_params=params(56, collective_id=1, has_side_effects=True),
        cost_estimate=pl.CostEstimate(flops=MIB, bytes_accessed=MIB, transcendentals=0),
        name="front",
    )(lengths, order_of, x, gain, wq, wk, wv, wo, cosine, sine, gain2, routes, order, dy)


def back_kernel(
    sizes, passes,
    lengths_ref, dy_ref, x_ref, gain_ref, gain2_ref, router_ref, hidden_ref, tables_ref,
    normed_ref, q_ref, k_ref, v_ref, heads_ref, logsum_ref, wq_ref, wk_ref, wv_ref, wo_ref, cos_ref, sin_ref,
    grad_in_ref, xown_ref, *rest,
):
    if passes:
        rest = rest[1:]
        other_ref = rest[7]
        rest = rest[:7] + rest[8:]
    (
        first_ref, tiny_ref, hidden_grad_ref, scale_ref, dense_ref, out_grad_ref, small_ref,
        grad, grad_landing, normed2, spread, back_ref, picked, send_sem, recv_sem, local_sem,
    ) = rest
    group_count, tensor_count, dp_count = sizes
    rows, width = x_ref.shape
    share = rows // tensor_count
    net = Net(send_sem, recv_sem)
    me_e, me_t, me_d = net.me["expert"], net.me["tensor"], net.me["dp"]
    here = me_e if group_count > 1 else 0
    expert_bits = [("expert", b) for b in bits_of(group_count)]
    tensor_bits = [("tensor", b) for b in bits_of(tensor_count)]
    load_grad = pltpu.make_async_copy(grad_in_ref, grad, local_sem.at[0])
    load_x = pltpu.make_async_copy(xown_ref.at[here], normed2, local_sem.at[1])
    load_grad.start()
    load_x.start()
    net.barrier(expert_bits + tensor_bits)
    load_grad.wait()
    high_bits = tensor_bits[1:]
    chunks = [(e, t) for e in range(group_count) for t in range(tensor_count)]
    sums = []
    size = share // 2
    for part_index, steps in enumerate((high_bits + expert_bits, expert_bits + high_bits)):

        def at(re, rt, offset=part_index * size):
            begin = pl.multiple_of(flip(me_t, rt) * share + offset, size)
            return grad.at[flip(here, re) if re else here, pl.ds(begin, size)]

        sums.append(Reduce(
            net, at, lambda i, p=part_index: grad_landing.at[p, i], tensor_bits[:1] + steps, chunks
        ))
    while sums[0].steps:
        for one in sums:
            one.start()
        for one in sums:
            one.finish()

    start = pl.multiple_of(me_t * share, share)
    gain2 = gain2_ref[...].astype(F32)[None, :]
    hidden = hidden_ref[...]
    scale2 = lax.rsqrt(jnp.mean(hidden * hidden, axis=-1, keepdims=True) + EPS)
    hat2 = hidden * scale2
    second_normed = (hat2 * gain2).astype(BF)
    picked[...] = given_table(tables_ref, me_e, me_d.astype(F32))
    table = picked[:, pl.ds(start, share)]
    table = jnp.concatenate([table, jnp.zeros((128 - EXPERTS, share), F32)], axis=0)
    table = jnp.transpose(table)[:, :EXPERTS]
    logits = dot(second_normed, router_ref[...], 1, 1)
    chosen = table > 0.5
    masked = jnp.where(chosen, logits, NEG)
    weights = jnp.where(chosen, jnp.exp(masked - jnp.max(masked, axis=-1, keepdims=True)), 0.0)
    total = jnp.sum(weights, axis=-1, keepdims=True)
    gates = weights / jnp.where(total > 0.0, total, 1.0)
    gate_in = grad[here, pl.ds(start, share), width:].astype(F32)[:, :EXPERTS]
    logit_grad = (gate_in - gates * jnp.sum(gate_in, axis=-1, keepdims=True)).astype(BF)
    normed_grad = grad[here, pl.ds(start, share), :width].astype(F32) + dot(logit_grad, router_ref[...])
    along2 = normed_grad * hat2
    gain2_part = jnp.sum(along2, axis=0, keepdims=True)
    scaled = normed_grad * gain2
    hidden_grad = dy_ref[pl.ds(start, share), :].astype(F32) + scale2 * (
        scaled - hat2 * jnp.mean(scaled * hat2, axis=-1, keepdims=True)
    )
    spread[me_t, 0:share, :width] = hidden_grad.astype(BF)
    spread[me_t, 0:share, width:] = jnp.concatenate(
        [logit_grad.astype(F32), jnp.zeros((share, 128 - EXPERTS), F32)], axis=1
    ).astype(BF)
    high = gain2_part.astype(BF).astype(F32)
    spread[me_t, share : share + 16, :width] = jnp.concatenate(
        [high, gain2_part - high, jnp.zeros((14, width), F32)], axis=0
    ).astype(BF)
    spread[me_t, share : share + 16, width:] = jnp.zeros((16, 128), BF)
    gather = Gather(net, lambda re, rt: spread.at[flip(me_t, rt)], high_bits[::-1] + tensor_bits[:1])
    while gather.steps:
        gather.start()
        gather.finish()

    row_parts = plane_gathers(net, other_ref, share, done=True) if passes else []
    for one in row_parts:
        one.start()
    length = lengths_ref[0, me_d]
    inv = HEAD_DIM**-0.5
    live = (sublanes((rows, 1)) < length).astype(F32)
    hidden_grad_all = spread[:, 0:share, :width].reshape(rows, width)
    hidden_grad_ref[...] = hidden_grad_all
    branch = (hidden_grad_all.astype(F32) * live).astype(BF)
    heads_grad = dot(branch, wo_ref[...], 1, 1).astype(BF)
    cosine, sine = cos_ref[...], -sin_ref[...]
    lane = lanes((rows, 128))
    low_half = lane % HEAD_DIM < HEAD_DIM // 2
    low_lane = lane < HEAD_DIM
    q, k, v = q_ref[...], k_ref[...], v_ref[...]
    k_b, v_b = swap(k), swap(v)
    key, query = sublanes((rows, rows)), lanes((rows, rows))
    allowed = (key <= query) & (key < length)
    logsum_rows = jnp.transpose(logsum_ref[...])
    dk = [jnp.zeros((rows, 128), F32), jnp.zeros((rows, 128), F32)]
    dv = [jnp.zeros((rows, 128), F32), jnp.zeros((rows, 128), F32)]
    q_width = q.shape[1]
    pair = None
    for index in range(q_width // HEAD_DIM):
        same = index % 2 == (index // 2) % 2
        q_one, k_one = head_parts(q, k, k_b, index, low_lane)
        g_one, v_one = head_parts(heads_grad, v, v_b, index, low_lane)
        scores = jnp.where(allowed, dot(k_one, q_one, 1, 1) * inv, NEG)
        prob = jnp.exp(scores - logsum_rows[index : index + 1, :])
        grad_prob = dot(v_one, g_one, 1, 1)
        center = jnp.sum(prob * grad_prob, axis=0, keepdims=True)
        score_grad = (prob * (grad_prob - center)).astype(BF)
        dq = dot(score_grad, k_one, 0, 0) * inv
        place = 0 if same else 1
        dk[place] = dk[place] + dot(score_grad, q_one) * inv
        dv[place] = dv[place] + dot(prob.astype(BF), g_one)
        if index % 2 == 0:
            pair = dq
        else:
            cut = slice((index // 2) * 128, (index // 2) * 128 + 128)
            both = jnp.where(low_lane, pair, dq)
            back_ref[:, cut] = rotate128(both, cosine, sine, low_half).astype(BF)
    k_width = k.shape[1]
    k_total = dk[0] + pltpu.roll(dk[1], HEAD_DIM, 1)
    v_total = dv[0] + pltpu.roll(dv[1], HEAD_DIM, 1)
    back_ref[:, q_width : q_width + k_width] = rotate128(k_total, cosine, sine, low_half).astype(BF)
    back_ref[:, q_width + k_width :] = v_total.astype(BF)
    back = back_ref[...]
    first = (
        dot(back[:, :q_width], wq_ref[...], 1, 1)
        + dot(back[:, q_width : q_width + k_width], wk_ref[...], 1, 1)
        + dot(back[:, q_width + k_width :], wv_ref[...], 1, 1)
    )
    columns = width // tensor_count
    for t in range(tensor_count):
        first_ref[t] = first[:, t * columns : (t + 1) * columns].astype(BF)
    x = x_ref[...].astype(F32)
    scale = lax.rsqrt(jnp.mean(x * x, axis=-1, keepdims=True) + EPS)
    scale_ref[...] = jnp.broadcast_to(scale, (rows, 128))
    along = first * (x * scale)
    stat = jnp.sum(along * gain_ref[...].astype(F32)[None, :], axis=-1, keepdims=True)
    tiny_ref[:, 0:rows] = jnp.transpose(jnp.broadcast_to(stat, (rows, 128)))[0:8, :]
    tiny_ref[:, rows:] = jnp.broadcast_to(jnp.sum(along, axis=0, keepdims=True), (8, width))
    dense_ref[...] = dot(normed_ref[...], back, 0, 0).astype(BF)
    out_grad_ref[...] = dot(heads_ref[...], branch, 0, 0).astype(BF)
    load_x.wait()
    router_rows = dot(spread[:, 0:share, width:].reshape(rows, 128), normed2[...], 0, 0)[0:EXPERTS]
    gain2_sum = jnp.zeros((1, width), F32)
    for t in range(tensor_count):
        block = spread[t, share : share + 16, :width].astype(F32)
        gain2_sum = gain2_sum + block[0:1] + block[1:2]
    half = width // 2
    pieces = [router_rows[:, :half], router_rows[:, half:], gain2_sum[:, :half], gain2_sum[:, half:]]
    for one in row_parts:
        one.finish()
    filled = sum(piece.shape[0] for piece in pieces)
    small_ref[...] = jnp.concatenate(pieces + [jnp.zeros((SMALL_ROWS - filled, half), F32)], axis=0).astype(BF)
    net.close()


def back_call(group_count, lengths, vmem_operands, grad, xown, other=None):
    dy, x = vmem_operands[0], vmem_operands[1]
    rows, width = x.shape
    wq, wk, wv, wo = vmem_operands[13:17]
    tensor_count, dp_count = lax.axis_size("tensor"), lax.axis_size("dp")
    share, columns = rows // tensor_count, width // tensor_count
    chunks = group_count * tensor_count
    inner = wq.shape[1] + wk.shape[1] + wv.shape[1]
    shape = jax.ShapeDtypeStruct
    copies = 64
    passed = [] if other is None else [other]
    return pl.pallas_call(
        functools.partial(back_kernel, (group_count, tensor_count, dp_count), other is not None),
        out_shape=(
            shape((tensor_count, rows, columns), BF), shape((8, rows + width), F32), shape((rows, width), BF),
            shape((rows, 128), F32), shape((width, inner), BF), shape(wo.shape, BF), shape((SMALL_ROWS, width // 2), BF),
            *[shape(one.shape, BF) for one in passed],
        ),
        in_specs=[pl.BlockSpec(memory_space=pltpu.SMEM)] + vmem(len(vmem_operands)) + [pl.BlockSpec(memory_space=pl.ANY)] * (2 + len(passed)),
        out_specs=tuple(vmem(7)) + (pl.BlockSpec(memory_space=pl.ANY),) * len(passed),
        input_output_aliases={len(vmem_operands) + 3: 7} if passed else {},
        scratch_shapes=[
            pltpu.VMEM(grad.shape, BF),
            pltpu.VMEM((2, chunks - 1, share // 2, width + 128), BF),
            pltpu.VMEM((rows, width), BF),
            pltpu.VMEM((tensor_count, share + 16, width + 128), BF),
            pltpu.VMEM((rows, inner), BF),
            pltpu.VMEM((EXPERTS, rows), F32),
            pltpu.SemaphoreType.DMA((copies,)),
            pltpu.SemaphoreType.DMA((copies,)),
            pltpu.SemaphoreType.DMA((2,)),
        ],
        compiler_params=params(60, collective_id=2, has_side_effects=True),
        cost_estimate=pl.CostEstimate(flops=MIB, bytes_accessed=MIB, transcendentals=0),
        name="back",
    )(lengths, *vmem_operands, grad, xown, *passed)


def gate_rows(router_t, rows, table):
    logits = dot(router_t, rows, 1, 1)
    chosen = table > 0.5
    masked = jnp.where(chosen, logits, NEG)
    weights = jnp.where(chosen, jnp.exp(masked - jnp.max(masked, axis=0, keepdims=True)), 0.0)
    total = jnp.sum(weights, axis=0, keepdims=True)
    return weights / jnp.where(total > 0.0, total, 1.0)


def bit_steps(expert_count, tensor_count):
    expert_bits = [("expert", b) for b in bits_of(expert_count)]
    tensor_bits = [("tensor", b) for b in bits_of(tensor_count)]
    return expert_bits, tensor_bits, tensor_bits[1:][::-1]


def plane_gathers(net, target, share, first=None, done=False):
    counts = lax.axis_size("expert"), lax.axis_size("tensor")
    expert_bits, _, high_bits = bit_steps(*counts)
    size = share // 2
    parts = []
    for index, steps in enumerate((high_bits + expert_bits, expert_bits + high_bits)):

        def at(re, rt, offset=index * size):
            begin = pl.multiple_of(flip(net.me["tensor"], rt) * share + offset, size)
            return target.at[:, flip(net.me["expert"], re), pl.ds(begin, size)]

        source = None if first is None else first.at[:, pl.ds(index * size, size)]
        known = [(0, 0)]
        if done:
            axis, mask = steps.pop(0)
            known.append((mask, 0) if axis == "expert" else (0, mask))
        parts.append(Gather(net, at, steps, known=known, first=source))
    return parts


def core_gather(net, target, share, known, which=slice(None)):
    def whole(re, rt):
        begin = pl.multiple_of(flip(net.me["tensor"], rt) * share, share)
        return target.at[which, flip(net.me["expert"], re), pl.ds(begin, share)]

    return Gather(net, whole, [("tensor", 1)], known=known)


def fill_units(table, gate, slot_id, first_expert, count, hits_ref, gated_ref):
    capacity = slot_id.shape[0]
    for j in range(count):
        rank = table(first_expert + j).astype(jnp.int32) - 1
        hit = slot_id == rank
        cut = slice(j * capacity, (j + 1) * capacity)
        hits_ref[cut, :] = jnp.where(hit, 1.0, 0.0).astype(BF)
        gated_ref[cut, :] = jnp.where(hit, gate(first_expert + j), 0.0).astype(BF)


def middle(both, grad_act, hidden):
    g_here, u_here = both[:, :hidden], both[:, hidden:]
    sig = 1.0 / (1.0 + jnp.exp(-g_here))
    silu = g_here * sig
    act = silu * u_here
    grad_gate = (grad_act * u_here * sig * (1.0 + g_here * (1.0 - sig))).astype(BF)
    grad_up = (grad_act * silu).astype(BF)
    return act, jnp.concatenate([grad_gate, grad_up], axis=1)


def own_kernel(
    sizes, groups, capacity, local, batch, gathers,
    x_ref, dy_ref, table_ref, router_ref, wg_ref, wu_ref, wd_ref, hidden_ref, share_ref, far_dy_ref,
    out_c_ref, out_g_ref, xs_out, ys_out, oth_ref, othy_ref,
    gates, ranks, hits, gated, xs, ys, made, back, gi_rows, acc_c, acc_g, send_sem, recv_sem, local_sem,
):
    chunk, pair = pl.program_id(0), pl.program_id(1)
    pairs = local // 2
    per_batch = batch // 2
    expert_count, tensor_count, dp_count = sizes
    net = Net(send_sem, recv_sem)
    dp_here, me_t, me_e = net.me["dp"], net.me["tensor"], net.me["expert"]
    rows, width = x_ref.shape[-2:]
    units = groups
    hidden = wg_ref.shape[2]
    slot_id = sublanes((capacity, rows))
    share = rows // tensor_count

    if gathers:
        expert_bits, tensor_bits, high_bits = bit_steps(expert_count, tensor_count)
        cotangent_parts = plane_gathers(net, othy_ref, share, first=far_dy_ref)
        row_parts = plane_gathers(net, oth_ref, share)
        mine = pl.ds(pl.multiple_of(me_t * share, share), share)
        keep = pltpu.make_async_copy(far_dy_ref, othy_ref.at[:, me_e, mine], local_sem.at[2])
        flight = []

        def first_steps():
            net.barrier(expert_bits + tensor_bits + [("dp", m) for m in range(1, dp_count)])
            keep.start()
            for one in cotangent_parts:
                one.start()
            for m in range(1, dp_count):
                flight.append(net.send(share_ref, lambda m=m: oth_ref.at[m - 1, me_e, mine], "dp", m))

        def second_steps():
            for one in cotangent_parts:
                one.finish()
            for one in cotangent_parts:
                one.start()

        def third_steps():
            for one in cotangent_parts:
                one.finish()
            keep.wait()
            cotangent_parts.append(core_gather(net, othy_ref, share, cotangent_parts[0].known))
            cotangent_parts[-1].start()
            for copy in flight:
                copy.wait_recv()
            for one in row_parts:
                one.start()

        def last_steps():
            cotangent_parts[-1].finish()
            for one in row_parts:
                one.finish()
            net.close()

        for time, steps in ((0, first_steps), (pairs * 2 // 8, second_steps), (pairs * 6 // 8, third_steps)):

            @pl.when(pair == time)
            def _(steps=steps):
                steps()

    @pl.when(pair == 0)
    def _():
        gi_rows[...] = jnp.zeros_like(gi_rows)

        @pl.loop(0, units)
        def _(i):
            table = given_table(table_ref, i, dp_here.astype(F32))
            ranks[i] = table
            gates[i] = gate_rows(router_ref[...], x_ref[i], table)

    place = lax.rem(pair, per_batch)
    half = lax.div(pair, per_batch)
    group_start = pl.multiple_of(chunk * groups, groups)
    outs = []
    for index, (source, target) in enumerate(((xs, xs_out), (ys, ys_out))):
        outs.append(pltpu.make_async_copy(
            source, target.at[pl.ds(half * batch, batch), pl.ds(group_start, groups)], local_sem.at[index]
        ))

    @pl.when(place == 0)
    def _():
        @pl.loop(0, units)
        def _(i):
            fill_units(
                lambda e: ranks[i, pl.ds(e, 1), :], lambda e: gates[i, pl.ds(e, 1), :], slot_id,
                me_e * local + half * batch, batch, hits.at[i], gated.at[i],
            )
            xs[:, i] = dot(hits[i], x_ref[i]).astype(BF).reshape(batch, capacity, width)
            ys[:, i] = dot(gated[i], dy_ref[i]).astype(BF).reshape(batch, capacity, width)

        for copy in outs:
            copy.start()

    for j in range(2):
        spot = place * 2 + j
        x_here = xs[spot].reshape(units * capacity, width)
        y_here = ys[spot].reshape(units * capacity, width)
        inner_w = jnp.concatenate([wg_ref[j], wu_ref[j]], axis=1)
        both = dot(x_here, inner_w)
        grad_act = dot(y_here, wd_ref[j], 1, 1)
        act, grads = middle(both, grad_act, hidden)
        result = dot(act.astype(BF), wd_ref[j]).astype(BF)
        moved = dot(grads, inner_w, 1, 1).astype(BF)
        inner = jnp.sum(act * grad_act, axis=-1, keepdims=True)
        at_slot = pl.ds(pl.multiple_of(spot * capacity, capacity), capacity)
        for i in range(units):
            cut = slice(i * capacity, (i + 1) * capacity)
            made[i, at_slot, :] = result[cut]
            back[i, at_slot, :] = moved[cut]
            gi_rows[i, pl.ds(me_e * local + pair * 2 + j, 1), :] = jnp.sum(
                hits[i, at_slot, :].astype(F32) * inner[cut], axis=0, keepdims=True
            )

    @pl.when(place == per_batch - 1)
    def _():
        for copy in outs:
            copy.wait()

        @pl.loop(0, units)
        def _(i):
            add_c = dot(gated[i], made[i], 0, 0)
            add_g = dot(hits[i], back[i], 0, 0)

            @pl.when(half == 0)
            def _():
                acc_c[i] = add_c
                acc_g[i] = add_g

            @pl.when(half != 0)
            def _():
                acc_c[i] += add_c
                acc_g[i] += add_g

    @pl.when(pair == pairs - 1)
    def _():
        blocks, columns = out_c_ref.shape[1], out_c_ref.shape[3]
        for i in range(units):

            @pl.when(chunk * groups + i == me_e)
            def _():
                cut = pl.ds(pl.multiple_of(me_t * share, share), share)
                acc_c[i, cut, :] += hidden_ref[...]

            for t in range(blocks):
                out_c_ref[i, t] = acc_c[i, :, t * columns : (t + 1) * columns].astype(BF)
            out_g_ref[i, :, :width] = acc_g[i].astype(BF)
            out_g_ref[i, :, width:] = jnp.transpose(gi_rows[i]).astype(BF)
        if gathers:
            last_steps()


def own_call(x, dy, table, router_t, wg, wu, wd, hidden_share, normed_share, far_dy):
    sizes = tuple(lax.axis_size(axis) for axis in ("expert", "tensor", "dp"))
    groups_all, dp_count = table.shape[:2]
    rows, width = x.shape[-2:]
    groups = 2
    chunks = groups_all // groups
    local, _, hidden = wg.shape
    pairs = local // 2
    assert chunks == 1 or pairs == 1
    batch = min(8, local)
    gathers = chunks == 1
    capacity = rows * TOP // EXPERTS
    shape = jax.ShapeDtypeStruct
    row_block = pl.BlockSpec((groups, rows, width), lambda c, p: (c, 0, 0), pipeline_mode=pl.Buffered(1))
    in_block = pl.BlockSpec((2, width, hidden), lambda c, p: (p, 0, 0))
    blocks = sizes[1]
    columns = width // blocks
    copies = 64
    slots = shape((local, groups_all, capacity, width), BF)
    anywhere = pl.BlockSpec(memory_space=pl.ANY)
    return pl.pallas_call(
        functools.partial(own_kernel, sizes, groups, capacity, local, batch, gathers),
        out_shape=(
            shape((groups_all, blocks, rows, columns), BF), shape((groups_all, rows, width + 128), BF), slots, slots,
            *[shape((dp_count - 1, groups_all, rows, width) if gathers else (16, 128), BF)] * 2,
        ),
        grid=(chunks, pairs),
        in_specs=[
            row_block, row_block,
            pl.BlockSpec((groups, dp_count, TABLE_ROWS, rows), lambda c, p: (c, 0, 0, 0)),
            pl.BlockSpec((EXPERTS, width), lambda c, p: (0, 0)),
            in_block, in_block, pl.BlockSpec((2, hidden, width), lambda c, p: (p, 0, 0)),
            pl.BlockSpec(hidden_share.shape, lambda c, p: (0, 0)), anywhere, anywhere,
        ],
        out_specs=(
            pl.BlockSpec((groups, blocks, rows, columns), lambda c, p: (c, 0, 0, 0)),
            pl.BlockSpec((groups, rows, width + 128), lambda c, p: (c, 0, 0)),
            anywhere, anywhere, anywhere, anywhere,
        ),
        scratch_shapes=[
            pltpu.VMEM((groups, EXPERTS, rows), F32),
            pltpu.VMEM((groups, EXPERTS, rows), F32),
            pltpu.VMEM((groups, batch * capacity, rows), BF),
            pltpu.VMEM((groups, batch * capacity, rows), BF),
            pltpu.VMEM((batch, groups, capacity, width), BF),
            pltpu.VMEM((batch, groups, capacity, width), BF),
            pltpu.VMEM((groups, batch * capacity, width), BF),
            pltpu.VMEM((groups, batch * capacity, width), BF),
            pltpu.VMEM((groups, 128, rows), F32),
            pltpu.VMEM((groups, rows, width), F32),
            pltpu.VMEM((groups, rows, width), F32),
            pltpu.SemaphoreType.DMA((copies,)),
            pltpu.SemaphoreType.DMA((copies,)),
            pltpu.SemaphoreType.DMA((4,)),
        ],
        compiler_params=params(
            60, dimension_semantics=("arbitrary", "arbitrary"),
            **(dict(collective_id=3, has_side_effects=True) if gathers else {}),
        ),
        cost_estimate=pl.CostEstimate(flops=MIB, bytes_accessed=MIB, transcendentals=0),
        name="experts_own",
    )(x, dy, table, router_t, wg, wu, wd, hidden_share, normed_share, far_dy)


def slots_kernel(
    sizes, masks, capacity, local, batch, reduces, x_hbm, dy_hbm, table_ref, router_ref, *rest,
):
    if reduces:
        (
            dense_in, heads_in, small_in, first_in, out_in, old_hbm, x_tok_hbm, stat_in, scale_ref, gain_ref,
            x_hbm, xs_ref, ys_ref, sums_ref, input_ref, block_ref, gain_out_ref,
            x_buf, y_buf, hits, gated, dense, heads, small, first, out, dense_land, heads_land, small_land, first_land, out_land,
            stat, stat_land, gains, gains_land, old, x_tok, load_sem, send_sem, recv_sem, local_sem,
        ) = rest
    else:
        xs_ref, ys_ref, x_buf, y_buf, hits, gated, load_sem = rest
    expert_count, tensor_count, dp_count = sizes
    unit = pl.program_id(0)
    units = pl.num_programs(0)
    rows, width = x_buf.shape[-2:]
    me_e, me_d = lax.axis_index("expert"), lax.axis_index("dp")
    per_mask = expert_count
    slot_id = sublanes((capacity, rows))

    def far_dp(m):
        value = me_d
        for bit in bits_of(dp_count):
            on = lax.rem(lax.div(m, bit), 2)
            value = value + on * (bit - 2 * bit * lax.rem(lax.div(me_d, bit), 2))
        return value

    def place(i):
        m = masks[0] + lax.div(i, per_mask)
        return m, lax.rem(i, per_mask), far_dp(m)

    def loads(i):
        m, group, d = place(i)
        slot = lax.rem(i, 2)
        y_source = dy_hbm.at[m - masks[0], group] if len(dy_hbm.shape) == 4 else dy_hbm.at[group]
        x_source = x_hbm.at[m - masks[0], group] if len(x_hbm.shape) == 4 else x_hbm.at[group]
        return (
            pltpu.make_async_copy(x_source, x_buf.at[slot], load_sem.at[slot, 0]),
            pltpu.make_async_copy(y_source, y_buf.at[slot], load_sem.at[slot, 1]),
        )

    if reduces:
        net = Net(send_sem, recv_sem)
        me_t = net.me["tensor"]
        ways = expert_count * dp_count
        expert_bits = [("expert", b) for b in bits_of(expert_count)]
        tensor_bits = [("tensor", b) for b in bits_of(tensor_count)]
        dp_bits = [("dp", b) for b in bits_of(dp_count)][::-1]
        chunks = [(e, d) for e in range(expert_count) for d in range(dp_count)]
        plane = [(e, t) for e in range(expert_count) for t in range(0, tensor_count, 2)]
        share = rows // tensor_count
        cores = [core_gather(net, x_hbm, share, plane, which) for which in range(dp_count - 1)]

        def chunk_of(ref):
            size = ref.shape[0] // ways

            def at(re, rd):
                index = flip(me_e, re) * dp_count + flip(me_d, rd)
                return ref.at[pl.ds(pl.multiple_of(index * size, size), size)]

            return at

        sums = [
            Reduce(net, chunk_of(dense), lambda i: dense_land.at[i], expert_bits + dp_bits, chunks),
            Reduce(net, chunk_of(heads), lambda i: heads_land.at[i], dp_bits + expert_bits, chunks),
            Reduce(net, chunk_of(small), lambda i: small_land.at[i], dp_bits + expert_bits, chunks),
            Reduce(
                net, lambda re, rt: out.at[flip(me_e, re), flip(me_t, rt)], lambda i: out_land.at[i],
                tensor_bits + expert_bits, [(e, t) for e in range(expert_count) for t in range(tensor_count)],
            ),
            Reduce(
                net, lambda re, rt: first.at[flip(me_t, rt)], lambda i: first_land.at[i], tensor_bits,
                [(0, t) for t in range(tensor_count)],
            ),
        ]
        chains = [
            AllReduce(net, stat, stat_land, tensor_bits),
            AllReduce(net, gains, gains_land, tensor_bits + expert_bits + dp_bits),
        ]
        columns = first.shape[2]
        begin = pl.multiple_of(me_t * columns, columns)

        count = len(masks) * expert_count
        times = [[0, 2, 4], [0, 2, 4], [0, 2, 4], [0, 2, 4], [0, 1]]

        def advance(k):
            for one, when in zip(sums, times):
                if k in when or k == count:
                    if one.flight:
                        one.finish()
                    if one.steps:
                        one.start()

        @pl.when(unit == 0)
        def _():
            pairs = (
                (dense_in, dense), (heads_in, heads), (small_in, small), (first_in, first), (out_in, out),
                (stat_in.at[:, 0:rows], stat.at[0]), (stat_in.at[:, rows:], gains.at[0]),
                (old_hbm.at[:, pl.ds(begin, columns)], old), (x_tok_hbm.at[:, pl.ds(begin, columns)], x_tok),
            )
            moves = [pltpu.make_async_copy(a, b, local_sem.at[i]) for i, (a, b) in enumerate(pairs)]
            for copy in moves:
                copy.start()
            net.barrier(expert_bits + tensor_bits + dp_bits)
            for one in cores:
                one.start()
            for copy in moves:
                copy.wait()
            advance(0)
            for chain in chains:
                chain.advance(0)

        for k in range(1, len(chains[1].steps)):

            @pl.when(unit == k)
            def _(k=k):
                advance(k)
                for chain in chains:
                    chain.advance(k)

        for m in range(dp_count - 1):

            @pl.when(unit == max(m * expert_count - 1, 0))
            def _(m=m):
                cores[m].finish()

    @pl.when(unit == 0)
    def _():
        for copy in loads(unit):
            copy.start()

    @pl.when(unit + 1 < units)
    def _():
        for copy in loads(unit + 1):
            copy.start()

    for copy in loads(unit):
        copy.wait()
    slot = lax.rem(unit, 2)
    _, group, d = place(unit)
    table = given_table(table_ref, group, d.astype(F32))
    gates = gate_rows(router_ref[...], x_buf[slot], table)
    router_rows = sublanes((EXPERTS, rows))

    def row_of(values):
        return lambda e: jnp.sum(jnp.where(router_rows == e, values, 0.0), axis=0, keepdims=True)

    for part in range(local // batch):
        fill_units(
            row_of(table), row_of(gates), slot_id, me_e * local + part * batch, batch, hits.at[part], gated.at[part]
        )
        cut = slice(part * batch, (part + 1) * batch)
        xs_ref[cut, 0] = dot(hits[part], x_buf[slot]).astype(BF).reshape(batch, capacity, width)
        ys_ref[cut, 0] = dot(gated[part], y_buf[slot]).astype(BF).reshape(batch, capacity, width)

    if reduces:

        @pl.when(unit == units - 1)
        def _():
            advance(count)
            chains[1].advance(len(chains[1].steps))
            here = me_e * dp_count + me_d
            d_rows, h_rows, s_rows = (ref.shape[0] // ways for ref in (dense, heads, small))
            half = heads.shape[1] // 2
            sums_ref[0:d_rows] = dense[pl.ds(pl.multiple_of(here * d_rows, d_rows), d_rows), :]
            mine = heads[pl.ds(pl.multiple_of(here * h_rows, h_rows), h_rows), :]
            sums_ref[d_rows : d_rows + h_rows] = mine[:, :half]
            sums_ref[d_rows + h_rows : d_rows + 2 * h_rows] = mine[:, half:]
            sums_ref[d_rows + 2 * h_rows :] = small[pl.ds(pl.multiple_of(here * s_rows, s_rows), s_rows), :]
            gain_out_ref[...] = gains[gains.shape[0] - 1]
            total = jnp.concatenate([stat[stat.shape[0] - 1], jnp.zeros((120, rows), F32)], axis=0)
            mean = jnp.transpose(total)[:, 0:1] / gain_ref.shape[0]
            scale = scale_ref[:, 0:1]
            input_ref[...] = (
                old[...].astype(F32) + scale * (
                    first[me_t].astype(F32) * gain_ref[pl.ds(begin, columns)].astype(F32)[None, :]
                    - x_tok[...].astype(F32) * scale * mean
                )
            ).astype(BF)
            block_ref[...] = out[me_e, me_t]
            net.close()


def slots_call(masks, x, dy, table, router_t, local, sums=None):
    sizes = tuple(lax.axis_size(axis) for axis in ("expert", "tensor", "dp"))
    expert_count, _, dp_count = sizes
    rows, width = x.shape[-2:]
    units = expert_count * len(masks)
    capacity = rows * TOP // EXPERTS
    batch = min(8, local)
    shape = jax.ShapeDtypeStruct
    anywhere = pl.BlockSpec(memory_space=pl.ANY)
    block = pl.BlockSpec((local, 1, capacity, width), lambda i: (0, i, 0, 0))
    whole = pl.BlockSpec(memory_space=pltpu.VMEM)
    out_shape = [shape((local, units, capacity, width), BF)] * 2
    out_specs = [block, block]
    aliases = {}
    operands = [x, dy, table, router_t]
    in_specs = [anywhere, anywhere, whole, whole]
    scratch = [
        pltpu.VMEM((2, rows, width), BF), pltpu.VMEM((2, rows, width), BF),
        pltpu.VMEM((local // batch, batch * capacity, rows), BF), pltpu.VMEM((local // batch, batch * capacity, rows), BF),
    ]
    tail = [pltpu.SemaphoreType.DMA((2, 2))]
    more = {}
    if sums is not None:
        dense, heads, small, first, out, old, tokens, stat, scale, gain = sums
        ways = expert_count * dp_count
        columns = first.shape[2]
        chunk = [values.shape[0] // ways for values in (dense, heads, small)]
        operands += [dense, heads, small, first, out, old, tokens, stat, scale, gain]
        in_specs += [anywhere] * 8 + [whole] * 2
        out_shape += [
            shape((chunk[0] + 2 * chunk[1] + chunk[2], dense.shape[1]), BF), shape((rows, columns), BF), shape((rows, columns), BF),
            shape((8, width), F32),
        ]
        out_specs += [whole] * 4
        out_shape = [shape(x.shape, BF)] + out_shape
        out_specs = [anywhere] + out_specs
        aliases = {0: 0}
        steps = len(bits_of(sizes[1]))
        rounds = steps + len(bits_of(ways))
        scratch += [pltpu.VMEM(values.shape, BF) for values in (dense, heads, small, first, out)]
        scratch += [
            pltpu.VMEM((ways - 1, chunk[0], dense.shape[1]), BF), pltpu.VMEM((ways - 1, chunk[1], heads.shape[1]), BF),
            pltpu.VMEM((ways - 1, chunk[2], small.shape[1]), BF), pltpu.VMEM((first.shape[0] - 1, rows, columns), BF),
            pltpu.VMEM((expert_count * sizes[1] - 1, rows, columns), BF),
            pltpu.VMEM((steps + 1, 8, rows), F32), pltpu.VMEM((steps, 8, rows), F32),
            pltpu.VMEM((rounds + 1, 8, width), F32), pltpu.VMEM((rounds, 8, width), F32),
            pltpu.VMEM((rows, columns), BF), pltpu.VMEM((rows, columns), BF),
        ]
        tail += [pltpu.SemaphoreType.DMA((64,)), pltpu.SemaphoreType.DMA((64,)), pltpu.SemaphoreType.DMA((9,))]
        more = dict(collective_id=4, has_side_effects=True)
    return pl.pallas_call(
        functools.partial(slots_kernel, sizes, masks, capacity, local, batch, sums is not None),
        out_shape=tuple(out_shape),
        grid=(units,),
        in_specs=in_specs,
        out_specs=tuple(out_specs),
        input_output_aliases=aliases,
        scratch_shapes=scratch + tail,
        compiler_params=params(60, dimension_semantics=("arbitrary",), **more),
        cost_estimate=pl.CostEstimate(flops=MIB, bytes_accessed=MIB, transcendentals=0),
        name="slots",
    )(*operands)


def weights_kernel(counts, chunks, capacity, has_partial, wg_ref, wu_ref, wd_ref, *rest):
    parts = len(counts)
    xs_refs, ys_refs, rest = rest[:parts], rest[parts : 2 * parts], rest[2 * parts :]
    if has_partial:
        in_g, in_u, in_d, gg_ref, gu_ref, gd_ref, x_buf, y_buf, sem = rest
    else:
        gg_ref, gu_ref, gd_ref, x_buf, y_buf, sem = rest
    expert, chunk = pl.program_id(0), pl.program_id(1)
    step = expert * chunks + chunk
    total = pl.num_programs(0) * chunks

    def loads(s):
        e, c, slot = lax.div(s, chunks), lax.rem(s, chunks), lax.rem(s, 2)
        copies, start = [], 0
        for index, count in enumerate(counts):
            take = count // chunks
            for which, (refs, buf) in enumerate(((xs_refs, x_buf), (ys_refs, y_buf))):
                copies.append(pltpu.make_async_copy(
                    refs[index].at[e, pl.ds(c * take, take)], buf.at[slot, pl.ds(start, take)], sem.at[slot, index, which]
                ))
            start += take
        return copies

    @pl.when(step == 0)
    def _():
        for copy in loads(step):
            copy.start()

    @pl.when(step + 1 < total)
    def _():
        for copy in loads(step + 1):
            copy.start()

    for copy in loads(step):
        copy.wait()
    slot = lax.rem(step, 2)
    width, hidden = wg_ref.shape[1:]
    x_here = x_buf[slot].reshape(-1, width)
    y_here = y_buf[slot].reshape(-1, width)
    both = dot(x_here, jnp.concatenate([wg_ref[0], wu_ref[0]], axis=1))
    grad_act = dot(y_here, wd_ref[0], 1, 1)
    act, grads = middle(both, grad_act, hidden)
    inner = dot(x_here, grads, 0, 0)
    down = dot(act.astype(BF), y_here, 0, 0)

    def put(ref, values, partial):
        if chunks == 1:
            ref[0] = values + partial[0] if has_partial else values
            return

        @pl.when(chunk == 0)
        def _():
            ref[0] = values + partial[0] if has_partial else values

        @pl.when(chunk != 0)
        def _():
            ref[0] += values

    put(gg_ref, inner[:, :hidden], in_g if has_partial else None)
    put(gu_ref, inner[:, hidden:], in_u if has_partial else None)
    put(gd_ref, down, in_d if has_partial else None)


def weights_call(slots, wg, wu, wd, partial=None):
    local, width, hidden = wg.shape
    capacity = slots[0][0].shape[2]
    counts = [xs.shape[1] for xs, _ in slots]
    chunks = max(1, sum(counts) // 8)
    assert len(counts) == 1 or chunks == 1
    shape = jax.ShapeDtypeStruct
    in_block = pl.BlockSpec((1, width, hidden), lambda e, c: (e, 0, 0))
    down_block = pl.BlockSpec((1, hidden, width), lambda e, c: (e, 0, 0))
    specs = (in_block, in_block, down_block)
    more = list(partial) if partial is not None else []
    buffer = pltpu.VMEM((2, sum(counts) // chunks, capacity, width), BF)
    return pl.pallas_call(
        functools.partial(weights_kernel, counts, chunks, capacity, partial is not None),
        out_shape=(shape(wg.shape, F32), shape(wu.shape, F32), shape(wd.shape, F32)),
        grid=(local, chunks),
        in_specs=list(specs) + [pl.BlockSpec(memory_space=pl.ANY)] * (2 * len(slots)) + (list(specs) if more else []),
        out_specs=specs,
        scratch_shapes=[buffer, buffer, pltpu.SemaphoreType.DMA((2, len(counts), 2))],
        compiler_params=params(60, dimension_semantics=("arbitrary", "arbitrary")),
        cost_estimate=pl.CostEstimate(flops=80 * 10**9, bytes_accessed=100 * MIB, transcendentals=0),
        name="weights",
    )(wg, wu, wd, *[xs for xs, _ in slots], *[ys for _, ys in slots], *more)


def unpack_kernel(sums_ref, q_ref, k_ref, v_ref, heads_ref, router_ref, gain_ref):
    ways = sums_ref.shape[0]
    d_rows, h_rows, s_rows = q_ref.shape[0] // ways, heads_ref.shape[0] // ways, SMALL_ROWS // ways
    q_width, k_width, half = q_ref.shape[1], k_ref.shape[1], heads_ref.shape[1] // 2
    small = []
    for i in range(ways):
        block = sums_ref[i].astype(F32)
        cut = slice(i * d_rows, (i + 1) * d_rows)
        q_ref[cut, :] = block[:d_rows, :q_width]
        k_ref[cut, :] = block[:d_rows, q_width : q_width + k_width]
        v_ref[cut, :] = block[:d_rows, q_width + k_width :]
        cut = slice(i * h_rows, (i + 1) * h_rows)
        heads_ref[cut, :half] = block[d_rows : d_rows + h_rows]
        heads_ref[cut, half:] = block[d_rows + h_rows : d_rows + 2 * h_rows]
        small.append(block[d_rows + 2 * h_rows :])
    small = jnp.concatenate(small, axis=0)
    router_ref[:, :half] = small[:EXPERTS]
    router_ref[:, half:] = small[EXPERTS : 2 * EXPERTS]
    gain_ref[...] = small[2 * EXPERTS : 2 * EXPERTS + 2]


def unpack_call(sums, q_width, k_width, heads_shape):
    ways = sums.shape[0]
    width = heads_shape[1]
    shape = jax.ShapeDtypeStruct
    return pl.pallas_call(
        unpack_kernel,
        out_shape=(
            shape((width, q_width), F32), shape((width, k_width), F32), shape((width, k_width), F32), shape(heads_shape, F32),
            shape((EXPERTS, width), F32), shape((2, width // 2), F32),
        ),
        in_specs=vmem(1),
        out_specs=tuple(vmem(6)),
        compiler_params=params(32),
        cost_estimate=pl.CostEstimate(flops=MIB, bytes_accessed=5 * MIB, transcendentals=0),
        name="unpack",
    )(sums)


def on_device(
    tokens, cotangent, seq_lengths, deal_order, routes, slot_order, first_gain, w_query, w_key, w_value, w_out,
    second_gain, w_router, w_gate, w_up, w_down,
):
    dp_count = lax.axis_size("dp")
    dp_index = lax.axis_index("dp")
    tensor_count = lax.axis_size("tensor")
    tensor_index = lax.axis_index("tensor")
    expert_count = lax.axis_size("expert")
    expert_index = lax.axis_index("expert")
    rows, width = tokens.shape
    share = rows // tensor_count
    everywhere = ("expert", "dp", "tensor")
    unit_shape = (expert_count, dp_count, rows, width)

    cosine, sine = (jnp.asarray(values) for values in rotary_tables(rows))
    gain1, gain2 = first_gain, second_gain
    router_t = w_router.T
    normed, q, k, v, heads, logsum, hidden, normed_share, tables, far_dy, x_own, dy_own = front(
        seq_lengths, deal_order, tokens, gain1, w_query, w_key, w_value, w_out, cosine, sine, gain2, routes.T, slot_order, cotangent
    )
    never = seq_lengths[0, 0] < 0
    rows_all = ("expert", "dp")

    def after(values, other):
        return jnp.where(never, other.astype(values.dtype), values)

    small_mesh = expert_count == 2
    out_c, out_g, xs_own, ys_own, x_other, dy_other = own_call(
        x_own, dy_own, tables, router_t, w_gate, w_up, w_down, hidden, normed_share, far_dy
    )
    group_count = expert_count
    if not small_mesh:
        out_c = lax.psum_scatter(out_c, "expert", scatter_dimension=0, tiled=True)
        out_g = lax.psum_scatter(out_g, "expert", scatter_dimension=0, tiled=True)
        x_own = lax.dynamic_slice_in_dim(x_own, expert_index, 1, 0)
        group_count = 1
    first, stat, hidden_grad, scale, dense, heads_grad, small, *x_passed = back_call(
        group_count, seq_lengths,
        (cotangent, tokens, gain1, gain2, router_t, hidden, tables, normed, q, k, v, heads, logsum,
         w_query, w_key, w_value, w_out, cosine, sine),
        out_g, x_own, x_other if small_mesh else None,
    )
    local = w_gate.shape[0]
    q_width, k_width = w_query.shape[1], w_key.shape[1]
    half, columns = width // 2, width // tensor_count
    if small_mesh:
        _, xs, ys, sums, input_grad, block_out, gain1_rows = slots_call(
            tuple(range(1, dp_count)), x_passed[0], dy_other, tables, router_t, local,
            (dense, heads_grad, small, first, out_c, hidden_grad, tokens, stat, scale, gain1),
        )
        gain1_sum = gain1_rows[0]
        ways = expert_count * dp_count
        sums = lax.all_gather(sums, rows_all, axis=0)
        gate_grad, up_grad, down_grad = weights_call([(xs_own, ys_own), (xs, ys)], w_gate, w_up, w_down)
        q_sum, k_sum, v_sum, out_sum, router_rows, gain2_rows = unpack_call(sums, q_width, k_width, w_out.shape)
        router_sum, gain2_sum = router_rows.T, gain2_rows.reshape(width)
    else:
        grads = weights_call([(xs_own, ys_own)], w_gate, w_up, w_down)
        for mask in range(1, dp_count):
            moved = (
                lax.all_gather(
                    after(values[mask - 1], grads[2][0, 0, 0]), ("expert", "tensor"), axis=0, tiled=True
                ).reshape(expert_count, rows, width)
                for values in (
                    [lax.ppermute(normed_share, "dp", [(i, i ^ m) for i in range(dp_count)]) for m in range(1, dp_count)],
                    far_dy,
                )
            )
            xs, ys = slots_call((mask,), *moved, tables, router_t, local)
            grads = weights_call([(xs, ys)], w_gate, w_up, w_down, grads)
        gate_grad, up_grad, down_grad = grads
        dense_sum, out_sum, small_sum = (
            values.astype(F32) for values in lax.psum((dense, heads_grad, small), rows_all)
        )
        gain1_sum = lax.psum(stat[0, rows:], everywhere)
        q_sum, k_sum, v_sum = jnp.split(dense_sum, [q_width, q_width + k_width], axis=1)
        router_sum = jnp.concatenate([small_sum[:EXPERTS], small_sum[EXPERTS : 2 * EXPERTS]], axis=1)
        gain2_sum = small_sum[2 * EXPERTS : 2 * EXPERTS + 2].reshape(width)
        router_sum = router_sum.T
        block_out = lax.psum_scatter(out_c[0], "tensor", scatter_dimension=0, tiled=True)[0]
        first_sum = lax.psum_scatter(first, "tensor", scatter_dimension=0, tiled=True)[0].astype(F32)
        mean = lax.psum(stat[0, :rows], "tensor")[:, None] / width

        def cols(values):
            return lax.dynamic_slice_in_dim(values, tensor_index * columns, columns, -1).astype(F32)

        input_grad = (
            cols(hidden_grad) + scale[:, :1] * (first_sum * cols(gain1) - cols(tokens) * scale[:, :1] * mean)
        ).astype(BF)
    return (
        block_out, input_grad, gain1_sum, q_sum, k_sum, v_sum, out_sum, gain2_sum, router_sum,
        gate_grad, up_grad, down_grad,
    )


def solution(mesh):
    rows2 = P(("expert", "dp"), None)
    placed = (
        rows2, rows2, P("expert", None), P("expert", None), rows2, rows2, P(),
        P(None, "tensor"), P(None, "tensor"), P(None, "tensor"), P("tensor", None), P(), P(),
        P("expert", None, "tensor"), P("expert", None, "tensor"), P("expert", "tensor", None),
    )
    return jax.shard_map(
        on_device,
        mesh=mesh,
        in_specs=placed,
        out_specs=(
            P(("expert", "dp"), "tensor"), P(("expert", "dp"), "tensor"), P(),
            P(None, "tensor"), P(None, "tensor"), P(None, "tensor"), P("tensor", None), P(), P(),
            P("expert", None, "tensor"), P("expert", None, "tensor"), P("expert", "tensor", None),
        ),
        check_vma=False,
    )
```

```python
import functools

import jax
import jax.numpy as jnp
import numpy as np
from jax import lax
from jax.experimental import pallas as pl
from jax.experimental.pallas import tpu as pltpu
from jax.sharding import PartitionSpec as P

HEADS = 16
KV_HEADS = 8
HEAD_DIM = 64
EXPERTS = 32
TOP = 8
SLOT = 512

EPS = 1e-06
THETA = 10000.0
NEG = -1e30
BF = jnp.bfloat16
F32 = jnp.float32
MIB = 1 << 20


def dot(a, b, ca=1, cb=0):
    return lax.dot_general(a, b, (((ca,), (cb,)), ((), ())), preferred_element_type=F32)


def vmem(count=1):
    return [pl.BlockSpec(memory_space=pltpu.VMEM)] * count


def params(mib, **more):
    return pltpu.CompilerParams(vmem_limit_bytes=mib * MIB, **more)


def rotary_tables(rows):
    places = np.arange(rows, dtype=np.float32)[:, None]
    halfway = HEAD_DIM // 2
    spread = np.float32(THETA) ** (-2.0 * np.arange(halfway, dtype=np.float32) / HEAD_DIM)
    angles = (places * spread.astype(np.float32)[None, :]).astype(np.float32)
    copies = 128 // halfway
    return (
        np.tile(np.cos(angles), (1, copies)).astype(np.float32),
        np.tile(np.sin(angles), (1, copies)).astype(np.float32),
    )


def rotate128(values, cosine, sine, low_half):
    half = HEAD_DIM // 2
    up = pltpu.roll(values, 128 - half, 1)
    down = pltpu.roll(values, half, 1)
    return values * cosine + jnp.where(low_half, -up, down) * sine


def lanes(shape):
    return lax.broadcasted_iota(jnp.int32, shape, len(shape) - 1)


def sublanes(shape):
    return lax.broadcasted_iota(jnp.int32, shape, len(shape) - 2)


def bits_of(count):
    return [1 << i for i in range(count.bit_length() - 1)]


def flip(value, mask):
    for bit in bits_of(1 << 16):
        if mask & bit:
            value = value + bit - 2 * bit * lax.rem(lax.div(value, bit), 2)
    return value


class Net:
    def __init__(self, send_sem, recv_sem):
        self.send_sem, self.recv_sem, self.used, self.copies = send_sem, recv_sem, 0, []
        self.me = {axis: lax.axis_index(axis) for axis in ("expert", "tensor", "dp")}

    def barrier(self, partners):
        sem = pltpu.get_barrier_semaphore()
        for partner in partners:
            pl.semaphore_signal(sem, inc=1, device_id=self.device(partner), device_id_type=pl.DeviceIdType.MESH)
        pl.semaphore_wait(sem, len(partners))

    def device(self, partner):
        pairs = [partner] if isinstance(partner[0], str) else partner
        return {axis: flip(self.me[axis], mask) for axis, mask in pairs}

    def send(self, source, target, *partner):
        k = self.used
        self.used += 1
        copy = Copy(self, k, source, target, partner)
        copy.build().start()
        self.copies.append(copy)
        return copy

    def close(self):
        for copy in self.copies:
            copy.build().wait_send()


class Copy:
    def __init__(self, net, index, source, target, partner):
        self.net, self.index, self.source, self.target, self.partner = net, index, source, target, partner

    def build(self):
        source = self.source() if callable(self.source) else self.source
        target = self.target() if callable(self.target) else self.target
        return pltpu.make_async_remote_copy(
            src_ref=source, dst_ref=target,
            send_sem=self.net.send_sem.at[self.index], recv_sem=self.net.recv_sem.at[self.index],
            device_id=self.net.device(self.partner), device_id_type=pl.DeviceIdType.MESH,
        )

    def wait_recv(self):
        self.build().wait_recv()


class Gather:
    def __init__(self, net, at, steps, known=((0, 0),), first=None):
        self.net, self.at, self.steps, self.known, self.first, self.flight = net, at, list(steps), list(known), first, []

    def start(self):
        axis, mask = self.steps.pop(0)
        fresh = []
        for re, rt in self.known:
            place = functools.partial(self.at, re, rt)
            source = self.first if self.first is not None and (re, rt) == (0, 0) else place
            self.flight.append(self.net.send(source, place, axis, mask))
            fresh.append((re ^ mask, rt) if axis == "expert" else (re, rt ^ mask))
        self.known += fresh

    def finish(self):
        for copy in self.flight:
            copy.wait_recv()
        self.flight = []


class Reduce:
    def __init__(self, net, at, landing, steps, chunks):
        self.net, self.at, self.landing, self.steps, self.live = net, at, landing, list(steps), list(chunks)
        self.used, self.flight = 0, []

    def start(self):
        axis, mask = self.steps.pop(0)
        side = 0 if axis == "expert" else 1
        going = [r for r in self.live if (r[side] & mask if mask else r[side])]
        self.live = [r for r in self.live if r not in going]
        for r in going:
            toward = mask or r[side]
            kept = (r[0] ^ toward, r[1]) if side == 0 else (r[0], r[1] ^ toward)
            copy = self.net.send(functools.partial(self.at, *r), functools.partial(self.landing, self.used), axis, toward)
            self.flight.append((kept, copy, self.used))
            self.used += 1

    def finish(self):
        for place in sorted({kept for kept, _, _ in self.flight}):
            total = self.at(*place)[...].astype(F32)
            for kept, copy, slot in self.flight:
                if kept == place:
                    copy.wait_recv()
                    total = total + self.landing(slot)[...].astype(F32)
            self.at(*place)[...] = total.astype(BF)
        self.flight = []


class Exchange:
    def __init__(self, net, stages, k, landing, partners):
        self.net, self.stages, self.k, self.landing, self.partners, self.flight = net, stages, k, landing, partners, []

    def start(self):
        for index, partner in enumerate(self.partners):
            self.flight.append(self.net.send(
                lambda: self.stages.at[self.k], lambda index=index: self.landing.at[index], *partner
            ))

    def finish(self):
        total = self.stages[self.k]
        for index, copy in enumerate(self.flight):
            copy.wait_recv()
            total = total + self.landing[index]
        self.stages[self.k + 1] = total


TABLE_ROWS = 48
SMALL_ROWS = 128


def table_of(length, routes_ref, order_ref):
    rows = routes_ref.shape[1]
    capacity = rows * TOP // EXPERTS
    entries = rows * TOP
    chunk = 512
    routes_t = routes_ref[...].astype(F32).astype(BF)
    upper = (sublanes((chunk, chunk)) < lanes((chunk, chunk))).astype(F32).astype(BF)
    expert_row = sublanes((EXPERTS, chunk))

    def body(step, carried):
        counts, table = carried
        entry = order_ref[:, pl.ds(pl.multiple_of(step * chunk, chunk), chunk)]
        row, choice = entry // TOP, entry % TOP
        onehot_row = (sublanes((rows, chunk)) == row).astype(F32).astype(BF)
        picked = dot(routes_t, onehot_row)
        expert = jnp.sum(jnp.where(sublanes((TOP, chunk)) == choice, picked, 0.0), axis=0, keepdims=True)
        member = (expert_row.astype(F32) == expert) & (row < length)
        member_f = member.astype(F32)
        before = dot(member_f.astype(BF), upper) + counts
        value = jnp.where(member, jnp.minimum(before, float(capacity)) + 1.0, 0.0)
        table = table + dot(value.astype(BF), onehot_row, 1, 1)
        return counts + jnp.sum(member_f, axis=1, keepdims=True), table

    _, table = lax.fori_loop(
        0, entries // chunk, body, (jnp.zeros((EXPERTS, 1), F32), jnp.zeros((EXPERTS, rows), F32))
    )
    return table


def given_table(tables, index, dp_here):
    total = 0.0
    for j in range(tables.shape[1]):
        source = tables[index, j, EXPERTS : EXPERTS + 16, :].astype(F32)[0:1]
        total = total + jnp.where(source == dp_here, tables[index, j, 0:EXPERTS, :].astype(F32), 0.0)
    return total


def head_parts(q, k_a, k_b, index, low_lane):
    block = q[:, (index // 2) * 128 : (index // 2) * 128 + 128]
    mine = low_lane if index % 2 == 0 else jnp.logical_not(low_lane)
    return jnp.where(mine, block, jnp.zeros((), block.dtype)), (k_a if index % 2 == (index // 2) % 2 else k_b)


def swap(block):
    return pltpu.roll(block.astype(F32), HEAD_DIM, 1).astype(BF)


def front_kernel(
    sizes,
    lengths_ref, order_of_ref, x_ref, gain_ref, wq_ref, wk_ref, wv_ref, wo_ref, cos_ref, sin_ref, gain2_ref, routes_ref, order_ref, dy_ref,
    normed_ref, q_ref, k_ref, v_ref, heads_ref, logsum_ref, hidden_ref, share_ref, tables_ref, far_dy_ref, xown_ref, dyown_ref,
    part, landing, send_sem, recv_sem, local_sem,
):
    expert_count, tensor_count, dp_count = sizes
    rows, width = x_ref.shape
    share = rows // tensor_count
    half = rows // 2
    net = Net(send_sem, recv_sem)
    me_e, me_t, me_d = net.me["expert"], net.me["tensor"], net.me["dp"]
    expert_bits = [("expert", b) for b in bits_of(expert_count)]
    tensor_bits = [("tensor", b) for b in bits_of(tensor_count)]
    net.barrier(expert_bits + tensor_bits + [("dp", m) for m in range(1, dp_count)])

    keep_dy = pltpu.make_async_copy(dy_ref, dyown_ref.at[me_e], local_sem.at[0])
    keep_dy.start()
    half_start = pl.multiple_of(lax.rem(me_t, 2) * half, half)
    dy_half = Gather(
        net, lambda re, rt: dyown_ref.at[flip(me_e, re), pl.ds(half_start, half)], expert_bits,
        first=dy_ref.at[pl.ds(half_start, half)],
    )
    dy_half.start()
    length, source, dealt_length = lengths_ref[0, me_d], order_of_ref[0, me_d], 0
    for i in range(dp_count):
        dealt_length = jnp.where(source == i, lengths_ref[0, i], dealt_length)
    x = x_ref[...].astype(F32)
    scale = lax.rsqrt(jnp.mean(x * x, axis=-1, keepdims=True) + EPS)
    normed = (x * scale * gain_ref[...].astype(F32)[None, :]).astype(BF)
    normed_ref[...] = normed
    cosine, sine = cos_ref[...], sin_ref[...]
    lane = lanes((rows, 128))
    low_half = lane % HEAD_DIM < HEAD_DIM // 2
    low_lane = lane < HEAD_DIM
    q_pre = dot(normed, wq_ref[...])
    for block in range(q_pre.shape[1] // 128):
        cut = slice(block * 128, block * 128 + 128)
        q_ref[:, cut] = rotate128(q_pre[:, cut], cosine, sine, low_half).astype(BF)
    k = rotate128(dot(normed, wk_ref[...]), cosine, sine, low_half).astype(BF)
    v = dot(normed, wv_ref[...]).astype(BF)
    k_ref[...] = k
    v_ref[...] = v
    q = q_ref[...]
    k_b, v_b = swap(k), swap(v)
    row, col = sublanes((rows, rows)), lanes((rows, rows))
    allowed = (col <= row) & (col < length)
    logsum = jnp.zeros((rows, 128), F32)
    pair = None
    for index in range(q.shape[1] // HEAD_DIM):
        q_one, k_one = head_parts(q, k, k_b, index, low_lane)
        v_one = v if index % 2 == (index // 2) % 2 else v_b
        scores = jnp.where(allowed, dot(q_one, k_one, 1, 1) * (HEAD_DIM**-0.5), NEG)
        highest = jnp.max(scores, axis=-1, keepdims=True)
        weights = jnp.exp(scores - highest)
        total = jnp.sum(weights, axis=-1, keepdims=True)
        mixed = dot((weights / total).astype(BF), v_one)
        logsum = jnp.where(lane == index, highest + jnp.log(total), logsum)
        if index % 2 == 0:
            pair = mixed
        else:
            cut = slice((index // 2) * 128, (index // 2) * 128 + 128)
            heads_ref[:, cut] = jnp.where(low_lane, pair, mixed).astype(BF)
    logsum_ref[...] = logsum
    live = (sublanes((rows, 1)) < length).astype(F32)
    part[...] = (dot(heads_ref[...], wo_ref[...]) * live).astype(BF).reshape(part.shape)

    attn = Reduce(
        net, lambda re, rt: part.at[flip(me_t, rt)], lambda i: landing.at[i], tensor_bits,
        [(0, r) for r in range(tensor_count)],
    )
    attn.start()
    table = table_of(dealt_length, routes_ref, order_ref)
    source = jnp.broadcast_to(source.astype(F32), (TABLE_ROWS - EXPERTS, rows))
    tables_ref[me_e, me_d] = jnp.concatenate([table, source], axis=0).astype(BF)
    mine = tables_ref.at[me_e, me_d]
    table_copies = [net.send(mine, mine, "dp", m) for m in range(1, dp_count)]
    mine_rows = pl.multiple_of(me_t * share, share)
    far_copies = [
        net.send(dy_ref.at[pl.ds(mine_rows, share)], far_dy_ref.at[m - 1], "dp", m) for m in range(1, dp_count)
    ]
    attn.finish()
    while attn.steps:
        attn.start()
        if not attn.steps:
            dy_half.finish()
            while dy_half.steps:
                dy_half.start()
                dy_half.finish()
            for re, _ in dy_half.known[1:]:
                place = dy_half.at(re, 0)
                dy_half.flight.append(net.send(place, place, "tensor", 1))
        attn.finish()

    start = pl.multiple_of(me_t * share, share)
    hidden = x_ref[pl.ds(start, share), :].astype(F32) + part[me_t].astype(F32)
    hidden_ref[...] = hidden
    scale2 = lax.rsqrt(jnp.mean(hidden * hidden, axis=-1, keepdims=True) + EPS)
    share_ref[...] = (hidden * scale2 * gain2_ref[...].astype(F32)[None, :]).astype(BF)
    keep_x = pltpu.make_async_copy(share_ref, xown_ref.at[me_e, pl.ds(start, share)], local_sem.at[1])
    keep_x.start()
    high_bits = tensor_bits[1:][::-1]
    gathers = []
    for part_index, steps in enumerate((high_bits + expert_bits, expert_bits + high_bits)):
        size = share // 2

        def at(re, rt, offset=part_index * size):
            begin = pl.multiple_of(flip(me_t, rt) * share + offset, size)
            return xown_ref.at[flip(me_e, re), pl.ds(begin, size)]

        gathers.append(
            Gather(net, at, steps + tensor_bits[:1], first=share_ref.at[pl.ds(part_index * size, size)])
        )
    table_all = Gather(net, lambda re, rt: tables_ref.at[flip(me_e, re)], expert_bits)
    first_step = True
    while gathers[0].steps:
        for gather in gathers:
            gather.start()
        if first_step:
            for copy in table_copies:
                copy.wait_recv()
            first_step = False
        else:
            table_all.finish()
        if table_all.steps:
            table_all.start()
        for gather in gathers:
            gather.finish()
    table_all.finish()
    dy_half.finish()
    for copy in far_copies:
        copy.wait_recv()
    net.close()
    keep_dy.wait()
    keep_x.wait()


def front(lengths, order_of, x, gain, wq, wk, wv, wo, cosine, sine, gain2, routes, order, dy):
    rows, width = x.shape
    sizes = tuple(lax.axis_size(axis) for axis in ("expert", "tensor", "dp"))
    expert_count, tensor_count, dp_count = sizes
    share = rows // tensor_count
    shape = jax.ShapeDtypeStruct
    copies = 96
    return pl.pallas_call(
        functools.partial(front_kernel, sizes),
        out_shape=(
            shape((rows, width), BF), shape((rows, wq.shape[1]), BF), shape((rows, wk.shape[1]), BF),
            shape((rows, wv.shape[1]), BF), shape((rows, wq.shape[1]), BF), shape((rows, 128), F32),
            shape((share, width), F32), shape((share, width), BF), shape((expert_count, dp_count, TABLE_ROWS, rows), BF),
            shape((dp_count - 1, share, width), BF), shape((expert_count, rows, width), BF), shape((expert_count, rows, width), BF),
        ),
        in_specs=[pl.BlockSpec(memory_space=pltpu.SMEM)] * 2 + vmem(11) + [pl.BlockSpec(memory_space=pl.ANY)],
        out_specs=tuple(vmem(10)) + (pl.BlockSpec(memory_space=pl.ANY),) * 2,
        scratch_shapes=[
            pltpu.VMEM((tensor_count, share, width), BF),
            pltpu.VMEM((tensor_count - 1, share, width), BF),
            pltpu.SemaphoreType.DMA((copies,)),
            pltpu.SemaphoreType.DMA((copies,)),
            pltpu.SemaphoreType.DMA((2,)),
        ],
        compiler_params=params(56, collective_id=1, has_side_effects=True),
        cost_estimate=pl.CostEstimate(flops=MIB, bytes_accessed=MIB, transcendentals=0),
        name="front",
    )(lengths, order_of, x, gain, wq, wk, wv, wo, cosine, sine, gain2, routes, order, dy)


def back_kernel(
    sizes, passes,
    lengths_ref, dy_ref, x_ref, gain_ref, gain2_ref, router_ref, hidden_ref, tables_ref,
    normed_ref, q_ref, k_ref, v_ref, heads_ref, logsum_ref, wq_ref, wk_ref, wv_ref, wo_ref, cos_ref, sin_ref,
    grad_in_ref, xown_ref, *rest,
):
    if passes:
        out_in_ref, rest = rest[0], rest[1:]
        out_pass_ref, rest = rest[7], rest[:7] + rest[8:]
        (out, out_landing), rest = rest[-2:], rest[:-2]
    (
        first_ref, tiny_ref, hidden_grad_ref, scale_ref, dense_ref, out_grad_ref, small_ref,
        grad, grad_landing, normed2, spread, back_ref, picked, send_sem, recv_sem, local_sem,
    ) = rest
    group_count, tensor_count, dp_count = sizes
    rows, width = x_ref.shape
    share = rows // tensor_count
    net = Net(send_sem, recv_sem)
    me_e, me_t, me_d = net.me["expert"], net.me["tensor"], net.me["dp"]
    here = me_e if group_count > 1 else 0
    expert_bits = [("expert", b) for b in bits_of(group_count)]
    tensor_bits = [("tensor", b) for b in bits_of(tensor_count)]
    load_grad = pltpu.make_async_copy(grad_in_ref, grad, local_sem.at[0])
    load_x = pltpu.make_async_copy(xown_ref.at[here], normed2, local_sem.at[1])
    load_grad.start()
    load_x.start()
    if passes:
        load_out = pltpu.make_async_copy(out_in_ref, out, local_sem.at[2])
        load_out.start()
    net.barrier(expert_bits + tensor_bits)
    load_grad.wait()
    high_bits = tensor_bits[1:]
    chunks = [(e, t) for e in range(group_count) for t in range(tensor_count)]
    sums = []
    size = share // 2
    for part_index, steps in enumerate((high_bits + expert_bits, expert_bits + high_bits)):

        def at(re, rt, offset=part_index * size):
            begin = pl.multiple_of(flip(me_t, rt) * share + offset, size)
            return grad.at[flip(here, re) if re else here, pl.ds(begin, size)]

        sums.append(Reduce(
            net, at, lambda i, p=part_index: grad_landing.at[p, i], tensor_bits[:1] + steps, chunks
        ))
    if passes:
        out_sum = Reduce(
            net, lambda re, rt: out.at[flip(me_e, re), flip(me_t, rt)], lambda i: out_landing.at[i],
            tensor_bits[:1] + expert_bits, chunks,
        )
    while sums[0].steps:
        for one in sums:
            one.start()
        if passes and not out_sum.used:
            load_out.wait()
            out_sum.start()
        for one in sums:
            one.finish()
    if passes:
        out_sum.finish()
        out_sum.start()

    start = pl.multiple_of(me_t * share, share)
    gain2 = gain2_ref[...].astype(F32)[None, :]
    hidden = hidden_ref[...]
    scale2 = lax.rsqrt(jnp.mean(hidden * hidden, axis=-1, keepdims=True) + EPS)
    hat2 = hidden * scale2
    second_normed = (hat2 * gain2).astype(BF)
    picked[...] = given_table(tables_ref, me_e, me_d.astype(F32))
    table = picked[:, pl.ds(start, share)]
    table = jnp.concatenate([table, jnp.zeros((128 - EXPERTS, share), F32)], axis=0)
    table = jnp.transpose(table)[:, :EXPERTS]
    logits = dot(second_normed, router_ref[...], 1, 1)
    chosen = table > 0.5
    masked = jnp.where(chosen, logits, NEG)
    weights = jnp.where(chosen, jnp.exp(masked - jnp.max(masked, axis=-1, keepdims=True)), 0.0)
    total = jnp.sum(weights, axis=-1, keepdims=True)
    gates = weights / jnp.where(total > 0.0, total, 1.0)
    gate_in = grad[here, pl.ds(start, share), width:].astype(F32)[:, :EXPERTS]
    logit_grad = (gate_in - gates * jnp.sum(gate_in, axis=-1, keepdims=True)).astype(BF)
    normed_grad = grad[here, pl.ds(start, share), :width].astype(F32) + dot(logit_grad, router_ref[...])
    along2 = normed_grad * hat2
    gain2_part = jnp.sum(along2, axis=0, keepdims=True)
    scaled = normed_grad * gain2
    hidden_grad = dy_ref[pl.ds(start, share), :].astype(F32) + scale2 * (
        scaled - hat2 * jnp.mean(scaled * hat2, axis=-1, keepdims=True)
    )
    spread[me_t, 0:share, :width] = hidden_grad.astype(BF)
    spread[me_t, 0:share, width:] = jnp.concatenate(
        [logit_grad.astype(F32), jnp.zeros((share, 128 - EXPERTS), F32)], axis=1
    ).astype(BF)
    high = gain2_part.astype(BF).astype(F32)
    spread[me_t, share : share + 16, :width] = jnp.concatenate(
        [high, gain2_part - high, jnp.zeros((14, width), F32)], axis=0
    ).astype(BF)
    spread[me_t, share : share + 16, width:] = jnp.zeros((16, 128), BF)
    gather = Gather(net, lambda re, rt: spread.at[flip(me_t, rt)], high_bits[::-1] + tensor_bits[:1])
    while gather.steps:
        gather.start()
        gather.finish()

    length = lengths_ref[0, me_d]
    inv = HEAD_DIM**-0.5
    live = (sublanes((rows, 1)) < length).astype(F32)
    hidden_grad_all = spread[:, 0:share, :width].reshape(rows, width)
    hidden_grad_ref[...] = hidden_grad_all
    branch = (hidden_grad_all.astype(F32) * live).astype(BF)
    out_grad_ref[...] = dot(heads_ref[...], branch, 0, 0).astype(BF)
    heads_grad = dot(branch, wo_ref[...], 1, 1).astype(BF)
    cosine, sine = cos_ref[...], -sin_ref[...]
    lane = lanes((rows, 128))
    low_half = lane % HEAD_DIM < HEAD_DIM // 2
    low_lane = lane < HEAD_DIM
    q, k, v = q_ref[...], k_ref[...], v_ref[...]
    k_b, v_b = swap(k), swap(v)
    key, query = sublanes((rows, rows)), lanes((rows, rows))
    allowed = (key <= query) & (key < length)
    logsum_rows = jnp.transpose(logsum_ref[...])
    dk = [jnp.zeros((rows, 128), F32), jnp.zeros((rows, 128), F32)]
    dv = [jnp.zeros((rows, 128), F32), jnp.zeros((rows, 128), F32)]
    q_width = q.shape[1]
    pair = None
    for index in range(q_width // HEAD_DIM):
        same = index % 2 == (index // 2) % 2
        q_one, k_one = head_parts(q, k, k_b, index, low_lane)
        g_one, v_one = head_parts(heads_grad, v, v_b, index, low_lane)
        scores = jnp.where(allowed, dot(k_one, q_one, 1, 1) * inv, NEG)
        prob = jnp.exp(scores - logsum_rows[index : index + 1, :])
        grad_prob = dot(v_one, g_one, 1, 1)
        center = jnp.sum(prob * grad_prob, axis=0, keepdims=True)
        score_grad = (prob * (grad_prob - center)).astype(BF)
        dq = dot(score_grad, k_one, 0, 0) * inv
        place = 0 if same else 1
        dk[place] = dk[place] + dot(score_grad, q_one) * inv
        dv[place] = dv[place] + dot(prob.astype(BF), g_one)
        if index % 2 == 0:
            pair = dq
        else:
            cut = slice((index // 2) * 128, (index // 2) * 128 + 128)
            both = jnp.where(low_lane, pair, dq)
            back_ref[:, cut] = rotate128(both, cosine, sine, low_half).astype(BF)
    k_width = k.shape[1]
    k_total = dk[0] + pltpu.roll(dk[1], HEAD_DIM, 1)
    v_total = dv[0] + pltpu.roll(dv[1], HEAD_DIM, 1)
    back_ref[:, q_width : q_width + k_width] = rotate128(k_total, cosine, sine, low_half).astype(BF)
    back_ref[:, q_width + k_width :] = v_total.astype(BF)
    back = back_ref[...]
    first = (
        dot(back[:, :q_width], wq_ref[...], 1, 1)
        + dot(back[:, q_width : q_width + k_width], wk_ref[...], 1, 1)
        + dot(back[:, q_width + k_width :], wv_ref[...], 1, 1)
    )
    columns = width // tensor_count
    for t in range(tensor_count):
        first_ref[t] = first[:, t * columns : (t + 1) * columns].astype(BF)
    x = x_ref[...].astype(F32)
    scale = lax.rsqrt(jnp.mean(x * x, axis=-1, keepdims=True) + EPS)
    scale_ref[...] = jnp.broadcast_to(scale, (rows, 128))
    along = first * (x * scale)
    stat = jnp.sum(along * gain_ref[...].astype(F32)[None, :], axis=-1, keepdims=True)
    tiny_ref[:, 0:rows] = jnp.transpose(jnp.broadcast_to(stat, (rows, 128)))[0:8, :]
    tiny_ref[:, rows:] = jnp.broadcast_to(jnp.sum(along, axis=0, keepdims=True), (8, width))
    dense_ref[...] = dot(normed_ref[...], back, 0, 0).astype(BF)
    load_x.wait()
    router_rows = dot(spread[:, 0:share, width:].reshape(rows, 128), normed2[...], 0, 0)[0:EXPERTS]
    gain2_sum = jnp.zeros((1, width), F32)
    for t in range(tensor_count):
        block = spread[t, share : share + 16, :width].astype(F32)
        gain2_sum = gain2_sum + block[0:1] + block[1:2]
    half = width // 2
    pieces = [router_rows[:, :half], router_rows[:, half:], gain2_sum[:, :half], gain2_sum[:, half:]]
    if passes:
        out_sum.finish()
        out_pass_ref[...] = out[me_e]
    filled = sum(piece.shape[0] for piece in pieces)
    small_ref[...] = jnp.concatenate(pieces + [jnp.zeros((SMALL_ROWS - filled, half), F32)], axis=0).astype(BF)
    net.close()


def back_call(group_count, lengths, vmem_operands, grad, xown, out=None):
    dy, x = vmem_operands[0], vmem_operands[1]
    rows, width = x.shape
    wq, wk, wv, wo = vmem_operands[13:17]
    tensor_count, dp_count = lax.axis_size("tensor"), lax.axis_size("dp")
    share, columns = rows // tensor_count, width // tensor_count
    chunks = group_count * tensor_count
    inner = wq.shape[1] + wk.shape[1] + wv.shape[1]
    shape = jax.ShapeDtypeStruct
    copies = 64
    passed = [] if out is None else [out]
    return pl.pallas_call(
        functools.partial(back_kernel, (group_count, tensor_count, dp_count), out is not None),
        out_shape=(
            shape((tensor_count, rows, columns), BF), shape((8, rows + width), F32), shape((rows, width), BF),
            shape((rows, 128), F32), shape((width, inner), BF), shape(wo.shape, BF), shape((SMALL_ROWS, width // 2), BF),
            *[shape(one.shape[1:], BF) for one in passed],
        ),
        in_specs=[pl.BlockSpec(memory_space=pltpu.SMEM)] + vmem(len(vmem_operands)) + [pl.BlockSpec(memory_space=pl.ANY)] * (2 + len(passed)),
        out_specs=tuple(vmem(7)) + tuple(vmem(len(passed))),
        scratch_shapes=[
            pltpu.VMEM(grad.shape, BF),
            pltpu.VMEM((2, chunks - 1, share // 2, width + 128), BF),
            pltpu.VMEM((rows, width), BF),
            pltpu.VMEM((tensor_count, share + 16, width + 128), BF),
            pltpu.VMEM((rows, inner), BF),
            pltpu.VMEM((EXPERTS, rows), F32),
            pltpu.SemaphoreType.DMA((copies,)),
            pltpu.SemaphoreType.DMA((copies,)),
            pltpu.SemaphoreType.DMA((3,)),
        ] + ([
            pltpu.VMEM(out.shape, BF),
            pltpu.VMEM((chunks, rows, columns), BF),
        ] if passed else []),
        compiler_params=params(60, collective_id=2, has_side_effects=True),
        cost_estimate=pl.CostEstimate(flops=MIB, bytes_accessed=MIB, transcendentals=0),
        name="back",
    )(lengths, *vmem_operands, grad, xown, *passed)


def gate_rows(router_t, rows, table):
    logits = dot(router_t, rows, 1, 1)
    chosen = table > 0.5
    masked = jnp.where(chosen, logits, NEG)
    weights = jnp.where(chosen, jnp.exp(masked - jnp.max(masked, axis=0, keepdims=True)), 0.0)
    total = jnp.sum(weights, axis=0, keepdims=True)
    return weights / jnp.where(total > 0.0, total, 1.0)


def bit_steps(expert_count, tensor_count):
    expert_bits = [("expert", b) for b in bits_of(expert_count)]
    tensor_bits = [("tensor", b) for b in bits_of(tensor_count)]
    return expert_bits, tensor_bits, tensor_bits[1:][::-1]


def plane_gathers(net, target, share, first=None, done=False, last=None, which=slice(None)):
    counts = lax.axis_size("expert"), lax.axis_size("tensor")
    expert_bits, _, high_bits = bit_steps(*counts)
    size = share // 2
    parts = []
    for index, steps in enumerate((high_bits + expert_bits, expert_bits + high_bits)):

        def at(re, rt, offset=index * size):
            begin = pl.multiple_of(flip(net.me["tensor"], rt) * share + offset, size)
            return target.at[which, flip(net.me["expert"], re), pl.ds(begin, size)]

        source = None if first is None else first.at[:, pl.ds(index * size, size)]
        known = [(0, 0)]
        if done:
            axis, mask = steps.pop(0)
            known.append((mask, 0) if axis == "expert" else (0, mask))
        parts.append(Gather(net, at, steps[:last], known=known, first=source))
    return parts


def core_gather(net, target, share, known, which=slice(None)):
    def whole(re, rt):
        begin = pl.multiple_of(flip(net.me["tensor"], rt) * share, share)
        return target.at[which, flip(net.me["expert"], re), pl.ds(begin, share)]

    return Gather(net, whole, [("tensor", 1)], known=known)


def slot_numbers(capacity, rows):
    return sublanes((capacity, rows)).astype(F32).astype(BF)


def placed(slot_id, table_row, weight):
    return jnp.where(slot_id == (table_row - 1.0).astype(BF), weight, jnp.zeros((), BF))


def fill_units(table, gate, slot_id, first_expert, count, hits_ref, gated_ref):
    capacity = slot_id.shape[0]
    for j in range(count):
        row = table(first_expert + j)
        cut = slice(j * capacity, (j + 1) * capacity)
        hits_ref[cut, :] = placed(slot_id, row, jnp.ones((), BF))
        gated_ref[cut, :] = placed(slot_id, row, gate(first_expert + j).astype(BF))


def middle(both, grad_act, hidden):
    g_here, u_here = both[:, :hidden], both[:, hidden:]
    sig = 1.0 / (1.0 + jnp.exp(-g_here))
    silu = g_here * sig
    act = silu * u_here
    grad_gate = (grad_act * u_here * sig * (1.0 + g_here * (1.0 - sig))).astype(BF)
    grad_up = (grad_act * silu).astype(BF)
    return act, jnp.concatenate([grad_gate, grad_up], axis=1)


def own_kernel(
    sizes, groups, capacity, local, batch, gathers,
    x_ref, dy_ref, table_ref, router_ref, wg_ref, wu_ref, wd_ref, hidden_ref, share_ref, far_dy_ref,
    out_c_ref, out_g_ref, xs_out, ys_out, oth_ref, othy_ref, gates_out,
    gates, gates_b, ranks, hits, gated, xs, ys, made, back, gi_rows, acc_c, acc_g, send_sem, recv_sem, local_sem,
):
    chunk, pair = pl.program_id(0), pl.program_id(1)
    pairs = local // 2
    per_batch = batch // 2
    expert_count, tensor_count, dp_count = sizes
    net = Net(send_sem, recv_sem)
    dp_here, me_t, me_e = net.me["dp"], net.me["tensor"], net.me["expert"]
    rows, width = x_ref.shape[-2:]
    units = groups
    hidden = wg_ref.shape[2]
    slot_id = slot_numbers(capacity, rows)
    share = rows // tensor_count

    if gathers:
        expert_bits, tensor_bits, high_bits = bit_steps(expert_count, tensor_count)
        cotangent_parts = plane_gathers(net, othy_ref, share, first=far_dy_ref)
        row_parts = plane_gathers(net, oth_ref, share, last=1)
        mine = pl.ds(pl.multiple_of(me_t * share, share), share)
        keep = pltpu.make_async_copy(far_dy_ref, othy_ref.at[:, me_e, mine], local_sem.at[2])
        flight = []

        def first_steps():
            net.barrier(expert_bits + tensor_bits + [("dp", m) for m in range(1, dp_count)])
            keep.start()
            for one in cotangent_parts:
                one.start()
            for m in range(1, dp_count):
                flight.append(net.send(share_ref, lambda m=m: oth_ref.at[m - 1, me_e, mine], "dp", m))

        def second_steps():
            for one in cotangent_parts:
                one.finish()
            for one in cotangent_parts:
                one.start()

        def third_steps():
            for one in cotangent_parts:
                one.finish()
            keep.wait()
            cotangent_parts.append(core_gather(net, othy_ref, share, cotangent_parts[0].known))
            cotangent_parts[-1].start()
            for copy in flight:
                copy.wait_recv()
            flight.clear()
            for one in row_parts:
                one.start()

        def last_steps():
            cotangent_parts[-1].finish()
            for one in row_parts:
                one.finish()
            for copy in flight:
                copy.wait_recv()
            net.close()

        for time, steps in ((0, first_steps), (pairs * 2 // 8, second_steps), (pairs * 6 // 8, third_steps)):

            @pl.when(pair == time)
            def _(steps=steps):
                steps()

    @pl.when(pair == 0)
    def _():
        gi_rows[...] = jnp.zeros_like(gi_rows)

        @pl.loop(0, units)
        def _(i):
            table = given_table(table_ref, i, dp_here.astype(F32))
            ranks[i] = table
            gates[i] = gate_rows(router_ref[...], x_ref[i], table)
            gates_b[i] = gates[i].astype(BF)

    @pl.when(pair == 0)
    def _():
        if not gathers:
            gates_out[...] = gates_b[...]
            return
        for m in range(1, dp_count):
            flight.append(net.send(gates_b, lambda m=m: gates_out.at[m - 1], "dp", m))

    place = lax.rem(pair, per_batch)
    half = lax.div(pair, per_batch)
    group_start = pl.multiple_of(chunk * groups, groups)
    outs = []
    for index, (source, target) in enumerate(((xs, xs_out), (ys, ys_out))):
        outs.append(pltpu.make_async_copy(
            source, target.at[pl.ds(half * batch, batch), pl.ds(group_start, groups)], local_sem.at[index]
        ))

    @pl.when(place == 0)
    def _():
        @pl.loop(0, units)
        def _(i):
            fill_units(
                lambda e: ranks[i, pl.ds(e, 1), :], lambda e: gates[i, pl.ds(e, 1), :], slot_id,
                me_e * local + half * batch, batch, hits.at[i], gated.at[i],
            )
            xs[:, i] = dot(hits[i], x_ref[i]).astype(BF).reshape(batch, capacity, width)
            ys[:, i] = dot(gated[i], dy_ref[i]).astype(BF).reshape(batch, capacity, width)

        for copy in outs:
            copy.start()

    spots = [place * 2 + j for j in range(2)]
    inner_w = [jnp.concatenate([wg_ref[j], wu_ref[j]], axis=1) for j in range(2)]
    both = [dot(xs[spots[j]].reshape(units * capacity, width), inner_w[j]) for j in range(2)]
    grad_act = [dot(ys[spots[j]].reshape(units * capacity, width), wd_ref[j], 1, 1) for j in range(2)]
    mids = [middle(both[j], grad_act[j], hidden) for j in range(2)]
    for j in range(2):
        act, grads = mids[j]
        result = dot(act.astype(BF), wd_ref[j]).astype(BF)
        moved = dot(grads, inner_w[j], 1, 1).astype(BF)
        inner = jnp.sum(act * grad_act[j], axis=-1, keepdims=True)
        at_slot = pl.ds(pl.multiple_of(spots[j] * capacity, capacity), capacity)
        for i in range(units):
            cut = slice(i * capacity, (i + 1) * capacity)
            made[i, at_slot, :] = result[cut]
            back[i, at_slot, :] = moved[cut]
            gi_rows[i, pl.ds(me_e * local + pair * 2 + j, 1), :] = jnp.sum(
                hits[i, at_slot, :].astype(F32) * inner[cut], axis=0, keepdims=True
            )

    @pl.when(place == per_batch - 1)
    def _():
        for copy in outs:
            copy.wait()

        @pl.loop(0, units)
        def _(i):
            add_c = dot(gated[i], made[i], 0, 0)
            add_g = dot(hits[i], back[i], 0, 0)

            @pl.when(half == 0)
            def _():
                acc_c[i] = add_c
                acc_g[i] = add_g

            @pl.when(half != 0)
            def _():
                acc_c[i] += add_c
                acc_g[i] += add_g

    @pl.when(pair == pairs - 1)
    def _():
        blocks, columns = out_c_ref.shape[1], out_c_ref.shape[3]
        for i in range(units):

            @pl.when(chunk * groups + i == me_e)
            def _():
                cut = pl.ds(pl.multiple_of(me_t * share, share), share)
                acc_c[i, cut, :] += hidden_ref[...]

            for t in range(blocks):
                out_c_ref[i, t] = acc_c[i, :, t * columns : (t + 1) * columns].astype(BF)
            out_g_ref[i, :, :width] = acc_g[i].astype(BF)
            out_g_ref[i, :, width:] = jnp.transpose(gi_rows[i]).astype(BF)
        if gathers:
            last_steps()


def own_call(x, dy, table, router_t, wg, wu, wd, hidden_share, normed_share, far_dy):
    sizes = tuple(lax.axis_size(axis) for axis in ("expert", "tensor", "dp"))
    groups_all, dp_count = table.shape[:2]
    rows, width = x.shape[-2:]
    groups = 2
    chunks = groups_all // groups
    local, _, hidden = wg.shape
    pairs = local // 2
    assert chunks == 1 or pairs == 1
    batch = min(8, local)
    gathers = chunks == 1
    capacity = rows * TOP // EXPERTS
    shape = jax.ShapeDtypeStruct
    row_block = pl.BlockSpec((groups, rows, width), lambda c, p: (c, 0, 0), pipeline_mode=pl.Buffered(1))
    in_block = pl.BlockSpec((2, width, hidden), lambda c, p: (p, 0, 0))
    blocks = sizes[1]
    columns = width // blocks
    copies = 64
    slots = shape((local, groups_all, capacity, width), BF)
    anywhere = pl.BlockSpec(memory_space=pl.ANY)
    return pl.pallas_call(
        functools.partial(own_kernel, sizes, groups, capacity, local, batch, gathers),
        out_shape=(
            shape((groups_all, blocks, rows, columns), BF), shape((groups_all, rows, width + 128), BF), slots, slots,
            *[shape((dp_count - 1, groups_all, rows, width) if gathers else (16, 128), BF)] * 2,
            shape((dp_count - 1, groups_all, EXPERTS, rows) if gathers else (groups_all, EXPERTS, rows), BF),
        ),
        grid=(chunks, pairs),
        in_specs=[
            row_block, row_block,
            pl.BlockSpec((groups, dp_count, TABLE_ROWS, rows), lambda c, p: (c, 0, 0, 0)),
            pl.BlockSpec((EXPERTS, width), lambda c, p: (0, 0)),
            in_block, in_block, pl.BlockSpec((2, hidden, width), lambda c, p: (p, 0, 0)),
            pl.BlockSpec(hidden_share.shape, lambda c, p: (0, 0)), anywhere, anywhere,
        ],
        out_specs=(
            pl.BlockSpec((groups, blocks, rows, columns), lambda c, p: (c, 0, 0, 0)),
            pl.BlockSpec((groups, rows, width + 128), lambda c, p: (c, 0, 0)),
            anywhere, anywhere, anywhere, anywhere,
            anywhere if gathers else pl.BlockSpec((groups, EXPERTS, rows), lambda c, p: (c, 0, 0)),
        ),
        scratch_shapes=[
            pltpu.VMEM((groups, EXPERTS, rows), F32),
            pltpu.VMEM((groups, EXPERTS, rows), BF),
            pltpu.VMEM((groups, EXPERTS, rows), F32),
            pltpu.VMEM((groups, batch * capacity, rows), BF),
            pltpu.VMEM((groups, batch * capacity, rows), BF),
            pltpu.VMEM((batch, groups, capacity, width), BF),
            pltpu.VMEM((batch, groups, capacity, width), BF),
            pltpu.VMEM((groups, batch * capacity, width), BF),
            pltpu.VMEM((groups, batch * capacity, width), BF),
            pltpu.VMEM((groups, 128, rows), F32),
            pltpu.VMEM((groups, rows, width), F32),
            pltpu.VMEM((groups, rows, width), F32),
            pltpu.SemaphoreType.DMA((copies,)),
            pltpu.SemaphoreType.DMA((copies,)),
            pltpu.SemaphoreType.DMA((4,)),
        ],
        compiler_params=params(
            60, dimension_semantics=("arbitrary", "arbitrary"),
            **(dict(collective_id=3, has_side_effects=True) if gathers else {}),
        ),
        cost_estimate=pl.CostEstimate(flops=MIB, bytes_accessed=MIB, transcendentals=0),
        name="experts_own",
    )(x, dy, table, router_t, wg, wu, wd, hidden_share, normed_share, far_dy)


def slots_kernel(sizes, masks, capacity, local, batch, reduces, x_hbm, dy_hbm, table_ref, gates_ref, *rest):
    if reduces:
        (
            dense_in, heads_in, small_in, first_in, out_in, old_hbm, x_tok_hbm, stat_in, scale_ref, gain_ref,
            x_hbm, xs_ref, ys_ref, sums_ref, input_ref, block_ref, gain_out_ref,
            buf, onehot, ranks, weights, dense, heads, small, first, out, dense_land, heads_land, small_land, first_land, out_land,
            stat, stat_land, gains, gains_land, gains_far_land, old, x_tok, load_sem, send_sem, recv_sem, local_sem,
        ) = rest
    else:
        xs_ref, ys_ref, buf, onehot, ranks, weights, load_sem = rest
    expert_count, tensor_count, dp_count = sizes
    step = pl.program_id(0)
    units = expert_count * len(masks)
    rows, width = buf.shape[-2:]
    me_e, me_d = lax.axis_index("expert"), lax.axis_index("dp")
    slot_id = slot_numbers(capacity, rows)

    def far_dp(m):
        value = me_d
        for bit in bits_of(dp_count):
            on = lax.rem(lax.div(m, bit), 2)
            value = value + on * (bit - 2 * bit * lax.rem(lax.div(me_d, bit), 2))
        return value

    def place(i):
        m = masks[0] + lax.div(i, expert_count)
        return m, lax.rem(i, expert_count), far_dp(m)

    def load(source, i, slot):
        m, group, _ = place(i)
        return pltpu.make_async_copy(source.at[m - masks[0], group], buf.at[slot], load_sem.at[slot])

    def start_load(s):
        @pl.when(s < units)
        def _():
            load(dy_hbm, s, lax.rem(s, 2)).start()

        @pl.when(s >= units)
        def _():
            load(x_hbm, s - units, lax.rem(s, 2)).start()

    if reduces:
        net = Net(send_sem, recv_sem)
        me_t = net.me["tensor"]
        ways = expert_count * dp_count
        expert_bits, tensor_bits, high_bits = bit_steps(expert_count, tensor_count)
        dp_bits = [("dp", b) for b in bits_of(dp_count)][::-1]
        chunks = [(e, d) for e in range(expert_count) for d in range(dp_count)]
        plane = [(e, t) for e in range(expert_count) for t in range(0, tensor_count, 2)]
        share = rows // tensor_count
        planes = [plane_gathers(net, x_hbm, share, done=True, which=m) for m in range(dp_count - 1)]
        cores = [core_gather(net, x_hbm, share, plane, which) for which in range(dp_count - 1)]

        def chunk_of(ref):
            size = ref.shape[0] // ways

            def at(re, rd):
                index = flip(me_e, re) * dp_count + flip(me_d, rd)
                return ref.at[pl.ds(pl.multiple_of(index * size, size), size)]

            return at

        def column_of(ref):
            return lambda re, rt: ref.at[flip(me_t, rt)]

        dense_sum = Reduce(net, chunk_of(dense), lambda i: dense_land.at[i], [("dp", 0)] + expert_bits, chunks)
        small_sum = Reduce(net, chunk_of(small), lambda i: small_land.at[i], [("dp", 0)] + expert_bits, chunks)
        heads_sum = Reduce(net, chunk_of(heads), lambda i: heads_land.at[i], expert_bits + [("dp", 0)], chunks)
        out_sum = Reduce(net, column_of(out), lambda i: out_land.at[i], high_bits, [(0, t) for t in range(0, tensor_count, 2)])
        first_sum = Reduce(net, column_of(first), lambda i: first_land.at[i], tensor_bits, [(0, t) for t in range(tensor_count)])
        last = 2 * units
        plan = [
            (dense_sum, [0, units + 2]), (small_sum, [0, units + 2]),
            (heads_sum, [2, units + 2]), (first_sum, [0, units - 1]), (out_sum, [units - 1]),
        ]
        near = [("tensor", m) for m in range(1, tensor_count)]
        far = [(("expert", e), ("dp", d)) for e, d in chunks if e or d]
        stat_sum = Exchange(net, stat, 0, stat_land, near)
        gains_near = Exchange(net, gains, 0, gains_land, near)
        gains_far = Exchange(net, gains, 1, gains_far_land, far)
        columns = first.shape[2]
        begin = pl.multiple_of(me_t * columns, columns)

        def advance(k):
            for one, when in plan:
                if k in when or k == last:
                    if one.flight:
                        one.finish()
                    if one.steps:
                        one.start()

        def moves():
            pairs = (
                (stat_in.at[:, 0:rows], stat.at[0]), (stat_in.at[:, rows:], gains.at[0]),
                (dense_in, dense), (small_in, small), (first_in, first),
                (heads_in, heads), (out_in, out),
                (old_hbm.at[:, pl.ds(begin, columns)], old), (x_tok_hbm.at[:, pl.ds(begin, columns)], x_tok),
            )
            return [pltpu.make_async_copy(a, b, local_sem.at[i]) for i, (a, b) in enumerate(pairs)]

        @pl.when(step == 0)
        def _():
            for copy in moves():
                copy.start()
            net.barrier(near + far)
            for copy in moves()[:2]:
                copy.wait()
            stat_sum.start()
            gains_near.start()
            for parts in planes:
                for one in parts:
                    one.start()
            for copy in moves()[2:5]:
                copy.wait()
            advance(0)

        for k in range(1, last):
            at_plane = [m for m in range(dp_count - 1) if k == max(units - 4 + m * expert_count, 1)]
            at_core = [m for m in range(dp_count - 1) if k == units - 1 + m * expert_count]
            if not (k <= 2 or at_plane or at_core or any(k in when for _, when in plan)):
                continue

            @pl.when(step == k)
            def _(k=k, at_plane=at_plane, at_core=at_core):
                if k == 1:
                    for copy in moves()[5:]:
                        copy.wait()
                for m in at_plane:
                    for one in planes[m]:
                        one.finish()
                    cores[m].start()
                advance(k)
                if k == 2:
                    stat_sum.finish()
                    gains_near.finish()
                    gains_far.start()
                for m in at_core:
                    cores[m].finish()

    @pl.when(step == 0)
    def _():
        start_load(step)

    @pl.when(step + 1 < 2 * units)
    def _():
        start_load(step + 1)

    slot = lax.rem(step, 2)

    def spread(unit, source, target_ref, gated):
        m, group, d = place(unit)
        ranks[...] = given_table(table_ref, group, d.astype(F32))
        if gated:
            weights[...] = gates_ref[m - masks[0], group].astype(F32)
        for part in range(local // batch):
            for j in range(batch):
                e = me_e * local + part * batch + j
                weight = weights[pl.ds(e, 1), :].astype(BF) if gated else jnp.ones((), BF)
                onehot[part, j * capacity : (j + 1) * capacity, :] = placed(slot_id, ranks[pl.ds(e, 1), :], weight)
        load(source, unit, slot).wait()
        for part in range(local // batch):
            moved = dot(onehot[part], buf[slot]).astype(BF)
            target_ref[part * batch : (part + 1) * batch, 0] = moved.reshape(batch, capacity, width)

    @pl.when(step < units)
    def _():
        spread(step, dy_hbm, ys_ref, True)

    @pl.when(step >= units)
    def _():
        spread(step - units, x_hbm, xs_ref, False)

    if reduces:

        @pl.when(step == last - 1)
        def _():
            for one, _ in plan:
                while one.flight or one.steps:
                    if one.flight:
                        one.finish()
                    if one.steps:
                        one.start()
            gains_far.finish()
            here = me_e * dp_count + me_d
            d_rows, h_rows, s_rows = (ref.shape[0] // ways for ref in (dense, heads, small))
            half = heads.shape[1] // 2
            sums_ref[0:d_rows] = dense[pl.ds(pl.multiple_of(here * d_rows, d_rows), d_rows), :]
            mine = heads[pl.ds(pl.multiple_of(here * h_rows, h_rows), h_rows), :]
            sums_ref[d_rows : d_rows + h_rows] = mine[:, :half]
            sums_ref[d_rows + h_rows : d_rows + 2 * h_rows] = mine[:, half:]
            sums_ref[d_rows + 2 * h_rows :] = small[pl.ds(pl.multiple_of(here * s_rows, s_rows), s_rows), :]
            gain_out_ref[...] = gains[gains.shape[0] - 1]
            total = jnp.concatenate([stat[stat.shape[0] - 1], jnp.zeros((120, rows), F32)], axis=0)
            mean = jnp.transpose(total)[:, 0:1] / gain_ref.shape[0]
            scale = scale_ref[:, 0:1]
            input_ref[...] = (
                old[...].astype(F32) + scale * (
                    first[me_t].astype(F32) * gain_ref[pl.ds(begin, columns)].astype(F32)[None, :]
                    - x_tok[...].astype(F32) * scale * mean
                )
            ).astype(BF)
            block_ref[...] = out[me_t]
            net.close()


def slots_call(masks, x, dy, table, gates, local, sums=None):
    sizes = tuple(lax.axis_size(axis) for axis in ("expert", "tensor", "dp"))
    expert_count, _, dp_count = sizes
    rows, width = x.shape[-2:]
    units = expert_count * len(masks)
    capacity = rows * TOP // EXPERTS
    batch = min(8, local)
    shape = jax.ShapeDtypeStruct
    anywhere = pl.BlockSpec(memory_space=pl.ANY)
    y_block = pl.BlockSpec((local, 1, capacity, width), lambda i: (0, jnp.minimum(i, units - 1), 0, 0))
    x_block = pl.BlockSpec((local, 1, capacity, width), lambda i: (0, jnp.maximum(i - units, 0), 0, 0))
    whole = pl.BlockSpec(memory_space=pltpu.VMEM)
    out_shape = [shape((local, units, capacity, width), BF)] * 2
    out_specs = [x_block, y_block]
    aliases = {}
    operands = [x, dy, table, gates]
    in_specs = [anywhere, anywhere, whole, whole]
    scratch = [
        pltpu.VMEM((2, rows, width), BF), pltpu.VMEM((local // batch, batch * capacity, rows), BF),
        pltpu.VMEM((EXPERTS, rows), F32), pltpu.VMEM((EXPERTS, rows), F32),
    ]
    tail = [pltpu.SemaphoreType.DMA((2,))]
    more = {}
    if sums is not None:
        dense, heads, small, first, out, old, tokens, stat, scale, gain = sums
        ways = expert_count * dp_count
        columns = first.shape[2]
        chunk = [values.shape[0] // ways for values in (dense, heads, small)]
        operands += [dense, heads, small, first, out, old, tokens, stat, scale, gain]
        in_specs += [anywhere] * 8 + [whole] * 2
        out_shape += [
            shape((chunk[0] + 2 * chunk[1] + chunk[2], dense.shape[1]), BF), shape((rows, columns), BF), shape((rows, columns), BF),
            shape((8, width), F32),
        ]
        out_specs += [whole] * 4
        out_shape = [shape(x.shape, BF)] + out_shape
        out_specs = [anywhere] + out_specs
        aliases = {0: 0}
        scratch += [pltpu.VMEM(values.shape, BF) for values in (dense, heads, small, first, out)]
        scratch += [
            pltpu.VMEM((ways - 1, chunk[0], dense.shape[1]), BF), pltpu.VMEM((ways - 1, chunk[1], heads.shape[1]), BF),
            pltpu.VMEM((ways - 1, chunk[2], small.shape[1]), BF), pltpu.VMEM((first.shape[0] - 1, rows, columns), BF),
            pltpu.VMEM((max(sizes[1] // 2 - 1, 1), rows, columns), BF),
            pltpu.VMEM((2, 8, rows), F32), pltpu.VMEM((sizes[1] - 1, 8, rows), F32),
            pltpu.VMEM((3, 8, width), F32), pltpu.VMEM((sizes[1] - 1, 8, width), F32), pltpu.VMEM((ways - 1, 8, width), F32),
            pltpu.VMEM((rows, columns), BF), pltpu.VMEM((rows, columns), BF),
        ]
        tail += [pltpu.SemaphoreType.DMA((96,)), pltpu.SemaphoreType.DMA((96,)), pltpu.SemaphoreType.DMA((9,))]
        more = dict(collective_id=4, has_side_effects=True)
    return pl.pallas_call(
        functools.partial(slots_kernel, sizes, masks, capacity, local, batch, sums is not None),
        out_shape=tuple(out_shape),
        grid=(2 * units,),
        in_specs=in_specs,
        out_specs=tuple(out_specs),
        input_output_aliases=aliases,
        scratch_shapes=scratch + tail,
        compiler_params=params(60, dimension_semantics=("arbitrary",), **more),
        cost_estimate=pl.CostEstimate(flops=MIB, bytes_accessed=MIB, transcendentals=0),
        name="slots",
    )(*operands)


def weights_kernel(counts, chunks, capacity, has_partial, wg_ref, wu_ref, wd_ref, *rest):
    parts = len(counts)
    xs_refs, ys_refs, rest = rest[:parts], rest[parts : 2 * parts], rest[2 * parts :]
    if has_partial:
        in_g, in_u, in_d, gg_ref, gu_ref, gd_ref, x_buf, y_buf, sem = rest
    else:
        gg_ref, gu_ref, gd_ref, x_buf, y_buf, sem = rest
    expert, chunk = pl.program_id(0), pl.program_id(1)
    step = expert * chunks + chunk
    total = pl.num_programs(0) * chunks

    def loads(s):
        e, c, slot = lax.div(s, chunks), lax.rem(s, chunks), lax.rem(s, 2)
        copies, start = [], 0
        for index, count in enumerate(counts):
            take = count // chunks
            for which, (refs, buf) in enumerate(((xs_refs, x_buf), (ys_refs, y_buf))):
                copies.append(pltpu.make_async_copy(
                    refs[index].at[pl.ds(2 * e, 2), pl.ds(c * take, take)], buf.at[slot, :, pl.ds(start, take)],
                    sem.at[slot, index, which],
                ))
            start += take
        return copies

    @pl.when(step == 0)
    def _():
        for copy in loads(step):
            copy.start()

    @pl.when(step + 1 < total)
    def _():
        for copy in loads(step + 1):
            copy.start()

    for copy in loads(step):
        copy.wait()
    slot = lax.rem(step, 2)
    width, hidden = wg_ref.shape[1:]
    x_here = [x_buf[slot, j].reshape(-1, width) for j in range(2)]
    y_here = [y_buf[slot, j].reshape(-1, width) for j in range(2)]
    both = [dot(x_here[j], jnp.concatenate([wg_ref[j], wu_ref[j]], axis=1)) for j in range(2)]
    grad_act = [dot(y_here[j], wd_ref[j], 1, 1) for j in range(2)]
    mids = [middle(both[j], grad_act[j], hidden) for j in range(2)]

    def put(j, ref, values, partial):
        if chunks == 1:
            ref[j] = values + partial[j] if has_partial else values
            return

        @pl.when(chunk == 0)
        def _():
            ref[j] = values + partial[j] if has_partial else values

        @pl.when(chunk != 0)
        def _():
            ref[j] += values

    for j in range(2):
        act, grads = mids[j]
        inner = dot(x_here[j], grads, 0, 0)
        put(j, gg_ref, inner[:, :hidden], in_g if has_partial else None)
        put(j, gu_ref, inner[:, hidden:], in_u if has_partial else None)
        put(j, gd_ref, dot(act.astype(BF), y_here[j], 0, 0), in_d if has_partial else None)


def weights_call(slots, wg, wu, wd, partial=None):
    local, width, hidden = wg.shape
    capacity = slots[0][0].shape[2]
    counts = [xs.shape[1] for xs, _ in slots]
    chunks = max(1, sum(counts) // 8)
    assert len(counts) == 1 or chunks == 1
    shape = jax.ShapeDtypeStruct
    in_block = pl.BlockSpec((2, width, hidden), lambda e, c: (e, 0, 0))
    down_block = pl.BlockSpec((2, hidden, width), lambda e, c: (e, 0, 0))
    specs = (in_block, in_block, down_block)
    more = list(partial) if partial is not None else []
    buffer = pltpu.VMEM((2, 2, sum(counts) // chunks, capacity, width), BF)
    return pl.pallas_call(
        functools.partial(weights_kernel, counts, chunks, capacity, partial is not None),
        out_shape=(shape(wg.shape, F32), shape(wu.shape, F32), shape(wd.shape, F32)),
        grid=(local // 2, chunks),
        in_specs=list(specs) + [pl.BlockSpec(memory_space=pl.ANY)] * (2 * len(slots)) + (list(specs) if more else []),
        out_specs=specs,
        scratch_shapes=[buffer, buffer, pltpu.SemaphoreType.DMA((2, len(counts), 2))],
        compiler_params=params(60, dimension_semantics=("arbitrary", "arbitrary")),
        cost_estimate=pl.CostEstimate(flops=80 * 10**9, bytes_accessed=100 * MIB, transcendentals=0),
        name="weights",
    )(wg, wu, wd, *[xs for xs, _ in slots], *[ys for _, ys in slots], *more)


def unpack_kernel(sums_ref, q_ref, k_ref, v_ref, heads_ref, router_ref, gain_ref):
    ways = sums_ref.shape[0]
    d_rows, h_rows, s_rows = q_ref.shape[0] // ways, heads_ref.shape[0] // ways, SMALL_ROWS // ways
    q_width, k_width, half = q_ref.shape[1], k_ref.shape[1], heads_ref.shape[1] // 2
    small = []
    for i in range(ways):
        block = sums_ref[i].astype(F32)
        cut = slice(i * d_rows, (i + 1) * d_rows)
        q_ref[cut, :] = block[:d_rows, :q_width]
        k_ref[cut, :] = block[:d_rows, q_width : q_width + k_width]
        v_ref[cut, :] = block[:d_rows, q_width + k_width :]
        cut = slice(i * h_rows, (i + 1) * h_rows)
        heads_ref[cut, :half] = block[d_rows : d_rows + h_rows]
        heads_ref[cut, half:] = block[d_rows + h_rows : d_rows + 2 * h_rows]
        small.append(block[d_rows + 2 * h_rows :])
    small = jnp.concatenate(small, axis=0)
    router_ref[:, :half] = small[:EXPERTS]
    router_ref[:, half:] = small[EXPERTS : 2 * EXPERTS]
    gain_ref[...] = small[2 * EXPERTS : 2 * EXPERTS + 2]


def unpack_call(sums, q_width, k_width, heads_shape):
    ways = sums.shape[0]
    width = heads_shape[1]
    shape = jax.ShapeDtypeStruct
    return pl.pallas_call(
        unpack_kernel,
        out_shape=(
            shape((width, q_width), F32), shape((width, k_width), F32), shape((width, k_width), F32), shape(heads_shape, F32),
            shape((EXPERTS, width), F32), shape((2, width // 2), F32),
        ),
        in_specs=vmem(1),
        out_specs=tuple(vmem(6)),
        compiler_params=params(32),
        cost_estimate=pl.CostEstimate(flops=MIB, bytes_accessed=5 * MIB, transcendentals=0),
        name="unpack",
    )(sums)


def on_device(
    tokens, cotangent, seq_lengths, deal_order, routes, slot_order, first_gain, w_query, w_key, w_value, w_out,
    second_gain, w_router, w_gate, w_up, w_down,
):
    dp_count = lax.axis_size("dp")
    dp_index = lax.axis_index("dp")
    tensor_count = lax.axis_size("tensor")
    tensor_index = lax.axis_index("tensor")
    expert_count = lax.axis_size("expert")
    expert_index = lax.axis_index("expert")
    rows, width = tokens.shape
    share = rows // tensor_count
    everywhere = ("expert", "dp", "tensor")
    unit_shape = (expert_count, dp_count, rows, width)

    cosine, sine = (jnp.asarray(values) for values in rotary_tables(rows))
    gain1, gain2 = first_gain, second_gain
    router_t = w_router.T
    normed, q, k, v, heads, logsum, hidden, normed_share, tables, far_dy, x_own, dy_own = front(
        seq_lengths, deal_order, tokens, gain1, w_query, w_key, w_value, w_out, cosine, sine, gain2, routes.T, slot_order, cotangent
    )
    never = seq_lengths[0, 0] < 0
    rows_all = ("expert", "dp")

    def after(values, other):
        return jnp.where(never, other.astype(values.dtype), values)

    small_mesh = expert_count == 2
    out_c, out_g, xs_own, ys_own, x_other, dy_other, gates = own_call(
        x_own, dy_own, tables, router_t, w_gate, w_up, w_down, hidden, normed_share, far_dy
    )
    group_count = expert_count
    if not small_mesh:
        out_c = lax.psum_scatter(out_c, "expert", scatter_dimension=0, tiled=True)
        out_g = lax.psum_scatter(out_g, "expert", scatter_dimension=0, tiled=True)
        x_own = lax.dynamic_slice_in_dim(x_own, expert_index, 1, 0)
        group_count = 1
    first, stat, hidden_grad, scale, dense, heads_grad, small, *out_passed = back_call(
        group_count, seq_lengths,
        (cotangent, tokens, gain1, gain2, router_t, hidden, tables, normed, q, k, v, heads, logsum,
         w_query, w_key, w_value, w_out, cosine, sine),
        out_g, x_own, *((out_c,) if small_mesh else ()),
    )
    local = w_gate.shape[0]
    q_width, k_width = w_query.shape[1], w_key.shape[1]
    half, columns = width // 2, width // tensor_count
    if small_mesh:
        _, xs, ys, sums, input_grad, block_out, gain1_rows = slots_call(
            tuple(range(1, dp_count)), x_other, dy_other, tables, gates, local,
            (dense, heads_grad, small, first, out_passed[0], hidden_grad, tokens, stat, scale, gain1),
        )
        gain1_sum = gain1_rows[0]
        ways = expert_count * dp_count
        sums = lax.all_gather(sums, rows_all, axis=0)
        gate_grad, up_grad, down_grad = weights_call([(xs_own, ys_own), (xs, ys)], w_gate, w_up, w_down)
        q_sum, k_sum, v_sum, out_sum, router_rows, gain2_rows = unpack_call(sums, q_width, k_width, w_out.shape)
        router_sum, gain2_sum = router_rows.T, gain2_rows.reshape(width)
    else:
        grads = weights_call([(xs_own, ys_own)], w_gate, w_up, w_down)
        for mask in range(1, dp_count):
            moved = (
                lax.all_gather(
                    after(values[mask - 1], grads[2][0, 0, 0]), ("expert", "tensor"), axis=0, tiled=True
                ).reshape(1, expert_count, rows, width)
                for values in (
                    [lax.ppermute(normed_share, "dp", [(i, i ^ m) for i in range(dp_count)]) for m in range(1, dp_count)],
                    far_dy,
                )
            )
            far_gates = lax.ppermute(gates, "dp", [(i, i ^ mask) for i in range(dp_count)])[None]
            xs, ys = slots_call((mask,), *moved, tables, far_gates, local)
            grads = weights_call([(xs, ys)], w_gate, w_up, w_down, grads)
        gate_grad, up_grad, down_grad = grads
        dense_sum, out_sum, small_sum = (
            values.astype(F32) for values in lax.psum((dense, heads_grad, small), rows_all)
        )
        gain1_sum = lax.psum(stat[0, rows:], everywhere)
        q_sum, k_sum, v_sum = jnp.split(dense_sum, [q_width, q_width + k_width], axis=1)
        router_sum = jnp.concatenate([small_sum[:EXPERTS], small_sum[EXPERTS : 2 * EXPERTS]], axis=1)
        gain2_sum = small_sum[2 * EXPERTS : 2 * EXPERTS + 2].reshape(width)
        router_sum = router_sum.T
        block_out = lax.psum_scatter(out_c[0], "tensor", scatter_dimension=0, tiled=True)[0]
        first_sum = lax.psum_scatter(first, "tensor", scatter_dimension=0, tiled=True)[0].astype(F32)
        mean = lax.psum(stat[0, :rows], "tensor")[:, None] / width

        def cols(values):
            return lax.dynamic_slice_in_dim(values, tensor_index * columns, columns, -1).astype(F32)

        input_grad = (
            cols(hidden_grad) + scale[:, :1] * (first_sum * cols(gain1) - cols(tokens) * scale[:, :1] * mean)
        ).astype(BF)
    return (
        block_out, input_grad, gain1_sum, q_sum, k_sum, v_sum, out_sum, gain2_sum, router_sum,
        gate_grad, up_grad, down_grad,
    )


def solution(mesh):
    rows2 = P(("expert", "dp"), None)
    placed = (
        rows2, rows2, P("expert", None), P("expert", None), rows2, rows2, P(),
        P(None, "tensor"), P(None, "tensor"), P(None, "tensor"), P("tensor", None), P(), P(),
        P("expert", None, "tensor"), P("expert", None, "tensor"), P("expert", "tensor", None),
    )
    return jax.shard_map(
        on_device,
        mesh=mesh,
        in_specs=placed,
        out_specs=(
            P(("expert", "dp"), "tensor"), P(("expert", "dp"), "tensor"), P(),
            P(None, "tensor"), P(None, "tensor"), P(None, "tensor"), P("tensor", None), P(), P(),
            P("expert", None, "tensor"), P("expert", None, "tensor"), P("expert", "tensor", None),
        ),
        check_vma=False,
    )
```

```python
import functools

import jax
import jax.numpy as jnp
import numpy as np
from jax import lax
from jax.experimental import pallas as pl
from jax.experimental.pallas import tpu as pltpu
from jax.sharding import PartitionSpec as P

HEADS = 16
KV_HEADS = 8
HEAD_DIM = 64
EXPERTS = 32
TOP = 8
SLOT = 512

EPS = 1e-06
THETA = 10000.0
NEG = -1e30
BF = jnp.bfloat16
F32 = jnp.float32
MIB = 1 << 20


def dot(a, b, ca=1, cb=0):
    return lax.dot_general(a, b, (((ca,), (cb,)), ((), ())), preferred_element_type=F32)


def vmem(count=1):
    return [pl.BlockSpec(memory_space=pltpu.VMEM)] * count


def params(mib, **more):
    return pltpu.CompilerParams(vmem_limit_bytes=mib * MIB, **more)


def rotary_tables(rows):
    places = np.arange(rows, dtype=np.float32)[:, None]
    halfway = HEAD_DIM // 2
    spread = np.float32(THETA) ** (-2.0 * np.arange(halfway, dtype=np.float32) / HEAD_DIM)
    angles = (places * spread.astype(np.float32)[None, :]).astype(np.float32)
    copies = 128 // halfway
    return (
        np.tile(np.cos(angles), (1, copies)).astype(np.float32),
        np.tile(np.sin(angles), (1, copies)).astype(np.float32),
    )


def rotate128(values, cosine, sine, low_half):
    half = HEAD_DIM // 2
    up = pltpu.roll(values, 128 - half, 1)
    down = pltpu.roll(values, half, 1)
    return values * cosine + jnp.where(low_half, -up, down) * sine


def lanes(shape):
    return lax.broadcasted_iota(jnp.int32, shape, len(shape) - 1)


def sublanes(shape):
    return lax.broadcasted_iota(jnp.int32, shape, len(shape) - 2)


def bits_of(count):
    return [1 << i for i in range(count.bit_length() - 1)]


def flip(value, mask):
    for bit in bits_of(1 << 16):
        if mask & bit:
            value = value + bit - 2 * bit * lax.rem(lax.div(value, bit), 2)
    return value


class Net:
    def __init__(self, send_sem, recv_sem):
        self.send_sem, self.recv_sem, self.used, self.copies = send_sem, recv_sem, 0, []
        self.me = {axis: lax.axis_index(axis) for axis in ("expert", "tensor", "dp")}

    def barrier(self, partners):
        sem = pltpu.get_barrier_semaphore()
        for partner in partners:
            pl.semaphore_signal(sem, inc=1, device_id=self.device(partner), device_id_type=pl.DeviceIdType.MESH)
        pl.semaphore_wait(sem, len(partners))

    def device(self, partner):
        pairs = [partner] if isinstance(partner[0], str) else partner
        return {axis: flip(self.me[axis], mask) for axis, mask in pairs}

    def send(self, source, target, *partner):
        k = self.used
        self.used += 1
        copy = Copy(self, k, source, target, partner)
        copy.build().start()
        self.copies.append(copy)
        return copy

    def close(self):
        for copy in self.copies:
            copy.build().wait_send()


class Copy:
    def __init__(self, net, index, source, target, partner):
        self.net, self.index, self.source, self.target, self.partner = net, index, source, target, partner

    def build(self):
        source = self.source() if callable(self.source) else self.source
        target = self.target() if callable(self.target) else self.target
        return pltpu.make_async_remote_copy(
            src_ref=source, dst_ref=target,
            send_sem=self.net.send_sem.at[self.index], recv_sem=self.net.recv_sem.at[self.index],
            device_id=self.net.device(self.partner), device_id_type=pl.DeviceIdType.MESH,
        )

    def wait_recv(self):
        self.build().wait_recv()


class Gather:
    def __init__(self, net, at, steps, known=((0, 0),), first=None):
        self.net, self.at, self.steps, self.known, self.first, self.flight = net, at, list(steps), list(known), first, []

    def start(self):
        axis, mask = self.steps.pop(0)
        fresh = []
        for re, rt in self.known:
            place = functools.partial(self.at, re, rt)
            source = self.first if self.first is not None and (re, rt) == (0, 0) else place
            self.flight.append(self.net.send(source, place, axis, mask))
            fresh.append((re ^ mask, rt) if axis == "expert" else (re, rt ^ mask))
        self.known += fresh

    def finish(self):
        for copy in self.flight:
            copy.wait_recv()
        self.flight = []


class Reduce:
    def __init__(self, net, at, landing, steps, chunks):
        self.net, self.at, self.landing, self.steps, self.live = net, at, landing, list(steps), list(chunks)
        self.used, self.flight = 0, []

    def start(self):
        axis, mask = self.steps.pop(0)
        side = 0 if axis == "expert" else 1
        going = [r for r in self.live if (r[side] & mask if mask else r[side])]
        self.live = [r for r in self.live if r not in going]
        for r in going:
            toward = mask or r[side]
            kept = (r[0] ^ toward, r[1]) if side == 0 else (r[0], r[1] ^ toward)
            copy = self.net.send(functools.partial(self.at, *r), functools.partial(self.landing, self.used), axis, toward)
            self.flight.append((kept, copy, self.used))
            self.used += 1

    def finish(self):
        for place in sorted({kept for kept, _, _ in self.flight}):
            total = self.at(*place)[...].astype(F32)
            for kept, copy, slot in self.flight:
                if kept == place:
                    copy.wait_recv()
                    total = total + self.landing(slot)[...].astype(F32)
            self.at(*place)[...] = total.astype(BF)
        self.flight = []


class Exchange:
    def __init__(self, net, stages, k, landing, partners):
        self.net, self.stages, self.k, self.landing, self.partners, self.flight = net, stages, k, landing, partners, []

    def start(self):
        for index, partner in enumerate(self.partners):
            self.flight.append(self.net.send(
                lambda: self.stages.at[self.k], lambda index=index: self.landing.at[index], *partner
            ))

    def finish(self):
        total = self.stages[self.k]
        for index, copy in enumerate(self.flight):
            copy.wait_recv()
            total = total + self.landing[index]
        self.stages[self.k + 1] = total


TABLE_ROWS = 48
SMALL_ROWS = 128


def table_of(length, routes_ref, order_ref):
    rows = routes_ref.shape[1]
    capacity = rows * TOP // EXPERTS
    entries = rows * TOP
    chunk = 512
    routes_t = routes_ref[...].astype(F32).astype(BF)
    upper = (sublanes((chunk, chunk)) < lanes((chunk, chunk))).astype(F32).astype(BF)
    expert_row = sublanes((EXPERTS, chunk))

    def body(step, carried):
        counts, table = carried
        entry = order_ref[:, pl.ds(pl.multiple_of(step * chunk, chunk), chunk)]
        row, choice = entry // TOP, entry % TOP
        onehot_row = (sublanes((rows, chunk)) == row).astype(F32).astype(BF)
        picked = dot(routes_t, onehot_row)
        expert = jnp.sum(jnp.where(sublanes((TOP, chunk)) == choice, picked, 0.0), axis=0, keepdims=True)
        member = (expert_row.astype(F32) == expert) & (row < length)
        member_f = member.astype(F32)
        before = dot(member_f.astype(BF), upper) + counts
        value = jnp.where(member, jnp.minimum(before, float(capacity)) + 1.0, 0.0)
        table = table + dot(value.astype(BF), onehot_row, 1, 1)
        return counts + jnp.sum(member_f, axis=1, keepdims=True), table

    _, table = lax.fori_loop(
        0, entries // chunk, body, (jnp.zeros((EXPERTS, 1), F32), jnp.zeros((EXPERTS, rows), F32))
    )
    return table


def given_table(tables, index, dp_here):
    total = 0.0
    for j in range(tables.shape[1]):
        source = tables[index, j, EXPERTS : EXPERTS + 16, :].astype(F32)[0:1]
        total = total + jnp.where(source == dp_here, tables[index, j, 0:EXPERTS, :].astype(F32), 0.0)
    return total


def head_parts(q, k_a, k_b, index, low_lane):
    block = q[:, (index // 2) * 128 : (index // 2) * 128 + 128]
    mine = low_lane if index % 2 == 0 else jnp.logical_not(low_lane)
    return jnp.where(mine, block, jnp.zeros((), block.dtype)), (k_a if index % 2 == (index // 2) % 2 else k_b)


def swap(block):
    return pltpu.roll(block.astype(F32), HEAD_DIM, 1).astype(BF)


def front_kernel(
    sizes,
    lengths_ref, order_of_ref, x_ref, gain_ref, wq_ref, wk_ref, wv_ref, wo_ref, cos_ref, sin_ref, gain2_ref, routes_ref, order_ref, dy_ref,
    normed_ref, q_ref, k_ref, v_ref, heads_ref, logsum_ref, hidden_ref, share_ref, tables_ref, far_dy_ref, xown_ref, dyown_ref,
    part, landing, send_sem, recv_sem, local_sem,
):
    expert_count, tensor_count, dp_count = sizes
    rows, width = x_ref.shape
    share = rows // tensor_count
    half = rows // 2
    net = Net(send_sem, recv_sem)
    me_e, me_t, me_d = net.me["expert"], net.me["tensor"], net.me["dp"]
    expert_bits = [("expert", b) for b in bits_of(expert_count)]
    tensor_bits = [("tensor", b) for b in bits_of(tensor_count)]
    net.barrier(expert_bits + tensor_bits + [("dp", m) for m in range(1, dp_count)])

    keep_dy = pltpu.make_async_copy(dy_ref, dyown_ref.at[me_e], local_sem.at[0])
    keep_dy.start()
    half_start = pl.multiple_of(lax.rem(me_t, 2) * half, half)
    dy_half = Gather(
        net, lambda re, rt: dyown_ref.at[flip(me_e, re), pl.ds(half_start, half)], expert_bits,
        first=dy_ref.at[pl.ds(half_start, half)],
    )
    dy_half.start()
    length, source, dealt_length = lengths_ref[0, me_d], order_of_ref[0, me_d], 0
    for i in range(dp_count):
        dealt_length = jnp.where(source == i, lengths_ref[0, i], dealt_length)
    x = x_ref[...].astype(F32)
    scale = lax.rsqrt(jnp.mean(x * x, axis=-1, keepdims=True) + EPS)
    normed = (x * scale * gain_ref[...].astype(F32)[None, :]).astype(BF)
    normed_ref[...] = normed
    cosine, sine = cos_ref[...], sin_ref[...]
    lane = lanes((rows, 128))
    low_half = lane % HEAD_DIM < HEAD_DIM // 2
    low_lane = lane < HEAD_DIM
    q_pre = dot(normed, wq_ref[...])
    for block in range(q_pre.shape[1] // 128):
        cut = slice(block * 128, block * 128 + 128)
        q_ref[:, cut] = rotate128(q_pre[:, cut], cosine, sine, low_half).astype(BF)
    k = rotate128(dot(normed, wk_ref[...]), cosine, sine, low_half).astype(BF)
    v = dot(normed, wv_ref[...]).astype(BF)
    k_ref[...] = k
    v_ref[...] = v
    q = q_ref[...]
    k_b, v_b = swap(k), swap(v)
    row, col = sublanes((rows, rows)), lanes((rows, rows))
    allowed = (col <= row) & (col < length)
    logsum = jnp.zeros((rows, 128), F32)
    pair = None
    for index in range(q.shape[1] // HEAD_DIM):
        q_one, k_one = head_parts(q, k, k_b, index, low_lane)
        v_one = v if index % 2 == (index // 2) % 2 else v_b
        scores = jnp.where(allowed, dot(q_one, k_one, 1, 1) * (HEAD_DIM**-0.5), NEG)
        highest = jnp.max(scores, axis=-1, keepdims=True)
        weights = jnp.exp(scores - highest)
        total = jnp.sum(weights, axis=-1, keepdims=True)
        mixed = dot((weights / total).astype(BF), v_one)
        logsum = jnp.where(lane == index, highest + jnp.log(total), logsum)
        if index % 2 == 0:
            pair = mixed
        else:
            cut = slice((index // 2) * 128, (index // 2) * 128 + 128)
            heads_ref[:, cut] = jnp.where(low_lane, pair, mixed).astype(BF)
    logsum_ref[...] = logsum
    live = (sublanes((rows, 1)) < length).astype(F32)
    part[...] = (dot(heads_ref[...], wo_ref[...]) * live).astype(BF).reshape(part.shape)

    attn = Reduce(
        net, lambda re, rt: part.at[flip(me_t, rt)], lambda i: landing.at[i], tensor_bits,
        [(0, r) for r in range(tensor_count)],
    )
    attn.start()
    table = table_of(dealt_length, routes_ref, order_ref)
    source = jnp.broadcast_to(source.astype(F32), (TABLE_ROWS - EXPERTS, rows))
    tables_ref[me_e, me_d] = jnp.concatenate([table, source], axis=0).astype(BF)
    mine = tables_ref.at[me_e, me_d]
    table_copies = [net.send(mine, mine, "dp", m) for m in range(1, dp_count)]
    mine_rows = pl.multiple_of(me_t * share, share)
    far_copies = [
        net.send(dy_ref.at[pl.ds(mine_rows, share)], far_dy_ref.at[m - 1], "dp", m) for m in range(1, dp_count)
    ]
    attn.finish()
    while attn.steps:
        attn.start()
        if not attn.steps:
            dy_half.finish()
            while dy_half.steps:
                dy_half.start()
                dy_half.finish()
            for re, _ in dy_half.known[1:]:
                place = dy_half.at(re, 0)
                dy_half.flight.append(net.send(place, place, "tensor", 1))
        attn.finish()

    start = pl.multiple_of(me_t * share, share)
    hidden = x_ref[pl.ds(start, share), :].astype(F32) + part[me_t].astype(F32)
    hidden_ref[...] = hidden
    scale2 = lax.rsqrt(jnp.mean(hidden * hidden, axis=-1, keepdims=True) + EPS)
    share_ref[...] = (hidden * scale2 * gain2_ref[...].astype(F32)[None, :]).astype(BF)
    keep_x = pltpu.make_async_copy(share_ref, xown_ref.at[me_e, pl.ds(start, share)], local_sem.at[1])
    keep_x.start()
    high_bits = tensor_bits[1:][::-1]
    gathers = []
    for part_index, steps in enumerate((high_bits + expert_bits, expert_bits + high_bits)):
        size = share // 2

        def at(re, rt, offset=part_index * size):
            begin = pl.multiple_of(flip(me_t, rt) * share + offset, size)
            return xown_ref.at[flip(me_e, re), pl.ds(begin, size)]

        gathers.append(
            Gather(net, at, steps + tensor_bits[:1], first=share_ref.at[pl.ds(part_index * size, size)])
        )
    table_all = Gather(net, lambda re, rt: tables_ref.at[flip(me_e, re)], expert_bits)
    first_step = True
    while gathers[0].steps:
        for gather in gathers:
            gather.start()
        if first_step:
            for copy in table_copies:
                copy.wait_recv()
            first_step = False
        else:
            table_all.finish()
        if table_all.steps:
            table_all.start()
        for gather in gathers:
            gather.finish()
    table_all.finish()
    dy_half.finish()
    for copy in far_copies:
        copy.wait_recv()
    net.close()
    keep_dy.wait()
    keep_x.wait()


def front(lengths, order_of, x, gain, wq, wk, wv, wo, cosine, sine, gain2, routes, order, dy):
    rows, width = x.shape
    sizes = tuple(lax.axis_size(axis) for axis in ("expert", "tensor", "dp"))
    expert_count, tensor_count, dp_count = sizes
    share = rows // tensor_count
    shape = jax.ShapeDtypeStruct
    copies = 96
    return pl.pallas_call(
        functools.partial(front_kernel, sizes),
        out_shape=(
            shape((rows, width), BF), shape((rows, wq.shape[1]), BF), shape((rows, wk.shape[1]), BF),
            shape((rows, wv.shape[1]), BF), shape((rows, wq.shape[1]), BF), shape((rows, 128), F32),
            shape((share, width), F32), shape((share, width), BF), shape((expert_count, dp_count, TABLE_ROWS, rows), BF),
            shape((dp_count - 1, share, width), BF), shape((expert_count, rows, width), BF), shape((expert_count, rows, width), BF),
        ),
        in_specs=[pl.BlockSpec(memory_space=pltpu.SMEM)] * 2 + vmem(11) + [pl.BlockSpec(memory_space=pl.ANY)],
        out_specs=tuple(vmem(10)) + (pl.BlockSpec(memory_space=pl.ANY),) * 2,
        scratch_shapes=[
            pltpu.VMEM((tensor_count, share, width), BF),
            pltpu.VMEM((tensor_count - 1, share, width), BF),
            pltpu.SemaphoreType.DMA((copies,)),
            pltpu.SemaphoreType.DMA((copies,)),
            pltpu.SemaphoreType.DMA((2,)),
        ],
        compiler_params=params(56, collective_id=1, has_side_effects=True),
        cost_estimate=pl.CostEstimate(flops=MIB, bytes_accessed=MIB, transcendentals=0),
        name="front",
    )(lengths, order_of, x, gain, wq, wk, wv, wo, cosine, sine, gain2, routes, order, dy)


def back_kernel(
    sizes, passes,
    lengths_ref, dy_ref, x_ref, gain_ref, gain2_ref, router_ref, hidden_ref, tables_ref,
    normed_ref, q_ref, k_ref, v_ref, heads_ref, logsum_ref, wq_ref, wk_ref, wv_ref, wo_ref, cos_ref, sin_ref,
    grad_in_ref, xown_ref, *rest,
):
    late_count = 13
    late_sem, rest = rest[-1], rest[:-1]
    late_refs, rest = rest[-late_count:], rest[:-late_count]
    late_hbm = (
        x_ref, normed_ref, q_ref, k_ref, v_ref, heads_ref, logsum_ref, wq_ref, wk_ref, wv_ref, wo_ref, cos_ref, sin_ref,
    )
    if passes:
        out_in_ref, rest = rest[0], rest[1:]
        out_pass_ref, rest = rest[7], rest[:7] + rest[8:]
        (out, out_landing), rest = rest[-2:], rest[:-2]
    (
        first_ref, tiny_ref, hidden_grad_ref, scale_ref, dense_ref, out_grad_ref, small_ref,
        grad, grad_landing, normed2, spread, back_ref, picked, send_sem, recv_sem, local_sem,
    ) = rest
    group_count, tensor_count, dp_count = sizes
    rows, width = x_ref.shape
    share = rows // tensor_count
    net = Net(send_sem, recv_sem)
    me_e, me_t, me_d = net.me["expert"], net.me["tensor"], net.me["dp"]
    here = me_e if group_count > 1 else 0
    expert_bits = [("expert", b) for b in bits_of(group_count)]
    tensor_bits = [("tensor", b) for b in bits_of(tensor_count)]
    load_grad = pltpu.make_async_copy(grad_in_ref, grad, local_sem.at[0])
    load_x = pltpu.make_async_copy(xown_ref.at[here], normed2, local_sem.at[1])
    load_grad.start()
    load_x.start()
    late = [pltpu.make_async_copy(a, b, late_sem.at[i]) for i, (a, b) in enumerate(zip(late_hbm, late_refs))]
    if passes:
        load_out = pltpu.make_async_copy(out_in_ref, out, local_sem.at[2])
        load_out.start()
    net.barrier(expert_bits + tensor_bits)
    load_grad.wait()
    for copy in late:
        copy.start()
    high_bits = tensor_bits[1:]
    chunks = [(e, t) for e in range(group_count) for t in range(tensor_count)]
    sums = []
    size = share // 2
    for part_index, steps in enumerate((high_bits + expert_bits, expert_bits + high_bits)):

        def at(re, rt, offset=part_index * size):
            begin = pl.multiple_of(flip(me_t, rt) * share + offset, size)
            return grad.at[flip(here, re) if re else here, pl.ds(begin, size)]

        sums.append(Reduce(
            net, at, lambda i, p=part_index: grad_landing.at[p, i], tensor_bits[:1] + steps, chunks
        ))
    if passes:
        out_sum = Reduce(
            net, lambda re, rt: out.at[flip(me_e, re), flip(me_t, rt)], lambda i: out_landing.at[i],
            tensor_bits[:1] + expert_bits, chunks,
        )
    while sums[0].steps:
        for one in sums:
            one.start()
        if passes and not out_sum.used:
            load_out.wait()
            out_sum.start()
        for one in sums:
            one.finish()
    if passes:
        out_sum.finish()
        out_sum.start()

    start = pl.multiple_of(me_t * share, share)
    gain2 = gain2_ref[...].astype(F32)[None, :]
    hidden = hidden_ref[...]
    scale2 = lax.rsqrt(jnp.mean(hidden * hidden, axis=-1, keepdims=True) + EPS)
    hat2 = hidden * scale2
    second_normed = (hat2 * gain2).astype(BF)
    picked[...] = given_table(tables_ref, me_e, me_d.astype(F32))
    table = picked[:, pl.ds(start, share)]
    table = jnp.concatenate([table, jnp.zeros((128 - EXPERTS, share), F32)], axis=0)
    table = jnp.transpose(table)[:, :EXPERTS]
    logits = dot(second_normed, router_ref[...], 1, 1)
    chosen = table > 0.5
    masked = jnp.where(chosen, logits, NEG)
    weights = jnp.where(chosen, jnp.exp(masked - jnp.max(masked, axis=-1, keepdims=True)), 0.0)
    total = jnp.sum(weights, axis=-1, keepdims=True)
    gates = weights / jnp.where(total > 0.0, total, 1.0)
    gate_in = grad[here, pl.ds(start, share), width:].astype(F32)[:, :EXPERTS]
    logit_grad = (gate_in - gates * jnp.sum(gate_in, axis=-1, keepdims=True)).astype(BF)
    normed_grad = grad[here, pl.ds(start, share), :width].astype(F32) + dot(logit_grad, router_ref[...])
    along2 = normed_grad * hat2
    gain2_part = jnp.sum(along2, axis=0, keepdims=True)
    scaled = normed_grad * gain2
    hidden_grad = dy_ref[pl.ds(start, share), :].astype(F32) + scale2 * (
        scaled - hat2 * jnp.mean(scaled * hat2, axis=-1, keepdims=True)
    )
    spread[me_t, 0:share, :width] = hidden_grad.astype(BF)
    spread[me_t, 0:share, width:] = jnp.concatenate(
        [logit_grad.astype(F32), jnp.zeros((share, 128 - EXPERTS), F32)], axis=1
    ).astype(BF)
    high = gain2_part.astype(BF).astype(F32)
    spread[me_t, share : share + 16, :width] = jnp.concatenate(
        [high, gain2_part - high, jnp.zeros((14, width), F32)], axis=0
    ).astype(BF)
    spread[me_t, share : share + 16, width:] = jnp.zeros((16, 128), BF)
    gather = Gather(net, lambda re, rt: spread.at[flip(me_t, rt)], high_bits[::-1] + tensor_bits[:1])
    while gather.steps:
        gather.start()
        gather.finish()

    for copy in late:
        copy.wait()
    (
        x_ref, normed_ref, q_ref, k_ref, v_ref, heads_ref, logsum_ref, wq_ref, wk_ref, wv_ref, wo_ref, cos_ref, sin_ref,
    ) = late_refs
    length = lengths_ref[0, me_d]
    inv = HEAD_DIM**-0.5
    live = (sublanes((rows, 1)) < length).astype(F32)
    hidden_grad_all = spread[:, 0:share, :width].reshape(rows, width)
    columns = width // tensor_count
    cut = pl.ds(pl.multiple_of(me_t * columns, columns), columns)
    hidden_grad_ref[...] = jnp.concatenate([spread[t, 0:share, cut] for t in range(tensor_count)], axis=0)
    branch = (hidden_grad_all.astype(F32) * live).astype(BF)
    out_grad_ref[...] = dot(heads_ref[...], branch, 0, 0).astype(BF)
    heads_grad = dot(branch, wo_ref[...], 1, 1).astype(BF)
    cosine, sine = cos_ref[...], -sin_ref[...]
    lane = lanes((rows, 128))
    low_half = lane % HEAD_DIM < HEAD_DIM // 2
    low_lane = lane < HEAD_DIM
    q, k, v = q_ref[...], k_ref[...], v_ref[...]
    k_b, v_b = swap(k), swap(v)
    key, query = sublanes((rows, rows)), lanes((rows, rows))
    allowed = (key <= query) & (key < length)
    logsum_rows = jnp.transpose(logsum_ref[...])
    dk = [jnp.zeros((rows, 128), F32), jnp.zeros((rows, 128), F32)]
    dv = [jnp.zeros((rows, 128), F32), jnp.zeros((rows, 128), F32)]
    q_width = q.shape[1]
    pair = None
    for index in range(q_width // HEAD_DIM):
        same = index % 2 == (index // 2) % 2
        q_one, k_one = head_parts(q, k, k_b, index, low_lane)
        g_one, v_one = head_parts(heads_grad, v, v_b, index, low_lane)
        scores = jnp.where(allowed, dot(k_one, q_one, 1, 1) * inv, NEG)
        prob = jnp.exp(scores - logsum_rows[index : index + 1, :])
        grad_prob = dot(v_one, g_one, 1, 1)
        center = jnp.sum(prob * grad_prob, axis=0, keepdims=True)
        score_grad = (prob * (grad_prob - center)).astype(BF)
        dq = dot(score_grad, k_one, 0, 0) * inv
        place = 0 if same else 1
        dk[place] = dk[place] + dot(score_grad, q_one) * inv
        dv[place] = dv[place] + dot(prob.astype(BF), g_one)
        if index % 2 == 0:
            pair = dq
        else:
            cut = slice((index // 2) * 128, (index // 2) * 128 + 128)
            both = jnp.where(low_lane, pair, dq)
            back_ref[:, cut] = rotate128(both, cosine, sine, low_half).astype(BF)
    k_width = k.shape[1]
    k_total = dk[0] + pltpu.roll(dk[1], HEAD_DIM, 1)
    v_total = dv[0] + pltpu.roll(dv[1], HEAD_DIM, 1)
    back_ref[:, q_width : q_width + k_width] = rotate128(k_total, cosine, sine, low_half).astype(BF)
    back_ref[:, q_width + k_width :] = v_total.astype(BF)
    back = back_ref[...]
    first = (
        dot(back[:, :q_width], wq_ref[...], 1, 1)
        + dot(back[:, q_width : q_width + k_width], wk_ref[...], 1, 1)
        + dot(back[:, q_width + k_width :], wv_ref[...], 1, 1)
    )
    columns = width // tensor_count
    for t in range(tensor_count):
        first_ref[t] = first[:, t * columns : (t + 1) * columns].astype(BF)
    x = x_ref[...].astype(F32)
    scale = lax.rsqrt(jnp.mean(x * x, axis=-1, keepdims=True) + EPS)
    scale_ref[...] = jnp.broadcast_to(scale, (rows, 128))
    along = first * (x * scale)
    stat = jnp.sum(along * gain_ref[...].astype(F32)[None, :], axis=-1, keepdims=True)
    tiny_ref[:, 0:rows] = jnp.transpose(jnp.broadcast_to(stat, (rows, 128)))[0:8, :]
    tiny_ref[:, rows:] = jnp.broadcast_to(jnp.sum(along, axis=0, keepdims=True), (8, width))
    dense_ref[...] = dot(normed_ref[...], back, 0, 0).astype(BF)
    load_x.wait()
    router_rows = dot(spread[:, 0:share, width:].reshape(rows, 128), normed2[...], 0, 0)[0:EXPERTS]
    gain2_sum = jnp.zeros((1, width), F32)
    for t in range(tensor_count):
        block = spread[t, share : share + 16, :width].astype(F32)
        gain2_sum = gain2_sum + block[0:1] + block[1:2]
    half = width // 2
    pieces = [router_rows[:, :half], router_rows[:, half:], gain2_sum[:, :half], gain2_sum[:, half:]]
    if passes:
        out_sum.finish()
        out_pass_ref[...] = out[me_e]
    filled = sum(piece.shape[0] for piece in pieces)
    small_ref[...] = jnp.concatenate(pieces + [jnp.zeros((SMALL_ROWS - filled, half), F32)], axis=0).astype(BF)
    net.close()


def back_call(group_count, lengths, vmem_operands, grad, xown, out=None):
    dy, x = vmem_operands[0], vmem_operands[1]
    rows, width = x.shape
    wq, wk, wv, wo = vmem_operands[13:17]
    tensor_count, dp_count = lax.axis_size("tensor"), lax.axis_size("dp")
    share, columns = rows // tensor_count, width // tensor_count
    chunks = group_count * tensor_count
    inner = wq.shape[1] + wk.shape[1] + wv.shape[1]
    shape = jax.ShapeDtypeStruct
    copies = 64
    passed = [] if out is None else [out]
    late = [1] + list(range(7, len(vmem_operands)))
    return pl.pallas_call(
        functools.partial(back_kernel, (group_count, tensor_count, dp_count), out is not None),
        out_shape=(
            shape((tensor_count, rows, columns), BF), shape((8, rows + width), F32), shape((rows, columns), BF),
            shape((rows, 128), F32), shape((width, inner), BF), shape(wo.shape, BF), shape((SMALL_ROWS, width // 2), BF),
            *[shape(one.shape[1:], BF) for one in passed],
        ),
        in_specs=[pl.BlockSpec(memory_space=pltpu.SMEM)] + [
            pl.BlockSpec(memory_space=pl.ANY if i in late else pltpu.VMEM) for i in range(len(vmem_operands))
        ] + [pl.BlockSpec(memory_space=pl.ANY)] * (2 + len(passed)),
        out_specs=tuple(vmem(7)) + tuple(vmem(len(passed))),
        scratch_shapes=[
            pltpu.VMEM(grad.shape, BF),
            pltpu.VMEM((2, chunks - 1, share // 2, width + 128), BF),
            pltpu.VMEM((rows, width), BF),
            pltpu.VMEM((tensor_count, share + 16, width + 128), BF),
            pltpu.VMEM((rows, inner), BF),
            pltpu.VMEM((EXPERTS, rows), F32),
            pltpu.SemaphoreType.DMA((copies,)),
            pltpu.SemaphoreType.DMA((copies,)),
            pltpu.SemaphoreType.DMA((3,)),
        ] + ([
            pltpu.VMEM(out.shape, BF),
            pltpu.VMEM((chunks, rows, columns), BF),
        ] if passed else []) + [pltpu.VMEM(vmem_operands[i].shape, vmem_operands[i].dtype) for i in late] + [
            pltpu.SemaphoreType.DMA((len(late),))
        ],
        compiler_params=params(60, collective_id=2, has_side_effects=True),
        cost_estimate=pl.CostEstimate(flops=MIB, bytes_accessed=MIB, transcendentals=0),
        name="back",
    )(lengths, *vmem_operands, grad, xown, *passed)


def gate_rows(router_t, rows, table):
    logits = dot(router_t, rows, 1, 1)
    chosen = table > 0.5
    masked = jnp.where(chosen, logits, NEG)
    weights = jnp.where(chosen, jnp.exp(masked - jnp.max(masked, axis=0, keepdims=True)), 0.0)
    total = jnp.sum(weights, axis=0, keepdims=True)
    return weights / jnp.where(total > 0.0, total, 1.0)


def bit_steps(expert_count, tensor_count):
    expert_bits = [("expert", b) for b in bits_of(expert_count)]
    tensor_bits = [("tensor", b) for b in bits_of(tensor_count)]
    return expert_bits, tensor_bits, tensor_bits[1:][::-1]


def plane_gathers(net, target, share, first=None, done=False, last=None, which=slice(None)):
    counts = lax.axis_size("expert"), lax.axis_size("tensor")
    expert_bits, _, high_bits = bit_steps(*counts)
    size = share // 2
    parts = []
    for index, steps in enumerate((high_bits + expert_bits, expert_bits + high_bits)):

        def at(re, rt, offset=index * size):
            begin = pl.multiple_of(flip(net.me["tensor"], rt) * share + offset, size)
            return target.at[which, flip(net.me["expert"], re), pl.ds(begin, size)]

        source = None if first is None else first.at[:, pl.ds(index * size, size)]
        known = [(0, 0)]
        if done:
            axis, mask = steps.pop(0)
            known.append((mask, 0) if axis == "expert" else (0, mask))
        parts.append(Gather(net, at, steps[:last], known=known, first=source))
    return parts


def core_gather(net, target, share, known, which=slice(None)):
    def whole(re, rt):
        begin = pl.multiple_of(flip(net.me["tensor"], rt) * share, share)
        return target.at[which, flip(net.me["expert"], re), pl.ds(begin, share)]

    return Gather(net, whole, [("tensor", 1)], known=known)


def slot_numbers(capacity, rows):
    return sublanes((capacity, rows)).astype(F32).astype(BF)


def placed(slot_id, table_row, weight):
    return jnp.where(slot_id == (table_row - 1.0).astype(BF), weight, jnp.zeros((), BF))


def fill_units(table, gate, slot_id, first_expert, count, hits_ref, gated_ref):
    capacity = slot_id.shape[0]
    for j in range(count):
        row = table(first_expert + j)
        cut = slice(j * capacity, (j + 1) * capacity)
        hits_ref[cut, :] = placed(slot_id, row, jnp.ones((), BF))
        gated_ref[cut, :] = placed(slot_id, row, gate(first_expert + j).astype(BF))


def middle(both, grad_act, hidden):
    g_here, u_here = both[:, :hidden], both[:, hidden:]
    sig = 1.0 / (1.0 + jnp.exp(-g_here))
    silu = g_here * sig
    act = silu * u_here
    grad_gate = (grad_act * u_here * sig * (1.0 + g_here * (1.0 - sig))).astype(BF)
    grad_up = (grad_act * silu).astype(BF)
    return act, jnp.concatenate([grad_gate, grad_up], axis=1)


def own_kernel(
    sizes, groups, capacity, local, batch, gathers,
    x_ref, dy_ref, table_ref, router_ref, wg_ref, wu_ref, wd_ref, hidden_ref, share_ref, far_dy_ref,
    out_c_ref, out_g_ref, xs_out, ys_out, oth_ref, othy_ref, gates_out,
    gates, gates_b, ranks, hits, gated, xs, ys, made, back, gi_rows, acc_c, acc_g, send_sem, recv_sem, local_sem,
):
    chunk, pair = pl.program_id(0), pl.program_id(1)
    pairs = local // 2
    per_batch = batch // 2
    expert_count, tensor_count, dp_count = sizes
    net = Net(send_sem, recv_sem)
    dp_here, me_t, me_e = net.me["dp"], net.me["tensor"], net.me["expert"]
    rows, width = x_ref.shape[-2:]
    units = groups
    hidden = wg_ref.shape[2]
    slot_id = slot_numbers(capacity, rows)
    share = rows // tensor_count

    if gathers:
        expert_bits, tensor_bits, high_bits = bit_steps(expert_count, tensor_count)
        cotangent_parts = plane_gathers(net, othy_ref, share, first=far_dy_ref)
        row_parts = plane_gathers(net, oth_ref, share, last=1)
        mine = pl.ds(pl.multiple_of(me_t * share, share), share)
        keep = pltpu.make_async_copy(far_dy_ref, othy_ref.at[:, me_e, mine], local_sem.at[2])
        flight = []

        def first_steps():
            net.barrier(expert_bits + tensor_bits + [("dp", m) for m in range(1, dp_count)])
            keep.start()
            for one in cotangent_parts:
                one.start()
            for m in range(1, dp_count):
                flight.append(net.send(share_ref, lambda m=m: oth_ref.at[m - 1, me_e, mine], "dp", m))

        def second_steps():
            for one in cotangent_parts:
                one.finish()
            for one in cotangent_parts:
                one.start()

        def third_steps():
            for one in cotangent_parts:
                one.finish()
            keep.wait()
            cotangent_parts.append(core_gather(net, othy_ref, share, cotangent_parts[0].known))
            cotangent_parts[-1].start()
            for copy in flight:
                copy.wait_recv()
            flight.clear()
            for one in row_parts:
                one.start()

        def last_steps():
            cotangent_parts[-1].finish()
            for one in row_parts:
                one.finish()
            for copy in flight:
                copy.wait_recv()
            net.close()

        for time, steps in ((0, first_steps), (pairs * 2 // 8, second_steps), (pairs * 6 // 8, third_steps)):

            @pl.when(pair == time)
            def _(steps=steps):
                steps()

    @pl.when(pair == 0)
    def _():
        gi_rows[...] = jnp.zeros_like(gi_rows)

        @pl.loop(0, units)
        def _(i):
            table = given_table(table_ref, i, dp_here.astype(F32))
            ranks[i] = table
            gates[i] = gate_rows(router_ref[...], x_ref[i], table)
            gates_b[i] = gates[i].astype(BF)

    @pl.when(pair == 0)
    def _():
        if not gathers:
            gates_out[...] = gates_b[...]
            return
        for m in range(1, dp_count):
            flight.append(net.send(gates_b, lambda m=m: gates_out.at[m - 1], "dp", m))

    place = lax.rem(pair, per_batch)
    half = lax.div(pair, per_batch)
    group_start = pl.multiple_of(chunk * groups, groups)
    outs = []
    for index, (source, target) in enumerate(((xs, xs_out), (ys, ys_out))):
        outs.append(pltpu.make_async_copy(
            source, target.at[pl.ds(half * batch, batch), pl.ds(group_start, groups)], local_sem.at[index]
        ))

    @pl.when(place == 0)
    def _():
        @pl.loop(0, units)
        def _(i):
            fill_units(
                lambda e: ranks[i, pl.ds(e, 1), :], lambda e: gates[i, pl.ds(e, 1), :], slot_id,
                me_e * local + half * batch, batch, hits.at[i], gated.at[i],
            )
            xs[:, i] = dot(hits[i], x_ref[i]).astype(BF).reshape(batch, capacity, width)
            ys[:, i] = dot(gated[i], dy_ref[i]).astype(BF).reshape(batch, capacity, width)

        for copy in outs:
            copy.start()

    spots = [place * 2 + j for j in range(2)]
    inner_w = [jnp.concatenate([wg_ref[j], wu_ref[j]], axis=1) for j in range(2)]
    both = [dot(xs[spots[j]].reshape(units * capacity, width), inner_w[j]) for j in range(2)]
    grad_act = [dot(ys[spots[j]].reshape(units * capacity, width), wd_ref[j], 1, 1) for j in range(2)]
    mids = [middle(both[j], grad_act[j], hidden) for j in range(2)]
    for j in range(2):
        act, grads = mids[j]
        result = dot(act.astype(BF), wd_ref[j]).astype(BF)
        moved = dot(grads, inner_w[j], 1, 1).astype(BF)
        inner = jnp.sum(act * grad_act[j], axis=-1, keepdims=True)
        at_slot = pl.ds(pl.multiple_of(spots[j] * capacity, capacity), capacity)
        for i in range(units):
            cut = slice(i * capacity, (i + 1) * capacity)
            made[i, at_slot, :] = result[cut]
            back[i, at_slot, :] = moved[cut]
            gi_rows[i, pl.ds(me_e * local + pair * 2 + j, 1), :] = jnp.sum(
                hits[i, at_slot, :].astype(F32) * inner[cut], axis=0, keepdims=True
            )

    @pl.when(place == per_batch - 1)
    def _():
        for copy in outs:
            copy.wait()

        @pl.loop(0, units)
        def _(i):
            add_c = dot(gated[i], made[i], 0, 0)
            add_g = dot(hits[i], back[i], 0, 0)

            @pl.when(half == 0)
            def _():
                acc_c[i] = add_c
                acc_g[i] = add_g

            @pl.when(half != 0)
            def _():
                acc_c[i] += add_c
                acc_g[i] += add_g

    @pl.when(pair == pairs - 1)
    def _():
        blocks, columns = out_c_ref.shape[1], out_c_ref.shape[3]
        for i in range(units):

            @pl.when(chunk * groups + i == me_e)
            def _():
                cut = pl.ds(pl.multiple_of(me_t * share, share), share)
                acc_c[i, cut, :] += hidden_ref[...]

            for t in range(blocks):
                out_c_ref[i, t] = acc_c[i, :, t * columns : (t + 1) * columns].astype(BF)
            out_g_ref[i, :, :width] = acc_g[i].astype(BF)
            out_g_ref[i, :, width:] = jnp.transpose(gi_rows[i]).astype(BF)
        if gathers:
            last_steps()


def own_call(x, dy, table, router_t, wg, wu, wd, hidden_share, normed_share, far_dy):
    sizes = tuple(lax.axis_size(axis) for axis in ("expert", "tensor", "dp"))
    groups_all, dp_count = table.shape[:2]
    rows, width = x.shape[-2:]
    groups = 2
    chunks = groups_all // groups
    local, _, hidden = wg.shape
    pairs = local // 2
    assert chunks == 1 or pairs == 1
    batch = min(8, local)
    gathers = chunks == 1
    capacity = rows * TOP // EXPERTS
    shape = jax.ShapeDtypeStruct
    row_block = pl.BlockSpec((groups, rows, width), lambda c, p: (c, 0, 0), pipeline_mode=pl.Buffered(1))
    in_block = pl.BlockSpec((2, width, hidden), lambda c, p: (p, 0, 0))
    blocks = sizes[1]
    columns = width // blocks
    copies = 64
    slots = shape((local, groups_all, capacity, width), BF)
    anywhere = pl.BlockSpec(memory_space=pl.ANY)
    return pl.pallas_call(
        functools.partial(own_kernel, sizes, groups, capacity, local, batch, gathers),
        out_shape=(
            shape((groups_all, blocks, rows, columns), BF), shape((groups_all, rows, width + 128), BF), slots, slots,
            *[shape((dp_count - 1, groups_all, rows, width) if gathers else (16, 128), BF)] * 2,
            shape((dp_count - 1, groups_all, EXPERTS, rows) if gathers else (groups_all, EXPERTS, rows), BF),
        ),
        grid=(chunks, pairs),
        in_specs=[
            row_block, row_block,
            pl.BlockSpec((groups, dp_count, TABLE_ROWS, rows), lambda c, p: (c, 0, 0, 0)),
            pl.BlockSpec((EXPERTS, width), lambda c, p: (0, 0)),
            in_block, in_block, pl.BlockSpec((2, hidden, width), lambda c, p: (p, 0, 0)),
            pl.BlockSpec(hidden_share.shape, lambda c, p: (0, 0)), anywhere, anywhere,
        ],
        out_specs=(
            pl.BlockSpec((groups, blocks, rows, columns), lambda c, p: (c, 0, 0, 0)),
            pl.BlockSpec((groups, rows, width + 128), lambda c, p: (c, 0, 0)),
            anywhere, anywhere, anywhere, anywhere,
            anywhere if gathers else pl.BlockSpec((groups, EXPERTS, rows), lambda c, p: (c, 0, 0)),
        ),
        scratch_shapes=[
            pltpu.VMEM((groups, EXPERTS, rows), F32),
            pltpu.VMEM((groups, EXPERTS, rows), BF),
            pltpu.VMEM((groups, EXPERTS, rows), F32),
            pltpu.VMEM((groups, batch * capacity, rows), BF),
            pltpu.VMEM((groups, batch * capacity, rows), BF),
            pltpu.VMEM((batch, groups, capacity, width), BF),
            pltpu.VMEM((batch, groups, capacity, width), BF),
            pltpu.VMEM((groups, batch * capacity, width), BF),
            pltpu.VMEM((groups, batch * capacity, width), BF),
            pltpu.VMEM((groups, 128, rows), F32),
            pltpu.VMEM((groups, rows, width), F32),
            pltpu.VMEM((groups, rows, width), F32),
            pltpu.SemaphoreType.DMA((copies,)),
            pltpu.SemaphoreType.DMA((copies,)),
            pltpu.SemaphoreType.DMA((4,)),
        ],
        compiler_params=params(
            60, dimension_semantics=("arbitrary", "arbitrary"),
            **(dict(collective_id=3, has_side_effects=True) if gathers else {}),
        ),
        cost_estimate=pl.CostEstimate(flops=MIB, bytes_accessed=MIB, transcendentals=0),
        name="experts_own",
    )(x, dy, table, router_t, wg, wu, wd, hidden_share, normed_share, far_dy)


def slots_kernel(sizes, masks, capacity, local, batch, reduces, x_hbm, dy_hbm, table_ref, gates_ref, *rest):
    if reduces:
        (
            dense_in, heads_in, small_in, first_in, out_in, old_hbm, x_tok_hbm, stat_in, scale_ref, gain_ref,
            x_hbm, xs_ref, ys_ref, sums_ref, input_ref, block_ref, gain_out_ref,
            buf, onehot, ranks, weights, dense, heads, small, first, out, dense_land, heads_land, small_land, first_land, out_land,
            stat, stat_land, gains, gains_land, gains_far_land, old, x_tok, load_sem, send_sem, recv_sem, local_sem,
        ) = rest
    else:
        xs_ref, ys_ref, buf, onehot, ranks, weights, load_sem = rest
    expert_count, tensor_count, dp_count = sizes
    step = pl.program_id(0)
    units = expert_count * len(masks)
    rows, width = buf.shape[-2:]
    me_e, me_d = lax.axis_index("expert"), lax.axis_index("dp")
    slot_id = slot_numbers(capacity, rows)

    def far_dp(m):
        value = me_d
        for bit in bits_of(dp_count):
            on = lax.rem(lax.div(m, bit), 2)
            value = value + on * (bit - 2 * bit * lax.rem(lax.div(me_d, bit), 2))
        return value

    def place(i):
        m = masks[0] + lax.div(i, expert_count)
        return m, lax.rem(i, expert_count), far_dp(m)

    def load(source, i, slot):
        m, group, _ = place(i)
        return pltpu.make_async_copy(source.at[m - masks[0], group], buf.at[slot], load_sem.at[slot])

    def start_load(s):
        @pl.when(s < units)
        def _():
            load(dy_hbm, s, lax.rem(s, 2)).start()

        @pl.when(s >= units)
        def _():
            load(x_hbm, s - units, lax.rem(s, 2)).start()

    if reduces:
        net = Net(send_sem, recv_sem)
        me_t = net.me["tensor"]
        ways = expert_count * dp_count
        expert_bits, tensor_bits, high_bits = bit_steps(expert_count, tensor_count)
        dp_bits = [("dp", b) for b in bits_of(dp_count)][::-1]
        chunks = [(e, d) for e in range(expert_count) for d in range(dp_count)]
        plane = [(e, t) for e in range(expert_count) for t in range(0, tensor_count, 2)]
        share = rows // tensor_count
        planes = [plane_gathers(net, x_hbm, share, done=True, which=m) for m in range(dp_count - 1)]
        cores = [core_gather(net, x_hbm, share, plane, which) for which in range(dp_count - 1)]

        def chunk_of(ref):
            size = ref.shape[0] // ways

            def at(re, rd):
                index = flip(me_e, re) * dp_count + flip(me_d, rd)
                return ref.at[pl.ds(pl.multiple_of(index * size, size), size)]

            return at

        def column_of(ref):
            return lambda re, rt: ref.at[flip(me_t, rt)]

        dense_sum = Reduce(net, chunk_of(dense), lambda i: dense_land.at[i], [("dp", 0)] + expert_bits, chunks)
        small_sum = Reduce(net, chunk_of(small), lambda i: small_land.at[i], [("dp", 0)] + expert_bits, chunks)
        heads_sum = Reduce(net, chunk_of(heads), lambda i: heads_land.at[i], expert_bits + [("dp", 0)], chunks)
        out_sum = Reduce(net, column_of(out), lambda i: out_land.at[i], high_bits, [(0, t) for t in range(0, tensor_count, 2)])
        first_sum = Reduce(net, column_of(first), lambda i: first_land.at[i], tensor_bits, [(0, t) for t in range(tensor_count)])
        last = 2 * units
        plan = [
            (dense_sum, [0, units + 4]), (small_sum, [0, units + 4]),
            (heads_sum, [4, units + 4]), (first_sum, [0, units]), (out_sum, [units]),
        ]
        near = [("tensor", m) for m in range(1, tensor_count)]
        far = [(("expert", e), ("dp", d)) for e, d in chunks if e or d]
        stat_sum = Exchange(net, stat, 0, stat_land, near)
        gains_near = Exchange(net, gains, 0, gains_land, near)
        gains_far = Exchange(net, gains, 1, gains_far_land, far)
        columns = first.shape[2]
        begin = pl.multiple_of(me_t * columns, columns)

        def advance(k):
            for one, when in plan:
                if k in when or k == last:
                    if one.flight:
                        one.finish()
                    if one.steps:
                        one.start()

        def moves():
            pairs = (
                (stat_in.at[:, 0:rows], stat.at[0]), (stat_in.at[:, rows:], gains.at[0]),
                (dense_in, dense), (small_in, small), (first_in, first),
                (heads_in, heads), (out_in, out),
                (old_hbm, old), (x_tok_hbm.at[:, pl.ds(begin, columns)], x_tok),
            )
            return [pltpu.make_async_copy(a, b, local_sem.at[i]) for i, (a, b) in enumerate(pairs)]

        @pl.when(step == 0)
        def _():
            for copy in moves():
                copy.start()
            net.barrier(near + far)
            for copy in moves()[:2]:
                copy.wait()
            stat_sum.start()
            gains_near.start()
            for parts in planes:
                for one in parts:
                    one.start()
            for copy in moves()[2:5]:
                copy.wait()
            advance(0)

        for k in range(1, last):
            at_plane = [m for m in range(dp_count - 1) if k == max(units - 3 + m * expert_count, 1)]
            at_core = [m for m in range(dp_count - 1) if k == units - 1 + m * expert_count]
            if not (k <= 2 or at_plane or at_core or any(k in when for _, when in plan)):
                continue

            @pl.when(step == k)
            def _(k=k, at_plane=at_plane, at_core=at_core):
                if k == 1:
                    for copy in moves()[5:]:
                        copy.wait()
                for m in at_plane:
                    for one in planes[m]:
                        one.finish()
                    cores[m].start()
                advance(k)
                if k == 2:
                    stat_sum.finish()
                    gains_near.finish()
                    gains_far.start()
                for m in at_core:
                    cores[m].finish()

    @pl.when(step == 0)
    def _():
        start_load(step)

    @pl.when(step + 1 < 2 * units)
    def _():
        start_load(step + 1)

    slot = lax.rem(step, 2)

    def spread(unit, source, target_ref, gated):
        m, group, d = place(unit)
        ranks[...] = given_table(table_ref, group, d.astype(F32))
        if gated:
            weights[...] = gates_ref[m - masks[0], group].astype(F32)
        for part in range(local // batch):
            for j in range(batch):
                e = me_e * local + part * batch + j
                weight = weights[pl.ds(e, 1), :].astype(BF) if gated else jnp.ones((), BF)
                onehot[part, j * capacity : (j + 1) * capacity, :] = placed(slot_id, ranks[pl.ds(e, 1), :], weight)
            if part == 0:
                load(source, unit, slot).wait()
            moved = dot(onehot[part], buf[slot]).astype(BF)
            target_ref[part * batch : (part + 1) * batch, 0] = moved.reshape(batch, capacity, width)

    @pl.when(step < units)
    def _():
        spread(step, dy_hbm, ys_ref, True)

    @pl.when(step >= units)
    def _():
        spread(step - units, x_hbm, xs_ref, False)

    if reduces:

        @pl.when(step == last - 1)
        def _():
            for one, _ in plan:
                while one.flight or one.steps:
                    if one.flight:
                        one.finish()
                    if one.steps:
                        one.start()
            gains_far.finish()
            here = me_e * dp_count + me_d
            d_rows, h_rows, s_rows = (ref.shape[0] // ways for ref in (dense, heads, small))
            half = heads.shape[1] // 2
            sums_ref[0:d_rows] = dense[pl.ds(pl.multiple_of(here * d_rows, d_rows), d_rows), :]
            mine = heads[pl.ds(pl.multiple_of(here * h_rows, h_rows), h_rows), :]
            sums_ref[d_rows : d_rows + h_rows] = mine[:, :half]
            sums_ref[d_rows + h_rows : d_rows + 2 * h_rows] = mine[:, half:]
            sums_ref[d_rows + 2 * h_rows :] = small[pl.ds(pl.multiple_of(here * s_rows, s_rows), s_rows), :]
            gain_out_ref[...] = gains[gains.shape[0] - 1]
            total = jnp.concatenate([stat[stat.shape[0] - 1], jnp.zeros((120, rows), F32)], axis=0)
            mean = jnp.transpose(total)[:, 0:1] / gain_ref.shape[0]
            scale = scale_ref[:, 0:1]
            input_ref[...] = (
                old[...].astype(F32) + scale * (
                    first[me_t].astype(F32) * gain_ref[pl.ds(begin, columns)].astype(F32)[None, :]
                    - x_tok[...].astype(F32) * scale * mean
                )
            ).astype(BF)
            block_ref[...] = out[me_t]
            net.close()


def slots_call(masks, x, dy, table, gates, local, sums=None):
    sizes = tuple(lax.axis_size(axis) for axis in ("expert", "tensor", "dp"))
    expert_count, _, dp_count = sizes
    rows, width = x.shape[-2:]
    units = expert_count * len(masks)
    capacity = rows * TOP // EXPERTS
    batch = min(8, local)
    shape = jax.ShapeDtypeStruct
    anywhere = pl.BlockSpec(memory_space=pl.ANY)
    y_block = pl.BlockSpec((local, 1, capacity, width), lambda i: (0, jnp.minimum(i, units - 1), 0, 0))
    x_block = pl.BlockSpec((local, 1, capacity, width), lambda i: (0, jnp.maximum(i - units, 0), 0, 0))
    whole = pl.BlockSpec(memory_space=pltpu.VMEM)
    out_shape = [shape((local, units, capacity, width), BF)] * 2
    out_specs = [x_block, y_block]
    aliases = {}
    operands = [x, dy, table, gates]
    in_specs = [anywhere, anywhere, whole, whole]
    scratch = [
        pltpu.VMEM((2, rows, width), BF), pltpu.VMEM((local // batch, batch * capacity, rows), BF),
        pltpu.VMEM((EXPERTS, rows), F32), pltpu.VMEM((EXPERTS, rows), F32),
    ]
    tail = [pltpu.SemaphoreType.DMA((2,))]
    more = {}
    if sums is not None:
        dense, heads, small, first, out, old, tokens, stat, scale, gain = sums
        ways = expert_count * dp_count
        columns = first.shape[2]
        chunk = [values.shape[0] // ways for values in (dense, heads, small)]
        operands += [dense, heads, small, first, out, old, tokens, stat, scale, gain]
        in_specs += [anywhere] * 8 + [whole] * 2
        out_shape += [
            shape((chunk[0] + 2 * chunk[1] + chunk[2], dense.shape[1]), BF), shape((rows, columns), BF), shape((rows, columns), BF),
            shape((8, width), F32),
        ]
        out_specs += [whole] * 4
        out_shape = [shape(x.shape, BF)] + out_shape
        out_specs = [anywhere] + out_specs
        aliases = {0: 0}
        scratch += [pltpu.VMEM(values.shape, BF) for values in (dense, heads, small, first, out)]
        scratch += [
            pltpu.VMEM((ways - 1, chunk[0], dense.shape[1]), BF), pltpu.VMEM((ways - 1, chunk[1], heads.shape[1]), BF),
            pltpu.VMEM((ways - 1, chunk[2], small.shape[1]), BF), pltpu.VMEM((first.shape[0] - 1, rows, columns), BF),
            pltpu.VMEM((max(sizes[1] // 2 - 1, 1), rows, columns), BF),
            pltpu.VMEM((2, 8, rows), F32), pltpu.VMEM((sizes[1] - 1, 8, rows), F32),
            pltpu.VMEM((3, 8, width), F32), pltpu.VMEM((sizes[1] - 1, 8, width), F32), pltpu.VMEM((ways - 1, 8, width), F32),
            pltpu.VMEM((rows, columns), BF), pltpu.VMEM((rows, columns), BF),
        ]
        tail += [pltpu.SemaphoreType.DMA((96,)), pltpu.SemaphoreType.DMA((96,)), pltpu.SemaphoreType.DMA((9,))]
        more = dict(collective_id=4, has_side_effects=True)
    return pl.pallas_call(
        functools.partial(slots_kernel, sizes, masks, capacity, local, batch, sums is not None),
        out_shape=tuple(out_shape),
        grid=(2 * units,),
        in_specs=in_specs,
        out_specs=tuple(out_specs),
        input_output_aliases=aliases,
        scratch_shapes=scratch + tail,
        compiler_params=params(60, dimension_semantics=("arbitrary",), **more),
        cost_estimate=pl.CostEstimate(flops=MIB, bytes_accessed=MIB, transcendentals=0),
        name="slots",
    )(*operands)


def weights_kernel(counts, chunks, capacity, has_partial, wg_ref, wu_ref, wd_ref, *rest):
    parts = len(counts)
    xs_refs, ys_refs, rest = rest[:parts], rest[parts : 2 * parts], rest[2 * parts :]
    if has_partial:
        in_g, in_u, in_d, gg_ref, gu_ref, gd_ref, x_buf, y_buf, sem = rest
    else:
        gg_ref, gu_ref, gd_ref, x_buf, y_buf, sem = rest
    expert, chunk = pl.program_id(0), pl.program_id(1)
    step = expert * chunks + chunk
    total = pl.num_programs(0) * chunks

    def loads(s):
        e, c, slot = lax.div(s, chunks), lax.rem(s, chunks), lax.rem(s, 2)
        copies, start = [], 0
        for index, count in enumerate(counts):
            take = count // chunks
            for which, (refs, buf) in enumerate(((xs_refs, x_buf), (ys_refs, y_buf))):
                copies.append(pltpu.make_async_copy(
                    refs[index].at[pl.ds(2 * e, 2), pl.ds(c * take, take)], buf.at[slot, :, pl.ds(start, take)],
                    sem.at[slot, index, which],
                ))
            start += take
        return copies

    @pl.when(step == 0)
    def _():
        for copy in loads(step):
            copy.start()

    @pl.when(step + 1 < total)
    def _():
        for copy in loads(step + 1):
            copy.start()

    for copy in loads(step):
        copy.wait()
    slot = lax.rem(step, 2)
    width, hidden = wg_ref.shape[1:]
    x_here = [x_buf[slot, j].reshape(-1, width) for j in range(2)]
    y_here = [y_buf[slot, j].reshape(-1, width) for j in range(2)]
    both = [dot(x_here[j], jnp.concatenate([wg_ref[j], wu_ref[j]], axis=1)) for j in range(2)]
    grad_act = [dot(y_here[j], wd_ref[j], 1, 1) for j in range(2)]
    mids = [middle(both[j], grad_act[j], hidden) for j in range(2)]

    def put(j, ref, values, partial):
        if chunks == 1:
            ref[j] = values + partial[j] if has_partial else values
            return

        @pl.when(chunk == 0)
        def _():
            ref[j] = values + partial[j] if has_partial else values

        @pl.when(chunk != 0)
        def _():
            ref[j] += values

    for j in range(2):
        act, grads = mids[j]
        inner = dot(x_here[j], grads, 0, 0)
        put(j, gg_ref, inner[:, :hidden], in_g if has_partial else None)
        put(j, gu_ref, inner[:, hidden:], in_u if has_partial else None)
        put(j, gd_ref, dot(act.astype(BF), y_here[j], 0, 0), in_d if has_partial else None)


def weights_call(slots, wg, wu, wd, partial=None):
    local, width, hidden = wg.shape
    capacity = slots[0][0].shape[2]
    counts = [xs.shape[1] for xs, _ in slots]
    chunks = max(1, sum(counts) // 8)
    assert len(counts) == 1 or chunks == 1
    shape = jax.ShapeDtypeStruct
    in_block = pl.BlockSpec((2, width, hidden), lambda e, c: (e, 0, 0))
    down_block = pl.BlockSpec((2, hidden, width), lambda e, c: (e, 0, 0))
    specs = (in_block, in_block, down_block)
    more = list(partial) if partial is not None else []
    buffer = pltpu.VMEM((2, 2, sum(counts) // chunks, capacity, width), BF)
    return pl.pallas_call(
        functools.partial(weights_kernel, counts, chunks, capacity, partial is not None),
        out_shape=(shape(wg.shape, F32), shape(wu.shape, F32), shape(wd.shape, F32)),
        grid=(local // 2, chunks),
        in_specs=list(specs) + [pl.BlockSpec(memory_space=pl.ANY)] * (2 * len(slots)) + (list(specs) if more else []),
        out_specs=specs,
        scratch_shapes=[buffer, buffer, pltpu.SemaphoreType.DMA((2, len(counts), 2))],
        compiler_params=params(60, dimension_semantics=("arbitrary", "arbitrary")),
        cost_estimate=pl.CostEstimate(flops=80 * 10**9, bytes_accessed=100 * MIB, transcendentals=0),
        name="weights",
    )(wg, wu, wd, *[xs for xs, _ in slots], *[ys for _, ys in slots], *more)


def unpack_kernel(
    sums_ref, gain1_rows_ref, block_in, input_in,
    q_ref, k_ref, v_ref, heads_ref, router_ref, gain_ref, gain1_ref, block_ref, input_ref,
):
    ways = sums_ref.shape[0]
    d_rows, h_rows, s_rows = q_ref.shape[0] // ways, heads_ref.shape[0] // ways, SMALL_ROWS // ways
    q_width, k_width, half = q_ref.shape[1], k_ref.shape[1], heads_ref.shape[1] // 2
    small = []
    for i in range(ways):
        block = sums_ref[i].astype(F32)
        cut = slice(i * d_rows, (i + 1) * d_rows)
        q_ref[cut, :] = block[:d_rows, :q_width]
        k_ref[cut, :] = block[:d_rows, q_width : q_width + k_width]
        v_ref[cut, :] = block[:d_rows, q_width + k_width :]
        cut = slice(i * h_rows, (i + 1) * h_rows)
        heads_ref[cut, :half] = block[d_rows : d_rows + h_rows]
        heads_ref[cut, half:] = block[d_rows + h_rows : d_rows + 2 * h_rows]
        small.append(block[d_rows + 2 * h_rows :])
    small = jnp.concatenate(small, axis=0)
    router_ref[:, :half] = small[:EXPERTS]
    router_ref[:, half:] = small[EXPERTS : 2 * EXPERTS]
    gain_ref[0:half] = small[2 * EXPERTS]
    gain_ref[half:] = small[2 * EXPERTS + 1]
    gain1_ref[...] = gain1_rows_ref[0]
    block_ref[...] = block_in[...]
    input_ref[...] = input_in[...]


def unpack_call(sums, gain1_rows, block, grad, q_width, k_width, heads_shape):
    ways = sums.shape[0]
    width = heads_shape[1]
    shape = jax.ShapeDtypeStruct
    return pl.pallas_call(
        unpack_kernel,
        out_shape=(
            shape((width, q_width), F32), shape((width, k_width), F32), shape((width, k_width), F32), shape(heads_shape, F32),
            shape((EXPERTS, width), F32), shape((width,), F32), shape((width,), F32), shape(block.shape, BF), shape(grad.shape, BF),
        ),
        in_specs=vmem(4),
        out_specs=tuple(vmem(9)),
        compiler_params=params(60),
        cost_estimate=pl.CostEstimate(flops=MIB, bytes_accessed=5 * MIB, transcendentals=0),
        name="unpack",
    )(sums, gain1_rows, block, grad)


def on_device(
    tokens, cotangent, seq_lengths, deal_order, routes, slot_order, first_gain, w_query, w_key, w_value, w_out,
    second_gain, w_router, w_gate, w_up, w_down,
):
    dp_count = lax.axis_size("dp")
    dp_index = lax.axis_index("dp")
    tensor_count = lax.axis_size("tensor")
    tensor_index = lax.axis_index("tensor")
    expert_count = lax.axis_size("expert")
    expert_index = lax.axis_index("expert")
    rows, width = tokens.shape
    share = rows // tensor_count
    everywhere = ("expert", "dp", "tensor")
    unit_shape = (expert_count, dp_count, rows, width)

    cosine, sine = (jnp.asarray(values) for values in rotary_tables(rows))
    gain1, gain2 = first_gain, second_gain
    router_t = w_router.T
    normed, q, k, v, heads, logsum, hidden, normed_share, tables, far_dy, x_own, dy_own = front(
        seq_lengths, deal_order, tokens, gain1, w_query, w_key, w_value, w_out, cosine, sine, gain2, routes.T, slot_order, cotangent
    )
    never = seq_lengths[0, 0] < 0
    rows_all = ("expert", "dp")

    def after(values, other):
        return jnp.where(never, other.astype(values.dtype), values)

    small_mesh = expert_count == 2
    out_c, out_g, xs_own, ys_own, x_other, dy_other, gates = own_call(
        x_own, dy_own, tables, router_t, w_gate, w_up, w_down, hidden, normed_share, far_dy
    )
    group_count = expert_count
    if not small_mesh:
        out_c = lax.psum_scatter(out_c, "expert", scatter_dimension=0, tiled=True)
        out_g = lax.psum_scatter(out_g, "expert", scatter_dimension=0, tiled=True)
        x_own = lax.dynamic_slice_in_dim(x_own, expert_index, 1, 0)
        group_count = 1
    first, stat, hidden_grad, scale, dense, heads_grad, small, *out_passed = back_call(
        group_count, seq_lengths,
        (cotangent, tokens, gain1, gain2, router_t, hidden, tables, normed, q, k, v, heads, logsum,
         w_query, w_key, w_value, w_out, cosine, sine),
        out_g, x_own, *((out_c,) if small_mesh else ()),
    )
    local = w_gate.shape[0]
    q_width, k_width = w_query.shape[1], w_key.shape[1]
    half, columns = width // 2, width // tensor_count
    if small_mesh:
        _, xs, ys, sums, input_grad, block_out, gain1_rows = slots_call(
            tuple(range(1, dp_count)), x_other, dy_other, tables, gates, local,
            (dense, heads_grad, small, first, out_passed[0], hidden_grad, tokens, stat, scale, gain1),
        )
        ways = expert_count * dp_count
        sums = lax.all_gather(sums, rows_all, axis=0)
        gate_grad, up_grad, down_grad = weights_call([(xs_own, ys_own), (xs, ys)], w_gate, w_up, w_down)
        q_sum, k_sum, v_sum, out_sum, router_rows, gain2_sum, gain1_sum, block_out, input_grad = unpack_call(
            sums, gain1_rows, block_out, input_grad, q_width, k_width, w_out.shape
        )
        router_sum = router_rows.T
    else:
        grads = weights_call([(xs_own, ys_own)], w_gate, w_up, w_down)
        for mask in range(1, dp_count):
            moved = (
                lax.all_gather(
                    after(values[mask - 1], grads[2][0, 0, 0]), ("expert", "tensor"), axis=0, tiled=True
                ).reshape(1, expert_count, rows, width)
                for values in (
                    [lax.ppermute(normed_share, "dp", [(i, i ^ m) for i in range(dp_count)]) for m in range(1, dp_count)],
                    far_dy,
                )
            )
            far_gates = lax.ppermute(gates, "dp", [(i, i ^ mask) for i in range(dp_count)])[None]
            xs, ys = slots_call((mask,), *moved, tables, far_gates, local)
            grads = weights_call([(xs, ys)], w_gate, w_up, w_down, grads)
        gate_grad, up_grad, down_grad = grads
        dense_sum, out_sum, small_sum = (
            values.astype(F32) for values in lax.psum((dense, heads_grad, small), rows_all)
        )
        gain1_sum = lax.psum(stat[0, rows:], everywhere)
        q_sum, k_sum, v_sum = jnp.split(dense_sum, [q_width, q_width + k_width], axis=1)
        router_sum = jnp.concatenate([small_sum[:EXPERTS], small_sum[EXPERTS : 2 * EXPERTS]], axis=1)
        gain2_sum = small_sum[2 * EXPERTS : 2 * EXPERTS + 2].reshape(width)
        router_sum = router_sum.T
        block_out = lax.psum_scatter(out_c[0], "tensor", scatter_dimension=0, tiled=True)[0]
        first_sum = lax.psum_scatter(first, "tensor", scatter_dimension=0, tiled=True)[0].astype(F32)
        mean = lax.psum(stat[0, :rows], "tensor")[:, None] / width

        def cols(values):
            return lax.dynamic_slice_in_dim(values, tensor_index * columns, columns, -1).astype(F32)

        input_grad = (
            hidden_grad.astype(F32) + scale[:, :1] * (first_sum * cols(gain1) - cols(tokens) * scale[:, :1] * mean)
        ).astype(BF)
    return (
        block_out, input_grad, gain1_sum, q_sum, k_sum, v_sum, out_sum, gain2_sum, router_sum,
        gate_grad, up_grad, down_grad,
    )


def solution(mesh):
    rows2 = P(("expert", "dp"), None)
    placed = (
        rows2, rows2, P("expert", None), P("expert", None), rows2, rows2, P(),
        P(None, "tensor"), P(None, "tensor"), P(None, "tensor"), P("tensor", None), P(), P(),
        P("expert", None, "tensor"), P("expert", None, "tensor"), P("expert", "tensor", None),
    )
    return jax.shard_map(
        on_device,
        mesh=mesh,
        in_specs=placed,
        out_specs=(
            P(("expert", "dp"), "tensor"), P(("expert", "dp"), "tensor"), P(),
            P(None, "tensor"), P(None, "tensor"), P(None, "tensor"), P("tensor", None), P(), P(),
            P("expert", None, "tensor"), P("expert", None, "tensor"), P("expert", "tensor", None),
        ),
        check_vma=False,
    )
```

```python
import functools

import jax
import jax.numpy as jnp
import numpy as np
from jax import lax
from jax.experimental import pallas as pl
from jax.experimental.pallas import tpu as pltpu
from jax.sharding import PartitionSpec as P

HEADS = 16
KV_HEADS = 8
HEAD_DIM = 64
EXPERTS = 32
TOP = 8
SLOT = 512

EPS = 1e-06
THETA = 10000.0
NEG = -1e30
BF = jnp.bfloat16
F32 = jnp.float32
MIB = 1 << 20


def dot(a, b, ca=1, cb=0):
    return lax.dot_general(a, b, (((ca,), (cb,)), ((), ())), preferred_element_type=F32)


def vmem(count=1):
    return [pl.BlockSpec(memory_space=pltpu.VMEM)] * count


def params(mib, **more):
    return pltpu.CompilerParams(vmem_limit_bytes=mib * MIB, **more)


def rotary_tables(rows):
    places = np.arange(rows, dtype=np.float32)[:, None]
    halfway = HEAD_DIM // 2
    spread = np.float32(THETA) ** (-2.0 * np.arange(halfway, dtype=np.float32) / HEAD_DIM)
    angles = (places * spread.astype(np.float32)[None, :]).astype(np.float32)
    copies = 128 // halfway
    return (
        np.tile(np.cos(angles), (1, copies)).astype(np.float32),
        np.tile(np.sin(angles), (1, copies)).astype(np.float32),
    )


def rotate128(values, cosine, sine, low_half):
    half = HEAD_DIM // 2
    up = pltpu.roll(values, 128 - half, 1)
    down = pltpu.roll(values, half, 1)
    return values * cosine + jnp.where(low_half, -up, down) * sine


def lanes(shape):
    return lax.broadcasted_iota(jnp.int32, shape, len(shape) - 1)


def sublanes(shape):
    return lax.broadcasted_iota(jnp.int32, shape, len(shape) - 2)


def bits_of(count):
    return [1 << i for i in range(count.bit_length() - 1)]


def flip(value, mask):
    for bit in bits_of(1 << 16):
        if mask & bit:
            value = value + bit - 2 * bit * lax.rem(lax.div(value, bit), 2)
    return value


class Net:
    def __init__(self, send_sem, recv_sem):
        self.send_sem, self.recv_sem, self.used, self.copies = send_sem, recv_sem, 0, []
        self.me = {axis: lax.axis_index(axis) for axis in ("expert", "tensor", "dp")}

    def barrier(self, partners):
        sem = pltpu.get_barrier_semaphore()
        for partner in partners:
            pl.semaphore_signal(sem, inc=1, device_id=self.device(partner), device_id_type=pl.DeviceIdType.MESH)
        pl.semaphore_wait(sem, len(partners))

    def device(self, partner):
        pairs = [partner] if isinstance(partner[0], str) else partner
        return {axis: flip(self.me[axis], mask) for axis, mask in pairs}

    def send(self, source, target, *partner):
        k = self.used
        self.used += 1
        copy = Copy(self, k, source, target, partner)
        copy.build().start()
        self.copies.append(copy)
        return copy

    def close(self):
        for copy in self.copies:
            copy.build().wait_send()


class Copy:
    def __init__(self, net, index, source, target, partner):
        self.net, self.index, self.source, self.target, self.partner = net, index, source, target, partner

    def build(self):
        source = self.source() if callable(self.source) else self.source
        target = self.target() if callable(self.target) else self.target
        return pltpu.make_async_remote_copy(
            src_ref=source, dst_ref=target,
            send_sem=self.net.send_sem.at[self.index], recv_sem=self.net.recv_sem.at[self.index],
            device_id=self.net.device(self.partner), device_id_type=pl.DeviceIdType.MESH,
        )

    def wait_recv(self):
        self.build().wait_recv()


class Gather:
    def __init__(self, net, at, steps, known=((0, 0),), first=None):
        self.net, self.at, self.steps, self.known, self.first, self.flight = net, at, list(steps), list(known), first, []

    def start(self):
        axis, mask = self.steps.pop(0)
        fresh = []
        for re, rt in self.known:
            place = functools.partial(self.at, re, rt)
            source = self.first if self.first is not None and (re, rt) == (0, 0) else place
            self.flight.append(self.net.send(source, place, axis, mask))
            fresh.append((re ^ mask, rt) if axis == "expert" else (re, rt ^ mask))
        self.known += fresh

    def finish(self):
        for copy in self.flight:
            copy.wait_recv()
        self.flight = []


class Reduce:
    def __init__(self, net, at, landing, steps, chunks):
        self.net, self.at, self.landing, self.steps, self.live = net, at, landing, list(steps), list(chunks)
        self.used, self.flight = 0, []

    def start(self):
        axis, mask = self.steps.pop(0)
        side = 0 if axis == "expert" else 1
        going = [r for r in self.live if (r[side] & mask if mask else r[side])]
        self.live = [r for r in self.live if r not in going]
        for r in going:
            toward = mask or r[side]
            kept = (r[0] ^ toward, r[1]) if side == 0 else (r[0], r[1] ^ toward)
            copy = self.net.send(functools.partial(self.at, *r), functools.partial(self.landing, self.used), axis, toward)
            self.flight.append((kept, copy, self.used))
            self.used += 1

    def finish(self):
        for place in sorted({kept for kept, _, _ in self.flight}):
            total = self.at(*place)[...].astype(F32)
            for kept, copy, slot in self.flight:
                if kept == place:
                    copy.wait_recv()
                    total = total + self.landing(slot)[...].astype(F32)
            self.at(*place)[...] = total.astype(BF)
        self.flight = []


class Exchange:
    def __init__(self, net, stages, k, landing, partners):
        self.net, self.stages, self.k, self.landing, self.partners, self.flight = net, stages, k, landing, partners, []

    def start(self):
        for index, partner in enumerate(self.partners):
            self.flight.append(self.net.send(
                lambda: self.stages.at[self.k], lambda index=index: self.landing.at[index], *partner
            ))

    def finish(self):
        total = self.stages[self.k]
        for index, copy in enumerate(self.flight):
            copy.wait_recv()
            total = total + self.landing[index]
        self.stages[self.k + 1] = total


TABLE_ROWS = 48
SMALL_ROWS = 128


def table_of(length, routes_ref, order_ref):
    rows = routes_ref.shape[1]
    capacity = rows * TOP // EXPERTS
    entries = rows * TOP
    chunk = 512
    routes_t = routes_ref[...].astype(F32).astype(BF)
    upper = (sublanes((chunk, chunk)) < lanes((chunk, chunk))).astype(F32).astype(BF)
    expert_row = sublanes((EXPERTS, chunk))

    def body(step, carried):
        counts, table = carried
        entry = order_ref[:, pl.ds(pl.multiple_of(step * chunk, chunk), chunk)]
        row, choice = entry // TOP, entry % TOP
        onehot_row = (sublanes((rows, chunk)) == row).astype(F32).astype(BF)
        picked = dot(routes_t, onehot_row)
        expert = jnp.sum(jnp.where(sublanes((TOP, chunk)) == choice, picked, 0.0), axis=0, keepdims=True)
        member = (expert_row.astype(F32) == expert) & (row < length)
        member_f = member.astype(F32)
        before = dot(member_f.astype(BF), upper) + counts
        value = jnp.where(member, jnp.minimum(before, float(capacity)) + 1.0, 0.0)
        table = table + dot(value.astype(BF), onehot_row, 1, 1)
        return counts + jnp.sum(member_f, axis=1, keepdims=True), table

    _, table = lax.fori_loop(
        0, entries // chunk, body, (jnp.zeros((EXPERTS, 1), F32), jnp.zeros((EXPERTS, rows), F32))
    )
    return table


def given_table(tables, index, dp_here):
    total = 0.0
    for j in range(tables.shape[1]):
        source = tables[index, j, EXPERTS : EXPERTS + 16, :].astype(F32)[0:1]
        total = total + jnp.where(source == dp_here, tables[index, j, 0:EXPERTS, :].astype(F32), 0.0)
    return total


def head_parts(q, k_a, k_b, index, low_lane):
    block = q[:, (index // 2) * 128 : (index // 2) * 128 + 128]
    mine = low_lane if index % 2 == 0 else jnp.logical_not(low_lane)
    return jnp.where(mine, block, jnp.zeros((), block.dtype)), (k_a if index % 2 == (index // 2) % 2 else k_b)


def swap(block):
    return pltpu.roll(block.astype(F32), HEAD_DIM, 1).astype(BF)


def front_kernel(
    sizes,
    lengths_ref, order_of_ref, x_ref, gain_ref, wq_ref, wk_ref, wv_ref, wo_ref, cos_ref, sin_ref, gain2_ref, routes_ref, order_ref, dy_ref,
    normed_out, q_out, k_out, v_out, heads_out, logsum_out, hidden_out, share_out, tables_ref, far_dy_ref, xown_ref, dyown_ref,
    part, landing, send_sem, recv_sem, local_sem,
    normed_ref, q_ref, k_ref, v_ref, heads_ref, logsum_ref, hidden_ref, share_ref,
    wq_late, wk_late, wv_late, wo_late, cos_late, sin_late, late_sem, early_sem,
):
    late = [pltpu.make_async_copy(a, b, late_sem.at[i]) for i, (a, b) in enumerate((
        (wq_ref, wq_late), (wk_ref, wk_late), (wv_ref, wv_late), (wo_ref, wo_late), (cos_ref, cos_late), (sin_ref, sin_late),
    ))]
    for copy in late:
        copy.start()
    early = [pltpu.make_async_copy(a, b, early_sem.at[i]) for i, (a, b) in enumerate((
        (normed_ref, normed_out), (q_ref, q_out), (k_ref, k_out), (v_ref, v_out), (heads_ref, heads_out),
        (logsum_ref, logsum_out), (hidden_ref, hidden_out), (share_ref, share_out),
    ))]
    wq_ref, wk_ref, wv_ref, wo_ref, cos_ref, sin_ref = wq_late, wk_late, wv_late, wo_late, cos_late, sin_late
    expert_count, tensor_count, dp_count = sizes
    rows, width = x_ref.shape
    share = rows // tensor_count
    half = rows // 2
    net = Net(send_sem, recv_sem)
    me_e, me_t, me_d = net.me["expert"], net.me["tensor"], net.me["dp"]
    expert_bits = [("expert", b) for b in bits_of(expert_count)]
    tensor_bits = [("tensor", b) for b in bits_of(tensor_count)]
    net.barrier(expert_bits + tensor_bits + [("dp", m) for m in range(1, dp_count)])

    keep_dy = pltpu.make_async_copy(dy_ref, dyown_ref.at[me_e], local_sem.at[0])
    keep_dy.start()
    half_start = pl.multiple_of(lax.rem(me_t, 2) * half, half)
    dy_half = Gather(
        net, lambda re, rt: dyown_ref.at[flip(me_e, re), pl.ds(half_start, half)], expert_bits,
        first=dy_ref.at[pl.ds(half_start, half)],
    )
    dy_half.start()
    length, source, dealt_length = lengths_ref[0, me_d], order_of_ref[0, me_d], 0
    for i in range(dp_count):
        dealt_length = jnp.where(source == i, lengths_ref[0, i], dealt_length)
    x = x_ref[...].astype(F32)
    scale = lax.rsqrt(jnp.mean(x * x, axis=-1, keepdims=True) + EPS)
    normed = (x * scale * gain_ref[...].astype(F32)[None, :]).astype(BF)
    normed_ref[...] = normed
    for copy in late:
        copy.wait()
    cosine, sine = cos_ref[...], sin_ref[...]
    lane = lanes((rows, 128))
    low_half = lane % HEAD_DIM < HEAD_DIM // 2
    low_lane = lane < HEAD_DIM
    q_pre = dot(normed, wq_ref[...])
    for block in range(q_pre.shape[1] // 128):
        cut = slice(block * 128, block * 128 + 128)
        q_ref[:, cut] = rotate128(q_pre[:, cut], cosine, sine, low_half).astype(BF)
    k = rotate128(dot(normed, wk_ref[...]), cosine, sine, low_half).astype(BF)
    v = dot(normed, wv_ref[...]).astype(BF)
    k_ref[...] = k
    v_ref[...] = v
    q = q_ref[...]
    k_b, v_b = swap(k), swap(v)
    row, col = sublanes((rows, rows)), lanes((rows, rows))
    allowed = (col <= row) & (col < length)
    logsum = jnp.zeros((rows, 128), F32)
    pair = None
    for index in range(q.shape[1] // HEAD_DIM):
        q_one, k_one = head_parts(q, k, k_b, index, low_lane)
        v_one = v if index % 2 == (index // 2) % 2 else v_b
        scores = jnp.where(allowed, dot(q_one, k_one, 1, 1) * (HEAD_DIM**-0.5), NEG)
        highest = jnp.max(scores, axis=-1, keepdims=True)
        weights = jnp.exp(scores - highest)
        total = jnp.sum(weights, axis=-1, keepdims=True)
        mixed = dot((weights / total).astype(BF), v_one)
        logsum = jnp.where(lane == index, highest + jnp.log(total), logsum)
        if index % 2 == 0:
            pair = mixed
        else:
            cut = slice((index // 2) * 128, (index // 2) * 128 + 128)
            heads_ref[:, cut] = jnp.where(low_lane, pair, mixed).astype(BF)
    logsum_ref[...] = logsum
    live = (sublanes((rows, 1)) < length).astype(F32)
    part[...] = (dot(heads_ref[...], wo_ref[...]) * live).astype(BF).reshape(part.shape)

    for copy in early[:6]:
        copy.start()
    attn = Reduce(
        net, lambda re, rt: part.at[flip(me_t, rt)], lambda i: landing.at[i], tensor_bits,
        [(0, r) for r in range(tensor_count)],
    )
    attn.start()
    table = table_of(dealt_length, routes_ref, order_ref)
    source = jnp.broadcast_to(source.astype(F32), (TABLE_ROWS - EXPERTS, rows))
    tables_ref[me_e, me_d] = jnp.concatenate([table, source], axis=0).astype(BF)
    mine = tables_ref.at[me_e, me_d]
    table_copies = [net.send(mine, mine, "dp", m) for m in range(1, dp_count)]
    mine_rows = pl.multiple_of(me_t * share, share)
    far_copies = [
        net.send(dy_ref.at[pl.ds(mine_rows, share)], far_dy_ref.at[m - 1], "dp", m) for m in range(1, dp_count)
    ]
    attn.finish()
    while attn.steps:
        attn.start()
        if not attn.steps:
            dy_half.finish()
            while dy_half.steps:
                dy_half.start()
                dy_half.finish()
            for re, _ in dy_half.known[1:]:
                place = dy_half.at(re, 0)
                dy_half.flight.append(net.send(place, place, "tensor", 1))
        attn.finish()

    start = pl.multiple_of(me_t * share, share)
    hidden = x_ref[pl.ds(start, share), :].astype(F32) + part[me_t].astype(F32)
    hidden_ref[...] = hidden
    scale2 = lax.rsqrt(jnp.mean(hidden * hidden, axis=-1, keepdims=True) + EPS)
    share_ref[...] = (hidden * scale2 * gain2_ref[...].astype(F32)[None, :]).astype(BF)
    keep_x = pltpu.make_async_copy(share_ref, xown_ref.at[me_e, pl.ds(start, share)], local_sem.at[1])
    keep_x.start()
    for copy in early[6:]:
        copy.start()
    high_bits = tensor_bits[1:][::-1]
    gathers = []
    for part_index, steps in enumerate((high_bits + expert_bits, expert_bits + high_bits)):
        size = share // 2

        def at(re, rt, offset=part_index * size):
            begin = pl.multiple_of(flip(me_t, rt) * share + offset, size)
            return xown_ref.at[flip(me_e, re), pl.ds(begin, size)]

        gathers.append(
            Gather(net, at, steps + tensor_bits[:1], first=share_ref.at[pl.ds(part_index * size, size)])
        )
    table_all = Gather(net, lambda re, rt: tables_ref.at[flip(me_e, re)], expert_bits)
    first_step = True
    while gathers[0].steps:
        for gather in gathers:
            gather.start()
        if first_step:
            for copy in table_copies:
                copy.wait_recv()
            first_step = False
        else:
            table_all.finish()
        if table_all.steps:
            table_all.start()
        for gather in gathers:
            gather.finish()
    table_all.finish()
    dy_half.finish()
    for copy in far_copies:
        copy.wait_recv()
    net.close()
    keep_dy.wait()
    keep_x.wait()
    for copy in early:
        copy.wait()


def front(lengths, order_of, x, gain, wq, wk, wv, wo, cosine, sine, gain2, routes, order, dy):
    rows, width = x.shape
    sizes = tuple(lax.axis_size(axis) for axis in ("expert", "tensor", "dp"))
    expert_count, tensor_count, dp_count = sizes
    share = rows // tensor_count
    shape = jax.ShapeDtypeStruct
    copies = 96
    anywhere = pl.BlockSpec(memory_space=pl.ANY)
    return pl.pallas_call(
        functools.partial(front_kernel, sizes),
        out_shape=(
            shape((rows, width), BF), shape((rows, wq.shape[1]), BF), shape((rows, wk.shape[1]), BF),
            shape((rows, wv.shape[1]), BF), shape((rows, wq.shape[1]), BF), shape((rows, 128), F32),
            shape((share, width), F32), shape((share, width), BF), shape((expert_count, dp_count, TABLE_ROWS, rows), BF),
            shape((dp_count - 1, share, width), BF), shape((expert_count, rows, width), BF), shape((expert_count, rows, width), BF),
        ),
        in_specs=[pl.BlockSpec(memory_space=pltpu.SMEM)] * 2 + vmem(2) + [anywhere] * 6 + vmem(3) + [anywhere],
        out_specs=(anywhere,) * 8 + (vmem()[0],) + (anywhere,) * 3,
        scratch_shapes=[
            pltpu.VMEM((tensor_count, share, width), BF),
            pltpu.VMEM((tensor_count - 1, share, width), BF),
            pltpu.SemaphoreType.DMA((copies,)),
            pltpu.SemaphoreType.DMA((copies,)),
            pltpu.SemaphoreType.DMA((2,)),
            pltpu.VMEM((rows, width), BF), pltpu.VMEM((rows, wq.shape[1]), BF), pltpu.VMEM((rows, wk.shape[1]), BF),
            pltpu.VMEM((rows, wv.shape[1]), BF), pltpu.VMEM((rows, wq.shape[1]), BF), pltpu.VMEM((rows, 128), F32),
            pltpu.VMEM((share, width), F32), pltpu.VMEM((share, width), BF),
            *[pltpu.VMEM(values.shape, values.dtype) for values in (wq, wk, wv, wo, cosine, sine)],
            pltpu.SemaphoreType.DMA((6,)),
            pltpu.SemaphoreType.DMA((8,)),
        ],
        compiler_params=params(56, collective_id=1, has_side_effects=True),
        cost_estimate=pl.CostEstimate(flops=MIB, bytes_accessed=MIB, transcendentals=0),
        name="front",
    )(lengths, order_of, x, gain, wq, wk, wv, wo, cosine, sine, gain2, routes, order, dy)


def back_kernel(
    sizes, passes,
    lengths_ref, dy_ref, x_ref, gain_ref, gain2_ref, router_ref, hidden_ref, tables_ref,
    normed_ref, q_ref, k_ref, v_ref, heads_ref, logsum_ref, wq_ref, wk_ref, wv_ref, wo_ref, cos_ref, sin_ref,
    grad_in_ref, xown_ref, *rest,
):
    late_count = 13
    late_sem, rest = rest[-1], rest[:-1]
    late_refs, rest = rest[-late_count:], rest[:-late_count]
    late_hbm = (
        x_ref, normed_ref, q_ref, k_ref, v_ref, heads_ref, logsum_ref, wq_ref, wk_ref, wv_ref, wo_ref, cos_ref, sin_ref,
    )
    if passes:
        out_in_ref, rest = rest[0], rest[1:]
        out_pass_ref, rest = rest[7], rest[:7] + rest[8:]
        (out, out_landing), rest = rest[-2:], rest[:-2]
    (
        first_ref, tiny_ref, hidden_grad_ref, scale_ref, dense_ref, out_grad_ref, small_ref,
        grad, grad_landing, normed2, spread, back_ref, picked, send_sem, recv_sem, local_sem,
    ) = rest
    group_count, tensor_count, dp_count = sizes
    rows, width = x_ref.shape
    share = rows // tensor_count
    net = Net(send_sem, recv_sem)
    me_e, me_t, me_d = net.me["expert"], net.me["tensor"], net.me["dp"]
    here = me_e if group_count > 1 else 0
    expert_bits = [("expert", b) for b in bits_of(group_count)]
    tensor_bits = [("tensor", b) for b in bits_of(tensor_count)]
    load_grad = pltpu.make_async_copy(grad_in_ref, grad, local_sem.at[0])
    load_x = pltpu.make_async_copy(xown_ref.at[here], normed2, local_sem.at[1])
    load_grad.start()
    load_x.start()
    late = [pltpu.make_async_copy(a, b, late_sem.at[i]) for i, (a, b) in enumerate(zip(late_hbm, late_refs))]
    if passes:
        load_out = pltpu.make_async_copy(out_in_ref, out, local_sem.at[2])
        load_out.start()
    net.barrier(expert_bits + tensor_bits)
    load_grad.wait()
    for copy in late:
        copy.start()
    high_bits = tensor_bits[1:]
    chunks = [(e, t) for e in range(group_count) for t in range(tensor_count)]
    sums = []
    size = share // 2
    for part_index, steps in enumerate((high_bits + expert_bits, expert_bits + high_bits)):

        def at(re, rt, offset=part_index * size):
            begin = pl.multiple_of(flip(me_t, rt) * share + offset, size)
            return grad.at[flip(here, re) if re else here, pl.ds(begin, size)]

        sums.append(Reduce(
            net, at, lambda i, p=part_index: grad_landing.at[p, i], tensor_bits[:1] + steps, chunks
        ))
    if passes:
        out_sum = Reduce(
            net, lambda re, rt: out.at[flip(me_e, re), flip(me_t, rt)], lambda i: out_landing.at[i],
            tensor_bits[:1] + expert_bits, chunks,
        )
    while sums[0].steps:
        for one in sums:
            one.start()
        if passes and not out_sum.used:
            load_out.wait()
            out_sum.start()
        for one in sums:
            one.finish()
    if passes:
        out_sum.finish()
        out_sum.start()

    start = pl.multiple_of(me_t * share, share)
    gain2 = gain2_ref[...].astype(F32)[None, :]
    hidden = hidden_ref[...]
    scale2 = lax.rsqrt(jnp.mean(hidden * hidden, axis=-1, keepdims=True) + EPS)
    hat2 = hidden * scale2
    second_normed = (hat2 * gain2).astype(BF)
    picked[...] = given_table(tables_ref, me_e, me_d.astype(F32))
    table = picked[:, pl.ds(start, share)]
    table = jnp.concatenate([table, jnp.zeros((128 - EXPERTS, share), F32)], axis=0)
    table = jnp.transpose(table)[:, :EXPERTS]
    logits = dot(second_normed, router_ref[...], 1, 1)
    chosen = table > 0.5
    masked = jnp.where(chosen, logits, NEG)
    weights = jnp.where(chosen, jnp.exp(masked - jnp.max(masked, axis=-1, keepdims=True)), 0.0)
    total = jnp.sum(weights, axis=-1, keepdims=True)
    gates = weights / jnp.where(total > 0.0, total, 1.0)
    gate_in = grad[here, pl.ds(start, share), width:].astype(F32)[:, :EXPERTS]
    logit_grad = (gate_in - gates * jnp.sum(gate_in, axis=-1, keepdims=True)).astype(BF)
    normed_grad = grad[here, pl.ds(start, share), :width].astype(F32) + dot(logit_grad, router_ref[...])
    along2 = normed_grad * hat2
    gain2_part = jnp.sum(along2, axis=0, keepdims=True)
    scaled = normed_grad * gain2
    hidden_grad = dy_ref[pl.ds(start, share), :].astype(F32) + scale2 * (
        scaled - hat2 * jnp.mean(scaled * hat2, axis=-1, keepdims=True)
    )
    spread[me_t, 0:share, :width] = hidden_grad.astype(BF)
    spread[me_t, 0:share, width:] = jnp.concatenate(
        [logit_grad.astype(F32), jnp.zeros((share, 128 - EXPERTS), F32)], axis=1
    ).astype(BF)
    high = gain2_part.astype(BF).astype(F32)
    spread[me_t, share : share + 16, :width] = jnp.concatenate(
        [high, gain2_part - high, jnp.zeros((14, width), F32)], axis=0
    ).astype(BF)
    spread[me_t, share : share + 16, width:] = jnp.zeros((16, 128), BF)
    gather = Gather(net, lambda re, rt: spread.at[flip(me_t, rt)], high_bits[::-1] + tensor_bits[:1])
    while gather.steps:
        gather.start()
        gather.finish()

    for copy in late:
        copy.wait()
    (
        x_ref, normed_ref, q_ref, k_ref, v_ref, heads_ref, logsum_ref, wq_ref, wk_ref, wv_ref, wo_ref, cos_ref, sin_ref,
    ) = late_refs
    length = lengths_ref[0, me_d]
    inv = HEAD_DIM**-0.5
    live = (sublanes((rows, 1)) < length).astype(F32)
    hidden_grad_all = spread[:, 0:share, :width].reshape(rows, width)
    columns = width // tensor_count
    cut = pl.ds(pl.multiple_of(me_t * columns, columns), columns)
    hidden_grad_ref[...] = jnp.concatenate([spread[t, 0:share, cut] for t in range(tensor_count)], axis=0)
    branch = (hidden_grad_all.astype(F32) * live).astype(BF)
    out_grad_ref[...] = dot(heads_ref[...], branch, 0, 0).astype(BF)
    heads_grad = dot(branch, wo_ref[...], 1, 1).astype(BF)
    cosine, sine = cos_ref[...], -sin_ref[...]
    lane = lanes((rows, 128))
    low_half = lane % HEAD_DIM < HEAD_DIM // 2
    low_lane = lane < HEAD_DIM
    q, k, v = q_ref[...], k_ref[...], v_ref[...]
    k_b, v_b = swap(k), swap(v)
    key, query = sublanes((rows, rows)), lanes((rows, rows))
    allowed = (key <= query) & (key < length)
    logsum_rows = jnp.transpose(logsum_ref[...])
    dk = [jnp.zeros((rows, 128), F32), jnp.zeros((rows, 128), F32)]
    dv = [jnp.zeros((rows, 128), F32), jnp.zeros((rows, 128), F32)]
    q_width = q.shape[1]
    pair = None
    for index in range(q_width // HEAD_DIM):
        same = index % 2 == (index // 2) % 2
        q_one, k_one = head_parts(q, k, k_b, index, low_lane)
        g_one, v_one = head_parts(heads_grad, v, v_b, index, low_lane)
        scores = jnp.where(allowed, dot(k_one, q_one, 1, 1) * inv, NEG)
        prob = jnp.exp(scores - logsum_rows[index : index + 1, :])
        grad_prob = dot(v_one, g_one, 1, 1)
        center = jnp.sum(prob * grad_prob, axis=0, keepdims=True)
        score_grad = (prob * (grad_prob - center)).astype(BF)
        dq = dot(score_grad, k_one, 0, 0) * inv
        place = 0 if same else 1
        dk[place] = dk[place] + dot(score_grad, q_one) * inv
        dv[place] = dv[place] + dot(prob.astype(BF), g_one)
        if index % 2 == 0:
            pair = dq
        else:
            cut = slice((index // 2) * 128, (index // 2) * 128 + 128)
            both = jnp.where(low_lane, pair, dq)
            back_ref[:, cut] = rotate128(both, cosine, sine, low_half).astype(BF)
    k_width = k.shape[1]
    k_total = dk[0] + pltpu.roll(dk[1], HEAD_DIM, 1)
    v_total = dv[0] + pltpu.roll(dv[1], HEAD_DIM, 1)
    back_ref[:, q_width : q_width + k_width] = rotate128(k_total, cosine, sine, low_half).astype(BF)
    back_ref[:, q_width + k_width :] = v_total.astype(BF)
    back = back_ref[...]
    first = (
        dot(back[:, :q_width], wq_ref[...], 1, 1)
        + dot(back[:, q_width : q_width + k_width], wk_ref[...], 1, 1)
        + dot(back[:, q_width + k_width :], wv_ref[...], 1, 1)
    )
    columns = width // tensor_count
    for t in range(tensor_count):
        first_ref[t] = first[:, t * columns : (t + 1) * columns].astype(BF)
    x = x_ref[...].astype(F32)
    scale = lax.rsqrt(jnp.mean(x * x, axis=-1, keepdims=True) + EPS)
    scale_ref[...] = jnp.broadcast_to(scale, (rows, 128))
    along = first * (x * scale)
    stat = jnp.sum(along * gain_ref[...].astype(F32)[None, :], axis=-1, keepdims=True)
    tiny_ref[:, 0:rows] = jnp.transpose(jnp.broadcast_to(stat, (rows, 128)))[0:8, :]
    tiny_ref[:, rows:] = jnp.broadcast_to(jnp.sum(along, axis=0, keepdims=True), (8, width))
    dense_ref[...] = dot(normed_ref[...], back, 0, 0).astype(BF)
    load_x.wait()
    router_rows = dot(spread[:, 0:share, width:].reshape(rows, 128), normed2[...], 0, 0)[0:EXPERTS]
    gain2_sum = jnp.zeros((1, width), F32)
    for t in range(tensor_count):
        block = spread[t, share : share + 16, :width].astype(F32)
        gain2_sum = gain2_sum + block[0:1] + block[1:2]
    half = width // 2
    pieces = [router_rows[:, :half], router_rows[:, half:], gain2_sum[:, :half], gain2_sum[:, half:]]
    if passes:
        out_sum.finish()
        out_pass_ref[...] = out[me_e]
    filled = sum(piece.shape[0] for piece in pieces)
    small_ref[...] = jnp.concatenate(pieces + [jnp.zeros((SMALL_ROWS - filled, half), F32)], axis=0).astype(BF)
    net.close()


def back_call(group_count, lengths, vmem_operands, grad, xown, out=None):
    dy, x = vmem_operands[0], vmem_operands[1]
    rows, width = x.shape
    wq, wk, wv, wo = vmem_operands[13:17]
    tensor_count, dp_count = lax.axis_size("tensor"), lax.axis_size("dp")
    share, columns = rows // tensor_count, width // tensor_count
    chunks = group_count * tensor_count
    inner = wq.shape[1] + wk.shape[1] + wv.shape[1]
    shape = jax.ShapeDtypeStruct
    copies = 64
    passed = [] if out is None else [out]
    late = [1] + list(range(7, len(vmem_operands)))
    return pl.pallas_call(
        functools.partial(back_kernel, (group_count, tensor_count, dp_count), out is not None),
        out_shape=(
            shape((tensor_count, rows, columns), BF), shape((8, rows + width), F32), shape((rows, columns), BF),
            shape((rows, 128), F32), shape((width, inner), BF), shape(wo.shape, BF), shape((SMALL_ROWS, width // 2), BF),
            *[shape(one.shape[1:], BF) for one in passed],
        ),
        in_specs=[pl.BlockSpec(memory_space=pltpu.SMEM)] + [
            pl.BlockSpec(memory_space=pl.ANY if i in late else pltpu.VMEM) for i in range(len(vmem_operands))
        ] + [pl.BlockSpec(memory_space=pl.ANY)] * (2 + len(passed)),
        out_specs=tuple(vmem(7)) + tuple(vmem(len(passed))),
        scratch_shapes=[
            pltpu.VMEM(grad.shape, BF),
            pltpu.VMEM((2, chunks - 1, share // 2, width + 128), BF),
            pltpu.VMEM((rows, width), BF),
            pltpu.VMEM((tensor_count, share + 16, width + 128), BF),
            pltpu.VMEM((rows, inner), BF),
            pltpu.VMEM((EXPERTS, rows), F32),
            pltpu.SemaphoreType.DMA((copies,)),
            pltpu.SemaphoreType.DMA((copies,)),
            pltpu.SemaphoreType.DMA((3,)),
        ] + ([
            pltpu.VMEM(out.shape, BF),
            pltpu.VMEM((chunks, rows, columns), BF),
        ] if passed else []) + [pltpu.VMEM(vmem_operands[i].shape, vmem_operands[i].dtype) for i in late] + [
            pltpu.SemaphoreType.DMA((len(late),))
        ],
        compiler_params=params(60, collective_id=2, has_side_effects=True),
        cost_estimate=pl.CostEstimate(flops=MIB, bytes_accessed=MIB, transcendentals=0),
        name="back",
    )(lengths, *vmem_operands, grad, xown, *passed)


def gate_rows(router_t, rows, table):
    logits = dot(router_t, rows, 1, 1)
    chosen = table > 0.5
    masked = jnp.where(chosen, logits, NEG)
    weights = jnp.where(chosen, jnp.exp(masked - jnp.max(masked, axis=0, keepdims=True)), 0.0)
    total = jnp.sum(weights, axis=0, keepdims=True)
    return weights / jnp.where(total > 0.0, total, 1.0)


def bit_steps(expert_count, tensor_count):
    expert_bits = [("expert", b) for b in bits_of(expert_count)]
    tensor_bits = [("tensor", b) for b in bits_of(tensor_count)]
    return expert_bits, tensor_bits, tensor_bits[1:][::-1]


def plane_gathers(net, target, share, first=None, done=False, last=None, which=slice(None)):
    counts = lax.axis_size("expert"), lax.axis_size("tensor")
    expert_bits, _, high_bits = bit_steps(*counts)
    size = share // 2
    parts = []
    for index, steps in enumerate((high_bits + expert_bits, expert_bits + high_bits)):

        def at(re, rt, offset=index * size):
            begin = pl.multiple_of(flip(net.me["tensor"], rt) * share + offset, size)
            return target.at[which, flip(net.me["expert"], re), pl.ds(begin, size)]

        source = None if first is None else first.at[:, pl.ds(index * size, size)]
        known = [(0, 0)]
        if done:
            axis, mask = steps.pop(0)
            known.append((mask, 0) if axis == "expert" else (0, mask))
        parts.append(Gather(net, at, steps[:last], known=known, first=source))
    return parts


def core_gather(net, target, share, known, which=slice(None)):
    def whole(re, rt):
        begin = pl.multiple_of(flip(net.me["tensor"], rt) * share, share)
        return target.at[which, flip(net.me["expert"], re), pl.ds(begin, share)]

    return Gather(net, whole, [("tensor", 1)], known=known)


def slot_numbers(capacity, rows):
    return sublanes((capacity, rows)).astype(F32).astype(BF)


def placed(slot_id, table_row, weight):
    return jnp.where(slot_id == (table_row - 1.0).astype(BF), weight, jnp.zeros((), BF))


def fill_units(table, gate, slot_id, first_expert, count, hits_ref, gated_ref):
    capacity = slot_id.shape[0]
    for j in range(count):
        row = table(first_expert + j)
        cut = slice(j * capacity, (j + 1) * capacity)
        hits_ref[cut, :] = placed(slot_id, row, jnp.ones((), BF))
        gated_ref[cut, :] = placed(slot_id, row, gate(first_expert + j).astype(BF))


def middle(both, grad_act, hidden):
    g_here, u_here = both[:, :hidden], both[:, hidden:]
    sig = 1.0 / (1.0 + jnp.exp(-g_here))
    silu = g_here * sig
    act = silu * u_here
    grad_gate = (grad_act * u_here * sig * (1.0 + g_here * (1.0 - sig))).astype(BF)
    grad_up = (grad_act * silu).astype(BF)
    return act, jnp.concatenate([grad_gate, grad_up], axis=1)


def own_kernel(
    sizes, groups, capacity, local, batch, gathers,
    x_ref, dy_ref, table_ref, router_ref, wg_ref, wu_ref, wd_ref, hidden_ref, share_ref, far_dy_ref,
    out_c_ref, out_g_ref, xs_out, ys_out, oth_ref, othy_ref, gates_out,
    gates, gates_b, ranks, hits, gated, xs, ys, made, back, gi_rows, acc_c, acc_g, send_sem, recv_sem, local_sem,
):
    chunk, pair = pl.program_id(0), pl.program_id(1)
    pairs = local // 2
    per_batch = batch // 2
    expert_count, tensor_count, dp_count = sizes
    net = Net(send_sem, recv_sem)
    dp_here, me_t, me_e = net.me["dp"], net.me["tensor"], net.me["expert"]
    rows, width = x_ref.shape[-2:]
    units = groups
    hidden = wg_ref.shape[2]
    slot_id = slot_numbers(capacity, rows)
    share = rows // tensor_count

    if gathers:
        expert_bits, tensor_bits, high_bits = bit_steps(expert_count, tensor_count)
        cotangent_parts = plane_gathers(net, othy_ref, share, first=far_dy_ref)
        row_parts = plane_gathers(net, oth_ref, share, last=1)
        mine = pl.ds(pl.multiple_of(me_t * share, share), share)
        keep = pltpu.make_async_copy(far_dy_ref, othy_ref.at[:, me_e, mine], local_sem.at[2])
        flight = []

        def first_steps():
            net.barrier(expert_bits + tensor_bits + [("dp", m) for m in range(1, dp_count)])
            keep.start()
            for one in cotangent_parts:
                one.start()
            for m in range(1, dp_count):
                flight.append(net.send(share_ref, lambda m=m: oth_ref.at[m - 1, me_e, mine], "dp", m))

        def second_steps():
            for one in cotangent_parts:
                one.finish()
            for one in cotangent_parts:
                one.start()

        def third_steps():
            for one in cotangent_parts:
                one.finish()
            keep.wait()
            cotangent_parts.append(core_gather(net, othy_ref, share, cotangent_parts[0].known))
            cotangent_parts[-1].start()
            for copy in flight:
                copy.wait_recv()
            flight.clear()
            for one in row_parts:
                one.start()

        def last_steps():
            cotangent_parts[-1].finish()
            for one in row_parts:
                one.finish()
            for copy in flight:
                copy.wait_recv()
            net.close()

        for time, steps in ((0, first_steps), (pairs * 2 // 8, second_steps), (pairs * 6 // 8, third_steps)):

            @pl.when(pair == time)
            def _(steps=steps):
                steps()

    @pl.when(pair == 0)
    def _():
        gi_rows[...] = jnp.zeros_like(gi_rows)

        @pl.loop(0, units)
        def _(i):
            table = given_table(table_ref, i, dp_here.astype(F32))
            ranks[i] = table
            gates[i] = gate_rows(router_ref[...], x_ref[i], table)
            gates_b[i] = gates[i].astype(BF)

    @pl.when(pair == 0)
    def _():
        if not gathers:
            gates_out[...] = gates_b[...]
            return
        for m in range(1, dp_count):
            flight.append(net.send(gates_b, lambda m=m: gates_out.at[m - 1], "dp", m))

    place = lax.rem(pair, per_batch)
    half = lax.div(pair, per_batch)
    group_start = pl.multiple_of(chunk * groups, groups)
    outs = []
    for index, (source, target) in enumerate(((xs, xs_out), (ys, ys_out))):
        outs.append(pltpu.make_async_copy(
            source, target.at[pl.ds(half * batch, batch), pl.ds(group_start, groups)], local_sem.at[index]
        ))

    @pl.when(place == 0)
    def _():
        @pl.loop(0, units)
        def _(i):
            fill_units(
                lambda e: ranks[i, pl.ds(e, 1), :], lambda e: gates[i, pl.ds(e, 1), :], slot_id,
                me_e * local + half * batch, batch, hits.at[i], gated.at[i],
            )
            xs[:, i] = dot(hits[i], x_ref[i]).astype(BF).reshape(batch, capacity, width)
            ys[:, i] = dot(gated[i], dy_ref[i]).astype(BF).reshape(batch, capacity, width)

        for copy in outs:
            copy.start()

    spots = [place * 2 + j for j in range(2)]
    inner_w = [jnp.concatenate([wg_ref[j], wu_ref[j]], axis=1) for j in range(2)]
    both = [dot(xs[spots[j]].reshape(units * capacity, width), inner_w[j]) for j in range(2)]
    grad_act = [dot(ys[spots[j]].reshape(units * capacity, width), wd_ref[j], 1, 1) for j in range(2)]
    mids = [middle(both[j], grad_act[j], hidden) for j in range(2)]
    for j in range(2):
        act, grads = mids[j]
        result = dot(act.astype(BF), wd_ref[j]).astype(BF)
        moved = dot(grads, inner_w[j], 1, 1).astype(BF)
        inner = jnp.sum(act * grad_act[j], axis=-1, keepdims=True)
        at_slot = pl.ds(pl.multiple_of(spots[j] * capacity, capacity), capacity)
        for i in range(units):
            cut = slice(i * capacity, (i + 1) * capacity)
            made[i, at_slot, :] = result[cut]
            back[i, at_slot, :] = moved[cut]
            gi_rows[i, pl.ds(me_e * local + pair * 2 + j, 1), :] = jnp.sum(
                hits[i, at_slot, :].astype(F32) * inner[cut], axis=0, keepdims=True
            )

    @pl.when(place == per_batch - 1)
    def _():
        for copy in outs:
            copy.wait()

        @pl.loop(0, units)
        def _(i):
            add_c = dot(gated[i], made[i], 0, 0)
            add_g = dot(hits[i], back[i], 0, 0)

            @pl.when(half == 0)
            def _():
                acc_c[i] = add_c
                acc_g[i] = add_g

            @pl.when(half != 0)
            def _():
                acc_c[i] += add_c
                acc_g[i] += add_g

    @pl.when(pair == pairs - 1)
    def _():
        blocks, columns = out_c_ref.shape[1], out_c_ref.shape[3]
        for i in range(units):

            @pl.when(chunk * groups + i == me_e)
            def _():
                cut = pl.ds(pl.multiple_of(me_t * share, share), share)
                acc_c[i, cut, :] += hidden_ref[...]

            for t in range(blocks):
                out_c_ref[i, t] = acc_c[i, :, t * columns : (t + 1) * columns].astype(BF)
            out_g_ref[i, :, :width] = acc_g[i].astype(BF)
            out_g_ref[i, :, width:] = jnp.transpose(gi_rows[i]).astype(BF)
        if gathers:
            last_steps()


def own_call(x, dy, table, router_t, wg, wu, wd, hidden_share, normed_share, far_dy):
    sizes = tuple(lax.axis_size(axis) for axis in ("expert", "tensor", "dp"))
    groups_all, dp_count = table.shape[:2]
    rows, width = x.shape[-2:]
    groups = 2
    chunks = groups_all // groups
    local, _, hidden = wg.shape
    pairs = local // 2
    assert chunks == 1 or pairs == 1
    batch = min(8, local)
    gathers = chunks == 1
    capacity = rows * TOP // EXPERTS
    shape = jax.ShapeDtypeStruct
    row_block = pl.BlockSpec((groups, rows, width), lambda c, p: (c, 0, 0), pipeline_mode=pl.Buffered(1))
    in_block = pl.BlockSpec((2, width, hidden), lambda c, p: (p, 0, 0))
    blocks = sizes[1]
    columns = width // blocks
    copies = 64
    slots = shape((local, groups_all, capacity, width), BF)
    anywhere = pl.BlockSpec(memory_space=pl.ANY)
    return pl.pallas_call(
        functools.partial(own_kernel, sizes, groups, capacity, local, batch, gathers),
        out_shape=(
            shape((groups_all, blocks, rows, columns), BF), shape((groups_all, rows, width + 128), BF), slots, slots,
            *[shape((dp_count - 1, groups_all, rows, width) if gathers else (16, 128), BF)] * 2,
            shape((dp_count - 1, groups_all, EXPERTS, rows) if gathers else (groups_all, EXPERTS, rows), BF),
        ),
        grid=(chunks, pairs),
        in_specs=[
            row_block, row_block,
            pl.BlockSpec((groups, dp_count, TABLE_ROWS, rows), lambda c, p: (c, 0, 0, 0)),
            pl.BlockSpec((EXPERTS, width), lambda c, p: (0, 0)),
            in_block, in_block, pl.BlockSpec((2, hidden, width), lambda c, p: (p, 0, 0)),
            pl.BlockSpec(hidden_share.shape, lambda c, p: (0, 0)), anywhere, anywhere,
        ],
        out_specs=(
            pl.BlockSpec((groups, blocks, rows, columns), lambda c, p: (c, 0, 0, 0)),
            pl.BlockSpec((groups, rows, width + 128), lambda c, p: (c, 0, 0)),
            anywhere, anywhere, anywhere, anywhere,
            anywhere if gathers else pl.BlockSpec((groups, EXPERTS, rows), lambda c, p: (c, 0, 0)),
        ),
        scratch_shapes=[
            pltpu.VMEM((groups, EXPERTS, rows), F32),
            pltpu.VMEM((groups, EXPERTS, rows), BF),
            pltpu.VMEM((groups, EXPERTS, rows), F32),
            pltpu.VMEM((groups, batch * capacity, rows), BF),
            pltpu.VMEM((groups, batch * capacity, rows), BF),
            pltpu.VMEM((batch, groups, capacity, width), BF),
            pltpu.VMEM((batch, groups, capacity, width), BF),
            pltpu.VMEM((groups, batch * capacity, width), BF),
            pltpu.VMEM((groups, batch * capacity, width), BF),
            pltpu.VMEM((groups, 128, rows), F32),
            pltpu.VMEM((groups, rows, width), F32),
            pltpu.VMEM((groups, rows, width), F32),
            pltpu.SemaphoreType.DMA((copies,)),
            pltpu.SemaphoreType.DMA((copies,)),
            pltpu.SemaphoreType.DMA((4,)),
        ],
        compiler_params=params(
            60, dimension_semantics=("arbitrary", "arbitrary"),
            **(dict(collective_id=3, has_side_effects=True) if gathers else {}),
        ),
        cost_estimate=pl.CostEstimate(flops=MIB, bytes_accessed=MIB, transcendentals=0),
        name="experts_own",
    )(x, dy, table, router_t, wg, wu, wd, hidden_share, normed_share, far_dy)


def slots_kernel(sizes, masks, capacity, local, batch, reduces, x_hbm, dy_hbm, table_ref, gates_ref, *rest):
    if reduces:
        (
            dense_in, heads_in, small_in, first_in, out_in, old_hbm, x_tok_hbm, stat_in, scale_ref, gain_ref,
            x_hbm, xs_ref, ys_ref, sums_ref, input_ref, block_ref, gain_out_ref,
            buf, onehot, ranks, weights, dense, heads, small, first, out, dense_land, heads_land, small_land, first_land, out_land,
            stat, stat_land, gains, gains_land, gains_far_land, old, x_tok, load_sem, send_sem, recv_sem, local_sem,
        ) = rest
    else:
        xs_ref, ys_ref, buf, onehot, ranks, weights, load_sem = rest
    expert_count, tensor_count, dp_count = sizes
    step = pl.program_id(0)
    units = expert_count * len(masks)
    rows, width = buf.shape[-2:]
    me_e, me_d = lax.axis_index("expert"), lax.axis_index("dp")
    slot_id = slot_numbers(capacity, rows)

    def far_dp(m):
        value = me_d
        for bit in bits_of(dp_count):
            on = lax.rem(lax.div(m, bit), 2)
            value = value + on * (bit - 2 * bit * lax.rem(lax.div(me_d, bit), 2))
        return value

    def place(i):
        m = masks[0] + lax.div(i, expert_count)
        return m, lax.rem(i, expert_count), far_dp(m)

    def load(source, i, slot):
        m, group, _ = place(i)
        return pltpu.make_async_copy(source.at[m - masks[0], group], buf.at[slot], load_sem.at[slot])

    def start_load(s):
        @pl.when(s < units)
        def _():
            load(dy_hbm, s, lax.rem(s, 2)).start()

        @pl.when(s >= units)
        def _():
            load(x_hbm, s - units, lax.rem(s, 2)).start()

    if reduces:
        net = Net(send_sem, recv_sem)
        me_t = net.me["tensor"]
        ways = expert_count * dp_count
        expert_bits, tensor_bits, high_bits = bit_steps(expert_count, tensor_count)
        dp_bits = [("dp", b) for b in bits_of(dp_count)][::-1]
        chunks = [(e, d) for e in range(expert_count) for d in range(dp_count)]
        plane = [(e, t) for e in range(expert_count) for t in range(0, tensor_count, 2)]
        share = rows // tensor_count
        planes = [plane_gathers(net, x_hbm, share, done=True, which=m) for m in range(dp_count - 1)]
        cores = [core_gather(net, x_hbm, share, plane, which) for which in range(dp_count - 1)]

        def chunk_of(ref):
            size = ref.shape[0] // ways

            def at(re, rd):
                index = flip(me_e, re) * dp_count + flip(me_d, rd)
                return ref.at[pl.ds(pl.multiple_of(index * size, size), size)]

            return at

        def column_of(ref):
            return lambda re, rt: ref.at[flip(me_t, rt)]

        dense_sum = Reduce(net, chunk_of(dense), lambda i: dense_land.at[i], [("dp", 0)] + expert_bits, chunks)
        small_sum = Reduce(net, chunk_of(small), lambda i: small_land.at[i], [("dp", 0)] + expert_bits, chunks)
        heads_sum = Reduce(net, chunk_of(heads), lambda i: heads_land.at[i], expert_bits + [("dp", 0)], chunks)
        out_sum = Reduce(net, column_of(out), lambda i: out_land.at[i], high_bits, [(0, t) for t in range(0, tensor_count, 2)])
        first_sum = Reduce(net, column_of(first), lambda i: first_land.at[i], tensor_bits, [(0, t) for t in range(tensor_count)])
        last = 2 * units
        plan = [
            (dense_sum, [0, units + 4]), (small_sum, [0, units + 4]),
            (heads_sum, [4, units + 4]), (first_sum, [0, units]), (out_sum, [units]),
        ]
        near = [("tensor", m) for m in range(1, tensor_count)]
        far = [(("expert", e), ("dp", d)) for e, d in chunks if e or d]
        stat_sum = Exchange(net, stat, 0, stat_land, near)
        gains_near = Exchange(net, gains, 0, gains_land, near)
        gains_far = Exchange(net, gains, 1, gains_far_land, far)
        columns = first.shape[2]
        begin = pl.multiple_of(me_t * columns, columns)

        def advance(k):
            for one, when in plan:
                if k in when or k == last:
                    if one.flight:
                        one.finish()
                    if one.steps:
                        one.start()

        def moves():
            pairs = (
                (stat_in.at[:, 0:rows], stat.at[0]), (stat_in.at[:, rows:], gains.at[0]),
                (dense_in, dense), (small_in, small), (first_in, first),
                (heads_in, heads), (out_in, out),
                (old_hbm, old), (x_tok_hbm.at[:, pl.ds(begin, columns)], x_tok),
            )
            return [pltpu.make_async_copy(a, b, local_sem.at[i]) for i, (a, b) in enumerate(pairs)]

        @pl.when(step == 0)
        def _():
            for copy in moves():
                copy.start()
            net.barrier(near + far)
            for copy in moves()[:2]:
                copy.wait()
            stat_sum.start()
            gains_near.start()
            for parts in planes:
                for one in parts:
                    one.start()
            for copy in moves()[2:5]:
                copy.wait()
            advance(0)

        for k in range(1, last):
            at_plane = [m for m in range(dp_count - 1) if k == max(units - 3 + m * expert_count, 1)]
            at_core = [m for m in range(dp_count - 1) if k == units - 1 + m * expert_count]
            if not (k <= 2 or at_plane or at_core or any(k in when for _, when in plan)):
                continue

            @pl.when(step == k)
            def _(k=k, at_plane=at_plane, at_core=at_core):
                if k == 1:
                    for copy in moves()[5:]:
                        copy.wait()
                for m in at_plane:
                    for one in planes[m]:
                        one.finish()
                    cores[m].start()
                advance(k)
                if k == 2:
                    stat_sum.finish()
                    gains_near.finish()
                    gains_far.start()
                for m in at_core:
                    cores[m].finish()

    @pl.when(step == 0)
    def _():
        start_load(step)

    @pl.when(step + 1 < 2 * units)
    def _():
        start_load(step + 1)

    slot = lax.rem(step, 2)

    def spread(unit, source, target_ref, gated):
        m, group, d = place(unit)
        ranks[...] = given_table(table_ref, group, d.astype(F32))
        if gated:
            weights[...] = gates_ref[m - masks[0], group].astype(F32)
        for part in range(local // batch):
            for j in range(batch):
                e = me_e * local + part * batch + j
                weight = weights[pl.ds(e, 1), :].astype(BF) if gated else jnp.ones((), BF)
                onehot[part, j * capacity : (j + 1) * capacity, :] = placed(slot_id, ranks[pl.ds(e, 1), :], weight)
            if part == 0:
                load(source, unit, slot).wait()
            moved = dot(onehot[part], buf[slot]).astype(BF)
            target_ref[part * batch : (part + 1) * batch, 0] = moved.reshape(batch, capacity, width)

    @pl.when(step < units)
    def _():
        spread(step, dy_hbm, ys_ref, True)

    @pl.when(step >= units)
    def _():
        spread(step - units, x_hbm, xs_ref, False)

    if reduces:

        @pl.when(step == last - 1)
        def _():
            for one, _ in plan:
                while one.flight or one.steps:
                    if one.flight:
                        one.finish()
                    if one.steps:
                        one.start()
            gains_far.finish()
            here = me_e * dp_count + me_d
            d_rows, h_rows, s_rows = (ref.shape[0] // ways for ref in (dense, heads, small))
            half = heads.shape[1] // 2
            sums_ref[0:d_rows] = dense[pl.ds(pl.multiple_of(here * d_rows, d_rows), d_rows), :]
            mine = heads[pl.ds(pl.multiple_of(here * h_rows, h_rows), h_rows), :]
            sums_ref[d_rows : d_rows + h_rows] = mine[:, :half]
            sums_ref[d_rows + h_rows : d_rows + 2 * h_rows] = mine[:, half:]
            sums_ref[d_rows + 2 * h_rows :] = small[pl.ds(pl.multiple_of(here * s_rows, s_rows), s_rows), :]
            gain_out_ref[...] = gains[gains.shape[0] - 1]
            total = jnp.concatenate([stat[stat.shape[0] - 1], jnp.zeros((120, rows), F32)], axis=0)
            mean = jnp.transpose(total)[:, 0:1] / gain_ref.shape[0]
            scale = scale_ref[:, 0:1]
            input_ref[...] = (
                old[...].astype(F32) + scale * (
                    first[me_t].astype(F32) * gain_ref[pl.ds(begin, columns)].astype(F32)[None, :]
                    - x_tok[...].astype(F32) * scale * mean
                )
            ).astype(BF)
            block_ref[...] = out[me_t]
            net.close()


def slots_call(masks, x, dy, table, gates, local, sums=None):
    sizes = tuple(lax.axis_size(axis) for axis in ("expert", "tensor", "dp"))
    expert_count, _, dp_count = sizes
    rows, width = x.shape[-2:]
    units = expert_count * len(masks)
    capacity = rows * TOP // EXPERTS
    batch = min(8, local)
    shape = jax.ShapeDtypeStruct
    anywhere = pl.BlockSpec(memory_space=pl.ANY)
    y_block = pl.BlockSpec((local, 1, capacity, width), lambda i: (0, jnp.minimum(i, units - 1), 0, 0))
    x_block = pl.BlockSpec((local, 1, capacity, width), lambda i: (0, jnp.maximum(i - units, 0), 0, 0))
    whole = pl.BlockSpec(memory_space=pltpu.VMEM)
    out_shape = [shape((local, units, capacity, width), BF)] * 2
    out_specs = [x_block, y_block]
    aliases = {}
    operands = [x, dy, table, gates]
    in_specs = [anywhere, anywhere, whole, whole]
    scratch = [
        pltpu.VMEM((2, rows, width), BF), pltpu.VMEM((local // batch, batch * capacity, rows), BF),
        pltpu.VMEM((EXPERTS, rows), F32), pltpu.VMEM((EXPERTS, rows), F32),
    ]
    tail = [pltpu.SemaphoreType.DMA((2,))]
    more = {}
    if sums is not None:
        dense, heads, small, first, out, old, tokens, stat, scale, gain = sums
        ways = expert_count * dp_count
        columns = first.shape[2]
        chunk = [values.shape[0] // ways for values in (dense, heads, small)]
        operands += [dense, heads, small, first, out, old, tokens, stat, scale, gain]
        in_specs += [anywhere] * 8 + [whole] * 2
        out_shape += [
            shape((chunk[0] + 2 * chunk[1] + chunk[2], dense.shape[1]), BF), shape((rows, columns), BF), shape((rows, columns), BF),
            shape((8, width), F32),
        ]
        out_specs += [whole] * 4
        out_shape = [shape(x.shape, BF)] + out_shape
        out_specs = [anywhere] + out_specs
        aliases = {0: 0}
        scratch += [pltpu.VMEM(values.shape, BF) for values in (dense, heads, small, first, out)]
        scratch += [
            pltpu.VMEM((ways - 1, chunk[0], dense.shape[1]), BF), pltpu.VMEM((ways - 1, chunk[1], heads.shape[1]), BF),
            pltpu.VMEM((ways - 1, chunk[2], small.shape[1]), BF), pltpu.VMEM((first.shape[0] - 1, rows, columns), BF),
            pltpu.VMEM((max(sizes[1] // 2 - 1, 1), rows, columns), BF),
            pltpu.VMEM((2, 8, rows), F32), pltpu.VMEM((sizes[1] - 1, 8, rows), F32),
            pltpu.VMEM((3, 8, width), F32), pltpu.VMEM((sizes[1] - 1, 8, width), F32), pltpu.VMEM((ways - 1, 8, width), F32),
            pltpu.VMEM((rows, columns), BF), pltpu.VMEM((rows, columns), BF),
        ]
        tail += [pltpu.SemaphoreType.DMA((96,)), pltpu.SemaphoreType.DMA((96,)), pltpu.SemaphoreType.DMA((9,))]
        more = dict(collective_id=4, has_side_effects=True)
    return pl.pallas_call(
        functools.partial(slots_kernel, sizes, masks, capacity, local, batch, sums is not None),
        out_shape=tuple(out_shape),
        grid=(2 * units,),
        in_specs=in_specs,
        out_specs=tuple(out_specs),
        input_output_aliases=aliases,
        scratch_shapes=scratch + tail,
        compiler_params=params(60, dimension_semantics=("arbitrary",), **more),
        cost_estimate=pl.CostEstimate(flops=MIB, bytes_accessed=MIB, transcendentals=0),
        name="slots",
    )(*operands)


def weights_kernel(counts, chunks, capacity, has_partial, wg_ref, wu_ref, wd_ref, *rest):
    parts = len(counts)
    xs_refs, ys_refs, rest = rest[:parts], rest[parts : 2 * parts], rest[2 * parts :]
    if has_partial:
        in_g, in_u, in_d, gg_ref, gu_ref, gd_ref, x_buf, y_buf, sem = rest
    else:
        gg_ref, gu_ref, gd_ref, x_buf, y_buf, sem = rest
    expert, chunk = pl.program_id(0), pl.program_id(1)
    step = expert * chunks + chunk
    total = pl.num_programs(0) * chunks

    def loads(s):
        e, c, slot = lax.div(s, chunks), lax.rem(s, chunks), lax.rem(s, 2)
        copies, start = [], 0
        for index, count in enumerate(counts):
            take = count // chunks
            for which, (refs, buf) in enumerate(((xs_refs, x_buf), (ys_refs, y_buf))):
                copies.append(pltpu.make_async_copy(
                    refs[index].at[pl.ds(2 * e, 2), pl.ds(c * take, take)], buf.at[slot, :, pl.ds(start, take)],
                    sem.at[slot, index, which],
                ))
            start += take
        return copies

    @pl.when(step == 0)
    def _():
        for copy in loads(step):
            copy.start()

    @pl.when(step + 1 < total)
    def _():
        for copy in loads(step + 1):
            copy.start()

    for copy in loads(step):
        copy.wait()
    slot = lax.rem(step, 2)
    width, hidden = wg_ref.shape[1:]
    x_here = [x_buf[slot, j].reshape(-1, width) for j in range(2)]
    y_here = [y_buf[slot, j].reshape(-1, width) for j in range(2)]
    both = [dot(x_here[j], jnp.concatenate([wg_ref[j], wu_ref[j]], axis=1)) for j in range(2)]
    grad_act = [dot(y_here[j], wd_ref[j], 1, 1) for j in range(2)]
    mids = [middle(both[j], grad_act[j], hidden) for j in range(2)]

    def put(j, ref, values, partial):
        if chunks == 1:
            ref[j] = values + partial[j] if has_partial else values
            return

        @pl.when(chunk == 0)
        def _():
            ref[j] = values + partial[j] if has_partial else values

        @pl.when(chunk != 0)
        def _():
            ref[j] += values

    for j in range(2):
        act, grads = mids[j]
        inner = dot(x_here[j], grads, 0, 0)
        put(j, gg_ref, inner[:, :hidden], in_g if has_partial else None)
        put(j, gu_ref, inner[:, hidden:], in_u if has_partial else None)
        put(j, gd_ref, dot(act.astype(BF), y_here[j], 0, 0), in_d if has_partial else None)


def weights_call(slots, wg, wu, wd, partial=None):
    local, width, hidden = wg.shape
    capacity = slots[0][0].shape[2]
    counts = [xs.shape[1] for xs, _ in slots]
    chunks = max(1, sum(counts) // 8)
    assert len(counts) == 1 or chunks == 1
    shape = jax.ShapeDtypeStruct
    in_block = pl.BlockSpec((2, width, hidden), lambda e, c: (e, 0, 0))
    down_block = pl.BlockSpec((2, hidden, width), lambda e, c: (e, 0, 0))
    specs = (in_block, in_block, down_block)
    more = list(partial) if partial is not None else []
    buffer = pltpu.VMEM((2, 2, sum(counts) // chunks, capacity, width), BF)
    return pl.pallas_call(
        functools.partial(weights_kernel, counts, chunks, capacity, partial is not None),
        out_shape=(shape(wg.shape, F32), shape(wu.shape, F32), shape(wd.shape, F32)),
        grid=(local // 2, chunks),
        in_specs=list(specs) + [pl.BlockSpec(memory_space=pl.ANY)] * (2 * len(slots)) + (list(specs) if more else []),
        out_specs=specs,
        scratch_shapes=[buffer, buffer, pltpu.SemaphoreType.DMA((2, len(counts), 2))],
        compiler_params=params(60, dimension_semantics=("arbitrary", "arbitrary")),
        cost_estimate=pl.CostEstimate(flops=80 * 10**9, bytes_accessed=100 * MIB, transcendentals=0),
        name="weights",
    )(wg, wu, wd, *[xs for xs, _ in slots], *[ys for _, ys in slots], *more)


def unpack_kernel(
    sums_ref, gain1_rows_ref, block_in, input_in,
    q_ref, k_ref, v_ref, heads_ref, router_ref, gain_ref, gain1_ref, block_ref, input_ref,
):
    ways = sums_ref.shape[0]
    d_rows, h_rows, s_rows = q_ref.shape[0] // ways, heads_ref.shape[0] // ways, SMALL_ROWS // ways
    q_width, k_width, half = q_ref.shape[1], k_ref.shape[1], heads_ref.shape[1] // 2
    small = []
    for i in range(ways):
        block = sums_ref[i].astype(F32)
        cut = slice(i * d_rows, (i + 1) * d_rows)
        q_ref[cut, :] = block[:d_rows, :q_width]
        k_ref[cut, :] = block[:d_rows, q_width : q_width + k_width]
        v_ref[cut, :] = block[:d_rows, q_width + k_width :]
        cut = slice(i * h_rows, (i + 1) * h_rows)
        heads_ref[cut, :half] = block[d_rows : d_rows + h_rows]
        heads_ref[cut, half:] = block[d_rows + h_rows : d_rows + 2 * h_rows]
        small.append(block[d_rows + 2 * h_rows :])
    small = jnp.concatenate(small, axis=0)
    router_ref[:, :half] = small[:EXPERTS]
    router_ref[:, half:] = small[EXPERTS : 2 * EXPERTS]
    gain_ref[0:half] = small[2 * EXPERTS]
    gain_ref[half:] = small[2 * EXPERTS + 1]
    gain1_ref[...] = gain1_rows_ref[0]
    block_ref[...] = block_in[...]
    input_ref[...] = input_in[...]


def unpack_call(sums, gain1_rows, block, grad, q_width, k_width, heads_shape):
    ways = sums.shape[0]
    width = heads_shape[1]
    shape = jax.ShapeDtypeStruct
    return pl.pallas_call(
        unpack_kernel,
        out_shape=(
            shape((width, q_width), F32), shape((width, k_width), F32), shape((width, k_width), F32), shape(heads_shape, F32),
            shape((EXPERTS, width), F32), shape((width,), F32), shape((width,), F32), shape(block.shape, BF), shape(grad.shape, BF),
        ),
        in_specs=vmem(4),
        out_specs=tuple(vmem(9)),
        compiler_params=params(60),
        cost_estimate=pl.CostEstimate(flops=MIB, bytes_accessed=5 * MIB, transcendentals=0),
        name="unpack",
    )(sums, gain1_rows, block, grad)


def on_device(
    tokens, cotangent, seq_lengths, deal_order, routes, slot_order, first_gain, w_query, w_key, w_value, w_out,
    second_gain, w_router, w_gate, w_up, w_down,
):
    dp_count = lax.axis_size("dp")
    dp_index = lax.axis_index("dp")
    tensor_count = lax.axis_size("tensor")
    tensor_index = lax.axis_index("tensor")
    expert_count = lax.axis_size("expert")
    expert_index = lax.axis_index("expert")
    rows, width = tokens.shape
    share = rows // tensor_count
    everywhere = ("expert", "dp", "tensor")
    unit_shape = (expert_count, dp_count, rows, width)

    cosine, sine = (jnp.asarray(values) for values in rotary_tables(rows))
    gain1, gain2 = first_gain, second_gain
    router_t = w_router.T
    normed, q, k, v, heads, logsum, hidden, normed_share, tables, far_dy, x_own, dy_own = front(
        seq_lengths, deal_order, tokens, gain1, w_query, w_key, w_value, w_out, cosine, sine, gain2, routes.T, slot_order, cotangent
    )
    never = seq_lengths[0, 0] < 0
    rows_all = ("expert", "dp")

    def after(values, other):
        return jnp.where(never, other.astype(values.dtype), values)

    small_mesh = expert_count == 2
    out_c, out_g, xs_own, ys_own, x_other, dy_other, gates = own_call(
        x_own, dy_own, tables, router_t, w_gate, w_up, w_down, hidden, normed_share, far_dy
    )
    group_count = expert_count
    if not small_mesh:
        out_c = lax.psum_scatter(out_c, "expert", scatter_dimension=0, tiled=True)
        out_g = lax.psum_scatter(out_g, "expert", scatter_dimension=0, tiled=True)
        x_own = lax.dynamic_slice_in_dim(x_own, expert_index, 1, 0)
        group_count = 1
    first, stat, hidden_grad, scale, dense, heads_grad, small, *out_passed = back_call(
        group_count, seq_lengths,
        (cotangent, tokens, gain1, gain2, router_t, hidden, tables, normed, q, k, v, heads, logsum,
         w_query, w_key, w_value, w_out, cosine, sine),
        out_g, x_own, *((out_c,) if small_mesh else ()),
    )
    local = w_gate.shape[0]
    q_width, k_width = w_query.shape[1], w_key.shape[1]
    half, columns = width // 2, width // tensor_count
    if small_mesh:
        _, xs, ys, sums, input_grad, block_out, gain1_rows = slots_call(
            tuple(range(1, dp_count)), x_other, dy_other, tables, gates, local,
            (dense, heads_grad, small, first, out_passed[0], hidden_grad, tokens, stat, scale, gain1),
        )
        ways = expert_count * dp_count
        sums = lax.all_gather(sums, rows_all, axis=0)
        gate_grad, up_grad, down_grad = weights_call([(xs_own, ys_own), (xs, ys)], w_gate, w_up, w_down)
        q_sum, k_sum, v_sum, out_sum, router_rows, gain2_sum, gain1_sum, block_out, input_grad = unpack_call(
            sums, gain1_rows, block_out, input_grad, q_width, k_width, w_out.shape
        )
        router_sum = router_rows.T
    else:
        grads = weights_call([(xs_own, ys_own)], w_gate, w_up, w_down)
        for mask in range(1, dp_count):
            moved = (
                lax.all_gather(
                    after(values[mask - 1], grads[2][0, 0, 0]), ("expert", "tensor"), axis=0, tiled=True
                ).reshape(1, expert_count, rows, width)
                for values in (
                    [lax.ppermute(normed_share, "dp", [(i, i ^ m) for i in range(dp_count)]) for m in range(1, dp_count)],
                    far_dy,
                )
            )
            far_gates = lax.ppermute(gates, "dp", [(i, i ^ mask) for i in range(dp_count)])[None]
            xs, ys = slots_call((mask,), *moved, tables, far_gates, local)
            grads = weights_call([(xs, ys)], w_gate, w_up, w_down, grads)
        gate_grad, up_grad, down_grad = grads
        dense_sum, out_sum, small_sum = (
            values.astype(F32) for values in lax.psum((dense, heads_grad, small), rows_all)
        )
        gain1_sum = lax.psum(stat[0, rows:], everywhere)
        q_sum, k_sum, v_sum = jnp.split(dense_sum, [q_width, q_width + k_width], axis=1)
        router_sum = jnp.concatenate([small_sum[:EXPERTS], small_sum[EXPERTS : 2 * EXPERTS]], axis=1)
        gain2_sum = small_sum[2 * EXPERTS : 2 * EXPERTS + 2].reshape(width)
        router_sum = router_sum.T
        block_out = lax.psum_scatter(out_c[0], "tensor", scatter_dimension=0, tiled=True)[0]
        first_sum = lax.psum_scatter(first, "tensor", scatter_dimension=0, tiled=True)[0].astype(F32)
        mean = lax.psum(stat[0, :rows], "tensor")[:, None] / width

        def cols(values):
            return lax.dynamic_slice_in_dim(values, tensor_index * columns, columns, -1).astype(F32)

        input_grad = (
            hidden_grad.astype(F32) + scale[:, :1] * (first_sum * cols(gain1) - cols(tokens) * scale[:, :1] * mean)
        ).astype(BF)
    return (
        block_out, input_grad, gain1_sum, q_sum, k_sum, v_sum, out_sum, gain2_sum, router_sum,
        gate_grad, up_grad, down_grad,
    )


def solution(mesh):
    rows2 = P(("expert", "dp"), None)
    placed = (
        rows2, rows2, P("expert", None), P("expert", None), rows2, rows2, P(),
        P(None, "tensor"), P(None, "tensor"), P(None, "tensor"), P("tensor", None), P(), P(),
        P("expert", None, "tensor"), P("expert", None, "tensor"), P("expert", "tensor", None),
    )
    return jax.shard_map(
        on_device,
        mesh=mesh,
        in_specs=placed,
        out_specs=(
            P(("expert", "dp"), "tensor"), P(("expert", "dp"), "tensor"), P(),
            P(None, "tensor"), P(None, "tensor"), P(None, "tensor"), P("tensor", None), P(), P(),
            P("expert", None, "tensor"), P("expert", None, "tensor"), P("expert", "tensor", None),
        ),
        check_vma=False,
    )
```

```python
import functools

import jax
import jax.numpy as jnp
import numpy as np
from jax import lax
from jax.experimental import pallas as pl
from jax.experimental.pallas import tpu as pltpu
from jax.sharding import PartitionSpec as P

HEADS = 16
KV_HEADS = 8
HEAD_DIM = 64
EXPERTS = 32
TOP = 8
SLOT = 512

EPS = 1e-06
THETA = 10000.0
NEG = -1e30
BF = jnp.bfloat16
F32 = jnp.float32
MIB = 1 << 20


def dot(a, b, ca=1, cb=0):
    return lax.dot_general(a, b, (((ca,), (cb,)), ((), ())), preferred_element_type=F32)


def vmem(count=1):
    return [pl.BlockSpec(memory_space=pltpu.VMEM)] * count


def params(mib, **more):
    return pltpu.CompilerParams(vmem_limit_bytes=mib * MIB, **more)


def rotary_tables(rows):
    places = np.arange(rows, dtype=np.float32)[:, None]
    halfway = HEAD_DIM // 2
    spread = np.float32(THETA) ** (-2.0 * np.arange(halfway, dtype=np.float32) / HEAD_DIM)
    angles = (places * spread.astype(np.float32)[None, :]).astype(np.float32)
    copies = 128 // halfway
    return (
        np.tile(np.cos(angles), (1, copies)).astype(np.float32),
        np.tile(np.sin(angles), (1, copies)).astype(np.float32),
    )


def rotate128(values, cosine, sine, low_half):
    half = HEAD_DIM // 2
    up = pltpu.roll(values, 128 - half, 1)
    down = pltpu.roll(values, half, 1)
    return values * cosine + jnp.where(low_half, -up, down) * sine


def lanes(shape):
    return lax.broadcasted_iota(jnp.int32, shape, len(shape) - 1)


def sublanes(shape):
    return lax.broadcasted_iota(jnp.int32, shape, len(shape) - 2)


def bits_of(count):
    return [1 << i for i in range(count.bit_length() - 1)]


def flip(value, mask):
    for bit in bits_of(1 << 16):
        if mask & bit:
            value = value + bit - 2 * bit * lax.rem(lax.div(value, bit), 2)
    return value


class Net:
    def __init__(self, send_sem, recv_sem):
        self.send_sem, self.recv_sem, self.used, self.copies = send_sem, recv_sem, 0, []
        self.me = {axis: lax.axis_index(axis) for axis in ("expert", "tensor", "dp")}

    def barrier(self, partners):
        sem = pltpu.get_barrier_semaphore()
        for partner in partners:
            pl.semaphore_signal(sem, inc=1, device_id=self.device(partner), device_id_type=pl.DeviceIdType.MESH)
        pl.semaphore_wait(sem, len(partners))

    def device(self, partner):
        pairs = [partner] if isinstance(partner[0], str) else partner
        return {axis: flip(self.me[axis], mask) for axis, mask in pairs}

    def send(self, source, target, *partner):
        k = self.used
        self.used += 1
        copy = Copy(self, k, source, target, partner)
        copy.build().start()
        self.copies.append(copy)
        return copy

    def close(self):
        for copy in self.copies:
            copy.build().wait_send()


class Copy:
    def __init__(self, net, index, source, target, partner):
        self.net, self.index, self.source, self.target, self.partner = net, index, source, target, partner

    def build(self):
        source = self.source() if callable(self.source) else self.source
        target = self.target() if callable(self.target) else self.target
        return pltpu.make_async_remote_copy(
            src_ref=source, dst_ref=target,
            send_sem=self.net.send_sem.at[self.index], recv_sem=self.net.recv_sem.at[self.index],
            device_id=self.net.device(self.partner), device_id_type=pl.DeviceIdType.MESH,
        )

    def wait_recv(self):
        self.build().wait_recv()


class Gather:
    def __init__(self, net, at, steps, known=((0, 0),), first=None):
        self.net, self.at, self.steps, self.known, self.first, self.flight = net, at, list(steps), list(known), first, []

    def start(self):
        axis, mask = self.steps.pop(0)
        fresh = []
        for re, rt in self.known:
            place = functools.partial(self.at, re, rt)
            source = self.first if self.first is not None and (re, rt) == (0, 0) else place
            self.flight.append(self.net.send(source, place, axis, mask))
            fresh.append((re ^ mask, rt) if axis == "expert" else (re, rt ^ mask))
        self.known += fresh

    def finish(self):
        for copy in self.flight:
            copy.wait_recv()
        self.flight = []


class Reduce:
    def __init__(self, net, at, landing, steps, chunks):
        self.net, self.at, self.landing, self.steps, self.live = net, at, landing, list(steps), list(chunks)
        self.used, self.flight = 0, []

    def start(self):
        axis, mask = self.steps.pop(0)
        side = 0 if axis == "expert" else 1
        going = [r for r in self.live if (r[side] & mask if mask else r[side])]
        self.live = [r for r in self.live if r not in going]
        for r in going:
            toward = mask or r[side]
            kept = (r[0] ^ toward, r[1]) if side == 0 else (r[0], r[1] ^ toward)
            copy = self.net.send(functools.partial(self.at, *r), functools.partial(self.landing, self.used), axis, toward)
            self.flight.append((kept, copy, self.used))
            self.used += 1

    def finish(self):
        for place in sorted({kept for kept, _, _ in self.flight}):
            total = self.at(*place)[...].astype(F32)
            for kept, copy, slot in self.flight:
                if kept == place:
                    copy.wait_recv()
                    total = total + self.landing(slot)[...].astype(F32)
            self.at(*place)[...] = total.astype(BF)
        self.flight = []


class Exchange:
    def __init__(self, net, stages, k, landing, partners):
        self.net, self.stages, self.k, self.landing, self.partners, self.flight = net, stages, k, landing, partners, []

    def start(self):
        for index, partner in enumerate(self.partners):
            self.flight.append(self.net.send(
                lambda: self.stages.at[self.k], lambda index=index: self.landing.at[index], *partner
            ))

    def finish(self):
        total = self.stages[self.k]
        for index, copy in enumerate(self.flight):
            copy.wait_recv()
            total = total + self.landing[index]
        self.stages[self.k + 1] = total


TABLE_ROWS = 48
SMALL_ROWS = 128


def table_of(length, routes_ref, order_ref):
    rows = routes_ref.shape[1]
    capacity = rows * TOP // EXPERTS
    entries = rows * TOP
    chunk = 512
    routes_t = routes_ref[...].astype(F32).astype(BF)
    upper = (sublanes((chunk, chunk)) < lanes((chunk, chunk))).astype(F32).astype(BF)
    expert_row = sublanes((EXPERTS, chunk))

    def body(step, carried):
        counts, table = carried
        entry = order_ref[:, pl.ds(pl.multiple_of(step * chunk, chunk), chunk)]
        row, choice = entry // TOP, entry % TOP
        onehot_row = (sublanes((rows, chunk)) == row).astype(F32).astype(BF)
        picked = dot(routes_t, onehot_row)
        expert = jnp.sum(jnp.where(sublanes((TOP, chunk)) == choice, picked, 0.0), axis=0, keepdims=True)
        member = (expert_row.astype(F32) == expert) & (row < length)
        member_f = member.astype(F32)
        before = dot(member_f.astype(BF), upper) + counts
        value = jnp.where(member, jnp.minimum(before, float(capacity)) + 1.0, 0.0)
        table = table + dot(value.astype(BF), onehot_row, 1, 1)
        return counts + jnp.sum(member_f, axis=1, keepdims=True), table

    _, table = lax.fori_loop(
        0, entries // chunk, body, (jnp.zeros((EXPERTS, 1), F32), jnp.zeros((EXPERTS, rows), F32))
    )
    return table


def given_table(tables, index, dp_here):
    total = 0.0
    for j in range(tables.shape[1]):
        source = tables[index, j, EXPERTS : EXPERTS + 16, :].astype(F32)[0:1]
        total = total + jnp.where(source == dp_here, tables[index, j, 0:EXPERTS, :].astype(F32), 0.0)
    return total


def head_parts(q, k_a, k_b, index, low_lane):
    block = q[:, (index // 2) * 128 : (index // 2) * 128 + 128]
    mine = low_lane if index % 2 == 0 else jnp.logical_not(low_lane)
    return jnp.where(mine, block, jnp.zeros((), block.dtype)), (k_a if index % 2 == (index // 2) % 2 else k_b)


def swap(block):
    return pltpu.roll(block.astype(F32), HEAD_DIM, 1).astype(BF)


def front_kernel(
    sizes,
    lengths_ref, order_of_ref, x_ref, gain_ref, wq_ref, wk_ref, wv_ref, wo_ref, cos_ref, sin_ref, gain2_ref, routes_ref, order_ref, dy_ref,
    normed_out, q_out, k_out, v_out, heads_out, logsum_out, hidden_out, share_out, tables_ref, far_dy_ref, xown_ref, dyown_ref,
    part, landing, send_sem, recv_sem, local_sem,
    normed_ref, q_ref, k_ref, v_ref, heads_ref, logsum_ref, hidden_ref, share_ref,
    wq_late, wk_late, wv_late, wo_late, cos_late, sin_late, late_sem, early_sem,
):
    late = [pltpu.make_async_copy(a, b, late_sem.at[i]) for i, (a, b) in enumerate((
        (wq_ref, wq_late), (wk_ref, wk_late), (wv_ref, wv_late), (wo_ref, wo_late), (cos_ref, cos_late), (sin_ref, sin_late),
    ))]
    for copy in late:
        copy.start()
    early = [pltpu.make_async_copy(a, b, early_sem.at[i]) for i, (a, b) in enumerate((
        (normed_ref, normed_out), (q_ref, q_out), (k_ref, k_out), (v_ref, v_out), (heads_ref, heads_out),
        (logsum_ref, logsum_out), (hidden_ref, hidden_out), (share_ref, share_out),
    ))]
    wq_ref, wk_ref, wv_ref, wo_ref, cos_ref, sin_ref = wq_late, wk_late, wv_late, wo_late, cos_late, sin_late
    expert_count, tensor_count, dp_count = sizes
    rows, width = x_ref.shape
    share = rows // tensor_count
    half = rows // 2
    net = Net(send_sem, recv_sem)
    me_e, me_t, me_d = net.me["expert"], net.me["tensor"], net.me["dp"]
    expert_bits = [("expert", b) for b in bits_of(expert_count)]
    tensor_bits = [("tensor", b) for b in bits_of(tensor_count)]
    net.barrier(expert_bits + tensor_bits + [("dp", m) for m in range(1, dp_count)])

    keep_dy = pltpu.make_async_copy(dy_ref, dyown_ref.at[me_e], local_sem.at[0])
    keep_dy.start()
    half_start = pl.multiple_of(lax.rem(me_t, 2) * half, half)
    dy_half = Gather(
        net, lambda re, rt: dyown_ref.at[flip(me_e, re), pl.ds(half_start, half)], expert_bits,
        first=dy_ref.at[pl.ds(half_start, half)],
    )
    dy_half.start()
    length, source, dealt_length = lengths_ref[0, me_d], order_of_ref[0, me_d], 0
    for i in range(dp_count):
        dealt_length = jnp.where(source == i, lengths_ref[0, i], dealt_length)
    x = x_ref[...].astype(F32)
    scale = lax.rsqrt(jnp.mean(x * x, axis=-1, keepdims=True) + EPS)
    normed = (x * scale * gain_ref[...].astype(F32)[None, :]).astype(BF)
    normed_ref[...] = normed
    for copy in late:
        copy.wait()
    cosine, sine = cos_ref[...], sin_ref[...]
    lane = lanes((rows, 128))
    low_half = lane % HEAD_DIM < HEAD_DIM // 2
    low_lane = lane < HEAD_DIM
    q_pre = dot(normed, wq_ref[...])
    for block in range(q_pre.shape[1] // 128):
        cut = slice(block * 128, block * 128 + 128)
        q_ref[:, cut] = rotate128(q_pre[:, cut], cosine, sine, low_half).astype(BF)
    k = rotate128(dot(normed, wk_ref[...]), cosine, sine, low_half).astype(BF)
    v = dot(normed, wv_ref[...]).astype(BF)
    k_ref[...] = k
    v_ref[...] = v
    q = q_ref[...]
    k_b, v_b = swap(k), swap(v)
    row, col = sublanes((rows, rows)), lanes((rows, rows))
    allowed = (col <= row) & (col < length)
    logsum = jnp.zeros((rows, 128), F32)
    pair = None
    for index in range(q.shape[1] // HEAD_DIM):
        q_one, k_one = head_parts(q, k, k_b, index, low_lane)
        v_one = v if index % 2 == (index // 2) % 2 else v_b
        scores = jnp.where(allowed, dot(q_one, k_one, 1, 1) * (HEAD_DIM**-0.5), NEG)
        highest = jnp.max(scores, axis=-1, keepdims=True)
        weights = jnp.exp(scores - highest)
        total = jnp.sum(weights, axis=-1, keepdims=True)
        mixed = dot((weights / total).astype(BF), v_one)
        logsum = jnp.where(lane == index, highest + jnp.log(total), logsum)
        if index % 2 == 0:
            pair = mixed
        else:
            cut = slice((index // 2) * 128, (index // 2) * 128 + 128)
            heads_ref[:, cut] = jnp.where(low_lane, pair, mixed).astype(BF)
    logsum_ref[...] = logsum
    live = (sublanes((rows, 1)) < length).astype(F32)
    part[...] = (dot(heads_ref[...], wo_ref[...]) * live).astype(BF).reshape(part.shape)

    for copy in early[:6]:
        copy.start()
    attn = Reduce(
        net, lambda re, rt: part.at[flip(me_t, rt)], lambda i: landing.at[i], tensor_bits,
        [(0, r) for r in range(tensor_count)],
    )
    attn.start()
    table = table_of(dealt_length, routes_ref, order_ref)
    source = jnp.broadcast_to(source.astype(F32), (TABLE_ROWS - EXPERTS, rows))
    tables_ref[me_e, me_d] = jnp.concatenate([table, source], axis=0).astype(BF)
    mine = tables_ref.at[me_e, me_d]
    table_copies = [net.send(mine, mine, "dp", m) for m in range(1, dp_count)]
    mine_rows = pl.multiple_of(me_t * share, share)
    far_copies = [
        net.send(dy_ref.at[pl.ds(mine_rows, share)], far_dy_ref.at[m - 1], "dp", m) for m in range(1, dp_count)
    ]
    attn.finish()
    while attn.steps:
        attn.start()
        if not attn.steps:
            dy_half.finish()
            while dy_half.steps:
                dy_half.start()
                dy_half.finish()
            for re, _ in dy_half.known[1:]:
                place = dy_half.at(re, 0)
                dy_half.flight.append(net.send(place, place, "tensor", 1))
        attn.finish()

    start = pl.multiple_of(me_t * share, share)
    hidden = x_ref[pl.ds(start, share), :].astype(F32) + part[me_t].astype(F32)
    hidden_ref[...] = hidden
    scale2 = lax.rsqrt(jnp.mean(hidden * hidden, axis=-1, keepdims=True) + EPS)
    share_ref[...] = (hidden * scale2 * gain2_ref[...].astype(F32)[None, :]).astype(BF)
    keep_x = pltpu.make_async_copy(share_ref, xown_ref.at[me_e, pl.ds(start, share)], local_sem.at[1])
    keep_x.start()
    for copy in early[6:]:
        copy.start()
    high_bits = tensor_bits[1:][::-1]
    gathers = []
    for part_index, steps in enumerate((high_bits + expert_bits, expert_bits + high_bits)):
        size = share // 2

        def at(re, rt, offset=part_index * size):
            begin = pl.multiple_of(flip(me_t, rt) * share + offset, size)
            return xown_ref.at[flip(me_e, re), pl.ds(begin, size)]

        gathers.append(
            Gather(net, at, steps + tensor_bits[:1], first=share_ref.at[pl.ds(part_index * size, size)])
        )
    table_all = Gather(net, lambda re, rt: tables_ref.at[flip(me_e, re)], expert_bits)
    first_step = True
    while gathers[0].steps:
        for gather in gathers:
            gather.start()
        if first_step:
            for copy in table_copies:
                copy.wait_recv()
            first_step = False
        else:
            table_all.finish()
        if table_all.steps:
            table_all.start()
        for gather in gathers:
            gather.finish()
    table_all.finish()
    dy_half.finish()
    for copy in far_copies:
        copy.wait_recv()
    net.close()
    keep_dy.wait()
    keep_x.wait()
    for copy in early:
        copy.wait()


def front(lengths, order_of, x, gain, wq, wk, wv, wo, cosine, sine, gain2, routes, order, dy):
    rows, width = x.shape
    sizes = tuple(lax.axis_size(axis) for axis in ("expert", "tensor", "dp"))
    expert_count, tensor_count, dp_count = sizes
    share = rows // tensor_count
    shape = jax.ShapeDtypeStruct
    copies = 96
    anywhere = pl.BlockSpec(memory_space=pl.ANY)
    return pl.pallas_call(
        functools.partial(front_kernel, sizes),
        out_shape=(
            shape((rows, width), BF), shape((rows, wq.shape[1]), BF), shape((rows, wk.shape[1]), BF),
            shape((rows, wv.shape[1]), BF), shape((rows, wq.shape[1]), BF), shape((rows, 128), F32),
            shape((share, width), F32), shape((share, width), BF), shape((expert_count, dp_count, TABLE_ROWS, rows), BF),
            shape((dp_count - 1, share, width), BF), shape((expert_count, rows, width), BF), shape((expert_count, rows, width), BF),
        ),
        in_specs=[pl.BlockSpec(memory_space=pltpu.SMEM)] * 2 + vmem(2) + [anywhere] * 6 + vmem(3) + [anywhere],
        out_specs=(anywhere,) * 8 + (vmem()[0],) + (anywhere,) * 3,
        scratch_shapes=[
            pltpu.VMEM((tensor_count, share, width), BF),
            pltpu.VMEM((tensor_count - 1, share, width), BF),
            pltpu.SemaphoreType.DMA((copies,)),
            pltpu.SemaphoreType.DMA((copies,)),
            pltpu.SemaphoreType.DMA((2,)),
            pltpu.VMEM((rows, width), BF), pltpu.VMEM((rows, wq.shape[1]), BF), pltpu.VMEM((rows, wk.shape[1]), BF),
            pltpu.VMEM((rows, wv.shape[1]), BF), pltpu.VMEM((rows, wq.shape[1]), BF), pltpu.VMEM((rows, 128), F32),
            pltpu.VMEM((share, width), F32), pltpu.VMEM((share, width), BF),
            *[pltpu.VMEM(values.shape, values.dtype) for values in (wq, wk, wv, wo, cosine, sine)],
            pltpu.SemaphoreType.DMA((6,)),
            pltpu.SemaphoreType.DMA((8,)),
        ],
        compiler_params=params(56, collective_id=1, has_side_effects=True),
        cost_estimate=pl.CostEstimate(flops=MIB, bytes_accessed=MIB, transcendentals=0),
        name="front",
    )(lengths, order_of, x, gain, wq, wk, wv, wo, cosine, sine, gain2, routes, order, dy)


def back_kernel(
    sizes, passes,
    lengths_ref, dy_ref, x_ref, gain_ref, gain2_ref, router_ref, hidden_ref, tables_ref,
    normed_ref, q_ref, k_ref, v_ref, heads_ref, logsum_ref, wq_ref, wk_ref, wv_ref, wo_ref, cos_ref, sin_ref,
    grad_in_ref, xown_ref, *rest,
):
    late_count = 13
    late_sem, rest = rest[-1], rest[:-1]
    late_refs, rest = rest[-late_count:], rest[:-late_count]
    late_hbm = (
        x_ref, normed_ref, q_ref, k_ref, v_ref, heads_ref, logsum_ref, wq_ref, wk_ref, wv_ref, wo_ref, cos_ref, sin_ref,
    )
    if passes:
        out_in_ref, rest = rest[0], rest[1:]
        out_pass_ref, rest = rest[7], rest[:7] + rest[8:]
        (out, out_landing), rest = rest[-2:], rest[:-2]
    (
        first_ref, tiny_ref, hidden_grad_ref, scale_ref, dense_ref, out_grad_ref, small_ref,
        grad, grad_landing, normed2, spread, back_ref, picked, send_sem, recv_sem, local_sem,
    ) = rest
    group_count, tensor_count, dp_count = sizes
    rows, width = x_ref.shape
    share = rows // tensor_count
    net = Net(send_sem, recv_sem)
    me_e, me_t, me_d = net.me["expert"], net.me["tensor"], net.me["dp"]
    here = me_e if group_count > 1 else 0
    expert_bits = [("expert", b) for b in bits_of(group_count)]
    tensor_bits = [("tensor", b) for b in bits_of(tensor_count)]
    load_grad = pltpu.make_async_copy(grad_in_ref, grad, local_sem.at[0])
    load_x = pltpu.make_async_copy(xown_ref.at[here], normed2, local_sem.at[1])
    load_grad.start()
    load_x.start()
    late = [pltpu.make_async_copy(a, b, late_sem.at[i]) for i, (a, b) in enumerate(zip(late_hbm, late_refs))]
    if passes:
        load_out = pltpu.make_async_copy(out_in_ref, out, local_sem.at[2])
        load_out.start()
    net.barrier(expert_bits + tensor_bits)
    load_grad.wait()
    for copy in late:
        copy.start()
    high_bits = tensor_bits[1:]
    chunks = [(e, t) for e in range(group_count) for t in range(tensor_count)]
    sums = []
    size = share // 2
    for part_index, steps in enumerate((high_bits + expert_bits, expert_bits + high_bits)):

        def at(re, rt, offset=part_index * size):
            begin = pl.multiple_of(flip(me_t, rt) * share + offset, size)
            return grad.at[flip(here, re) if re else here, pl.ds(begin, size)]

        sums.append(Reduce(
            net, at, lambda i, p=part_index: grad_landing.at[p, i], tensor_bits[:1] + steps, chunks
        ))
    if passes:
        out_sum = Reduce(
            net, lambda re, rt: out.at[flip(me_e, re), flip(me_t, rt)], lambda i: out_landing.at[i],
            tensor_bits[:1] + expert_bits, chunks,
        )
    while sums[0].steps:
        for one in sums:
            one.start()
        if passes and not out_sum.used:
            load_out.wait()
            out_sum.start()
        for one in sums:
            one.finish()
    if passes:
        out_sum.finish()
        out_sum.start()

    start = pl.multiple_of(me_t * share, share)
    gain2 = gain2_ref[...].astype(F32)[None, :]
    hidden = hidden_ref[...]
    scale2 = lax.rsqrt(jnp.mean(hidden * hidden, axis=-1, keepdims=True) + EPS)
    hat2 = hidden * scale2
    second_normed = (hat2 * gain2).astype(BF)
    picked[...] = given_table(tables_ref, me_e, me_d.astype(F32))
    table = picked[:, pl.ds(start, share)]
    table = jnp.concatenate([table, jnp.zeros((128 - EXPERTS, share), F32)], axis=0)
    table = jnp.transpose(table)[:, :EXPERTS]
    logits = dot(second_normed, router_ref[...], 1, 1)
    chosen = table > 0.5
    masked = jnp.where(chosen, logits, NEG)
    weights = jnp.where(chosen, jnp.exp(masked - jnp.max(masked, axis=-1, keepdims=True)), 0.0)
    total = jnp.sum(weights, axis=-1, keepdims=True)
    gates = weights / jnp.where(total > 0.0, total, 1.0)
    gate_in = grad[here, pl.ds(start, share), width:].astype(F32)[:, :EXPERTS]
    logit_grad = (gate_in - gates * jnp.sum(gate_in, axis=-1, keepdims=True)).astype(BF)
    normed_grad = grad[here, pl.ds(start, share), :width].astype(F32) + dot(logit_grad, router_ref[...])
    along2 = normed_grad * hat2
    gain2_part = jnp.sum(along2, axis=0, keepdims=True)
    scaled = normed_grad * gain2
    hidden_grad = dy_ref[pl.ds(start, share), :].astype(F32) + scale2 * (
        scaled - hat2 * jnp.mean(scaled * hat2, axis=-1, keepdims=True)
    )
    spread[me_t, 0:share, :width] = hidden_grad.astype(BF)
    spread[me_t, 0:share, width:] = jnp.concatenate(
        [logit_grad.astype(F32), jnp.zeros((share, 128 - EXPERTS), F32)], axis=1
    ).astype(BF)
    high = gain2_part.astype(BF).astype(F32)
    spread[me_t, share : share + 16, :width] = jnp.concatenate(
        [high, gain2_part - high, jnp.zeros((14, width), F32)], axis=0
    ).astype(BF)
    spread[me_t, share : share + 16, width:] = jnp.zeros((16, 128), BF)
    gather = Gather(net, lambda re, rt: spread.at[flip(me_t, rt)], high_bits[::-1] + tensor_bits[:1])
    while gather.steps:
        gather.start()
        gather.finish()

    for copy in late:
        copy.wait()
    (
        x_ref, normed_ref, q_ref, k_ref, v_ref, heads_ref, logsum_ref, wq_ref, wk_ref, wv_ref, wo_ref, cos_ref, sin_ref,
    ) = late_refs
    length = lengths_ref[0, me_d]
    inv = HEAD_DIM**-0.5
    live = (sublanes((rows, 1)) < length).astype(F32)
    hidden_grad_all = spread[:, 0:share, :width].reshape(rows, width)
    columns = width // tensor_count
    cut = pl.ds(pl.multiple_of(me_t * columns, columns), columns)
    hidden_grad_ref[...] = jnp.concatenate([spread[t, 0:share, cut] for t in range(tensor_count)], axis=0)
    branch = (hidden_grad_all.astype(F32) * live).astype(BF)
    out_grad_ref[...] = dot(heads_ref[...], branch, 0, 0).astype(BF)
    heads_grad = dot(branch, wo_ref[...], 1, 1).astype(BF)
    cosine, sine = cos_ref[...], -sin_ref[...]
    lane = lanes((rows, 128))
    low_half = lane % HEAD_DIM < HEAD_DIM // 2
    low_lane = lane < HEAD_DIM
    q, k, v = q_ref[...], k_ref[...], v_ref[...]
    k_b, v_b = swap(k), swap(v)
    key, query = sublanes((rows, rows)), lanes((rows, rows))
    allowed = (key <= query) & (key < length)
    logsum_rows = jnp.transpose(logsum_ref[...])
    dk = [jnp.zeros((rows, 128), F32), jnp.zeros((rows, 128), F32)]
    dv = [jnp.zeros((rows, 128), F32), jnp.zeros((rows, 128), F32)]
    q_width = q.shape[1]
    pair = None
    for index in range(q_width // HEAD_DIM):
        same = index % 2 == (index // 2) % 2
        q_one, k_one = head_parts(q, k, k_b, index, low_lane)
        g_one, v_one = head_parts(heads_grad, v, v_b, index, low_lane)
        scores = jnp.where(allowed, dot(k_one, q_one, 1, 1) * inv, NEG)
        prob = jnp.exp(scores - logsum_rows[index : index + 1, :])
        grad_prob = dot(v_one, g_one, 1, 1)
        center = jnp.sum(prob * grad_prob, axis=0, keepdims=True)
        score_grad = (prob * (grad_prob - center)).astype(BF)
        dq = dot(score_grad, k_one, 0, 0) * inv
        place = 0 if same else 1
        dk[place] = dk[place] + dot(score_grad, q_one) * inv
        dv[place] = dv[place] + dot(prob.astype(BF), g_one)
        if index % 2 == 0:
            pair = dq
        else:
            cut = slice((index // 2) * 128, (index // 2) * 128 + 128)
            both = jnp.where(low_lane, pair, dq)
            back_ref[:, cut] = rotate128(both, cosine, sine, low_half).astype(BF)
    k_width = k.shape[1]
    k_total = dk[0] + pltpu.roll(dk[1], HEAD_DIM, 1)
    v_total = dv[0] + pltpu.roll(dv[1], HEAD_DIM, 1)
    back_ref[:, q_width : q_width + k_width] = rotate128(k_total, cosine, sine, low_half).astype(BF)
    back_ref[:, q_width + k_width :] = v_total.astype(BF)
    back = back_ref[...]
    first = (
        dot(back[:, :q_width], wq_ref[...], 1, 1)
        + dot(back[:, q_width : q_width + k_width], wk_ref[...], 1, 1)
        + dot(back[:, q_width + k_width :], wv_ref[...], 1, 1)
    )
    columns = width // tensor_count
    for t in range(tensor_count):
        first_ref[t] = first[:, t * columns : (t + 1) * columns].astype(BF)
    x = x_ref[...].astype(F32)
    scale = lax.rsqrt(jnp.mean(x * x, axis=-1, keepdims=True) + EPS)
    scale_ref[...] = jnp.broadcast_to(scale, (rows, 128))
    along = first * (x * scale)
    stat = jnp.sum(along * gain_ref[...].astype(F32)[None, :], axis=-1, keepdims=True)
    tiny_ref[:, 0:rows] = jnp.transpose(jnp.broadcast_to(stat, (rows, 128)))[0:8, :]
    tiny_ref[:, rows:] = jnp.broadcast_to(jnp.sum(along, axis=0, keepdims=True), (8, width))
    dense_ref[...] = dot(normed_ref[...], back, 0, 0).astype(BF)
    load_x.wait()
    router_rows = dot(spread[:, 0:share, width:].reshape(rows, 128), normed2[...], 0, 0)[0:EXPERTS]
    gain2_sum = jnp.zeros((1, width), F32)
    for t in range(tensor_count):
        block = spread[t, share : share + 16, :width].astype(F32)
        gain2_sum = gain2_sum + block[0:1] + block[1:2]
    half = width // 2
    pieces = [router_rows[:, :half], router_rows[:, half:], gain2_sum[:, :half], gain2_sum[:, half:]]
    if passes:
        out_sum.finish()
        out_pass_ref[...] = out[me_e]
    filled = sum(piece.shape[0] for piece in pieces)
    small_ref[...] = jnp.concatenate(pieces + [jnp.zeros((SMALL_ROWS - filled, half), F32)], axis=0).astype(BF)
    net.close()


def back_call(group_count, lengths, vmem_operands, grad, xown, out=None):
    dy, x = vmem_operands[0], vmem_operands[1]
    rows, width = x.shape
    wq, wk, wv, wo = vmem_operands[13:17]
    tensor_count, dp_count = lax.axis_size("tensor"), lax.axis_size("dp")
    share, columns = rows // tensor_count, width // tensor_count
    chunks = group_count * tensor_count
    inner = wq.shape[1] + wk.shape[1] + wv.shape[1]
    shape = jax.ShapeDtypeStruct
    copies = 64
    passed = [] if out is None else [out]
    late = [1] + list(range(7, len(vmem_operands)))
    return pl.pallas_call(
        functools.partial(back_kernel, (group_count, tensor_count, dp_count), out is not None),
        out_shape=(
            shape((tensor_count, rows, columns), BF), shape((8, rows + width), F32), shape((rows, columns), BF),
            shape((rows, 128), F32), shape((width, inner), BF), shape(wo.shape, BF), shape((SMALL_ROWS, width // 2), BF),
            *[shape(one.shape[1:], BF) for one in passed],
        ),
        in_specs=[pl.BlockSpec(memory_space=pltpu.SMEM)] + [
            pl.BlockSpec(memory_space=pl.ANY if i in late else pltpu.VMEM) for i in range(len(vmem_operands))
        ] + [pl.BlockSpec(memory_space=pl.ANY)] * (2 + len(passed)),
        out_specs=tuple(vmem(7)) + tuple(vmem(len(passed))),
        scratch_shapes=[
            pltpu.VMEM(grad.shape, BF),
            pltpu.VMEM((2, chunks - 1, share // 2, width + 128), BF),
            pltpu.VMEM((rows, width), BF),
            pltpu.VMEM((tensor_count, share + 16, width + 128), BF),
            pltpu.VMEM((rows, inner), BF),
            pltpu.VMEM((EXPERTS, rows), F32),
            pltpu.SemaphoreType.DMA((copies,)),
            pltpu.SemaphoreType.DMA((copies,)),
            pltpu.SemaphoreType.DMA((3,)),
        ] + ([
            pltpu.VMEM(out.shape, BF),
            pltpu.VMEM((chunks, rows, columns), BF),
        ] if passed else []) + [pltpu.VMEM(vmem_operands[i].shape, vmem_operands[i].dtype) for i in late] + [
            pltpu.SemaphoreType.DMA((len(late),))
        ],
        compiler_params=params(60, collective_id=2, has_side_effects=True),
        cost_estimate=pl.CostEstimate(flops=MIB, bytes_accessed=MIB, transcendentals=0),
        name="back",
    )(lengths, *vmem_operands, grad, xown, *passed)


def gate_rows(router_t, rows, table):
    logits = dot(router_t, rows, 1, 1)
    chosen = table > 0.5
    masked = jnp.where(chosen, logits, NEG)
    weights = jnp.where(chosen, jnp.exp(masked - jnp.max(masked, axis=0, keepdims=True)), 0.0)
    total = jnp.sum(weights, axis=0, keepdims=True)
    return weights / jnp.where(total > 0.0, total, 1.0)


def bit_steps(expert_count, tensor_count):
    expert_bits = [("expert", b) for b in bits_of(expert_count)]
    tensor_bits = [("tensor", b) for b in bits_of(tensor_count)]
    return expert_bits, tensor_bits, tensor_bits[1:][::-1]


def plane_gathers(net, target, share, first=None, done=False, last=None, which=slice(None)):
    counts = lax.axis_size("expert"), lax.axis_size("tensor")
    expert_bits, _, high_bits = bit_steps(*counts)
    size = share // 2
    parts = []
    for index, steps in enumerate((high_bits + expert_bits, expert_bits + high_bits)):

        def at(re, rt, offset=index * size):
            begin = pl.multiple_of(flip(net.me["tensor"], rt) * share + offset, size)
            return target.at[which, flip(net.me["expert"], re), pl.ds(begin, size)]

        source = None if first is None else first.at[:, pl.ds(index * size, size)]
        known = [(0, 0)]
        if done:
            axis, mask = steps.pop(0)
            known.append((mask, 0) if axis == "expert" else (0, mask))
        parts.append(Gather(net, at, steps[:last], known=known, first=source))
    return parts


def core_gather(net, target, share, known, which=slice(None)):
    def whole(re, rt):
        begin = pl.multiple_of(flip(net.me["tensor"], rt) * share, share)
        return target.at[which, flip(net.me["expert"], re), pl.ds(begin, share)]

    return Gather(net, whole, [("tensor", 1)], known=known)


def slot_numbers(capacity, rows):
    return sublanes((capacity, rows)).astype(F32).astype(BF)


def placed(slot_id, table_row, weight):
    return jnp.where(slot_id == (table_row - 1.0).astype(BF), weight, jnp.zeros((), BF))


def fill_units(table, gate, slot_id, first_expert, count, hits_ref, gated_ref):
    capacity = slot_id.shape[0]
    for j in range(count):
        row = table(first_expert + j)
        cut = slice(j * capacity, (j + 1) * capacity)
        hits_ref[cut, :] = placed(slot_id, row, jnp.ones((), BF))
        gated_ref[cut, :] = placed(slot_id, row, gate(first_expert + j).astype(BF))


def middle(both, grad_act, hidden):
    g_here, u_here = both[:, :hidden], both[:, hidden:]
    sig = 1.0 / (1.0 + jnp.exp(-g_here))
    silu = g_here * sig
    act = silu * u_here
    grad_gate = (grad_act * u_here * sig * (1.0 + g_here * (1.0 - sig))).astype(BF)
    grad_up = (grad_act * silu).astype(BF)
    return act, jnp.concatenate([grad_gate, grad_up], axis=1)


def own_kernel(
    sizes, groups, capacity, local, batch, gathers,
    x_ref, dy_ref, table_ref, router_ref, wg_ref, wu_ref, wd_ref, hidden_ref, share_ref, far_dy_ref,
    out_c_ref, out_g_ref, xs_out, ys_out, oth_ref, othy_ref, gates_out,
    gates, gates_b, ranks, hits, gated, xs, ys, made, back, gi_rows, acc_c, acc_g, send_sem, recv_sem, local_sem,
):
    chunk, pair = pl.program_id(0), pl.program_id(1)
    pairs = local // 2
    per_batch = batch // 2
    expert_count, tensor_count, dp_count = sizes
    net = Net(send_sem, recv_sem)
    dp_here, me_t, me_e = net.me["dp"], net.me["tensor"], net.me["expert"]
    rows, width = x_ref.shape[-2:]
    units = groups
    hidden = wg_ref.shape[2]
    slot_id = slot_numbers(capacity, rows)
    share = rows // tensor_count

    if gathers:
        expert_bits, tensor_bits, high_bits = bit_steps(expert_count, tensor_count)
        cotangent_parts = plane_gathers(net, othy_ref, share, first=far_dy_ref)
        row_parts = plane_gathers(net, oth_ref, share, last=1)
        mine = pl.ds(pl.multiple_of(me_t * share, share), share)
        keep = pltpu.make_async_copy(far_dy_ref, othy_ref.at[:, me_e, mine], local_sem.at[2])
        flight = []

        def first_steps():
            net.barrier(expert_bits + tensor_bits + [("dp", m) for m in range(1, dp_count)])
            keep.start()
            for one in cotangent_parts:
                one.start()
            for m in range(1, dp_count):
                flight.append(net.send(share_ref, lambda m=m: oth_ref.at[m - 1, me_e, mine], "dp", m))

        def second_steps():
            for one in cotangent_parts:
                one.finish()
            for one in cotangent_parts:
                one.start()

        def third_steps():
            for one in cotangent_parts:
                one.finish()
            keep.wait()
            cotangent_parts.append(core_gather(net, othy_ref, share, cotangent_parts[0].known))
            cotangent_parts[-1].start()
            for copy in flight:
                copy.wait_recv()
            flight.clear()
            for one in row_parts:
                one.start()

        def last_steps():
            cotangent_parts[-1].finish()
            for one in row_parts:
                one.finish()
            for copy in flight:
                copy.wait_recv()
            net.close()

        for time, steps in ((0, first_steps), (pairs * 2 // 8, second_steps), (pairs * 6 // 8, third_steps)):

            @pl.when(pair == time)
            def _(steps=steps):
                steps()

    @pl.when(pair == 0)
    def _():
        gi_rows[...] = jnp.zeros_like(gi_rows)

        @pl.loop(0, units)
        def _(i):
            table = given_table(table_ref, i, dp_here.astype(F32))
            ranks[i] = table
            gates[i] = gate_rows(router_ref[...], x_ref[i], table)
            gates_b[i] = gates[i].astype(BF)

    @pl.when(pair == 0)
    def _():
        if not gathers:
            gates_out[...] = gates_b[...]
            return
        for m in range(1, dp_count):
            flight.append(net.send(gates_b, lambda m=m: gates_out.at[m - 1], "dp", m))

    place = lax.rem(pair, per_batch)
    half = lax.div(pair, per_batch)
    group_start = pl.multiple_of(chunk * groups, groups)
    outs = []
    for index, (source, target) in enumerate(((xs, xs_out), (ys, ys_out))):
        outs.append(pltpu.make_async_copy(
            source, target.at[pl.ds(half * batch, batch), pl.ds(group_start, groups)], local_sem.at[index]
        ))

    @pl.when(place == 0)
    def _():
        @pl.loop(0, units)
        def _(i):
            fill_units(
                lambda e: ranks[i, pl.ds(e, 1), :], lambda e: gates[i, pl.ds(e, 1), :], slot_id,
                me_e * local + half * batch, batch, hits.at[i], gated.at[i],
            )
            xs[:, i] = dot(hits[i], x_ref[i]).astype(BF).reshape(batch, capacity, width)
            ys[:, i] = dot(gated[i], dy_ref[i]).astype(BF).reshape(batch, capacity, width)

        for copy in outs:
            copy.start()

    spots = [place * 2 + j for j in range(2)]
    inner_w = [jnp.concatenate([wg_ref[j], wu_ref[j]], axis=1) for j in range(2)]
    both = [dot(xs[spots[j]].reshape(units * capacity, width), inner_w[j]) for j in range(2)]
    grad_act = [dot(ys[spots[j]].reshape(units * capacity, width), wd_ref[j], 1, 1) for j in range(2)]
    mids = [middle(both[j], grad_act[j], hidden) for j in range(2)]
    for j in range(2):
        act, grads = mids[j]
        result = dot(act.astype(BF), wd_ref[j]).astype(BF)
        moved = dot(grads, inner_w[j], 1, 1).astype(BF)
        inner = jnp.sum(act * grad_act[j], axis=-1, keepdims=True)
        at_slot = pl.ds(pl.multiple_of(spots[j] * capacity, capacity), capacity)
        for i in range(units):
            cut = slice(i * capacity, (i + 1) * capacity)
            made[i, at_slot, :] = result[cut]
            back[i, at_slot, :] = moved[cut]
            gi_rows[i, pl.ds(me_e * local + pair * 2 + j, 1), :] = jnp.sum(
                hits[i, at_slot, :].astype(F32) * inner[cut], axis=0, keepdims=True
            )

    @pl.when(place == per_batch - 1)
    def _():
        for copy in outs:
            copy.wait()

        @pl.loop(0, units)
        def _(i):
            add_c = dot(gated[i], made[i], 0, 0)
            add_g = dot(hits[i], back[i], 0, 0)

            @pl.when(half == 0)
            def _():
                acc_c[i] = add_c
                acc_g[i] = add_g

            @pl.when(half != 0)
            def _():
                acc_c[i] += add_c
                acc_g[i] += add_g

    @pl.when(pair == pairs - 1)
    def _():
        blocks, columns = out_c_ref.shape[1], out_c_ref.shape[3]
        for i in range(units):

            @pl.when(chunk * groups + i == me_e)
            def _():
                cut = pl.ds(pl.multiple_of(me_t * share, share), share)
                acc_c[i, cut, :] += hidden_ref[...]

            for t in range(blocks):
                out_c_ref[i, t] = acc_c[i, :, t * columns : (t + 1) * columns].astype(BF)
            out_g_ref[i, :, :width] = acc_g[i].astype(BF)
            out_g_ref[i, :, width:] = jnp.transpose(gi_rows[i]).astype(BF)
        if gathers:
            last_steps()


def own_call(x, dy, table, router_t, wg, wu, wd, hidden_share, normed_share, far_dy):
    sizes = tuple(lax.axis_size(axis) for axis in ("expert", "tensor", "dp"))
    groups_all, dp_count = table.shape[:2]
    rows, width = x.shape[-2:]
    groups = 2
    chunks = groups_all // groups
    local, _, hidden = wg.shape
    pairs = local // 2
    assert chunks == 1 or pairs == 1
    batch = min(8, local)
    gathers = chunks == 1
    capacity = rows * TOP // EXPERTS
    shape = jax.ShapeDtypeStruct
    row_block = pl.BlockSpec((groups, rows, width), lambda c, p: (c, 0, 0), pipeline_mode=pl.Buffered(1))
    in_block = pl.BlockSpec((2, width, hidden), lambda c, p: (p, 0, 0))
    blocks = sizes[1]
    columns = width // blocks
    copies = 64
    slots = shape((local, groups_all, capacity, width), BF)
    anywhere = pl.BlockSpec(memory_space=pl.ANY)
    return pl.pallas_call(
        functools.partial(own_kernel, sizes, groups, capacity, local, batch, gathers),
        out_shape=(
            shape((groups_all, blocks, rows, columns), BF), shape((groups_all, rows, width + 128), BF), slots, slots,
            *[shape((dp_count - 1, groups_all, rows, width) if gathers else (16, 128), BF)] * 2,
            shape((dp_count - 1, groups_all, EXPERTS, rows) if gathers else (groups_all, EXPERTS, rows), BF),
        ),
        grid=(chunks, pairs),
        in_specs=[
            row_block, row_block,
            pl.BlockSpec((groups, dp_count, TABLE_ROWS, rows), lambda c, p: (c, 0, 0, 0)),
            pl.BlockSpec((EXPERTS, width), lambda c, p: (0, 0)),
            in_block, in_block, pl.BlockSpec((2, hidden, width), lambda c, p: (p, 0, 0)),
            pl.BlockSpec(hidden_share.shape, lambda c, p: (0, 0)), anywhere, anywhere,
        ],
        out_specs=(
            pl.BlockSpec((groups, blocks, rows, columns), lambda c, p: (c, 0, 0, 0)),
            pl.BlockSpec((groups, rows, width + 128), lambda c, p: (c, 0, 0)),
            anywhere, anywhere, anywhere, anywhere,
            anywhere if gathers else pl.BlockSpec((groups, EXPERTS, rows), lambda c, p: (c, 0, 0)),
        ),
        scratch_shapes=[
            pltpu.VMEM((groups, EXPERTS, rows), F32),
            pltpu.VMEM((groups, EXPERTS, rows), BF),
            pltpu.VMEM((groups, EXPERTS, rows), F32),
            pltpu.VMEM((groups, batch * capacity, rows), BF),
            pltpu.VMEM((groups, batch * capacity, rows), BF),
            pltpu.VMEM((batch, groups, capacity, width), BF),
            pltpu.VMEM((batch, groups, capacity, width), BF),
            pltpu.VMEM((groups, batch * capacity, width), BF),
            pltpu.VMEM((groups, batch * capacity, width), BF),
            pltpu.VMEM((groups, 128, rows), F32),
            pltpu.VMEM((groups, rows, width), F32),
            pltpu.VMEM((groups, rows, width), F32),
            pltpu.SemaphoreType.DMA((copies,)),
            pltpu.SemaphoreType.DMA((copies,)),
            pltpu.SemaphoreType.DMA((4,)),
        ],
        compiler_params=params(
            60, dimension_semantics=("arbitrary", "arbitrary"),
            **(dict(collective_id=3, has_side_effects=True) if gathers else {}),
        ),
        cost_estimate=pl.CostEstimate(flops=MIB, bytes_accessed=MIB, transcendentals=0),
        name="experts_own",
    )(x, dy, table, router_t, wg, wu, wd, hidden_share, normed_share, far_dy)


def slots_kernel(sizes, masks, capacity, local, batch, reduces, x_hbm, dy_hbm, table_ref, gates_ref, *rest):
    if reduces:
        (
            dense_in, heads_in, small_in, first_in, out_in, old_hbm, x_tok_hbm, stat_in, scale_ref, gain_ref,
            x_hbm, xs_ref, ys_ref, sums_ref, input_ref, block_ref, gain_out_ref,
            buf, onehot, ranks, weights, dense, heads, small, first, out, dense_land, heads_land, small_land, first_land, out_land,
            stat, stat_land, gains, gains_land, gains_far_land, old, x_tok, load_sem, send_sem, recv_sem, local_sem,
        ) = rest
    else:
        xs_ref, ys_ref, buf, onehot, ranks, weights, load_sem = rest
    expert_count, tensor_count, dp_count = sizes
    step = pl.program_id(0)
    units = expert_count * len(masks)
    rows, width = buf.shape[-2:]
    me_e, me_d = lax.axis_index("expert"), lax.axis_index("dp")
    slot_id = slot_numbers(capacity, rows)

    def far_dp(m):
        value = me_d
        for bit in bits_of(dp_count):
            on = lax.rem(lax.div(m, bit), 2)
            value = value + on * (bit - 2 * bit * lax.rem(lax.div(me_d, bit), 2))
        return value

    def place(i):
        m = masks[0] + lax.div(i, expert_count)
        return m, lax.rem(i, expert_count), far_dp(m)

    def load(source, i, slot):
        m, group, _ = place(i)
        return pltpu.make_async_copy(source.at[m - masks[0], group], buf.at[slot], load_sem.at[slot])

    def start_load(s):
        @pl.when(s < units)
        def _():
            load(dy_hbm, s, lax.rem(s, 2)).start()

        @pl.when(s >= units)
        def _():
            load(x_hbm, s - units, lax.rem(s, 2)).start()

    if reduces:
        net = Net(send_sem, recv_sem)
        me_t = net.me["tensor"]
        ways = expert_count * dp_count
        expert_bits, tensor_bits, high_bits = bit_steps(expert_count, tensor_count)
        dp_bits = [("dp", b) for b in bits_of(dp_count)][::-1]
        chunks = [(e, d) for e in range(expert_count) for d in range(dp_count)]
        plane = [(e, t) for e in range(expert_count) for t in range(0, tensor_count, 2)]
        share = rows // tensor_count
        planes = [plane_gathers(net, x_hbm, share, done=True, which=m) for m in range(dp_count - 1)]
        cores = [core_gather(net, x_hbm, share, plane, which) for which in range(dp_count - 1)]

        def chunk_of(ref):
            size = ref.shape[0] // ways

            def at(re, rd):
                index = flip(me_e, re) * dp_count + flip(me_d, rd)
                return ref.at[pl.ds(pl.multiple_of(index * size, size), size)]

            return at

        def column_of(ref):
            return lambda re, rt: ref.at[flip(me_t, rt)]

        dense_sum = Reduce(net, chunk_of(dense), lambda i: dense_land.at[i], [("dp", 0)] + expert_bits, chunks)
        small_sum = Reduce(net, chunk_of(small), lambda i: small_land.at[i], [("dp", 0)] + expert_bits, chunks)
        heads_sum = Reduce(net, chunk_of(heads), lambda i: heads_land.at[i], expert_bits + [("dp", 0)], chunks)
        out_sum = Reduce(net, column_of(out), lambda i: out_land.at[i], high_bits, [(0, t) for t in range(0, tensor_count, 2)])
        first_sum = Reduce(net, column_of(first), lambda i: first_land.at[i], tensor_bits, [(0, t) for t in range(tensor_count)])
        last = 2 * units
        plan = [
            (dense_sum, [0, units + 4]), (small_sum, [0, units + 4]),
            (heads_sum, [4, units + 4]), (first_sum, [0, units]), (out_sum, [units]),
        ]
        near = [("tensor", m) for m in range(1, tensor_count)]
        far = [(("expert", e), ("dp", d)) for e, d in chunks if e or d]
        stat_sum = Exchange(net, stat, 0, stat_land, near)
        gains_near = Exchange(net, gains, 0, gains_land, near)
        gains_far = Exchange(net, gains, 1, gains_far_land, far)
        columns = first.shape[2]
        begin = pl.multiple_of(me_t * columns, columns)

        def advance(k):
            for one, when in plan:
                if k in when or k == last:
                    if one.flight:
                        one.finish()
                    if one.steps:
                        one.start()

        def moves():
            pairs = (
                (stat_in.at[:, 0:rows], stat.at[0]), (stat_in.at[:, rows:], gains.at[0]),
                (dense_in, dense), (small_in, small), (first_in, first),
                (heads_in, heads), (out_in, out),
                (old_hbm, old), (x_tok_hbm.at[:, pl.ds(begin, columns)], x_tok),
            )
            return [pltpu.make_async_copy(a, b, local_sem.at[i]) for i, (a, b) in enumerate(pairs)]

        @pl.when(step == 0)
        def _():
            for copy in moves():
                copy.start()
            net.barrier(near + far)
            for copy in moves()[:2]:
                copy.wait()
            stat_sum.start()
            gains_near.start()
            for parts in planes:
                for one in parts:
                    one.start()
            for copy in moves()[2:5]:
                copy.wait()
            advance(0)

        for k in range(1, last):
            at_plane = [m for m in range(dp_count - 1) if k == max(units - 3 + m * expert_count, 1)]
            at_core = [m for m in range(dp_count - 1) if k == units - 1 + m * expert_count]
            if not (k <= 2 or at_plane or at_core or any(k in when for _, when in plan)):
                continue

            @pl.when(step == k)
            def _(k=k, at_plane=at_plane, at_core=at_core):
                if k == 1:
                    for copy in moves()[5:]:
                        copy.wait()
                for m in at_plane:
                    for one in planes[m]:
                        one.finish()
                    cores[m].start()
                advance(k)
                if k == 2:
                    stat_sum.finish()
                    gains_near.finish()
                    gains_far.start()
                for m in at_core:
                    cores[m].finish()

    @pl.when(step == 0)
    def _():
        start_load(step)

    @pl.when(step + 1 < 2 * units)
    def _():
        start_load(step + 1)

    slot = lax.rem(step, 2)

    def spread(unit, source, target_ref, gated):
        m, group, d = place(unit)
        ranks[...] = given_table(table_ref, group, d.astype(F32))
        if gated:
            weights[...] = gates_ref[m - masks[0], group].astype(F32)
        for part in range(local // batch):
            for j in range(batch):
                e = me_e * local + part * batch + j
                weight = weights[pl.ds(e, 1), :].astype(BF) if gated else jnp.ones((), BF)
                onehot[part, j * capacity : (j + 1) * capacity, :] = placed(slot_id, ranks[pl.ds(e, 1), :], weight)
            if part == 0:
                load(source, unit, slot).wait()
            moved = dot(onehot[part], buf[slot]).astype(BF)
            target_ref[part * batch : (part + 1) * batch, 0] = moved.reshape(batch, capacity, width)

    @pl.when(step < units)
    def _():
        spread(step, dy_hbm, ys_ref, True)

    @pl.when(step >= units)
    def _():
        spread(step - units, x_hbm, xs_ref, False)

    if reduces:

        @pl.when(step == last - 1)
        def _():
            for one, _ in plan:
                while one.flight or one.steps:
                    if one.flight:
                        one.finish()
                    if one.steps:
                        one.start()
            gains_far.finish()
            here = me_e * dp_count + me_d
            d_rows, h_rows, s_rows = (ref.shape[0] // ways for ref in (dense, heads, small))
            half = heads.shape[1] // 2
            sums_ref[0:d_rows] = dense[pl.ds(pl.multiple_of(here * d_rows, d_rows), d_rows), :]
            mine = heads[pl.ds(pl.multiple_of(here * h_rows, h_rows), h_rows), :]
            sums_ref[d_rows : d_rows + h_rows] = mine[:, :half]
            sums_ref[d_rows + h_rows : d_rows + 2 * h_rows] = mine[:, half:]
            sums_ref[d_rows + 2 * h_rows :] = small[pl.ds(pl.multiple_of(here * s_rows, s_rows), s_rows), :]
            gain_out_ref[...] = gains[gains.shape[0] - 1]
            total = jnp.concatenate([stat[stat.shape[0] - 1], jnp.zeros((120, rows), F32)], axis=0)
            mean = jnp.transpose(total)[:, 0:1] / gain_ref.shape[0]
            scale = scale_ref[:, 0:1]
            input_ref[...] = (
                old[...].astype(F32) + scale * (
                    first[me_t].astype(F32) * gain_ref[pl.ds(begin, columns)].astype(F32)[None, :]
                    - x_tok[...].astype(F32) * scale * mean
                )
            ).astype(BF)
            block_ref[...] = out[me_t]
            net.close()


def slots_call(masks, x, dy, table, gates, local, sums=None):
    sizes = tuple(lax.axis_size(axis) for axis in ("expert", "tensor", "dp"))
    expert_count, _, dp_count = sizes
    rows, width = x.shape[-2:]
    units = expert_count * len(masks)
    capacity = rows * TOP // EXPERTS
    batch = min(8, local)
    shape = jax.ShapeDtypeStruct
    anywhere = pl.BlockSpec(memory_space=pl.ANY)
    y_block = pl.BlockSpec((local, 1, capacity, width), lambda i: (0, jnp.minimum(i, units - 1), 0, 0))
    x_block = pl.BlockSpec((local, 1, capacity, width), lambda i: (0, jnp.maximum(i - units, 0), 0, 0))
    whole = pl.BlockSpec(memory_space=pltpu.VMEM)
    out_shape = [shape((local, units, capacity, width), BF)] * 2
    out_specs = [x_block, y_block]
    aliases = {}
    operands = [x, dy, table, gates]
    in_specs = [anywhere, anywhere, whole, whole]
    scratch = [
        pltpu.VMEM((2, rows, width), BF), pltpu.VMEM((local // batch, batch * capacity, rows), BF),
        pltpu.VMEM((EXPERTS, rows), F32), pltpu.VMEM((EXPERTS, rows), F32),
    ]
    tail = [pltpu.SemaphoreType.DMA((2,))]
    more = {}
    if sums is not None:
        dense, heads, small, first, out, old, tokens, stat, scale, gain = sums
        ways = expert_count * dp_count
        columns = first.shape[2]
        chunk = [values.shape[0] // ways for values in (dense, heads, small)]
        operands += [dense, heads, small, first, out, old, tokens, stat, scale, gain]
        in_specs += [anywhere] * 8 + [whole] * 2
        out_shape += [
            shape((chunk[0] + 2 * chunk[1] + chunk[2], dense.shape[1]), BF), shape((rows, columns), BF), shape((rows, columns), BF),
            shape((8, width), F32),
        ]
        out_specs += [whole] * 4
        out_shape = [shape(x.shape, BF)] + out_shape
        out_specs = [anywhere] + out_specs
        aliases = {0: 0}
        scratch += [pltpu.VMEM(values.shape, BF) for values in (dense, heads, small, first, out)]
        scratch += [
            pltpu.VMEM((ways - 1, chunk[0], dense.shape[1]), BF), pltpu.VMEM((ways - 1, chunk[1], heads.shape[1]), BF),
            pltpu.VMEM((ways - 1, chunk[2], small.shape[1]), BF), pltpu.VMEM((first.shape[0] - 1, rows, columns), BF),
            pltpu.VMEM((max(sizes[1] // 2 - 1, 1), rows, columns), BF),
            pltpu.VMEM((2, 8, rows), F32), pltpu.VMEM((sizes[1] - 1, 8, rows), F32),
            pltpu.VMEM((3, 8, width), F32), pltpu.VMEM((sizes[1] - 1, 8, width), F32), pltpu.VMEM((ways - 1, 8, width), F32),
            pltpu.VMEM((rows, columns), BF), pltpu.VMEM((rows, columns), BF),
        ]
        tail += [pltpu.SemaphoreType.DMA((96,)), pltpu.SemaphoreType.DMA((96,)), pltpu.SemaphoreType.DMA((9,))]
        more = dict(collective_id=4, has_side_effects=True)
    return pl.pallas_call(
        functools.partial(slots_kernel, sizes, masks, capacity, local, batch, sums is not None),
        out_shape=tuple(out_shape),
        grid=(2 * units,),
        in_specs=in_specs,
        out_specs=tuple(out_specs),
        input_output_aliases=aliases,
        scratch_shapes=scratch + tail,
        compiler_params=params(60, dimension_semantics=("arbitrary",), **more),
        cost_estimate=pl.CostEstimate(flops=MIB, bytes_accessed=MIB, transcendentals=0),
        name="slots",
    )(*operands)


def weights_kernel(counts, chunks, capacity, has_partial, wg_ref, wu_ref, wd_ref, *rest):
    parts = len(counts)
    xs_refs, ys_refs, rest = rest[:parts], rest[parts : 2 * parts], rest[2 * parts :]
    if has_partial:
        in_g, in_u, in_d, gg_ref, gu_ref, gd_ref, x_buf, y_buf, sem = rest
    else:
        gg_ref, gu_ref, gd_ref, x_buf, y_buf, sem = rest
    expert, chunk = pl.program_id(0), pl.program_id(1)
    step = expert * chunks + chunk
    total = pl.num_programs(0) * chunks

    def loads(s):
        e, c, slot = lax.div(s, chunks), lax.rem(s, chunks), lax.rem(s, 2)
        copies, start = [], 0
        for index, count in enumerate(counts):
            take = count // chunks
            for which, (refs, buf) in enumerate(((xs_refs, x_buf), (ys_refs, y_buf))):
                copies.append(pltpu.make_async_copy(
                    refs[index].at[pl.ds(2 * e, 2), pl.ds(c * take, take)], buf.at[slot, :, pl.ds(start, take)],
                    sem.at[slot, index, which],
                ))
            start += take
        return copies

    @pl.when(step == 0)
    def _():
        for copy in loads(step):
            copy.start()

    @pl.when(step + 1 < total)
    def _():
        for copy in loads(step + 1):
            copy.start()

    for copy in loads(step):
        copy.wait()
    slot = lax.rem(step, 2)
    width, hidden = wg_ref.shape[1:]
    x_here = [x_buf[slot, j].reshape(-1, width) for j in range(2)]
    y_here = [y_buf[slot, j].reshape(-1, width) for j in range(2)]
    both = [dot(x_here[j], jnp.concatenate([wg_ref[j], wu_ref[j]], axis=1)) for j in range(2)]
    grad_act = [dot(y_here[j], wd_ref[j], 1, 1) for j in range(2)]
    mids = [middle(both[j], grad_act[j], hidden) for j in range(2)]

    def put(j, ref, values, partial):
        if chunks == 1:
            ref[j] = values + partial[j] if has_partial else values
            return

        @pl.when(chunk == 0)
        def _():
            ref[j] = values + partial[j] if has_partial else values

        @pl.when(chunk != 0)
        def _():
            ref[j] += values

    for j in range(2):
        act, grads = mids[j]
        inner = dot(x_here[j], grads, 0, 0)
        put(j, gg_ref, inner[:, :hidden], in_g if has_partial else None)
        put(j, gu_ref, inner[:, hidden:], in_u if has_partial else None)
        put(j, gd_ref, dot(act.astype(BF), y_here[j], 0, 0), in_d if has_partial else None)


def weights_call(slots, wg, wu, wd, partial=None):
    local, width, hidden = wg.shape
    capacity = slots[0][0].shape[2]
    counts = [xs.shape[1] for xs, _ in slots]
    chunks = max(1, sum(counts) // 8)
    assert len(counts) == 1 or chunks == 1
    shape = jax.ShapeDtypeStruct
    in_block = pl.BlockSpec((2, width, hidden), lambda e, c: (e, 0, 0))
    down_block = pl.BlockSpec((2, hidden, width), lambda e, c: (e, 0, 0))
    specs = (in_block, in_block, down_block)
    more = list(partial) if partial is not None else []
    buffer = pltpu.VMEM((2, 2, sum(counts) // chunks, capacity, width), BF)
    return pl.pallas_call(
        functools.partial(weights_kernel, counts, chunks, capacity, partial is not None),
        out_shape=(shape(wg.shape, F32), shape(wu.shape, F32), shape(wd.shape, F32)),
        grid=(local // 2, chunks),
        in_specs=list(specs) + [pl.BlockSpec(memory_space=pl.ANY)] * (2 * len(slots)) + (list(specs) if more else []),
        out_specs=specs,
        scratch_shapes=[buffer, buffer, pltpu.SemaphoreType.DMA((2, len(counts), 2))],
        compiler_params=params(60, dimension_semantics=("arbitrary", "arbitrary")),
        cost_estimate=pl.CostEstimate(flops=80 * 10**9, bytes_accessed=100 * MIB, transcendentals=0),
        name="weights",
    )(wg, wu, wd, *[xs for xs, _ in slots], *[ys for _, ys in slots], *more)


def unpack_kernel(
    sums_ref, gain1_rows_ref, block_in, input_in,
    q_ref, k_ref, v_ref, heads_ref, router_ref, gain_ref, gain1_ref, block_ref, input_ref, sem,
):
    moves = [
        pltpu.make_async_copy(block_in, block_ref, sem.at[0]), pltpu.make_async_copy(input_in, input_ref, sem.at[1]),
    ]
    for copy in moves:
        copy.start()
    ways = sums_ref.shape[0]
    d_rows, h_rows, s_rows = q_ref.shape[0] // ways, heads_ref.shape[0] // ways, SMALL_ROWS // ways
    q_width, k_width, half = q_ref.shape[1], k_ref.shape[1], heads_ref.shape[1] // 2
    small = []
    for i in range(ways):
        block = sums_ref[i].astype(F32)
        cut = slice(i * d_rows, (i + 1) * d_rows)
        q_ref[cut, :] = block[:d_rows, :q_width]
        k_ref[cut, :] = block[:d_rows, q_width : q_width + k_width]
        v_ref[cut, :] = block[:d_rows, q_width + k_width :]
        cut = slice(i * h_rows, (i + 1) * h_rows)
        heads_ref[cut, :half] = block[d_rows : d_rows + h_rows]
        heads_ref[cut, half:] = block[d_rows + h_rows : d_rows + 2 * h_rows]
        small.append(block[d_rows + 2 * h_rows :])
    small = jnp.concatenate(small, axis=0)
    router_ref[:, :half] = small[:EXPERTS]
    router_ref[:, half:] = small[EXPERTS : 2 * EXPERTS]
    gain_ref[0:half] = small[2 * EXPERTS]
    gain_ref[half:] = small[2 * EXPERTS + 1]
    gain1_ref[...] = gain1_rows_ref[0]
    for copy in moves:
        copy.wait()


def unpack_call(sums, gain1_rows, block, grad, q_width, k_width, heads_shape):
    ways = sums.shape[0]
    width = heads_shape[1]
    shape = jax.ShapeDtypeStruct
    return pl.pallas_call(
        unpack_kernel,
        out_shape=(
            shape((width, q_width), F32), shape((width, k_width), F32), shape((width, k_width), F32), shape(heads_shape, F32),
            shape((EXPERTS, width), F32), shape((width,), F32), shape((width,), F32), shape(block.shape, BF), shape(grad.shape, BF),
        ),
        in_specs=vmem(2) + [pl.BlockSpec(memory_space=pl.ANY)] * 2,
        out_specs=tuple(vmem(7)) + (pl.BlockSpec(memory_space=pl.ANY),) * 2,
        scratch_shapes=[pltpu.SemaphoreType.DMA((2,))],
        compiler_params=params(60),
        cost_estimate=pl.CostEstimate(flops=MIB, bytes_accessed=5 * MIB, transcendentals=0),
        name="unpack",
    )(sums, gain1_rows, block, grad)


def on_device(
    tokens, cotangent, seq_lengths, deal_order, routes, slot_order, first_gain, w_query, w_key, w_value, w_out,
    second_gain, w_router, w_gate, w_up, w_down,
):
    dp_count = lax.axis_size("dp")
    dp_index = lax.axis_index("dp")
    tensor_count = lax.axis_size("tensor")
    tensor_index = lax.axis_index("tensor")
    expert_count = lax.axis_size("expert")
    expert_index = lax.axis_index("expert")
    rows, width = tokens.shape
    share = rows // tensor_count
    everywhere = ("expert", "dp", "tensor")
    unit_shape = (expert_count, dp_count, rows, width)

    cosine, sine = (jnp.asarray(values) for values in rotary_tables(rows))
    gain1, gain2 = first_gain, second_gain
    router_t = w_router.T
    normed, q, k, v, heads, logsum, hidden, normed_share, tables, far_dy, x_own, dy_own = front(
        seq_lengths, deal_order, tokens, gain1, w_query, w_key, w_value, w_out, cosine, sine, gain2, routes.T, slot_order, cotangent
    )
    never = seq_lengths[0, 0] < 0
    rows_all = ("expert", "dp")

    def after(values, other):
        return jnp.where(never, other.astype(values.dtype), values)

    small_mesh = expert_count == 2
    out_c, out_g, xs_own, ys_own, x_other, dy_other, gates = own_call(
        x_own, dy_own, tables, router_t, w_gate, w_up, w_down, hidden, normed_share, far_dy
    )
    group_count = expert_count
    if not small_mesh:
        out_c = lax.psum_scatter(out_c, "expert", scatter_dimension=0, tiled=True)
        out_g = lax.psum_scatter(out_g, "expert", scatter_dimension=0, tiled=True)
        x_own = lax.dynamic_slice_in_dim(x_own, expert_index, 1, 0)
        group_count = 1
    first, stat, hidden_grad, scale, dense, heads_grad, small, *out_passed = back_call(
        group_count, seq_lengths,
        (cotangent, tokens, gain1, gain2, router_t, hidden, tables, normed, q, k, v, heads, logsum,
         w_query, w_key, w_value, w_out, cosine, sine),
        out_g, x_own, *((out_c,) if small_mesh else ()),
    )
    local = w_gate.shape[0]
    q_width, k_width = w_query.shape[1], w_key.shape[1]
    half, columns = width // 2, width // tensor_count
    if small_mesh:
        _, xs, ys, sums, input_grad, block_out, gain1_rows = slots_call(
            tuple(range(1, dp_count)), x_other, dy_other, tables, gates, local,
            (dense, heads_grad, small, first, out_passed[0], hidden_grad, tokens, stat, scale, gain1),
        )
        ways = expert_count * dp_count
        sums = lax.all_gather(sums, rows_all, axis=0)
        gate_grad, up_grad, down_grad = weights_call([(xs_own, ys_own), (xs, ys)], w_gate, w_up, w_down)
        q_sum, k_sum, v_sum, out_sum, router_rows, gain2_sum, gain1_sum, block_out, input_grad = unpack_call(
            sums, gain1_rows, block_out, input_grad, q_width, k_width, w_out.shape
        )
        router_sum = router_rows.T
    else:
        grads = weights_call([(xs_own, ys_own)], w_gate, w_up, w_down)
        for mask in range(1, dp_count):
            moved = (
                lax.all_gather(
                    after(values[mask - 1], grads[2][0, 0, 0]), ("expert", "tensor"), axis=0, tiled=True
                ).reshape(1, expert_count, rows, width)
                for values in (
                    [lax.ppermute(normed_share, "dp", [(i, i ^ m) for i in range(dp_count)]) for m in range(1, dp_count)],
                    far_dy,
                )
            )
            far_gates = lax.ppermute(gates, "dp", [(i, i ^ mask) for i in range(dp_count)])[None]
            xs, ys = slots_call((mask,), *moved, tables, far_gates, local)
            grads = weights_call([(xs, ys)], w_gate, w_up, w_down, grads)
        gate_grad, up_grad, down_grad = grads
        dense_sum, out_sum, small_sum = (
            values.astype(F32) for values in lax.psum((dense, heads_grad, small), rows_all)
        )
        gain1_sum = lax.psum(stat[0, rows:], everywhere)
        q_sum, k_sum, v_sum = jnp.split(dense_sum, [q_width, q_width + k_width], axis=1)
        router_sum = jnp.concatenate([small_sum[:EXPERTS], small_sum[EXPERTS : 2 * EXPERTS]], axis=1)
        gain2_sum = small_sum[2 * EXPERTS : 2 * EXPERTS + 2].reshape(width)
        router_sum = router_sum.T
        block_out = lax.psum_scatter(out_c[0], "tensor", scatter_dimension=0, tiled=True)[0]
        first_sum = lax.psum_scatter(first, "tensor", scatter_dimension=0, tiled=True)[0].astype(F32)
        mean = lax.psum(stat[0, :rows], "tensor")[:, None] / width

        def cols(values):
            return lax.dynamic_slice_in_dim(values, tensor_index * columns, columns, -1).astype(F32)

        input_grad = (
            hidden_grad.astype(F32) + scale[:, :1] * (first_sum * cols(gain1) - cols(tokens) * scale[:, :1] * mean)
        ).astype(BF)
    return (
        block_out, input_grad, gain1_sum, q_sum, k_sum, v_sum, out_sum, gain2_sum, router_sum,
        gate_grad, up_grad, down_grad,
    )


def solution(mesh):
    rows2 = P(("expert", "dp"), None)
    placed = (
        rows2, rows2, P("expert", None), P("expert", None), rows2, rows2, P(),
        P(None, "tensor"), P(None, "tensor"), P(None, "tensor"), P("tensor", None), P(), P(),
        P("expert", None, "tensor"), P("expert", None, "tensor"), P("expert", "tensor", None),
    )
    return jax.shard_map(
        on_device,
        mesh=mesh,
        in_specs=placed,
        out_specs=(
            P(("expert", "dp"), "tensor"), P(("expert", "dp"), "tensor"), P(),
            P(None, "tensor"), P(None, "tensor"), P(None, "tensor"), P("tensor", None), P(), P(),
            P("expert", None, "tensor"), P("expert", None, "tensor"), P("expert", "tensor", None),
        ),
        check_vma=False,
    )
```
